32 devices in a mesh: seq: 8 (over z, x), doc: 4 (over y, core).
Axes of the slice: x: 2, y: 2, z: 4, core: 2. Of those that a mesh axis runs over, the one named last changes fastest.
Arguments:
- tokens: bfloat16 [4, 3072, 1024], P('doc', 'seq'), may hold values from -7 to 7
- doc_lengths: int32 [4, 4], P('doc'), may hold values from 1 to 2752, as said below
- out_grad: bfloat16 [4, 3072, 1024], P('doc', 'seq'), may hold values from -6 to 6
- first_gain: float32 [1024], replicated, may hold values from 0.5 to 1.5
- query_weight: bfloat16 [1024, 1024], replicated, may hold values from -0.1875 to 0.1875
- key_weight: bfloat16 [1024, 1024], replicated, may hold values from -0.1875 to 0.1875
- value_weight: bfloat16 [1024, 1024], replicated, may hold values from -0.1875 to 0.1875
- gate_weight: bfloat16 [1024, 1024], replicated, may hold values from -0.1875 to 0.1875
- beta_weight: bfloat16 [1024, 8], replicated, may hold values from -1 to 1
- conv_weight: float32 [3, 4, 1024], replicated, may hold values from -3 to 3
- head_gain: float32 [128], replicated, may hold values from 0.5 to 1.5
- out_weight: bfloat16 [1024, 1024], replicated, may hold values from -0.1875 to 0.1875
- second_gain: float32 [1024], replicated, may hold values from 0.5 to 1.5
- hidden_gate: bfloat16 [1024, 2816], replicated, may hold values from -0.1875 to 0.1875
- hidden_up: bfloat16 [1024, 2816], replicated, may hold values from -0.1875 to 0.1875
- hidden_down: bfloat16 [2816, 1024], replicated, may hold values from -0.109375 to 0.109375
Outputs:
- block_out: bfloat16 [4, 3072, 1024], P('doc', 'seq')
- input_grad: bfloat16 [4, 3072, 1024], P('doc', 'seq')
- first_gain_grad: float32 [1024], P('seq')
- query_grad: float32 [1024, 1024], P('seq')
- key_grad: float32 [1024, 1024], P('seq')
- value_grad: float32 [1024, 1024], P('seq')
- gate_grad: float32 [1024, 1024], P('seq')
- beta_grad: float32 [1024, 8], P('seq')
- conv_grad: float32 [3, 4, 1024], P(None, None, 'seq')
- head_gain_grad: float32 [128], P('seq')
- out_grad_weight: float32 [1024, 1024], P('seq')
- second_gain_grad: float32 [1024], P('seq')
- hidden_gate_grad: float32 [1024, 2816], P('seq')
- hidden_up_grad: float32 [1024, 2816], P('seq')
- hidden_down_grad: float32 [2816, 1024], P('seq')
The draws below stay inside these ranges and needn't reach their ends.
Inputs may be any that keep to these rules, and one draw needn't show every extreme that they name: `doc_lengths`: in each group the lengths rounded up to multiples of 64 add up to 3072; one document of each group, at a place drawn from the seed, has exactly 2752 tokens and the others fill the remaining 384 - 64 slots; some document of each group has a single token.
All inputs are finite; a program needn't handle non-finite values.
Results may differ from the reference program's by a relative error of at most 0.011.
Values sent between devices are 32-bit elements; how exact they have to be, the bound alone decides.
No kernel may reach another device: no remote copies, remote signals or barrier semaphores. Data moves between devices by JAX's collectives and lax.ppermute only.
A program may use at most 384 MiB of HBM per device.

```python
import jax
import jax.numpy as jnp
from jax import lax

D = 1024
H = 8
DK = 128
FF = 2816
CW = 4
CK = 64
NDOC = 4
TOK_DEV = 384
SEQ_TOK = 3072
GROUPS = 4


def common_signs(key):
    return jnp.where(jax.random.bernoulli(key, 0.5, (D,)), 1.0, -1.0).astype(jnp.float32)


def draw_tokens(key, part):
    signs = common_signs(key)
    key = jax.random.fold_in(key, 21)
    noise = jnp.clip(jax.random.normal(key, (GROUPS, SEQ_TOK, D), jnp.float32), -6.0, 6.0)
    return (noise + 0.3 * signs[None, None, :]).astype(jnp.bfloat16)


def draw_beta_weight(key, part):
    signs = common_signs(key)
    key = jax.random.fold_in(key, 23)
    noise_key, order_key, shift_key = jax.random.split(key, 3)
    noise = jnp.clip(jax.random.normal(noise_key, (D, H), jnp.float32), -6.0, 6.0) * D ** (-0.5)
    ranks = jax.random.permutation(order_key, H).astype(jnp.int32)
    slow_count = H // 2
    slow = (ranks < slow_count).astype(jnp.float32)[None, :]
    shift = jax.random.uniform(shift_key, (H,), jnp.float32, -6.5, -5.5)
    column = signs[:, None] * shift[None, :] * (3.5 / D)
    weight = noise * (1.0 - 0.5 * slow) + slow * column
    return weight.astype(jnp.bfloat16)


def draw_doc_lengths(key, part):
    key = jax.random.fold_in(key, 11)
    cut_key, order_key, long_key, pad_key = jax.random.split(key, 4)
    spans_all = SEQ_TOK // CK
    per_device = TOK_DEV // CK
    spare = per_device - NDOC
    cuts = jnp.sort(jax.random.randint(cut_key, (GROUPS, NDOC - 3), 0, spare + 1).astype(jnp.int32), 1)
    bounds = jnp.concatenate([jnp.zeros((GROUPS, 1), jnp.int32), cuts, jnp.full((GROUPS, 1), spare, jnp.int32)], 1)
    pieces = (1 + bounds[:, 1:] - bounds[:, :-1]).astype(jnp.int32)
    small = jnp.concatenate([jnp.ones((GROUPS, 1), jnp.int32), pieces], 1)
    pads_small = jax.random.randint(pad_key, (GROUPS, NDOC - 1), 0, CK).astype(jnp.int32)
    first_slot = (jnp.arange(NDOC - 1, dtype=jnp.int32) == 0)[None, :]
    pads_small = jnp.where(first_slot, CK - 1, pads_small).astype(jnp.int32)
    order_keys = jax.random.split(order_key, GROUPS)
    orders = jax.vmap(lambda batch_entry: jax.random.permutation(batch_entry, NDOC - 1))(order_keys).astype(jnp.int32)
    small = jnp.take_along_axis(small, orders, 1).astype(jnp.int32)
    pads_small = jnp.take_along_axis(pads_small, orders, 1).astype(jnp.int32)
    small_len = (small * CK - pads_small).astype(jnp.int32)
    long_len = jnp.full((GROUPS, 1), (spans_all - per_device + 1) * CK, jnp.int32)
    where = jax.random.randint(long_key, (GROUPS, 1), 0, NDOC).astype(jnp.int32)
    slot = jnp.arange(NDOC, dtype=jnp.int32)[None, :]
    filler = jnp.zeros((GROUPS, 1), jnp.int32)
    before = jnp.concatenate([small_len, filler], 1)
    after = jnp.concatenate([filler, small_len], 1)
    return jnp.where(slot < where, before, jnp.where(slot == where, long_len, after)).astype(jnp.int32)


def shard_levels(own_key, extent, shards, least, high):
    level, own = 1.0, jax.random.fold_in(own_key, 6)
    for dim, shards_of in shards:
        steps = jnp.exp(jax.random.uniform(jax.random.fold_in(own, dim), (shards_of,), jnp.float32, least / len(shards), high / len(shards)))
        level = level * jnp.repeat(steps, extent[dim] // shards_of).reshape([-1 if axis == dim else 1 for axis in range(len(extent))])
    return level


def normal_values(stream_key, extent, spread, limit, shards=(), held_as=jnp.bfloat16):
    array = jax.random.normal(stream_key, extent, jnp.float32) * spread
    if len(shards) > 0:
        array = shard_levels(stream_key, extent, shards, -0.22, 0.18) * array
    return jnp.clip(array, min=-limit, max=limit).astype(held_as)


def setup_inputs(seed: int = 0) -> dict:
    keys = jax.random.split(jax.random.key(seed), 17)
    return {
        "tokens": draw_tokens(jax.random.fold_in(keys[16], 71), 0),
        "doc_lengths": draw_doc_lengths(jax.random.fold_in(keys[16], 71), 0),
        "out_grad": normal_values(keys[2], (GROUPS, SEQ_TOK, D), 1.0, 6.0, ((0, 4), (1, 8))),
        "first_gain": jnp.clip(1.0 + 0.1 * jax.random.normal(keys[3], (D,), jnp.float32), 0.5, 1.5),
        "query_weight": normal_values(keys[4], (D, D), D ** -0.5, 0.1875),
        "key_weight": normal_values(keys[5], (D, D), D ** -0.5, 0.1875),
        "value_weight": normal_values(keys[6], (D, D), D ** -0.5, 0.1875),
        "gate_weight": normal_values(keys[7], (D, D), D ** -0.5, 0.1875),
        "beta_weight": draw_beta_weight(jax.random.fold_in(keys[16], 71), 0),
        "conv_weight": normal_values(keys[9], (3, CW, D), CW ** -0.5, 3.0, (), jnp.float32),
        "head_gain": jnp.clip(1.0 + 0.1 * jax.random.normal(keys[10], (DK,), jnp.float32), 0.5, 1.5),
        "out_weight": normal_values(keys[11], (D, D), D ** -0.5, 0.1875),
        "second_gain": jnp.clip(1.0 + 0.1 * jax.random.normal(keys[12], (D,), jnp.float32), 0.5, 1.5),
        "hidden_gate": normal_values(keys[13], (D, FF), D ** -0.5, 0.1875),
        "hidden_up": normal_values(keys[14], (D, FF), D ** -0.5, 0.1875),
        "hidden_down": normal_values(keys[15], (FF, D), FF ** -0.5, 0.109375),
    }


EPS = 1e-05
KEY_EPS = 1e-06
HIGH = lax.Precision.HIGHEST

@jax.custom_vjp
def low(v):
    return lax.optimization_barrier(v.astype(jnp.bfloat16)).astype(jnp.float32)

@jax.custom_vjp
def low_back(v):
    return v

def low_keep(v):
    return (low(v), None)

def low_pass(kept, grad):
    return (grad,)

def back_keep(v):
    return (v, None)

def back_low(kept, grad):
    return (low(grad),)
low.defvjp(low_keep, low_pass)
low_back.defvjp(back_keep, back_low)

def linear_map_result(form, left, right):
    return jnp.einsum(form, left, right, precision=HIGH)

def matmul(left, right):
    return jnp.dot(left, right, precision=HIGH)

def root_norm(value, gain):
    return value * lax.rsqrt(lax.optimization_barrier(jnp.mean(value * value, -1, keepdims=True)) + EPS) * gain

def unit_norm(value):
    return value * lax.rsqrt(lax.optimization_barrier(jnp.sum(value * value, -1, keepdims=True)) + KEY_EPS)

def doc_info(lengths, first, count):
    padded = ((lengths + CK - 1) // CK * CK).astype(jnp.int32)
    ends = jnp.cumsum(padded).astype(jnp.int32)
    starts = (ends - padded).astype(jnp.int32)
    place = first + jnp.arange(count, dtype=jnp.int32)
    inside = ((place[:, None] >= starts[None, :]) & (place[:, None] < ends[None, :])).astype(jnp.int32)
    position = (place - lax.optimization_barrier(jnp.sum(inside * starts[None, :], 1))).astype(jnp.int32)
    length = lax.optimization_barrier(jnp.sum(inside * lengths[None, :], 1)).astype(jnp.int32)
    live = (position < length).astype(jnp.float32)
    return (position, live)

def short_conv(extended, weight, position):
    count = position.shape[0]
    width = weight.shape[0]
    running_total = jnp.zeros((count, extended.shape[1]), jnp.float32)
    for tap in range(width):
        valid = (position >= width - 1 - tap).astype(jnp.float32)[:, None]
        running_total = running_total + weight[tap][None, :] * extended[tap:tap + count] * valid
    return jax.nn.silu(running_total)

def features(extended, conv_weight, beta_pre, position, live, head_count):
    weight = conv_weight.transpose(1, 0, 2).reshape(conv_weight.shape[1], -1)
    mixed = short_conv(extended, weight, position)
    count = mixed.shape[0]
    width = mixed.shape[1] // 3
    query = unit_norm(mixed[:, :width].reshape(count, head_count, -1)).reshape(count, width)
    key_rows = (unit_norm(mixed[:, width:2 * width].reshape(count, head_count, -1)) * live[:, None, None]).reshape(count, width)
    values = mixed[:, 2 * width:]
    betas = jax.nn.sigmoid(beta_pre) * live[:, None]
    return (query, key_rows, values, betas)

def to_spans(flat, head_count, size):
    count, width = flat.shape
    return flat.reshape(count // size, size, head_count, width // head_count).transpose(0, 2, 1, 3)

def beta_spans(betas, size):
    count, head_count = betas.shape
    return betas.reshape(count // size, size, head_count).transpose(0, 2, 1)

def from_spans(blocks):
    number, head_count, size, layer_count = blocks.shape
    return blocks.transpose(0, 2, 1, 3).reshape(number * size, head_count * layer_count)

def lower_inverse(strict):
    size = strict.shape[-1]
    identity_matrix = jnp.eye(size, dtype=jnp.float32)
    result = identity_matrix - strict
    power = strict
    for level in range(1, size.bit_length() - 1):
        power = linear_map_result('...ij,...jk->...ik', power, power)
        result = linear_map_result('...ij,...jk->...ik', result, identity_matrix + power)
    return result

def span_prep(query, key_rows, values, betas):
    size = key_rows.shape[2]
    lower = jnp.tril(jnp.ones((size, size), jnp.float32), -1)
    inclusive = jnp.tril(jnp.ones((size, size), jnp.float32))
    scores = linear_map_result('bhid,bhjd->bhij', key_rows, key_rows)
    solved = lower_inverse(betas[..., :, None] * scores * lower)
    erase_terms = linear_map_result('bhij,bhjd->bhid', solved, betas[..., None] * key_rows)
    updates = linear_map_result('bhij,bhjd->bhid', solved, betas[..., None] * values)
    attend = linear_map_result('bhid,bhjd->bhij', query, key_rows) * inclusive
    state_loader = query - linear_map_result('bhij,bhjd->bhid', attend, erase_terms)
    local_state = linear_map_result('bhij,bhjd->bhid', attend, updates)
    identity_matrix = jnp.eye(key_rows.shape[3], dtype=jnp.float32)
    recurrent_memory_slot = identity_matrix - linear_map_result('pfxt,pfxa->pfta', key_rows, erase_terms)
    feature_supplier = linear_map_result('pfxt,pfxa->pfta', key_rows, updates)
    return (state_loader, local_state, recurrent_memory_slot, feature_supplier)

def span_run(data, keep_mask, state):

    def scan_step(carried_state, batch_entry):
        state_loader, local_state, recurrent_memory_slot, feature_supplier, genuine_token_flag = batch_entry
        interval_first_place = carried_state * genuine_token_flag
        residual_unit_result = linear_map_result('hid,hde->hie', state_loader, interval_first_place) + local_state
        return (linear_map_result('jlr,jrd->jld', recurrent_memory_slot, interval_first_place) + feature_supplier, residual_unit_result)
    final, outputs = lax.scan(scan_step, state, data + (keep_mask,))
    return (outputs, final)

def head_norm(mixed, gate_pre, gain, head_count):
    count, width = mixed.shape
    shaped = root_norm(mixed.reshape(count, head_count, -1), gain)
    return (shaped * jax.nn.silu(gate_pre.reshape(count, head_count, -1))).reshape(count, width)

def block(tokens, first_gain, query_weight, key_weight, value_weight, gate_weight, beta_weight, conv_weight, head_gain, out_weight, second_gain, hidden_gate, hidden_up, hidden_down, position, live, keep_mask):
    normed_one = low(root_norm(tokens, first_gain))
    query_pre = low_back(matmul(normed_one, query_weight))
    key_pre = low_back(matmul(normed_one, key_weight))
    value_pre = low_back(matmul(normed_one, value_weight))
    gate_pre = low_back(matmul(normed_one, gate_weight))
    beta_pre = low_back(matmul(normed_one, beta_weight))
    mixed_pre = jnp.concatenate([query_pre, key_pre, value_pre], 1)
    extended = jnp.concatenate([jnp.zeros((CW - 1, 3 * D), jnp.float32), mixed_pre], 0)
    query, key_rows, values, betas = features(extended, conv_weight, beta_pre, position, live, H)
    data = span_prep(to_spans(query, H, CK), to_spans(key_rows, H, CK), to_spans(values, H, CK), beta_spans(betas, CK))
    outputs, final = span_run(data, keep_mask, jnp.zeros((H, DK, DK), jnp.float32))
    normed_head = low(head_norm(from_spans(outputs), gate_pre, head_gain, H))
    hidden_state = tokens + low_back(matmul(normed_head, out_weight))
    normed_two = low(root_norm(hidden_state, second_gain))
    gate = low_back(matmul(normed_two, hidden_gate))
    up = low_back(matmul(normed_two, hidden_up))
    inner = low(jax.nn.silu(gate) * up)
    return hidden_state + low_back(matmul(inner, hidden_down))

def reference(tokens, doc_lengths, out_grad, first_gain, query_weight, key_weight, value_weight, gate_weight, beta_weight, conv_weight, head_gain, out_weight, second_gain, hidden_gate, hidden_up, hidden_down):
    weights = tuple((batch_entry.astype(jnp.float32) for batch_entry in (first_gain, query_weight, key_weight, value_weight, gate_weight, beta_weight, conv_weight, head_gain, out_weight, second_gain, hidden_gate, hidden_up, hidden_down)))
    inputs = tokens.astype(jnp.float32)
    cotangents = out_grad.astype(jnp.float32)

    def one_group(totals, group):
        values, cotangent, lengths = group
        position, live = doc_info(lengths, jnp.int32(0), SEQ_TOK)
        keep_mask = 1.0 - (position[::CK] == 0).astype(jnp.float32)

        def forward(interval_first_place, *params):
            return block(interval_first_place, *params, position, live, keep_mask)
        result, pull = jax.vjp(forward, values, *weights)
        gradient_list = pull(cotangent)
        totals = tuple((left + right for left, right in zip(totals, gradient_list[1:])))
        return (totals, (result.astype(jnp.bfloat16), gradient_list[0].astype(jnp.bfloat16)))
    interval_first_place = tuple((jnp.zeros_like(batch_entry) for batch_entry in weights))
    totals, (outputs, input_grads) = lax.scan(one_group, interval_first_place, (inputs, cotangents, doc_lengths))
    return (outputs, input_grads, totals[0], totals[1], totals[2], totals[3], totals[4], totals[5], totals[6], totals[7], totals[8], totals[9], totals[10], totals[11], totals[12])
```

```python
import jax
import jax.numpy as jnp
from jax import lax
from jax.experimental import pallas as pl
from jax.experimental.pallas import tpu as pltpu
from jax.sharding import PartitionSpec as P

CK = 64


EPS = 1e-05
KEY_EPS = 1e-06
HIGH = lax.Precision.HIGHEST


def doc_info(lengths, first, count):
    padded = (lengths + CK - 1) // CK * CK
    ends = jnp.cumsum(padded)
    starts = ends - padded
    place = first + jnp.arange(count, dtype=jnp.int32)
    inside = ((place[:, None] >= starts[None, :]) & (place[:, None] < ends[None, :])).astype(
        jnp.int32
    )
    position = place - jnp.sum(inside * starts[None, :], 1)
    length = jnp.sum(inside * lengths[None, :], 1)
    live = (position < length).astype(jnp.float32)
    return (position, live)


SPAN = CK
LANES = 128
LOW = jnp.bfloat16
NN = (((1,), (0,)), ((), ()))
NT = (((1,), (1,)), ((), ()))
TN = (((0,), (0,)), ((), ()))


def params(mib=48):
    return pltpu.CompilerParams(vmem_limit_bytes=mib * 2**20)


def cost(flops, moved):
    return pl.CostEstimate(flops=int(flops), bytes_accessed=int(moved), transcendentals=0)


def mxu(left, right, dims):
    return lax.dot_general(left, right, dims, preferred_element_type=jnp.float32)


def halves(value):
    high = value.astype(LOW)
    return high, (value - high.astype(jnp.float32)).astype(LOW)


def fold(value):
    half = value.shape[1] // 2
    return value[:, :half] + value[:, half:]


def product(left, right):
    left_high, left_low = halves(left)
    right_high, right_low = halves(right)
    both = jnp.concatenate([left_high, left_low], 1)
    if right.shape[1] <= LANES:
        wide = jnp.concatenate([right_high, right_low], 1)
        return fold(mxu(both, jnp.concatenate([wide, wide], 0), NN))
    return mxu(both, jnp.concatenate([right_high, right_high], 0), NN) + mxu(
        left_high, right_low, NN
    )


def product_t(left, right):
    left_high, left_low = halves(left)
    right_high, right_low = halves(right)
    both = jnp.concatenate([left_high, left_low], 1)
    if right.shape[0] <= LANES:
        rows = jnp.concatenate(
            [
                jnp.concatenate([right_high, right_high], 1),
                jnp.concatenate([right_low, right_low], 1),
            ],
            0,
        )
        return fold(mxu(both, rows, NT))
    return mxu(both, jnp.concatenate([right_high, right_high], 1), NT) + mxu(
        left_high, right_low, NT
    )


def t_product(left, right):
    left_high, left_low = halves(left)
    right_high, right_low = halves(right)
    both = jnp.concatenate([left_high, left_low], 0)
    if right.shape[1] <= LANES:
        wide = jnp.concatenate([right_high, right_low], 1)
        return fold(mxu(both, jnp.concatenate([wide, wide], 0), TN))
    return mxu(both, jnp.concatenate([right_high, right_high], 0), TN) + mxu(
        left_high, right_low, TN
    )


def head(value, h):
    return value[:, h * LANES : (h + 1) * LANES]


def pair(value, p):
    return jnp.concatenate([head(value, 2 * p), head(value, 2 * p + 1)], 0)


def pair_column(value, p):
    return jnp.concatenate([value[:, 2 * p : 2 * p + 1], value[:, 2 * p + 1 : 2 * p + 2]], 0)


def masks(rows):
    i = lax.broadcasted_iota(jnp.int32, (rows, rows), 0)
    j = lax.broadcasted_iota(jnp.int32, (rows, rows), 1)
    same = (i >= SPAN) == (j >= SPAN)
    strict = jnp.where(same & (j < i), 1.0, 0.0)
    inclusive = jnp.where(same & (j <= i), 1.0, 0.0)
    upper = jnp.where(same & (j >= i), 1.0, 0.0)
    return strict, inclusive, upper, jnp.where(i == j, 1.0, 0.0)


def inverse(strict_part, identity):
    rows = strict_part.shape[0]
    result = identity - strict_part
    power = product(strict_part, strict_part)
    for level in range(SPAN.bit_length() - 3):
        both = product(jnp.concatenate([result, power], 0), power)
        result = result + both[:rows]
        power = both[rows:]
    return result + product(result, power)


def sigmoid(value):
    return 1.0 / (1.0 + jnp.exp(-value))


HALO = 16


def project_kernel(
    tokens, halo, gain, position, live, query_w, key_w, value_w, gate_w, beta_w, conv,
    normed_out, pre_out, feature_out, gate_out, beta_pre_out, beta_out, normed,
):
    count = tokens.shape[0]

    @pl.when(pl.program_id(0) == 0)
    def _():
        def norm(rows):
            return (
                rows * lax.rsqrt(jnp.mean(rows * rows, -1, keepdims=True) + EPS) * gain[...]
            ).astype(LOW)

        normed[:HALO, :] = norm(halo[...])
        rounded = norm(tokens[...].astype(jnp.float32))
        normed[HALO:, :] = rounded
        normed_out[...] = rounded.astype(jnp.float32).T
        beta_pre = mxu(rounded, beta_w[...], NN)
        beta_pre_out[...] = beta_pre
        beta_out[...] = sigmoid(beta_pre) * live[...]

    gate_out[...] = mxu(normed[HALO:, :], gate_w[...], NN)
    valid = [
        jnp.where(position[...] >= conv.shape[1] - 1 - tap, 1.0, 0.0)
        for tap in range(conv.shape[1])
    ]
    for which, weight in enumerate((query_w, key_w, value_w)):
        pre_out[which] = mxu(normed[...], weight[...], NN)
        for part in range(pre_out.shape[2] // LANES):
            lanes = slice(part * LANES, (part + 1) * LANES)
            total = conv_total(pre_out, which, HALO, count, lanes, conv, valid)
            value = total * sigmoid(total)
            if which < 2:
                value = value * lax.rsqrt(jnp.sum(value * value, -1, keepdims=True) + KEY_EPS)
            if which == 1:
                value = value * live[...]
            feature_out[which, :, lanes] = value


def conv_total(pre, which, first, count, lanes, conv, valid):
    taps = conv.shape[1]
    total = None
    for tap in range(taps):
        start = first - (taps - 1) + tap
        term = conv[which, tap : tap + 1, lanes] * pre[which, start : start + count, lanes] * valid[tap]
        total = term if total is None else total + term
    return total


def project(tokens, halo, gain, position, live, query_w, key_w, value_w, gate_w, beta_w, conv):
    count, width = tokens.shape
    heads = beta_w.shape[1]
    block = 2 * LANES
    whole = lambda shape: pl.BlockSpec(shape, lambda j: (0,) * len(shape))
    weight = pl.BlockSpec((width, block), lambda j: (0, j))
    f32 = lambda shape: jax.ShapeDtypeStruct(shape, jnp.float32)
    return pl.pallas_call(
        project_kernel,
        grid=(width // block,),
        in_specs=[
            whole((count, width)), whole((HALO, width)), whole((1, width)), whole((count, 1)),
            whole((count, 1)), weight, weight, weight, weight, whole((width, heads)),
            pl.BlockSpec((3, conv.shape[1], block), lambda j: (0, 0, j)),
        ],
        out_specs=[
            whole((width, count)),
            pl.BlockSpec((3, HALO + count, block), lambda j: (0, 0, j)),
            pl.BlockSpec((3, count, block), lambda j: (0, 0, j)),
            pl.BlockSpec((count, block), lambda j: (0, j)),
            whole((count, heads)), whole((count, heads)),
        ],
        out_shape=[
            f32((width, count)), f32((3, HALO + count, width)), f32((3, count, width)),
            f32((count, width)), f32((count, heads)), f32((count, heads)),
        ],
        scratch_shapes=[pltpu.VMEM((HALO + count, width), LOW)],
        compiler_params=params(),
        cost_estimate=cost(8 * count * width * width, 8 * width * width + 40 * count * width),
        name="project",
    )(tokens, halo, gain, position, live, query_w, key_w, value_w, gate_w, beta_w, conv)


def prepare_kernel(keep, features, beta, solved_out, inverse_out, attend_out, state):
    span = pl.program_id(0)
    heads = state.shape[0]
    size = state.shape[1]
    strict, inclusive, upper, identity = masks(2 * SPAN)

    @pl.when(span == 0)
    def _():
        i = lax.broadcasted_iota(jnp.int32, (size, 2 * size), 0)
        j = lax.broadcasted_iota(jnp.int32, (size, 2 * size), 1)
        for h in range(heads):
            state[h] = jnp.where(j == i + size, 1.0, 0.0)

    query, key, value = features[0], features[1], features[2]
    betas = beta[...]
    flag = keep[span]
    for p in range(heads // 2):
        q, k, v, b = pair(query, p), pair(key, p), pair(value, p), pair_column(betas, p)
        scores = product_t(jnp.concatenate([k, q], 0), k)
        solved = inverse(b * scores[: 2 * SPAN] * strict, identity)
        both = product(solved, jnp.concatenate([b * k, b * v], 1))
        inverse_out[0, p] = solved
        attend_out[0, p] = scores[2 * SPAN :] * inclusive
        for i in range(2):
            h = 2 * p + i
            erase = both[i * SPAN : (i + 1) * SPAN, :size]
            update = both[i * SPAN : (i + 1) * SPAN, size:]
            solved_out[0, :, h * size : (h + 1) * size] = erase
            solved_out[1, :, h * size : (h + 1) * size] = update
            start = state[h] * flag
            new = jnp.concatenate([update, jnp.zeros_like(update)], 1) - product(erase, start)
            state[h] = start + t_product(head(key, h), new)


def prepare(keep, features, beta):
    _, count, width = features.shape
    heads = beta.shape[1]
    size = width // heads
    spans = count // SPAN
    f32 = lambda shape: jax.ShapeDtypeStruct(shape, jnp.float32)
    matrix = pl.BlockSpec((1, heads // 2, 2 * SPAN, 2 * SPAN), lambda c: (c, 0, 0, 0))
    return pl.pallas_call(
        prepare_kernel,
        grid=(spans,),
        in_specs=[
            pl.BlockSpec(memory_space=pltpu.SMEM),
            pl.BlockSpec((3, SPAN, width), lambda c: (0, c, 0)),
            pl.BlockSpec((SPAN, heads), lambda c: (c, 0)),
        ],
        out_specs=[
            pl.BlockSpec((2, SPAN, width), lambda c: (0, c, 0)), matrix, matrix,
            pl.BlockSpec((heads, size, 2 * size), lambda c: (0, 0, 0)),
        ],
        out_shape=[
            f32((2, count, width)), f32((spans, heads // 2, 2 * SPAN, 2 * SPAN)),
            f32((spans, heads // 2, 2 * SPAN, 2 * SPAN)), f32((heads, size, 2 * size)),
        ],
        compiler_params=params(),
        cost_estimate=cost(40 * count * width * size * 4, 60 * count * width),
        name="prepare",
    )(keep, features, beta)


def mix_kernel(
    keep, features, solved, attend, gate, gain, state_in, starts_out, new_out, mixed_out, normed_out,
    state,
):
    span = pl.program_id(0)
    heads = state.shape[0]

    @pl.when(span == 0)
    def _():
        state[...] = state_in[...]

    query, key = features[0], features[1]
    erase, update = solved[0], solved[1]
    flag = keep[span]
    for p in range(heads // 2):
        reads, news = [], []
        for h in (2 * p, 2 * p + 1):
            start = state[h] * flag
            starts_out[0, h] = start
            both = product(jnp.concatenate([head(erase, h), head(query, h)], 0), start)
            new = head(update, h) - both[:SPAN]
            state[h] = start + t_product(head(key, h), new)
            new_out[:, h * LANES : (h + 1) * LANES] = new
            reads.append(both[SPAN:])
            news.append(new)
        mixed = jnp.concatenate(reads, 0) + product(attend[0, p], jnp.concatenate(news, 0))
        for i in range(2):
            lanes = slice((2 * p + i) * LANES, (2 * p + i + 1) * LANES)
            rows = mixed[i * SPAN : (i + 1) * SPAN]
            mixed_out[:, lanes] = rows
            shaped = rows * lax.rsqrt(jnp.mean(rows * rows, -1, keepdims=True) + EPS) * gain[...]
            gates = gate[:, lanes]
            normed = (shaped * (gates * sigmoid(gates))).astype(LOW)
            normed_out[:, lanes] = normed


def mix(keep, features, solved, attend, gate, gain, state_in):
    _, count, width = features.shape
    heads, size, _ = state_in.shape
    spans = count // SPAN
    f32 = lambda shape: jax.ShapeDtypeStruct(shape, jnp.float32)
    rows = pl.BlockSpec((SPAN, width), lambda c: (c, 0))
    pairs = pl.BlockSpec((2, SPAN, width), lambda c: (0, c, 0))
    return pl.pallas_call(
        mix_kernel,
        grid=(spans,),
        in_specs=[
            pl.BlockSpec(memory_space=pltpu.SMEM), pairs, pairs,
            pl.BlockSpec((1, heads // 2, 2 * SPAN, 2 * SPAN), lambda c: (c, 0, 0, 0)),
            rows, pl.BlockSpec((1, size), lambda c: (0, 0)),
            pl.BlockSpec((heads, size, size), lambda c: (0, 0, 0)),
        ],
        out_specs=[
            pl.BlockSpec((1, heads, size, size), lambda c: (c, 0, 0, 0)), rows, rows, rows,
        ],
        out_shape=[
            f32((spans, heads, size, size)), f32((count, width)), f32((count, width)),
            jax.ShapeDtypeStruct((count, width), LOW),
        ],
        scratch_shapes=[pltpu.VMEM((heads, size, size), jnp.float32)],
        compiler_params=params(),
        cost_estimate=cost(8 * count * width * size * 4, 40 * count * width),
        name="mix",
    )(keep, features, solved, attend, gate, gain, state_in)


def feed_kernel(
    core, tokens, normed_head, grad_top, second_gain, out_w, gate_w, up_w, down_w,
    block_out, normed_out, inner_out, kept_out, sent_out, grad_hidden_out, branch_out, grad_head_out,
    gain_grad_out, hidden, normed, total, grad_total,
):
    step = pl.program_id(0)

    @pl.when(step == 0)
    def _():
        state = tokens[...].astype(jnp.float32) + mxu(normed_head[...], out_w[...], NN)
        hidden[...] = state
        rounded = (
            state * lax.rsqrt(jnp.mean(state * state, -1, keepdims=True) + EPS) * second_gain[...]
        ).astype(LOW)
        normed[...] = rounded
        normed_out[...] = rounded.astype(jnp.float32).T

    gate = mxu(normed[...], gate_w[...], NN)
    up = mxu(normed[...], up_w[...], NN)
    grad_inner = mxu(grad_top[...], down_w[...], NT)
    sigma = sigmoid(gate)
    inner = (gate * sigma * up).astype(LOW)
    inner_out[...] = inner.astype(jnp.float32).T
    grad_gate = (grad_inner * up * sigma * (1.0 + gate * (1.0 - sigma))).astype(LOW)
    grad_up = (grad_inner * gate * sigma).astype(LOW)
    first = core[0] == 0
    wide_gate, wide_up = grad_gate.astype(jnp.float32), grad_up.astype(jnp.float32)
    kept_out[...] = jnp.where(first, wide_gate, wide_up).astype(LOW)
    sent_out[...] = jnp.where(first, wide_up, wide_gate)
    out_term = mxu(inner, down_w[...], NN)
    grad_term = mxu(grad_gate, gate_w[...], NT) + mxu(grad_up, up_w[...], NT)

    @pl.when(step == 0)
    def _():
        total[...] = out_term
        grad_total[...] = grad_term

    @pl.when(step > 0)
    def _():
        total[...] += out_term
        grad_total[...] += grad_term

    @pl.when(step == pl.num_programs(0) - 1)
    def _():
        state = hidden[...]
        block_out[...] = (state + total[...]).astype(LOW)
        part, gain_part = norm_back(state, second_gain[...], grad_total[...])
        gain_grad_out[...] = gain_part
        grad_hidden = grad_top[...].astype(jnp.float32) + part
        grad_hidden_out[...] = grad_hidden
        branch = grad_hidden.astype(LOW)
        branch_out[...] = branch.astype(jnp.float32)
        grad_head_out[...] = mxu(branch, out_w[...], NT)


def norm_back(value, gain, grad):
    scale = lax.rsqrt(jnp.mean(value * value, -1, keepdims=True) + EPS)
    unit = value * scale
    gain_grad = jnp.sum(grad * unit, 0, keepdims=True)
    inward = grad * gain
    return scale * (inward - unit * jnp.mean(inward * unit, -1, keepdims=True)), gain_grad


def feed(core, tokens, normed_head, grad_top, second_gain, out_w, gate_w, up_w, down_w):
    count, width = tokens.shape
    hidden = gate_w.shape[1]
    block = 2 * LANES
    whole = lambda shape: pl.BlockSpec(shape, lambda j: (0,) * len(shape))
    f32 = lambda shape: jax.ShapeDtypeStruct(shape, jnp.float32)
    low = lambda shape: jax.ShapeDtypeStruct(shape, LOW)
    rows = whole((count, width))
    columns = pl.BlockSpec((count, block), lambda j: (0, j))
    return pl.pallas_call(
        feed_kernel,
        grid=(hidden // block,),
        in_specs=[
            pl.BlockSpec(memory_space=pltpu.SMEM), rows, rows, rows, whole((1, width)),
            whole((width, width)), pl.BlockSpec((width, block), lambda j: (0, j)),
            pl.BlockSpec((width, block), lambda j: (0, j)),
            pl.BlockSpec((block, width), lambda j: (j, 0)),
        ],
        out_specs=[
            rows, whole((width, count)), pl.BlockSpec((block, count), lambda j: (j, 0)), columns,
            columns, rows, rows, rows, whole((1, width)),
        ],
        out_shape=[
            low((count, width)), f32((width, count)), f32((hidden, count)), low((count, hidden)),
            f32((count, hidden)), f32((count, width)), f32((count, width)), f32((count, width)),
            f32((1, width)),
        ],
        scratch_shapes=[
            pltpu.VMEM((count, width), jnp.float32), pltpu.VMEM((count, width), LOW),
            pltpu.VMEM((count, width), jnp.float32), pltpu.VMEM((count, width), jnp.float32),
        ],
        compiler_params=params(),
        cost_estimate=cost(
            12 * count * width * hidden + 4 * count * width * width,
            6 * width * hidden + 10 * count * hidden + 30 * count * width,
        ),
        name="feed",
    )(core, tokens, normed_head, grad_top, second_gain, out_w, gate_w, up_w, down_w)


def gather_kernel(
    keep, grad_head, mixed, gate, gain, features, solved, grad_mixed_out, grad_gate_out, gain_out,
    state,
):
    step = pl.program_id(0)
    span = pl.num_programs(0) - 1 - step
    heads = state.shape[0]
    strict, inclusive, upper, identity = masks(2 * SPAN)

    @pl.when(step == 0)
    def _():
        state[...] = jnp.zeros_like(state)
        gain_out[...] = jnp.zeros_like(gain_out)

    query, key = features[0], features[1]
    erase = solved[0]
    flag = keep[span]
    gain_total = jnp.zeros_like(gain_out[...])
    for p in range(heads // 2):
        grads = []
        for h in (2 * p, 2 * p + 1):
            lanes = slice(h * LANES, (h + 1) * LANES)
            gates = gate[:, lanes]
            sigma = sigmoid(gates)
            rows = mixed[:, lanes]
            grad = grad_head[:, lanes]
            scale = lax.rsqrt(jnp.mean(rows * rows, -1, keepdims=True) + EPS)
            unit = rows * scale
            grad_gate = grad * unit * gain[...] * sigma * (1.0 + gates * (1.0 - sigma))
            grad_gate_out[:, lanes] = grad_gate.astype(LOW).astype(jnp.float32)
            shaped = grad * gates * sigma
            gain_total = gain_total + jnp.sum(shaped * unit, 0, keepdims=True)
            inward = shaped * gain[...]
            grad_rows = scale * (inward - unit * jnp.mean(inward * unit, -1, keepdims=True))
            grad_mixed_out[:, lanes] = grad_rows
            grads.append(grad_rows)
        q, k = pair(query, p), pair(key, p)
        passed = product(product_t(k, q) * upper, jnp.concatenate(grads, 0))
        for i in range(2):
            h = 2 * p + i
            end = state[h]
            grad_new = passed[i * SPAN : (i + 1) * SPAN] + product(head(key, h), end)
            state[h] = flag * (
                end
                + t_product(
                    jnp.concatenate([head(query, h), -head(erase, h)], 0),
                    jnp.concatenate([grads[i], grad_new], 0),
                )
            )
    gain_out[...] += gain_total


def gather_states(keep, grad_head, mixed, gate, gain, features, solved, heads):
    _, count, width = features.shape
    size = width // heads
    spans = count // SPAN
    f32 = lambda shape: jax.ShapeDtypeStruct(shape, jnp.float32)
    rows = pl.BlockSpec((SPAN, width), lambda c: (spans - 1 - c, 0))
    pairs = pl.BlockSpec((2, SPAN, width), lambda c: (0, spans - 1 - c, 0))
    one = pl.BlockSpec((1, SPAN, width), lambda c: (0, spans - 1 - c, 0))
    return pl.pallas_call(
        gather_kernel,
        grid=(spans,),
        in_specs=[
            pl.BlockSpec(memory_space=pltpu.SMEM), rows, rows, rows,
            pl.BlockSpec((1, size), lambda c: (0, 0)), pairs, one,
        ],
        out_specs=[
            rows, rows, pl.BlockSpec((1, size), lambda c: (0, 0)),
            pl.BlockSpec((heads, size, size), lambda c: (0, 0, 0)),
        ],
        out_shape=[
            f32((count, width)), f32((count, width)), f32((1, size)), f32((heads, size, size)),
        ],
        compiler_params=params(),
        cost_estimate=cost(8 * count * width * size * 4, 32 * count * width),
        name="gather_states",
    )(keep, grad_head, mixed, gate, gain, features, solved)


def back_kernel(
    keep, features, beta, beta_pre, solved, inverses, starts, news, grad_mixed, state_in, pre, conv,
    position, live, grad_pre_out, borrowed_out, conv_out, grad_beta_out, state, later,
):
    step = pl.program_id(0)
    span = pl.num_programs(0) - 1 - step
    heads = state.shape[0]
    taps = conv.shape[1]
    strict, inclusive, upper, identity = masks(2 * SPAN)

    @pl.when(step == 0)
    def _():
        state[...] = state_in[...]
        conv_out[...] = jnp.zeros_like(conv_out)
        later[...] = jnp.zeros_like(later)

    @pl.when(step > 0)
    def _():
        later[:, 8 + SPAN :, :] = later[:, 8:16, :]

    query, key, value = features[0], features[1], features[2]
    erase, update = solved[0], solved[1]
    betas = beta[...]
    flag = keep[span]
    base = pl.multiple_of(span * SPAN, SPAN)
    places = position[pl.ds(base, SPAN + 16), :]
    lives = live[pl.ds(base, SPAN), :]
    valid = [jnp.where(places >= taps - 1 - tap, 1.0, 0.0) for tap in range(taps)]
    beta_columns = []
    for p in range(heads // 2):
        q, k, v, b = pair(query, p), pair(key, p), pair(value, p), pair_column(betas, p)
        grad_out = pair(grad_mixed, p)
        new = pair(news, p)
        scores = product_t(k, jnp.concatenate([k, q], 0))
        passed = product(scores[:, 2 * SPAN :] * upper, grad_out)
        grad_query, grad_key, grad_new, grad_erase = [], [], [], []
        for i in range(2):
            h = 2 * p + i
            rows = slice(i * SPAN, (i + 1) * SPAN)
            end = state[h]
            grad_new_h = passed[rows] + product(k[rows], end)
            both = product_t(jnp.concatenate([grad_out[rows], grad_new_h], 0), starts[0, h])
            grad_query.append(both[:SPAN])
            grad_erase.append(-both[SPAN:])
            grad_key.append(product_t(new[rows], end))
            grad_new.append(grad_new_h)
            state[h] = flag * (
                end
                + t_product(
                    jnp.concatenate([q[rows], -head(erase, h)], 0),
                    jnp.concatenate([grad_out[rows], grad_new_h], 0),
                )
            )
        grad_new = jnp.concatenate(grad_new, 0)
        grad_erase = jnp.concatenate(grad_erase, 0)
        grad_attend = product_t(grad_out, new) * inclusive
        grad_q = jnp.concatenate(grad_query, 0) + product(grad_attend, k)
        grad_k = jnp.concatenate(grad_key, 0) + product(grad_attend.T, q)
        turned = product(inverses[0, p].T, jnp.concatenate([grad_new, grad_erase], 1))
        grad_bv, grad_bk = turned[:, :LANES], turned[:, LANES:]
        grad_lower = -strict * (
            product_t(grad_bv, pair(update, p)) + product_t(grad_bk, pair(erase, p))
        )
        grad_b = (
            jnp.sum(grad_lower * scores[:, : 2 * SPAN], -1, keepdims=True)
            + jnp.sum(grad_bv * v, -1, keepdims=True)
            + jnp.sum(grad_bk * k, -1, keepdims=True)
        )
        inner = b * grad_lower
        grad_k = grad_k + product(inner + inner.T, k) + b * grad_bk
        grad_v = b * grad_bv
        beta_columns += [grad_b[:SPAN], grad_b[SPAN:]]
        for i in range(2):
            h = 2 * p + i
            rows = slice(i * SPAN, (i + 1) * SPAN)
            lanes = slice(h * LANES, (h + 1) * LANES)
            for which, grad in enumerate((grad_q[rows], grad_k[rows] * lives, grad_v[rows])):
                window = pre[which, pl.ds(base + HALO - 8, SPAN + 8), lanes]
                shifted = [window[8 - (taps - 1) + tap :][:SPAN] for tap in range(taps)]
                total = None
                for tap in range(taps):
                    term = conv[which, tap : tap + 1, lanes] * shifted[tap] * valid[tap][8 : 8 + SPAN]
                    total = term if total is None else total + term
                sigma = sigmoid(total)
                if which < 2:
                    act = total * sigma
                    scale = lax.rsqrt(jnp.sum(act * act, -1, keepdims=True) + KEY_EPS)
                    unit = act * scale
                    grad = scale * (grad - unit * jnp.sum(grad * unit, -1, keepdims=True))
                grad = grad * sigma * (1.0 + total * (1.0 - sigma))
                for tap in range(taps):
                    conv_out[which, tap : tap + 1, lanes] += jnp.sum(
                        grad * valid[tap][8 : 8 + SPAN] * shifted[tap], 0, keepdims=True
                    )
                later[which, 8 : 8 + SPAN, lanes] = grad
                result = None
                for tap in range(taps):
                    ahead = 8 + taps - 1 - tap
                    term = (
                        conv[which, tap : tap + 1, lanes]
                        * later[which, ahead : ahead + SPAN, lanes]
                        * valid[tap][ahead : ahead + SPAN]
                    )
                    result = term if result is None else result + term
                grad_pre_out[which, :, lanes] = result
    columns = lax.broadcasted_iota(jnp.int32, (SPAN, heads), 1)
    grad_beta = jnp.zeros((SPAN, heads), jnp.float32)
    for h in range(heads):
        grad_beta = jnp.where(columns == h, beta_columns[h], grad_beta)
    sigma = sigmoid(beta_pre[...])
    grad_beta_out[...] = (
        (grad_beta * lives * sigma * (1.0 - sigma)).astype(LOW).astype(jnp.float32)
    )

    @pl.when(span == 0)
    def _():
        for which in range(3):
            result = None
            for tap in range(taps):
                ahead = taps - 1 - tap
                term = (
                    conv[which, tap : tap + 1, :]
                    * later[which, ahead : ahead + 8, :]
                    * valid[tap][ahead : ahead + 8]
                )
                result = term if result is None else result + term
            borrowed_out[which] = result


def back(
    keep, features, beta, beta_pre, solved, inverses, starts, news, grad_mixed, state_in, pre, conv,
    position, live,
):
    _, count, width = features.shape
    heads, size, _ = state_in.shape
    spans = count // SPAN
    taps = conv.shape[1]
    f32 = lambda shape: jax.ShapeDtypeStruct(shape, jnp.float32)
    whole = lambda shape: pl.BlockSpec(shape, lambda c: (0,) * len(shape))
    rows = pl.BlockSpec((SPAN, width), lambda c: (spans - 1 - c, 0))
    triple = pl.BlockSpec((3, SPAN, width), lambda c: (0, spans - 1 - c, 0))
    column = pl.BlockSpec((SPAN, heads), lambda c: (spans - 1 - c, 0))
    position = jnp.pad(position, ((8, 8), (0, 0)))
    return pl.pallas_call(
        back_kernel,
        grid=(spans,),
        in_specs=[
            pl.BlockSpec(memory_space=pltpu.SMEM), triple, column, column,
            pl.BlockSpec((2, SPAN, width), lambda c: (0, spans - 1 - c, 0)),
            pl.BlockSpec((1, heads // 2, 2 * SPAN, 2 * SPAN), lambda c: (spans - 1 - c, 0, 0, 0)),
            pl.BlockSpec((1, heads, size, size), lambda c: (spans - 1 - c, 0, 0, 0)),
            rows, rows, whole((heads, size, size)), whole(pre.shape), whole(conv.shape),
            whole(position.shape), whole(live.shape),
        ],
        out_specs=[triple, whole((3, 8, width)), whole((3, taps, width)), column],
        out_shape=[
            f32((3, count, width)), f32((3, 8, width)), f32((3, taps, width)), f32((count, heads)),
        ],
        scratch_shapes=[
            pltpu.VMEM((heads, size, size), jnp.float32),
            pltpu.VMEM((3, SPAN + 16, width), jnp.float32),
        ],
        compiler_params=params(),
        cost_estimate=cost(30 * count * width * size * 4, 60 * count * width),
        name="back",
    )(
        keep, features, beta, beta_pre, solved, inverses, starts, news, grad_mixed, state_in, pre,
        conv, position, live,
    )


def enter_kernel(
    tokens, gain, grad_hidden, grads, grad_gate, grad_beta, query_w, key_w, value_w, gate_w, beta_w,
    input_grad_out, gain_out, total,
):
    step = pl.program_id(0)
    term = mxu(grad_gate[...].astype(LOW), gate_w[...], NT)
    for which, weight in enumerate((query_w, key_w, value_w)):
        term = term + mxu(grads[which], weight[...], NT)

    @pl.when(step == 0)
    def _():
        total[...] = term + mxu(grad_beta[...].astype(LOW), beta_w[...], NT)

    @pl.when(step > 0)
    def _():
        total[...] += term

    @pl.when(step == pl.num_programs(0) - 1)
    def _():
        part, gain_part = norm_back(tokens[...].astype(jnp.float32), gain[...], total[...])
        gain_out[...] = gain_part
        input_grad_out[...] = (grad_hidden[...] + part).astype(LOW)


def enter(
    tokens, gain, grad_hidden, grads, grad_gate, grad_beta, query_w, key_w, value_w, gate_w, beta_w
):
    count, width = tokens.shape
    heads = beta_w.shape[1]
    block = 2 * LANES
    whole = lambda shape: pl.BlockSpec(shape, lambda j: (0,) * len(shape))
    weight = pl.BlockSpec((width, block), lambda j: (0, j))
    return pl.pallas_call(
        enter_kernel,
        grid=(width // block,),
        in_specs=[
            whole((count, width)), whole((1, width)), whole((count, width)),
            pl.BlockSpec((3, count, block), lambda j: (0, 0, j)),
            pl.BlockSpec((count, block), lambda j: (0, j)), whole((count, heads)),
            weight, weight, weight, weight, whole((width, heads)),
        ],
        out_specs=[whole((count, width)), whole((1, width))],
        out_shape=[
            jax.ShapeDtypeStruct((count, width), LOW), jax.ShapeDtypeStruct((1, width), jnp.float32),
        ],
        scratch_shapes=[pltpu.VMEM((count, width), jnp.float32)],
        compiler_params=params(),
        cost_estimate=cost(8 * count * width * width, 8 * width * width + 20 * count * width),
        name="enter",
    )(
        tokens, gain, grad_hidden, grads, grad_gate, grad_beta, query_w, key_w, value_w, gate_w,
        beta_w,
    )


def passed_along(value, axis, by):
    devices = lax.axis_size(axis)
    pairs = [(i, i + by) for i in range(devices) if 0 <= i + by < devices]
    return lax.ppermute(value, axis, pairs)


def tuned():
    return (lax.axis_size("seq"), lax.axis_size("doc")) == (8, 4)


HOPS = {"core": ("doc", 1), "y": ("doc", 2), "x": ("seq", 1), "near": ("seq", 2), "far": ("seq", 4)}


def hop(value, way):
    axis, bit = HOPS[way]
    return lax.ppermute(value, axis, [(i, i ^ bit) for i in range(lax.axis_size(axis))])


def side(way):
    axis, bit = HOPS[way]
    return lax.axis_index(axis) // bit % 2


def apply_kernel(maps, state, out, *, turned):
    size = maps.shape[1]
    for h in range(maps.shape[0]):
        matrix = maps[h, :, size:]
        moved = (t_product if turned else product)(matrix, state[h])
        if state.shape[2] == size:
            out[h] = moved + maps[h, :, :size]
        else:
            out[h] = moved + jnp.concatenate([maps[h, :, :size], jnp.zeros_like(matrix)], 1)


def apply_map(maps, state, turned=False):
    return pl.pallas_call(
        lambda *refs: apply_kernel(*refs, turned=turned),
        out_shape=jax.ShapeDtypeStruct(state.shape, jnp.float32),
        compiler_params=params(),
        cost_estimate=cost(2 * maps.size * state.shape[2], 4 * (maps.size + 2 * state.size)),
        name="apply_map",
    )(maps, state)


def carried_forward(maps):
    heads, size, _ = maps.shape
    if not tuned():
        gathered = lax.all_gather(maps, "seq")

        def one(lap, state):
            return apply_map(lax.dynamic_index_in_dim(gathered, lap, 0, False), state)

        zeros = jnp.zeros((heads, size, size), jnp.float32)
        return lax.fori_loop(0, lax.axis_index("seq"), one, zeros), (maps,)
    half = heads // 2
    here, z = side("x") == 0, lax.axis_index("seq") // 2
    kept = jnp.where(here, maps[:half], maps[half:])
    other = hop(jnp.where(here, maps[half:], maps[:half]), "x")
    first, second = jnp.where(here, kept, other), jnp.where(here, other, kept)
    pair_map = apply_map(second, first)
    state = jnp.zeros((half, size, size), jnp.float32)
    for step in range(3):
        sent = pair_map[:, :, :size] if step == 0 else apply_map(pair_map, state)
        state = state + lax.ppermute(sent, "seq", [(2 * step + x, 2 * step + 2 + x) for x in range(2)])
    moved = apply_map(first, state)
    mine = jnp.where(here, state, moved)
    other = hop(jnp.where(here, moved, state), "x")
    low, high = jnp.where(here, mine, other), jnp.where(here, other, mine)
    return jnp.concatenate([low, high], 0), (first, second, pair_map)


def carried_back(shift, context):
    heads, size, _ = shift.shape
    if not tuned():
        gathered = lax.all_gather(
            jnp.concatenate([shift, context[0][:, :, size:]], 2), "seq"
        )
        count = lax.axis_size("seq")

        def one(lap, state):
            maps = lax.dynamic_index_in_dim(gathered, count - 1 - lap, 0, False)
            return apply_map(maps, state, True)

        zeros = jnp.zeros((heads, size, size), jnp.float32)
        return lax.fori_loop(0, count - 1 - lax.axis_index("seq"), one, zeros)
    first, second, pair_map = context
    half = heads // 2
    here = side("x") == 0
    kept = jnp.where(here, shift[:half], shift[half:])
    other = hop(jnp.where(here, shift[half:], shift[:half]), "x")
    first = jnp.concatenate([jnp.where(here, kept, other), first[:, :, size:]], 2)
    second = jnp.concatenate([jnp.where(here, other, kept), second[:, :, size:]], 2)
    pair_map = jnp.concatenate([apply_map(first, second[:, :, :size], True), pair_map[:, :, size:]], 2)
    state = jnp.zeros((half, size, size), jnp.float32)
    for step in range(3, 0, -1):
        sent = pair_map[:, :, :size] if step == 3 else apply_map(pair_map, state, True)
        state = state + lax.ppermute(sent, "seq", [(2 * step + x, 2 * step - 2 + x) for x in range(2)])
    moved = apply_map(second, state, True)
    mine = jnp.where(here, moved, state)
    other = hop(jnp.where(here, state, moved), "x")
    low, high = jnp.where(here, mine, other), jnp.where(here, other, mine)
    return jnp.concatenate([low, high], 0)


def outer_kernel(bit, *refs, blocks, post):
    count = len(blocks)
    lefts, rights = refs[: 2 * count], refs[2 * count : 4 * count]
    keep, send, stacked = refs[4 * count :]
    step = pl.program_id(0)
    tokens = lefts[0].shape[1]
    half = keep.shape[0]

    @pl.when(step == 0)
    def _():
        for piece in range(count):
            for which in range(2):
                for start in range(0, half, post):
                    for place, mine in ((start, bit[0]), (half + start, 1 - bit[0])):
                        rows = pl.ds(pl.multiple_of(2 * start + mine * post, 8), post)
                        stacked[
                            piece, place : place + post, which * tokens : (which + 1) * tokens
                        ] = lefts[2 * piece + which][rows, :].astype(LOW)

    for piece in range(count):
        low = sum(blocks[:piece])

        @pl.when((step >= low) & (step < low + blocks[piece]))
        def _(piece=piece):
            right = jnp.concatenate(
                [rights[2 * piece][...].astype(LOW), rights[2 * piece + 1][...].astype(LOW)], 0
            )
            keep[...] = mxu(stacked[piece, :half, :], right, NN)
            send[...] = mxu(stacked[piece, half:, :], right, NN)


def outer(pieces, way):
    rows, tokens = pieces[0][0].shape
    block = 2 * LANES
    post = rows // 8 * {"near": 2, "x": 1}.get(way, 0) or rows // 16
    counts = [piece[5] for piece in pieces]
    left = pl.BlockSpec((rows, tokens), lambda j: (0, 0), pipeline_mode=pl.Buffered(1))
    lefts, rights, specs = [], [], []
    for index, piece in enumerate(pieces):
        lefts += piece[:2]
        rights += piece[2:4]

        def place(j, low=sum(counts[:index]), first=piece[4], number=piece[5]):
            return 0, first + jnp.clip(j - low, 0, number - 1)

        specs += [pl.BlockSpec((tokens, block), place)] * 2
    total = sum(counts)
    out = pl.BlockSpec((rows // 2, block), lambda j: (0, j))
    shape = jax.ShapeDtypeStruct((rows // 2, total * block), jnp.float32)
    return pl.pallas_call(
        lambda *refs: outer_kernel(*refs, blocks=counts, post=post),
        grid=(total,),
        in_specs=[pl.BlockSpec(memory_space=pltpu.SMEM)] + [left] * len(lefts) + specs,
        out_specs=[out, out],
        out_shape=[shape, shape],
        scratch_shapes=[pltpu.VMEM((len(pieces), rows, 2 * tokens), LOW)],
        compiler_params=params(),
        cost_estimate=cost(
            4 * rows * tokens * total * block, 4 * rows * total * block + 8 * tokens * rows
        ),
        name="outer",
    )(side(way).astype(jnp.int32).reshape(1), *lefts, *rights)


def take(value, place, axis):
    return lax.dynamic_index_in_dim(value, place, axis, False)


def reduced(keep, send, order):
    names = ["far", "near", "x", "y"]
    names.remove(order[0])
    shape = (2, 2, 2, keep.shape[0] // 8, keep.shape[1])
    keep, come = keep.reshape(shape), hop(send, order[0]).reshape(shape)
    for way in order[1:]:
        at, bit = names.index(way), side(way)
        names.remove(way)
        send = take(keep, 1 - bit, at) + take(come, 1 - bit, at)
        keep = take(keep, bit, at) + take(come, bit, at)
        come = hop(send, way)
    keep = keep + come
    come = hop(keep, "y")
    first = side("y") == 0
    return jnp.concatenate([jnp.where(first, keep, come), jnp.where(first, come, keep)], 0)


XYZ, YZX, ZXY = ("x", "y", "near", "far"), ("y", "near", "x", "far"), ("near", "x", "y", "far")


def small_sums(small):
    first_gain, beta, conv, head_gain, second_gain = small
    seq = lax.axis_size("seq")
    flat = jnp.concatenate(
        [
            first_gain.reshape(seq, -1), beta.reshape(seq, -1),
            conv.reshape(conv.shape[0] * conv.shape[1], seq, -1).transpose(1, 0, 2).reshape(seq, -1),
            head_gain.reshape(seq, -1), second_gain.reshape(seq, -1),
        ],
        1,
    )
    size = flat.shape[1]
    rows = -(-size // 2048) * 16
    flat = jnp.pad(flat, ((0, 0), (0, rows * 128 - size))).reshape(seq * rows, 128)
    flat = flat + hop(flat, "core")
    split = flat.reshape(4, 2, rows, 128)
    here = side("x")
    halves_of = [take(split, place, 1).reshape(-1, 128) for place in (here, 1 - here)]
    flat = reduced(*halves_of, XYZ).reshape(-1)
    sizes = [a.size // seq for a in small]
    places = [sum(sizes[:i]) for i in range(len(sizes))]
    pieces = [flat[p : p + s] for p, s in zip(places, sizes)]
    return (
        pieces[0], pieces[1].reshape(-1, beta.shape[1]),
        pieces[2].reshape(conv.shape[0], conv.shape[1], -1), pieces[3], pieces[4],
    )


def outer_sum(left, right):
    return mxu(left.astype(LOW), right.astype(LOW), TN)


def local(
    tokens,
    doc_lengths,
    out_grad,
    first_gain,
    query_weight,
    key_weight,
    value_weight,
    gate_weight,
    beta_weight,
    conv_weight,
    head_gain,
    out_weight,
    second_gain,
    hidden_gate,
    hidden_up,
    hidden_down,
):
    count, width = (tokens.shape[1], tokens.shape[2])
    heads = beta_weight.shape[1]
    reach = conv_weight.shape[1] - 1
    first = lax.axis_index("seq") * count
    position, live = doc_info(doc_lengths[0], first, count)
    keep = 1.0 - (position[::CK] == 0).astype(jnp.float32)
    position, live = position[:, None], live[:, None]
    core = (lax.axis_index("doc") % 2).astype(jnp.int32).reshape(1)
    here = core[0] == 0
    rows, top = tokens[0], out_grad[0]
    halo = passed_along(rows[count - HALO :].astype(jnp.float32), "seq", 1)
    normed_one, pre, features, gate_pre, beta_pre, beta = project(
        rows, halo, first_gain[None], position, live, query_weight, key_weight, value_weight,
        gate_weight, beta_weight, conv_weight,
    )
    solved, inverses, attend, maps = prepare(keep, features, beta)
    state_in, context = carried_forward(maps)
    starts, news, mixed, normed_head = mix(
        keep, features, solved, attend, gate_pre, head_gain[None], state_in
    )
    head_turned = normed_head.T.astype(jnp.float32)
    (
        block_out, two_turned, inner_turned, kept, sent, grad_hidden, grad_branch, grad_head,
        grad_second_gain,
    ) = feed(
        core, rows, normed_head, top, second_gain[None], out_weight, hidden_gate, hidden_up,
        hidden_down,
    )
    grad_mixed, grad_gate_pre, grad_head_gain, shift = gather_states(
        keep, grad_head, mixed, gate_pre, head_gain[None], features, solved, heads
    )
    state_grad = carried_back(shift, context)
    grads, borrowed, grad_conv, grad_beta_pre = back(
        keep, features, beta, beta_pre, solved, inverses, starts, news, grad_mixed, state_grad, pre,
        conv_weight, position, live,
    )
    returned = passed_along(borrowed, "seq", -1)
    tail = grads[:, count - 8 :] + returned
    grads = lax.dynamic_update_slice(grads, tail, (0, count - 8, 0))
    grads = grads.astype(LOW)
    input_grad, grad_first_gain = enter(
        rows, first_gain[None], grad_hidden, grads, grad_gate_pre, grad_beta_pre, query_weight,
        key_weight, value_weight, gate_weight, beta_weight,
    )
    small = (
        grad_first_gain[0], outer_sum(normed_one.T, grad_beta_pre), grad_conv, grad_head_gain[0],
        grad_second_gain[0],
    )
    if tuned():
        half = width // 2

        def pick(zero, one):
            return jnp.where(here, zero, one)

        def both(value, send=None):
            return value, hop(value if send is None else send, "core")

        wide_top = top.astype(jnp.float32)
        tops = both(
            pick(top[:, :half], top[:, half:]), pick(wide_top[:, half:], wide_top[:, :half])
        )
        one = both(normed_one)
        two = both(two_turned)
        inners = both(inner_turned)
        heads_turned = both(head_turned)
        gate_up = both(kept, sent)
        out_left = pick(heads_turned[0], one[0]), pick(heads_turned[1], one[1])
        out_right = both(pick(grad_branch, grad_gate_pre), pick(grad_gate_pre, grad_branch))
        blocks = hidden_gate.shape[1] // 256
        low = blocks // 2
        some = width // 256 * 3 // 4
        early = (
            reduced(
                *outer([(*two, *gate_up, 0, low), (*out_left, *out_right, 0, some)], "x"), XYZ
            ),
            reduced(
                *outer(
                    [
                        (*two, *gate_up, low, blocks - low),
                        (*out_left, *out_right, some, width // 256 - some),
                    ],
                    "y",
                ),
                YZX,
            ),
            reduced(*outer([(*inners, *tops, 0, half // 256)], "near"), ZXY),
        )
        wide = grads.astype(jnp.float32)
        query_key = both(pick(grads[0], grads[1]), pick(wide[1], wide[0]))
        value = both(
            pick(grads[2, :, :half], grads[2, :, half:]), pick(wide[2, :, half:], wide[2, :, :half])
        )
        late = (
            reduced(*outer([(*one, *query_key, 0, half // 256)], "x"), XYZ),
            reduced(*outer([(*one, *query_key, half // 256, half // 256)], "y"), YZX),
            reduced(*outer([(*one, *value, 0, half // 256)], "near"), ZXY),
        )
        a, b = low * 256, (blocks - low) * 256
        own = (
            jnp.concatenate([early[0][:, :a], early[1][:, :b]], 1), early[2],
            jnp.concatenate([early[0][:, a:], early[1][:, b:]], 1),
            jnp.concatenate(late[:2], 1), late[2],
        )
        other = tuple(hop(v, "core") for v in own)
        zero = [pick(m, o) for m, o in zip(own, other)]
        one_ = [pick(o, m) for m, o in zip(own, other)]
        query_g, key_g = zero[3], one_[3]
        value_g = jnp.concatenate([zero[4], one_[4]], 1)
        gate_g, out_g, hidden_gate_g, hidden_up_g = one_[2], zero[2], zero[0], one_[0]
        hidden_down_g = jnp.concatenate([zero[1], one_[1]], 1)
        first_g, beta_g, conv_g, head_g, second_g = small_sums(small)
    else:

        def whole(term, dimension):
            part = lax.psum_scatter(term, "seq", scatter_dimension=dimension, tiled=True)
            return lax.psum(part, "doc")

        gate_grad, up_grad = jnp.where(here, kept, sent), jnp.where(here, sent, kept)
        terms = (
            outer_sum(normed_one.T, grads[0]), outer_sum(normed_one.T, grads[1]),
            outer_sum(normed_one.T, grads[2]), outer_sum(normed_one.T, grad_gate_pre),
            outer_sum(head_turned.T, grad_branch), outer_sum(two_turned.T, gate_grad),
            outer_sum(two_turned.T, up_grad), outer_sum(inner_turned.T, top),
        )
        query_g, key_g, value_g, gate_g, out_g, hidden_gate_g, hidden_up_g, hidden_down_g = (
            whole(term, 0) for term in terms
        )
        first_g, beta_g, conv_g, head_g, second_g = (
            whole(term, d) for term, d in zip(small, (0, 0, 2, 0, 0))
        )
    return (
        block_out[None], input_grad[None], first_g, query_g, key_g, value_g, gate_g, beta_g, conv_g,
        head_g, out_g, second_g, hidden_gate_g, hidden_up_g, hidden_down_g,
    )


def solution(mesh):
    in_specs = (
        P("doc", "seq", None),
        P("doc", None),
        P("doc", "seq", None),
        P(),
        P(),
        P(),
        P(),
        P(),
        P(),
        P(),
        P(),
        P(),
        P(),
        P(),
        P(),
        P(),
    )
    out_specs = (
        P("doc", "seq", None),
        P("doc", "seq", None),
        P("seq"),
        P("seq", None),
        P("seq", None),
        P("seq", None),
        P("seq", None),
        P("seq", None),
        P(None, None, "seq"),
        P("seq"),
        P("seq", None),
        P("seq"),
        P("seq", None),
        P("seq", None),
        P("seq", None),
    )
    return jax.shard_map(local, mesh=mesh, in_specs=in_specs, out_specs=out_specs, check_vma=False)
```

```python
import jax
import jax.numpy as jnp
from jax import lax
from jax.experimental import pallas as pl
from jax.experimental.pallas import tpu as pltpu
from jax.sharding import PartitionSpec as P

CK = 64


EPS = 1e-05
KEY_EPS = 1e-06
HIGH = lax.Precision.HIGHEST


def doc_info(lengths, first, count):
    padded = (lengths + CK - 1) // CK * CK
    ends = jnp.cumsum(padded)
    starts = ends - padded
    place = first + jnp.arange(count, dtype=jnp.int32)
    inside = ((place[:, None] >= starts[None, :]) & (place[:, None] < ends[None, :])).astype(
        jnp.int32
    )
    position = place - jnp.sum(inside * starts[None, :], 1)
    length = jnp.sum(inside * lengths[None, :], 1)
    live = (position < length).astype(jnp.float32)
    return (position, live)


SPAN = CK
LANES = 128
LOW = jnp.bfloat16
NN = (((1,), (0,)), ((), ()))
NT = (((1,), (1,)), ((), ()))
TN = (((0,), (0,)), ((), ()))


def params(mib=48):
    return pltpu.CompilerParams(vmem_limit_bytes=mib * 2**20)


def cost(flops, moved):
    return pl.CostEstimate(flops=1, bytes_accessed=1, transcendentals=0)


def mxu(left, right, dims):
    return lax.dot_general(left, right, dims, preferred_element_type=jnp.float32)


def halves(value):
    high = value.astype(LOW)
    return high, (value - high.astype(jnp.float32)).astype(LOW)


def split(value):
    return value if isinstance(value, tuple) else halves(value)


def stack(first, second):
    return tuple(jnp.concatenate(both, 0) for both in zip(first, second))


def fold(value):
    half = value.shape[1] // 2
    return value[:, :half] + value[:, half:]


def product(left, right):
    left_high, left_low = split(left)
    right_high, right_low = split(right)
    both = jnp.concatenate([left_high, left_low], 1)
    if right_high.shape[1] <= LANES:
        wide = jnp.concatenate([right_high, right_low], 1)
        return fold(mxu(both, jnp.concatenate([wide, wide], 0), NN))
    return mxu(both, jnp.concatenate([right_high, right_high], 0), NN) + mxu(
        left_high, right_low, NN
    )


def product_t(left, right):
    left_high, left_low = split(left)
    right_high, right_low = split(right)
    both = jnp.concatenate([left_high, left_low], 1)
    if right_high.shape[0] <= LANES:
        rows = jnp.concatenate(
            [
                jnp.concatenate([right_high, right_high], 1),
                jnp.concatenate([right_low, right_low], 1),
            ],
            0,
        )
        return fold(mxu(both, rows, NT))
    return mxu(both, jnp.concatenate([right_high, right_high], 1), NT) + mxu(
        left_high, right_low, NT
    )


def t_product(left, right):
    left_high, left_low = split(left)
    right_high, right_low = split(right)
    both = jnp.concatenate([left_high, left_low], 0)
    if right_high.shape[1] <= LANES:
        wide = jnp.concatenate([right_high, right_low], 1)
        return fold(mxu(both, jnp.concatenate([wide, wide], 0), TN))
    return mxu(both, jnp.concatenate([right_high, right_high], 0), TN) + mxu(
        left_high, right_low, TN
    )


def head(value, h):
    return value[:, h * LANES : (h + 1) * LANES]


def pair(value, p):
    return jnp.concatenate([head(value, 2 * p), head(value, 2 * p + 1)], 0)


def pair_column(value, p):
    return jnp.concatenate([value[:, 2 * p : 2 * p + 1], value[:, 2 * p + 1 : 2 * p + 2]], 0)


def masks(rows):
    i = lax.broadcasted_iota(jnp.int32, (rows, rows), 0)
    j = lax.broadcasted_iota(jnp.int32, (rows, rows), 1)
    same = (i >= SPAN) == (j >= SPAN)
    strict = jnp.where(same & (j < i), 1.0, 0.0)
    inclusive = jnp.where(same & (j <= i), 1.0, 0.0)
    upper = jnp.where(same & (j >= i), 1.0, 0.0)
    return strict, inclusive, upper, jnp.where(i == j, 1.0, 0.0)


def inverses_of(strict_parts, identity):
    rows = identity.shape[0]
    results = [identity - part for part in strict_parts]
    powers = [split(part) for part in strict_parts]
    powers = [split(product(power, power)) for power in powers]
    for level in range(SPAN.bit_length() - 3):
        both = [
            product(stack(split(result), power), power) for result, power in zip(results, powers)
        ]
        results = [result + pair_[:rows] for result, pair_ in zip(results, both)]
        powers = [split(pair_[rows:]) for pair_ in both]
    return [result + product(result, power) for result, power in zip(results, powers)]


def sigmoid(value):
    return 1.0 / (1.0 + jnp.exp(-value))


HALO = 16


def project_kernel(
    tokens, halo, gain, position, live, query_w, key_w, value_w, gate_w, beta_w, conv,
    normed_out, pre_out, feature_out, gate_out, beta_pre_out, beta_out, normed, pre,
):
    count = tokens.shape[0]

    @pl.when(pl.program_id(0) == 0)
    def _():
        def norm(rows):
            return (
                rows * lax.rsqrt(jnp.mean(rows * rows, -1, keepdims=True) + EPS) * gain[...]
            ).astype(LOW)

        normed[:HALO, :] = norm(halo[...])
        rounded = norm(tokens[...].astype(jnp.float32))
        normed[HALO:, :] = rounded
        normed_out[...] = rounded.astype(jnp.float32).T
        beta_pre = mxu(rounded, beta_w[...], NN)
        beta_pre_out[...] = beta_pre
        beta_out[...] = sigmoid(beta_pre) * live[...]

    gate_out[...] = mxu(normed[HALO:, :], gate_w[...], NN)
    valid = [
        jnp.broadcast_to(
            jnp.where(position[...] >= conv.shape[1] - 1 - tap, 1.0, 0.0), (count, LANES)
        )
        for tap in range(conv.shape[1] - 1)
    ]
    for which, weight in enumerate((query_w, key_w, value_w)):
        pre[which] = mxu(normed[...], weight[...], NN)
        for span in range(count // SPAN):
            start = HALO + span * SPAN
            pre_out[which, span] = pre[which, start - 8 : start + SPAN, :]
        for part in range(pre.shape[2] // LANES):
            lanes = slice(part * LANES, (part + 1) * LANES)
            total = conv_total(pre, which, HALO, count, lanes, conv, valid)
            value = total * sigmoid(total)
            if which < 2:
                value = value * lax.rsqrt(jnp.sum(value * value, -1, keepdims=True) + KEY_EPS)
            if which == 1:
                value = value * live[...]
            feature_out[which, :, lanes] = value


def conv_total(pre, which, first, count, lanes, conv, valid):
    taps = conv.shape[1]
    total = None
    for tap in range(taps):
        start = first - (taps - 1) + tap
        term = conv[which, tap : tap + 1, lanes] * pre[which, start : start + count, lanes]
        if tap < taps - 1:
            term = term * valid[tap]
        total = term if total is None else total + term
    return total


def project(tokens, halo, gain, position, live, query_w, key_w, value_w, gate_w, beta_w, conv):
    count, width = tokens.shape
    heads = beta_w.shape[1]
    block = 2 * LANES
    whole = lambda shape: pl.BlockSpec(shape, lambda j: (0,) * len(shape))
    weight = pl.BlockSpec((width, block), lambda j: (0, j))
    f32 = lambda shape: jax.ShapeDtypeStruct(shape, jnp.float32)
    return pl.pallas_call(
        project_kernel,
        grid=(width // block,),
        in_specs=[
            whole((count, width)), whole((HALO, width)), whole((1, width)), whole((count, 1)),
            whole((count, 1)), weight, weight, weight, weight, whole((width, heads)),
            pl.BlockSpec((3, conv.shape[1], block), lambda j: (0, 0, j)),
        ],
        out_specs=[
            whole((width, count)),
            pl.BlockSpec((3, count // SPAN, SPAN + 8, block), lambda j: (0, 0, 0, j)),
            pl.BlockSpec((3, count, block), lambda j: (0, 0, j)),
            pl.BlockSpec((count, block), lambda j: (0, j)),
            whole((count, heads)), whole((count, heads)),
        ],
        out_shape=[
            f32((width, count)), f32((3, count // SPAN, SPAN + 8, width)), f32((3, count, width)),
            f32((count, width)), f32((count, heads)), f32((count, heads)),
        ],
        scratch_shapes=[
            pltpu.VMEM((HALO + count, width), LOW),
            pltpu.VMEM((3, HALO + count, block), jnp.float32),
        ],
        compiler_params=params(),
        cost_estimate=cost(8 * count * width * width, 8 * width * width + 40 * count * width),
        name="project",
    )(tokens, halo, gain, position, live, query_w, key_w, value_w, gate_w, beta_w, conv)


def prepare_kernel(keep, features, beta, solved_out, inverse_out, attend_out, state):
    span = pl.program_id(0)
    heads = state.shape[0]
    size = state.shape[1]
    strict, inclusive, upper, identity = masks(2 * SPAN)

    @pl.when(span == 0)
    def _():
        i = lax.broadcasted_iota(jnp.int32, (size, 2 * size), 0)
        j = lax.broadcasted_iota(jnp.int32, (size, 2 * size), 1)
        for h in range(heads):
            state[h] = jnp.where(j == i + size, 1.0, 0.0)

    query, key, value = features[0], features[1], features[2]
    betas = beta[...]
    flag = keep[span]
    pairs = range(heads // 2)
    keys = [split(pair(key, p)) for p in pairs]
    columns = [pair_column(betas, p) for p in pairs]
    scores = [product_t(stack(keys[p], split(pair(query, p))), keys[p]) for p in pairs]
    solved = inverses_of([columns[p] * scores[p][: 2 * SPAN] * strict for p in pairs], identity)
    both = [
        product(
            solved[p],
            jnp.concatenate([columns[p] * pair(key, p), columns[p] * pair(value, p)], 1),
        )
        for p in pairs
    ]
    for p in pairs:
        inverse_out[0, p] = solved[p]
        attend_out[0, p] = scores[p][2 * SPAN :] * inclusive
    starts, news = [], []
    for h in range(heads):
        rows = slice(h % 2 * SPAN, (h % 2 + 1) * SPAN)
        erase, update = both[h // 2][rows, :size], both[h // 2][rows, size:]
        solved_out[0, :, h * size : (h + 1) * size] = erase
        solved_out[1, :, h * size : (h + 1) * size] = update
        start = state[h] * flag
        starts.append(start)
        news.append(
            jnp.concatenate([update, jnp.zeros_like(update)], 1) - product(erase, start)
        )
    for h in range(heads):
        rows = slice(h % 2 * SPAN, (h % 2 + 1) * SPAN)
        state[h] = starts[h] + t_product(tuple(k[rows] for k in keys[h // 2]), news[h])


def prepare(keep, features, beta):
    _, count, width = features.shape
    heads = beta.shape[1]
    size = width // heads
    spans = count // SPAN
    f32 = lambda shape: jax.ShapeDtypeStruct(shape, jnp.float32)
    matrix = pl.BlockSpec((1, heads // 2, 2 * SPAN, 2 * SPAN), lambda c: (c, 0, 0, 0))
    return pl.pallas_call(
        prepare_kernel,
        grid=(spans,),
        in_specs=[
            pl.BlockSpec(memory_space=pltpu.SMEM),
            pl.BlockSpec((3, SPAN, width), lambda c: (0, c, 0)),
            pl.BlockSpec((SPAN, heads), lambda c: (c, 0)),
        ],
        out_specs=[
            pl.BlockSpec((2, SPAN, width), lambda c: (0, c, 0)), matrix, matrix,
            pl.BlockSpec((heads, size, 2 * size), lambda c: (0, 0, 0)),
        ],
        out_shape=[
            f32((2, count, width)), f32((spans, heads // 2, 2 * SPAN, 2 * SPAN)),
            f32((spans, heads // 2, 2 * SPAN, 2 * SPAN)), f32((heads, size, 2 * size)),
        ],
        compiler_params=params(),
        cost_estimate=cost(40 * count * width * size * 4, 60 * count * width),
        name="prepare",
    )(keep, features, beta)


def mix_kernel(
    keep, features, solved, attend, gate, gain, state_in, starts_out, new_out, mixed_out, normed_out,
    state,
):
    span = pl.program_id(0)
    heads = state.shape[0]

    @pl.when(span == 0)
    def _():
        state[...] = state_in[...]

    query, key = features[0], features[1]
    erase, update = solved[0], solved[1]
    flag = keep[span]
    every, pairs = range(heads), range(heads // 2)
    starts = [state[h] * flag for h in every]
    both = [
        product(jnp.concatenate([head(erase, h), head(query, h)], 0), starts[h]) for h in every
    ]
    news = [split(head(update, h) - both[h][:SPAN]) for h in every]
    after = [starts[h] + t_product(head(key, h), news[h]) for h in every]
    inner = [product(attend[0, p], stack(news[2 * p], news[2 * p + 1])) for p in pairs]
    for h in every:
        lanes = slice(h * LANES, (h + 1) * LANES)
        starts_out[0, h] = starts[h]
        state[h] = after[h]
        new_out[:, lanes] = head(update, h) - both[h][:SPAN]
        rows = both[h][SPAN:] + inner[h // 2][h % 2 * SPAN : (h % 2 + 1) * SPAN]
        mixed_out[:, lanes] = rows
        shaped = rows * lax.rsqrt(jnp.mean(rows * rows, -1, keepdims=True) + EPS) * gain[...]
        gates = gate[:, lanes]
        normed_out[:, lanes] = (shaped * (gates * sigmoid(gates))).astype(LOW)


def mix(keep, features, solved, attend, gate, gain, state_in):
    _, count, width = features.shape
    heads, size, _ = state_in.shape
    spans = count // SPAN
    f32 = lambda shape: jax.ShapeDtypeStruct(shape, jnp.float32)
    rows = pl.BlockSpec((SPAN, width), lambda c: (c, 0))
    pairs = pl.BlockSpec((2, SPAN, width), lambda c: (0, c, 0))
    return pl.pallas_call(
        mix_kernel,
        grid=(spans,),
        in_specs=[
            pl.BlockSpec(memory_space=pltpu.SMEM), pairs, pairs,
            pl.BlockSpec((1, heads // 2, 2 * SPAN, 2 * SPAN), lambda c: (c, 0, 0, 0)),
            rows, pl.BlockSpec((1, size), lambda c: (0, 0)),
            pl.BlockSpec((heads, size, size), lambda c: (0, 0, 0)),
        ],
        out_specs=[
            pl.BlockSpec((1, heads, size, size), lambda c: (c, 0, 0, 0)), rows, rows, rows,
        ],
        out_shape=[
            f32((spans, heads, size, size)), f32((count, width)), f32((count, width)),
            jax.ShapeDtypeStruct((count, width), LOW),
        ],
        scratch_shapes=[pltpu.VMEM((heads, size, size), jnp.float32)],
        compiler_params=params(),
        cost_estimate=cost(8 * count * width * size * 4, 40 * count * width),
        name="mix",
    )(keep, features, solved, attend, gate, gain, state_in)


def feed_kernel(
    core, tokens, normed_head, grad_top, second_gain, out_w, gate_w, up_w, down_w,
    block_out, normed_out, inner_out, kept_out, sent_out, grad_hidden_out, branch_out, grad_head_out,
    gain_grad_out, hidden, normed, total, grad_total,
):
    step = pl.program_id(0)

    @pl.when(step == 0)
    def _():
        state = tokens[...].astype(jnp.float32) + mxu(normed_head[...], out_w[...], NN)
        hidden[...] = state
        rounded = (
            state * lax.rsqrt(jnp.mean(state * state, -1, keepdims=True) + EPS) * second_gain[...]
        ).astype(LOW)
        normed[...] = rounded
        normed_out[...] = rounded.astype(jnp.float32).T

    @pl.when(step == 0)
    def _():
        total[...] = jnp.zeros_like(total)
        grad_total[...] = jnp.zeros_like(grad_total)

    first = core[0] == 0
    size = normed.shape[0] // 1
    parts = [slice(i * size, (i + 1) * size) for i in range(1)]
    gates = [mxu(normed[part, :], gate_w[...], NN) for part in parts]
    ups = [mxu(normed[part, :], up_w[...], NN) for part in parts]
    grad_inners = [mxu(grad_top[part, :], down_w[...], NT) for part in parts]
    for part, gate, up, grad_inner in zip(parts, gates, ups, grad_inners):
        sigma = sigmoid(gate)
        act = gate * sigma
        inner = (act * up).astype(LOW)
        inner_out[:, part] = inner.astype(jnp.float32).T
        wide_gate = grad_inner * up * (sigma + act * (1.0 - sigma))
        wide_up = grad_inner * act
        grad_gate, grad_up = wide_gate.astype(LOW), wide_up.astype(LOW)
        kept_out[part, :] = jnp.where(first, wide_gate, wide_up).astype(LOW)
        sent_out[part, :] = jnp.where(first, wide_up, wide_gate).astype(LOW).astype(jnp.float32)
        total[part, :] += mxu(inner, down_w[...], NN)
        grad_total[part, :] += mxu(grad_gate, gate_w[...], NT) + mxu(grad_up, up_w[...], NT)

    @pl.when(step == pl.num_programs(0) - 1)
    def _():
        state = hidden[...]
        block_out[...] = (state + total[...]).astype(LOW)
        part, gain_part = norm_back(state, second_gain[...], grad_total[...])
        gain_grad_out[...] = gain_part
        grad_hidden = grad_top[...].astype(jnp.float32) + part
        grad_hidden_out[...] = grad_hidden
        branch = grad_hidden.astype(LOW)
        branch_out[...] = branch.astype(jnp.float32)
        grad_head_out[...] = mxu(branch, out_w[...], NT)


def norm_back(value, gain, grad):
    scale = lax.rsqrt(jnp.mean(value * value, -1, keepdims=True) + EPS)
    unit = value * scale
    gain_grad = jnp.sum(grad * unit, 0, keepdims=True)
    inward = grad * gain
    return scale * (inward - unit * jnp.mean(inward * unit, -1, keepdims=True)), gain_grad


def feed(core, tokens, normed_head, grad_top, second_gain, out_w, gate_w, up_w, down_w):
    count, width = tokens.shape
    hidden = gate_w.shape[1]
    block = 2 * LANES
    whole = lambda shape: pl.BlockSpec(shape, lambda j: (0,) * len(shape))
    f32 = lambda shape: jax.ShapeDtypeStruct(shape, jnp.float32)
    low = lambda shape: jax.ShapeDtypeStruct(shape, LOW)
    rows = whole((count, width))
    columns = pl.BlockSpec((count, block), lambda j: (0, j))
    return pl.pallas_call(
        feed_kernel,
        grid=(hidden // block,),
        in_specs=[
            pl.BlockSpec(memory_space=pltpu.SMEM), rows, rows, rows, whole((1, width)),
            whole((width, width)), pl.BlockSpec((width, block), lambda j: (0, j)),
            pl.BlockSpec((width, block), lambda j: (0, j)),
            pl.BlockSpec((block, width), lambda j: (j, 0)),
        ],
        out_specs=[
            rows, whole((width, count)), pl.BlockSpec((block, count), lambda j: (j, 0)), columns,
            columns, rows, rows, rows, whole((1, width)),
        ],
        out_shape=[
            low((count, width)), f32((width, count)), f32((hidden, count)), low((count, hidden)),
            f32((count, hidden)), f32((count, width)), f32((count, width)), f32((count, width)),
            f32((1, width)),
        ],
        scratch_shapes=[
            pltpu.VMEM((count, width), jnp.float32), pltpu.VMEM((count, width), LOW),
            pltpu.VMEM((count, width), jnp.float32), pltpu.VMEM((count, width), jnp.float32),
        ],
        compiler_params=params(),
        cost_estimate=cost(
            12 * count * width * hidden + 4 * count * width * width,
            6 * width * hidden + 10 * count * hidden + 30 * count * width,
        ),
        name="feed",
    )(core, tokens, normed_head, grad_top, second_gain, out_w, gate_w, up_w, down_w)


def gather_kernel(
    keep, grad_head, mixed, gate, gain, features, solved, grad_mixed_out, grad_gate_out, gain_out,
    state,
):
    step = pl.program_id(0)
    span = pl.num_programs(0) - 1 - step
    heads = state.shape[0]
    strict, inclusive, upper, identity = masks(2 * SPAN)

    @pl.when(step == 0)
    def _():
        state[...] = jnp.zeros_like(state)
        gain_out[...] = jnp.zeros_like(gain_out)

    query, key = features[0], features[1]
    erase = solved[0]
    flag = keep[span]
    gain_total = jnp.zeros_like(gain_out[...])
    every, pairs = range(heads), range(heads // 2)
    passes = [product_t(pair(key, p), pair(query, p)) * upper for p in pairs]
    grads = []
    for h in every:
        lanes = slice(h * LANES, (h + 1) * LANES)
        gates = gate[:, lanes]
        sigma = sigmoid(gates)
        rows = mixed[:, lanes]
        grad = grad_head[:, lanes]
        scale = lax.rsqrt(jnp.mean(rows * rows, -1, keepdims=True) + EPS)
        unit = rows * scale
        grad_gate = grad * unit * gain[...] * sigma * (1.0 + gates * (1.0 - sigma))
        grad_gate_out[:, lanes] = grad_gate.astype(LOW).astype(jnp.float32)
        shaped = grad * gates * sigma
        gain_total = gain_total + jnp.sum(shaped * unit, 0, keepdims=True)
        inward = shaped * gain[...]
        grad_rows = scale * (inward - unit * jnp.mean(inward * unit, -1, keepdims=True))
        grad_mixed_out[:, lanes] = grad_rows
        grads.append(split(grad_rows))
    passed = [product(passes[p], stack(grads[2 * p], grads[2 * p + 1])) for p in pairs]
    ends = [state[h] for h in every]
    grad_new = [
        passed[h // 2][h % 2 * SPAN : (h % 2 + 1) * SPAN] + product(head(key, h), ends[h])
        for h in every
    ]
    for h in every:
        state[h] = flag * (
            ends[h]
            + t_product(
                jnp.concatenate([head(query, h), -head(erase, h)], 0),
                stack(grads[h], split(grad_new[h])),
            )
        )
    gain_out[...] += gain_total


def gather_states(keep, grad_head, mixed, gate, gain, features, solved, heads):
    _, count, width = features.shape
    size = width // heads
    spans = count // SPAN
    f32 = lambda shape: jax.ShapeDtypeStruct(shape, jnp.float32)
    rows = pl.BlockSpec((SPAN, width), lambda c: (spans - 1 - c, 0))
    pairs = pl.BlockSpec((2, SPAN, width), lambda c: (0, spans - 1 - c, 0))
    one = pl.BlockSpec((1, SPAN, width), lambda c: (0, spans - 1 - c, 0))
    return pl.pallas_call(
        gather_kernel,
        grid=(spans,),
        in_specs=[
            pl.BlockSpec(memory_space=pltpu.SMEM), rows, rows, rows,
            pl.BlockSpec((1, size), lambda c: (0, 0)), pairs, one,
        ],
        out_specs=[
            rows, rows, pl.BlockSpec((1, size), lambda c: (0, 0)),
            pl.BlockSpec((heads, size, size), lambda c: (0, 0, 0)),
        ],
        out_shape=[
            f32((count, width)), f32((count, width)), f32((1, size)), f32((heads, size, size)),
        ],
        compiler_params=params(),
        cost_estimate=cost(8 * count * width * size * 4, 32 * count * width),
        name="gather_states",
    )(keep, grad_head, mixed, gate, gain, features, solved)


def back_kernel(
    keep, features, beta, beta_pre, solved, inverses, starts, news, grad_mixed, state_in, pre, conv,
    position, live, grad_pre_out, borrowed_out, conv_out, grad_beta_out, state, later, sums,
):
    step = pl.program_id(0)
    span = pl.num_programs(0) - 1 - step
    heads = state.shape[0]
    taps = conv.shape[1]
    strict, inclusive, upper, identity = masks(2 * SPAN)

    @pl.when(step == 0)
    def _():
        state[...] = state_in[...]
        sums[...] = jnp.zeros_like(sums)
        later[...] = jnp.zeros_like(later)

    query, key, value = features[0], features[1], features[2]
    erase, update = solved[0], solved[1]
    betas = beta[...]
    flag = keep[span]
    base = pl.multiple_of(span * SPAN, SPAN)
    places = position[pl.ds(base, SPAN), :]
    lives = live[pl.ds(base, SPAN), :]
    valid = [
        jnp.broadcast_to(jnp.where(places >= taps - 1 - tap, 1.0, 0.0), (SPAN, LANES))
        for tap in range(taps - 1)
    ]
    every, pairs = range(heads), range(heads // 2)
    part = [slice(h % 2 * SPAN, (h % 2 + 1) * SPAN) for h in every]
    q = [split(pair(query, p)) for p in pairs]
    k = [split(pair(key, p)) for p in pairs]
    b = [pair_column(betas, p) for p in pairs]
    grad_out = [split(pair(grad_mixed, p)) for p in pairs]
    new = [split(pair(news, p)) for p in pairs]
    erases = [split(pair(erase, p)) for p in pairs]
    row = lambda value, h: tuple(v[part[h]] for v in value[h // 2])
    scores = [product_t(k[p], stack(k[p], q[p])) for p in pairs]
    passed = [product(scores[p][:, 2 * SPAN :] * upper, grad_out[p]) for p in pairs]
    ends = [split(state[h]) for h in every]
    begin = [split(starts[0, h]) for h in every]
    grad_new = [passed[h // 2][part[h]] + product(row(k, h), ends[h]) for h in every]
    grad_news = [split(value) for value in grad_new]
    both = [product_t(stack(row(grad_out, h), grad_news[h]), begin[h]) for h in every]
    grad_key = [product_t(row(new, h), ends[h]) for h in every]
    for h in every:
        state[h] = flag * (
            state[h]
            + t_product(
                stack(row(q, h), tuple(-v for v in row(erases, h))),
                stack(row(grad_out, h), grad_news[h]),
            )
        )
    grad_attend = [product_t(grad_out[p], new[p]) * inclusive for p in pairs]
    joined = lambda values, p: jnp.concatenate([values[2 * p], values[2 * p + 1]], 0)
    grad_q = [
        joined([value[:SPAN] for value in both], p) + product(grad_attend[p], k[p]) for p in pairs
    ]
    grad_k = [joined(grad_key, p) + product(grad_attend[p].T, q[p]) for p in pairs]
    turned = [
        product(
            inverses[0, p].T,
            jnp.concatenate(
                [joined(grad_new, p), -joined([value[SPAN:] for value in both], p)], 1
            ),
        )
        for p in pairs
    ]
    grad_bv = [value[:, :LANES] for value in turned]
    grad_bk = [value[:, LANES:] for value in turned]
    grad_lower = [
        -strict * (product_t(grad_bv[p], pair(update, p)) + product_t(grad_bk[p], erases[p]))
        for p in pairs
    ]
    inner = [b[p] * grad_lower[p] for p in pairs]
    grad_k = [
        grad_k[p] + product(inner[p] + inner[p].T, k[p]) + b[p] * grad_bk[p] for p in pairs
    ]
    grad_v = [b[p] * grad_bv[p] for p in pairs]
    beta_columns = []
    for p in pairs:
        grad_b = (
            jnp.sum(grad_lower[p] * scores[p][:, : 2 * SPAN], -1, keepdims=True)
            + jnp.sum(grad_bv[p] * pair(value, p), -1, keepdims=True)
            + jnp.sum(grad_bk[p] * pair(key, p), -1, keepdims=True)
        )
        beta_columns += [grad_b[:SPAN], grad_b[SPAN:]]
    chunks = [(which, h) for which in range(3) for h in every]
    for start in range(0, len(chunks), 4):
        group = chunks[start : start + 4]
        places = [(which, slice(h * LANES, (h + 1) * LANES)) for which, h in group]
        grads = [(grad_q, grad_k, grad_v)[which][h // 2][part[h]] for which, h in group]
        shifted = [
            [
                pre[which, 0, pl.ds(8 - (taps - 1) + tap, SPAN), lanes]
                for tap in range(taps)
            ]
            for which, lanes in places
        ]
        shifted = [
            [value * valid[tap] for tap, value in enumerate(moved[:-1])] + moved[-1:]
            for moved in shifted
        ]
        totals = [
            sum(
                conv[which, tap : tap + 1, lanes] * moved[tap] for tap in range(taps)
            )
            for moved, (which, lanes) in zip(shifted, places)
        ]
        sigmas = [sigmoid(total) for total in totals]
        acts = [total * sigma for total, sigma in zip(totals, sigmas)]
        slopes = [sigma + act * (1.0 - sigma) for sigma, act in zip(sigmas, acts)]
        squares = [
            jnp.sum(act * act, -1, keepdims=True) if which < 2 else None
            for act, (which, _) in zip(acts, group)
        ]
        grads = [
            grad * lives if which == 1 else grad for grad, (which, _) in zip(grads, group)
        ]
        scales = [None if square is None else lax.rsqrt(square + KEY_EPS) for square in squares]
        units = [act if scale is None else act * scale for act, scale in zip(acts, scales)]
        along = [
            None if scale is None else jnp.sum(grad * unit, -1, keepdims=True)
            for grad, unit, scale in zip(grads, units, scales)
        ]
        grads = [
            slope * (grad if scale is None else scale * (grad - unit * dot))
            for slope, grad, scale, unit, dot in zip(slopes, grads, scales, units, along)
        ]
        for grad, moved, (which, lanes) in zip(grads, shifted, places):
            result = conv[which, taps - 1 : taps, lanes] * grad
            for tap in range(taps):
                product_ = grad * moved[tap]
                sums[which, tap, :, lanes] += sum(
                    product_[8 * r : 8 * (r + 1)] for r in range(SPAN // 8)
                )
                if tap < taps - 1:
                    masked = grad * valid[tap]
                    later[which, tap, SPAN:, lanes] = later[which, tap, :8, lanes]
                    later[which, tap, :SPAN, lanes] = masked
                    result = result + conv[which, tap : tap + 1, lanes] * (
                        later[which, tap, pl.ds(taps - 1 - tap, SPAN), lanes]
                    )
            grad_pre_out[which, :, lanes] = result
    columns = lax.broadcasted_iota(jnp.int32, (SPAN, heads), 1)
    grad_beta = jnp.zeros((SPAN, heads), jnp.float32)
    for h in range(heads):
        grad_beta = jnp.where(columns == h, beta_columns[h], grad_beta)
    sigma = sigmoid(beta_pre[...])
    grad_beta_out[...] = (
        (grad_beta * lives * sigma * (1.0 - sigma)).astype(LOW).astype(jnp.float32)
    )

    @pl.when(span == 0)
    def _():
        conv_out[...] = jnp.sum(sums[...], 2)
        for which in range(3):
            result = None
            for tap in range(taps - 1):
                ahead = taps - 1 - tap
                rows = jnp.concatenate([jnp.zeros((8, later.shape[3]), jnp.float32), later[which, tap, :8]], 0)
                term = conv[which, tap : tap + 1, :] * rows[ahead:][:8]
                result = term if result is None else result + term
            borrowed_out[which] = result


def back(
    keep, features, beta, beta_pre, solved, inverses, starts, news, grad_mixed, state_in, pre, conv,
    position, live,
):
    _, count, width = features.shape
    heads, size, _ = state_in.shape
    spans = count // SPAN
    taps = conv.shape[1]
    f32 = lambda shape: jax.ShapeDtypeStruct(shape, jnp.float32)
    whole = lambda shape: pl.BlockSpec(shape, lambda c: (0,) * len(shape))
    rows = pl.BlockSpec((SPAN, width), lambda c: (spans - 1 - c, 0))
    triple = pl.BlockSpec((3, SPAN, width), lambda c: (0, spans - 1 - c, 0))
    column = pl.BlockSpec((SPAN, heads), lambda c: (spans - 1 - c, 0))
    return pl.pallas_call(
        back_kernel,
        grid=(spans,),
        in_specs=[
            pl.BlockSpec(memory_space=pltpu.SMEM), triple, column, column,
            pl.BlockSpec((2, SPAN, width), lambda c: (0, spans - 1 - c, 0)),
            pl.BlockSpec((1, heads // 2, 2 * SPAN, 2 * SPAN), lambda c: (spans - 1 - c, 0, 0, 0)),
            pl.BlockSpec((1, heads, size, size), lambda c: (spans - 1 - c, 0, 0, 0)),
            rows, rows, whole((heads, size, size)),
            pl.BlockSpec((3, 1, SPAN + 8, width), lambda c: (0, spans - 1 - c, 0, 0)),
            whole(conv.shape),
            whole(position.shape), whole(live.shape),
        ],
        out_specs=[triple, whole((3, 8, width)), whole((3, taps, width)), column],
        out_shape=[
            f32((3, count, width)), f32((3, 8, width)), f32((3, taps, width)), f32((count, heads)),
        ],
        scratch_shapes=[
            pltpu.VMEM((heads, size, size), jnp.float32),
            pltpu.VMEM((3, taps - 1, SPAN + 8, width), jnp.float32),
            pltpu.VMEM((3, taps, 8, width), jnp.float32),
        ],
        compiler_params=params(),
        cost_estimate=cost(30 * count * width * size * 4, 60 * count * width),
        name="back",
    )(
        keep, features, beta, beta_pre, solved, inverses, starts, news, grad_mixed, state_in, pre,
        conv, position, live,
    )


def enter_kernel(
    tokens, gain, grad_hidden, grads, grad_gate, grad_beta, query_w, key_w, value_w, gate_w, beta_w,
    input_grad_out, gain_out, total,
):
    step = pl.program_id(0)
    term = mxu(grad_gate[...].astype(LOW), gate_w[...], NT)
    for which, weight in enumerate((query_w, key_w, value_w)):
        term = term + mxu(grads[which], weight[...], NT)

    @pl.when(step == 0)
    def _():
        total[...] = term + mxu(grad_beta[...].astype(LOW), beta_w[...], NT)

    @pl.when(step > 0)
    def _():
        total[...] += term

    @pl.when(step == pl.num_programs(0) - 1)
    def _():
        part, gain_part = norm_back(tokens[...].astype(jnp.float32), gain[...], total[...])
        gain_out[...] = gain_part
        input_grad_out[...] = (grad_hidden[...] + part).astype(LOW)


def enter(
    tokens, gain, grad_hidden, grads, grad_gate, grad_beta, query_w, key_w, value_w, gate_w, beta_w
):
    count, width = tokens.shape
    heads = beta_w.shape[1]
    block = 2 * LANES
    whole = lambda shape: pl.BlockSpec(shape, lambda j: (0,) * len(shape))
    weight = pl.BlockSpec((width, block), lambda j: (0, j))
    return pl.pallas_call(
        enter_kernel,
        grid=(width // block,),
        in_specs=[
            whole((count, width)), whole((1, width)), whole((count, width)),
            pl.BlockSpec((3, count, block), lambda j: (0, 0, j)),
            pl.BlockSpec((count, block), lambda j: (0, j)), whole((count, heads)),
            weight, weight, weight, weight, whole((width, heads)),
        ],
        out_specs=[whole((count, width)), whole((1, width))],
        out_shape=[
            jax.ShapeDtypeStruct((count, width), LOW), jax.ShapeDtypeStruct((1, width), jnp.float32),
        ],
        scratch_shapes=[pltpu.VMEM((count, width), jnp.float32)],
        compiler_params=params(),
        cost_estimate=cost(8 * count * width * width, 8 * width * width + 20 * count * width),
        name="enter",
    )(
        tokens, gain, grad_hidden, grads, grad_gate, grad_beta, query_w, key_w, value_w, gate_w,
        beta_w,
    )


def passed_along(value, axis, by):
    devices = lax.axis_size(axis)
    pairs = [(i, i + by) for i in range(devices) if 0 <= i + by < devices]
    return lax.ppermute(value, axis, pairs)


def tuned():
    return (lax.axis_size("seq"), lax.axis_size("doc")) == (8, 4)


HOPS = {"core": ("doc", 1), "y": ("doc", 2), "x": ("seq", 1), "near": ("seq", 2), "far": ("seq", 4)}


def hop(value, way):
    axis, bit = HOPS[way]
    return lax.ppermute(value, axis, [(i, i ^ bit) for i in range(lax.axis_size(axis))])


def side(way):
    axis, bit = HOPS[way]
    return lax.axis_index(axis) // bit % 2


def apply_kernel(maps, state, out, *, turned):
    size = maps.shape[1]
    for h in range(maps.shape[0]):
        matrix = maps[h, :, size:]
        moved = (t_product if turned else product)(matrix, state[h])
        if state.shape[2] == size:
            out[h] = moved + maps[h, :, :size]
        else:
            out[h] = moved + jnp.concatenate([maps[h, :, :size], jnp.zeros_like(matrix)], 1)


def apply_map(maps, state, turned=False):
    return pl.pallas_call(
        lambda *refs: apply_kernel(*refs, turned=turned),
        out_shape=jax.ShapeDtypeStruct(state.shape, jnp.float32),
        compiler_params=params(),
        cost_estimate=cost(2 * maps.size * state.shape[2], 4 * (maps.size + 2 * state.size)),
        name="apply_map",
    )(maps, state)


def carried_forward(maps):
    heads, size, _ = maps.shape
    if not tuned():
        gathered = lax.all_gather(maps, "seq")

        def one(lap, state):
            return apply_map(lax.dynamic_index_in_dim(gathered, lap, 0, False), state)

        zeros = jnp.zeros((heads, size, size), jnp.float32)
        return lax.fori_loop(0, lax.axis_index("seq"), one, zeros), (maps,)
    half = heads // 2
    here, z = side("x") == 0, lax.axis_index("seq") // 2
    kept = jnp.where(here, maps[:half], maps[half:])
    other = hop(jnp.where(here, maps[half:], maps[:half]), "x")
    first, second = jnp.where(here, kept, other), jnp.where(here, other, kept)
    pair_map = apply_map(second, first)
    state = jnp.zeros((half, size, size), jnp.float32)
    for step in range(3):
        sent = pair_map[:, :, :size] if step == 0 else apply_map(pair_map, state)
        state = state + lax.ppermute(sent, "seq", [(2 * step + x, 2 * step + 2 + x) for x in range(2)])
    moved = apply_map(first, state)
    mine = jnp.where(here, state, moved)
    other = hop(jnp.where(here, moved, state), "x")
    low, high = jnp.where(here, mine, other), jnp.where(here, other, mine)
    return jnp.concatenate([low, high], 0), (first, second, pair_map)


def together(value, *others):
    return lax.optimization_barrier((value, *others))


def carried_back(shift, context, beside=((), (), ())):
    heads, size, _ = shift.shape
    if not tuned():
        gathered = lax.all_gather(
            jnp.concatenate([shift, context[0][:, :, size:]], 2), "seq"
        )
        count = lax.axis_size("seq")

        def one(lap, state):
            maps = lax.dynamic_index_in_dim(gathered, count - 1 - lap, 0, False)
            return apply_map(maps, state, True)

        zeros = jnp.zeros((heads, size, size), jnp.float32)
        return lax.fori_loop(0, count - 1 - lax.axis_index("seq"), one, zeros), ()
    first, second, pair_map = context
    half = heads // 2
    here = side("x") == 0
    kept = jnp.where(here, shift[:half], shift[half:])
    other = hop(jnp.where(here, shift[half:], shift[:half]), "x")
    other, *done = together(other, *beside[0])
    first = jnp.concatenate([jnp.where(here, kept, other), first[:, :, size:]], 2)
    second = jnp.concatenate([jnp.where(here, other, kept), second[:, :, size:]], 2)
    pair_map = jnp.concatenate([apply_map(first, second[:, :, :size], True), pair_map[:, :, size:]], 2)
    state = jnp.zeros((half, size, size), jnp.float32)
    for step in range(3, 0, -1):
        sent = pair_map[:, :, :size] if step == 3 else apply_map(pair_map, state, True)
        come = lax.ppermute(sent, "seq", [(2 * step + x, 2 * step - 2 + x) for x in range(2)])
        if step > 1:
            come, *more = together(come, *beside[4 - step])
            done += more
        state = state + come
    moved = apply_map(second, state, True)
    mine = jnp.where(here, moved, state)
    other = jnp.where(here, state, moved)
    other = hop(other, "x")
    low, high = jnp.where(here, mine, other), jnp.where(here, other, mine)
    return jnp.concatenate([low, high], 0), done


def outer_kernel(bit, *refs, blocks, post):
    count = len(blocks)
    lefts, rights = refs[: 2 * count], refs[2 * count : 4 * count]
    *outs, stacked = refs[4 * count :]
    step = pl.program_id(0)
    tokens = lefts[0].shape[1]
    half = outs[0].shape[0]

    @pl.when(step == 0)
    def _():
        for piece in range(count):
            for which in range(2):
                if len(outs) == 1:
                    stacked[piece, :, which * tokens : (which + 1) * tokens] = lefts[
                        2 * piece + which
                    ][...].astype(LOW)
                    continue
                for start in range(0, half, post):
                    for place, mine in ((start, bit[0]), (half + start, 1 - bit[0])):
                        rows = pl.ds(pl.multiple_of(2 * start + mine * post, 8), post)
                        stacked[
                            piece, place : place + post, which * tokens : (which + 1) * tokens
                        ] = lefts[2 * piece + which][rows, :].astype(LOW)

    for piece in range(count):
        low = sum(blocks[:piece])

        @pl.when((step >= low) & (step < low + blocks[piece]))
        def _(piece=piece):
            right = jnp.concatenate(
                [rights[2 * piece][...].astype(LOW), rights[2 * piece + 1][...].astype(LOW)], 0
            )
            for index, out in enumerate(outs):
                out[...] = mxu(stacked[piece, index * half : (index + 1) * half, :], right, NN)


def outer(pieces, way=None):
    rows, tokens = pieces[0][0].shape
    block = 2 * LANES
    post = rows // 8 * {"near": 2, "x": 1}.get(way, 0) or rows // 16
    counts = [piece[5] for piece in pieces]
    left = pl.BlockSpec((rows, tokens), lambda j: (0, 0), pipeline_mode=pl.Buffered(1))
    lefts, rights, specs = [], [], []
    for index, piece in enumerate(pieces):
        lefts += piece[:2]
        rights += piece[2:4]

        def place(j, low=sum(counts[:index]), first=piece[4], number=piece[5]):
            return 0, first + jnp.clip(j - low, 0, number - 1)

        specs += [pl.BlockSpec((tokens, block), place)] * 2
    total = sum(counts)
    number = 2 if way else 1
    out = pl.BlockSpec((rows // number, block), lambda j: (0, j))
    shape = jax.ShapeDtypeStruct((rows // number, total * block), jnp.float32)
    bit = side(way).astype(jnp.int32).reshape(1) if way else jnp.zeros((1,), jnp.int32)
    return pl.pallas_call(
        lambda *refs: outer_kernel(*refs, blocks=counts, post=post),
        grid=(total,),
        in_specs=[pl.BlockSpec(memory_space=pltpu.SMEM)] + [left] * len(lefts) + specs,
        out_specs=[out] * number,
        out_shape=[shape] * number,
        scratch_shapes=[pltpu.VMEM((len(pieces), rows, 2 * tokens), LOW)],
        compiler_params=params(),
        cost_estimate=cost(
            4 * rows * tokens * total * block, 4 * rows * total * block + 8 * tokens * rows
        ),
        name="outer",
    )(bit, *lefts, *rights)


def take(value, place, axis):
    return lax.dynamic_index_in_dim(value, place, axis, False)


class Part:
    def __init__(self, keep, first):
        names = ["far", "near", "x", "y"]
        names.remove(first)
        self.names, self.come = names, None
        self.keep = keep.reshape(2, 2, 2, keep.shape[0] // 8, keep.shape[1])

    def arrived(self, come):
        self.come = come.reshape(self.keep.shape)

    def split(self, way):
        at, bit = self.names.index(way), side(way)
        self.names.remove(way)
        send = take(self.keep, 1 - bit, at) + take(self.come, 1 - bit, at)
        self.keep = take(self.keep, bit, at) + take(self.come, bit, at)
        return send

    def total(self):
        self.keep = self.keep + self.come
        return self.keep

    def whole(self, come):
        first = side("y") == 0
        return jnp.concatenate(
            [jnp.where(first, self.keep, come), jnp.where(first, come, self.keep)], 0
        )


def swaps(moves):
    values = together(*[value for value, _ in moves])
    return together(*[hop(value, way) for value, (_, way) in zip(values, moves)])


def flatten_small(small):
    first_gain, beta, conv, head_gain, second_gain = small
    seq = lax.axis_size("seq")
    flat = jnp.concatenate(
        [
            first_gain.reshape(seq, -1), beta.reshape(seq, -1),
            conv.reshape(conv.shape[0] * conv.shape[1], seq, -1).transpose(1, 0, 2).reshape(seq, -1),
            head_gain.reshape(seq, -1), second_gain.reshape(seq, -1),
        ],
        1,
    )
    size = flat.shape[1]
    rows = -(-size // 2048) * 16
    return jnp.pad(flat, ((0, 0), (0, rows * 128 - size))).reshape(seq * rows, 128)


def unflatten_small(flat, small):
    first_gain, beta, conv, head_gain, second_gain = small
    seq = lax.axis_size("seq")
    flat = flat.reshape(-1)
    sizes = [a.size // seq for a in small]
    places = [sum(sizes[:i]) for i in range(len(sizes))]
    pieces = [flat[p : p + s] for p, s in zip(places, sizes)]
    return (
        pieces[0], pieces[1].reshape(-1, beta.shape[1]),
        pieces[2].reshape(conv.shape[0], conv.shape[1], -1), pieces[3], pieces[4],
    )


def outer_sum(left, right):
    return mxu(left.astype(LOW), right.astype(LOW), TN)


def local(
    tokens,
    doc_lengths,
    out_grad,
    first_gain,
    query_weight,
    key_weight,
    value_weight,
    gate_weight,
    beta_weight,
    conv_weight,
    head_gain,
    out_weight,
    second_gain,
    hidden_gate,
    hidden_up,
    hidden_down,
):
    count, width = (tokens.shape[1], tokens.shape[2])
    heads = beta_weight.shape[1]
    reach = conv_weight.shape[1] - 1
    first = lax.axis_index("seq") * count
    position, live = doc_info(doc_lengths[0], first, count)
    keep = 1.0 - (position[::CK] == 0).astype(jnp.float32)
    position, live = position[:, None], live[:, None]
    core = (lax.axis_index("doc") % 2).astype(jnp.int32).reshape(1)
    here = core[0] == 0
    rows, top = tokens[0], out_grad[0]
    halo = passed_along(rows[count - HALO :].astype(jnp.float32), "seq", 1)
    normed_one, pre, features, gate_pre, beta_pre, beta = project(
        rows, halo, first_gain[None], position, live, query_weight, key_weight, value_weight,
        gate_weight, beta_weight, conv_weight,
    )
    solved, inverses, attend, maps = prepare(keep, features, beta)
    state_in, context = carried_forward(maps)
    starts, news, mixed, normed_head = mix(
        keep, features, solved, attend, gate_pre, head_gain[None], state_in
    )
    head_turned = normed_head.T.astype(jnp.float32)
    (
        block_out, two_turned, inner_turned, kept, sent, grad_hidden, grad_branch, grad_head,
        grad_second_gain,
    ) = feed(
        core, rows, normed_head, top, second_gain[None], out_weight, hidden_gate, hidden_up,
        hidden_down,
    )
    grad_mixed, grad_gate_pre, grad_head_gain, shift = gather_states(
        keep, grad_head, mixed, gate_pre, head_gain[None], features, solved, heads
    )
    if tuned():
        half = width // 2

        def pick(zero, one):
            return jnp.where(here, zero, one)

        def both(value, send=None):
            return value, hop(value if send is None else send, "core")

        wide_top = top.astype(jnp.float32)
        tops = both(
            pick(top[:, :half], top[:, half:]), pick(wide_top[:, half:], wide_top[:, :half])
        )
        one = both(normed_one)
        two = both(two_turned)
        inners = both(inner_turned)
        heads_turned = both(head_turned)
        gate_up = both(kept, sent)
        out_left = pick(heads_turned[0], one[0]), pick(heads_turned[1], one[1])
        out_right = both(pick(grad_branch, grad_gate_pre), pick(grad_gate_pre, grad_branch))
        blocks = hidden_gate.shape[1] // 256
        low = blocks // 2
        some = width // 512
        early = (
            outer([(*two, *gate_up, 0, low), (*out_left, *out_right, 0, some)], "x"),
            outer(
                [
                    (*two, *gate_up, low, blocks - low),
                    (*out_left, *out_right, some, width // 256 - some),
                ],
                "y",
            ),
            outer([(*inners, *tops, 0, half // 256)], "near"),
        )
        state_grad, done = carried_back(shift, context, early)
        keeps, sends = done[0::2], done[1::2]
        ways = ("x", "y", "near")
        cuts = [send.shape[0] // 2 for send in sends]
        state_grad, *begun = together(state_grad, *(s[:c] for s, c in zip(sends, cuts)))
        begun = [hop(value, way) for value, way in zip(begun, ways)]
    else:
        state_grad, _ = carried_back(shift, context)
    grads, borrowed, grad_conv, grad_beta_pre = back(
        keep, features, beta, beta_pre, solved, inverses, starts, news, grad_mixed, state_grad, pre,
        conv_weight, position, live,
    )
    if tuned():
        borrowed, *begun = together(borrowed, *begun)
    returned = passed_along(borrowed, "seq", -1)
    tail = grads[:, count - 8 :] + returned
    grads = lax.dynamic_update_slice(grads, tail, (0, count - 8, 0))
    grads = grads.astype(LOW)
    if tuned():
        grads, *rest = together(grads, *(s[c:] for s, c in zip(sends, cuts)))
        rest = [hop(value, way) for value, way in zip(rest, ways)]
        wide = grads.astype(jnp.float32)
        query_key = both(pick(grads[0], grads[1]), pick(wide[1], wide[0]))
        value = both(
            pick(grads[2, :, :half], grads[2, :, half:]), pick(wide[2, :, half:], wide[2, :, :half])
        )
        late = (
            outer([(*one, *query_key, 0, half // 256)], "x"),
            outer([(*one, *query_key, half // 256, half // 256)], "y"),
            outer([(*one, *value, 0, half // 256)], "near"),
        )
        input_grad, grad_first_gain = enter(
            rows, first_gain[None], grad_hidden, grads, grad_gate_pre, grad_beta_pre, query_weight,
            key_weight, value_weight, gate_weight, beta_weight,
        )
        small = (
            grad_first_gain[0], outer_sum(normed_one.T, grad_beta_pre), grad_conv, grad_head_gain[0],
            grad_second_gain[0],
        )
        flat = flatten_small(small)
        sends = [send for _, send in late]
        early = [Part(keep_, way) for keep_, way in zip(keeps, ways)]
        late = [Part(keep_, way) for (keep_, _), way in zip(late, ways)]
        input_grad, flat, *joined = together(input_grad, flat, *rest, *sends)
        rest, sends = joined[:3], joined[3:]
        for part, one_half, other_half in zip(early, begun, rest):
            part.arrived(jnp.concatenate([one_half, other_half], 0))
        orders = (("y", "near", "far"), ("near", "x", "far"), ("x", "y", "far"))

        def stage(parts, lap):
            return [(part.split(order[lap]), order[lap]) for part, order in zip(parts, orders)]

        def arrive(parts, comes):
            for part, come in zip(parts, comes):
                part.arrived(come)

        *comes, flat_come = swaps(stage(early, 0) + list(zip(sends, ways)) + [(flat, "core")])
        flat = (flat + flat_come).reshape(4, 2, -1, 128)
        bit = side("x")
        tiny = Part(take(flat, bit, 1).reshape(-1, 128), "x")
        tiny_send = take(flat, 1 - bit, 1).reshape(-1, 128)
        arrive(early + late, comes)
        for lap, way, following in ((0, "x", "y"), (1, "y", "near")):
            *comes, flat_come = swaps(
                stage(early, lap + 1) + stage(late, lap) + [(tiny_send, way)]
            )
            tiny.arrived(flat_come)
            tiny_send = tiny.split(following)
            arrive(early + late, comes)
        *comes, flat_come = swaps(
            [(part.total(), "y") for part in early] + stage(late, 2) + [(tiny_send, "near")]
        )
        tiny.arrived(flat_come)
        early = [part.whole(come) for part, come in zip(early, comes)]
        arrive(late, comes[3:])
        a, b = low * 256, (blocks - low) * 256
        own = (
            jnp.concatenate([early[0][:, :a], early[1][:, :b]], 1), early[2],
            jnp.concatenate([early[0][:, a:], early[1][:, b:]], 1),
        )
        *comes, flat_come, other_a, other_b, other_c = swaps(
            [(part.total(), "y") for part in late] + [(tiny.split("far"), "far")]
            + [(value, "core") for value in own]
        )
        late = [part.whole(come) for part, come in zip(late, comes)]
        tiny.arrived(flat_come)
        own = (*own, jnp.concatenate(late[:2], 1), late[2])
        *last, flat_come = swaps([(own[3], "core"), (own[4], "core"), (tiny.total(), "y")])
        other = (other_a, other_b, other_c, *last)
        zero = [pick(m, o) for m, o in zip(own, other)]
        one_ = [pick(o, m) for m, o in zip(own, other)]
        query_g, key_g = zero[3], one_[3]
        value_g = jnp.concatenate([zero[4], one_[4]], 1)
        gate_g, out_g, hidden_gate_g, hidden_up_g = one_[2], zero[2], zero[0], one_[0]
        hidden_down_g = jnp.concatenate([zero[1], one_[1]], 1)
        first_g, beta_g, conv_g, head_g, second_g = unflatten_small(tiny.whole(flat_come), small)
    else:
        input_grad, grad_first_gain = enter(
            rows, first_gain[None], grad_hidden, grads, grad_gate_pre, grad_beta_pre, query_weight,
            key_weight, value_weight, gate_weight, beta_weight,
        )
        small = (
            grad_first_gain[0], outer_sum(normed_one.T, grad_beta_pre), grad_conv, grad_head_gain[0],
            grad_second_gain[0],
        )

        def whole(term, dimension):
            part = lax.psum_scatter(term, "seq", scatter_dimension=dimension, tiled=True)
            return lax.psum(part, "doc")

        gate_grad, up_grad = jnp.where(here, kept, sent), jnp.where(here, sent, kept)
        terms = (
            outer_sum(normed_one.T, grads[0]), outer_sum(normed_one.T, grads[1]),
            outer_sum(normed_one.T, grads[2]), outer_sum(normed_one.T, grad_gate_pre),
            outer_sum(head_turned.T, grad_branch), outer_sum(two_turned.T, gate_grad),
            outer_sum(two_turned.T, up_grad), outer_sum(inner_turned.T, top),
        )
        query_g, key_g, value_g, gate_g, out_g, hidden_gate_g, hidden_up_g, hidden_down_g = (
            whole(term, 0) for term in terms
        )
        first_g, beta_g, conv_g, head_g, second_g = (
            whole(term, d) for term, d in zip(small, (0, 0, 2, 0, 0))
        )
    return (
        block_out[None], input_grad[None], first_g, query_g, key_g, value_g, gate_g, beta_g, conv_g,
        head_g, out_g, second_g, hidden_gate_g, hidden_up_g, hidden_down_g,
    )


def solution(mesh):
    in_specs = (
        P("doc", "seq", None),
        P("doc", None),
        P("doc", "seq", None),
        P(),
        P(),
        P(),
        P(),
        P(),
        P(),
        P(),
        P(),
        P(),
        P(),
        P(),
        P(),
        P(),
    )
    out_specs = (
        P("doc", "seq", None),
        P("doc", "seq", None),
        P("seq"),
        P("seq", None),
        P("seq", None),
        P("seq", None),
        P("seq", None),
        P("seq", None),
        P(None, None, "seq"),
        P("seq"),
        P("seq", None),
        P("seq"),
        P("seq", None),
        P("seq", None),
        P("seq", None),
    )
    return jax.shard_map(local, mesh=mesh, in_specs=in_specs, out_specs=out_specs, check_vma=False)
```

```python
import jax
import jax.numpy as jnp
from jax import lax
from jax.experimental import pallas as pl
from jax.experimental.pallas import tpu as pltpu
from jax.sharding import PartitionSpec as P

CK = 64


EPS = 1e-05
KEY_EPS = 1e-06
HIGH = lax.Precision.HIGHEST


def doc_info(lengths, first, count):
    padded = (lengths + CK - 1) // CK * CK
    ends = jnp.cumsum(padded)
    starts = ends - padded
    place = first + jnp.arange(count, dtype=jnp.int32)
    inside = ((place[:, None] >= starts[None, :]) & (place[:, None] < ends[None, :])).astype(
        jnp.int32
    )
    position = place - jnp.sum(inside * starts[None, :], 1)
    length = jnp.sum(inside * lengths[None, :], 1)
    live = (position < length).astype(jnp.float32)
    return (position, live)


SPAN = CK
LANES = 128
LOW = jnp.bfloat16
NN = (((1,), (0,)), ((), ()))
NT = (((1,), (1,)), ((), ()))
TN = (((0,), (0,)), ((), ()))


def params(mib=52):
    return pltpu.CompilerParams(vmem_limit_bytes=mib * 2**20)


def cost(flops, moved):
    return pl.CostEstimate(flops=1, bytes_accessed=1, transcendentals=0)


def mxu(left, right, dims):
    return lax.dot_general(left, right, dims, preferred_element_type=jnp.float32)


def halves(value):
    high = value.astype(LOW)
    return high, (value - high.astype(jnp.float32)).astype(LOW)


def split(value):
    return value if isinstance(value, tuple) else halves(value)


def stack(first, second):
    return tuple(jnp.concatenate(both, 0) for both in zip(first, second))


def fold(value):
    half = value.shape[1] // 2
    return value[:, :half] + value[:, half:]


def product(left, right):
    left_high, left_low = split(left)
    right_high, right_low = split(right)
    both = jnp.concatenate([left_high, left_low], 1)
    if right_high.shape[1] <= LANES:
        wide = jnp.concatenate([right_high, right_low], 1)
        return fold(mxu(both, jnp.concatenate([wide, wide], 0), NN))
    return mxu(both, jnp.concatenate([right_high, right_high], 0), NN) + mxu(
        left_high, right_low, NN
    )


def product_t(left, right):
    left_high, left_low = split(left)
    right_high, right_low = split(right)
    both = jnp.concatenate([left_high, left_low], 1)
    if right_high.shape[0] <= LANES:
        rows = jnp.concatenate(
            [
                jnp.concatenate([right_high, right_high], 1),
                jnp.concatenate([right_low, right_low], 1),
            ],
            0,
        )
        return fold(mxu(both, rows, NT))
    return mxu(both, jnp.concatenate([right_high, right_high], 1), NT) + mxu(
        left_high, right_low, NT
    )


def t_product(left, right):
    left_high, left_low = split(left)
    right_high, right_low = split(right)
    both = jnp.concatenate([left_high, left_low], 0)
    if right_high.shape[1] <= LANES:
        wide = jnp.concatenate([right_high, right_low], 1)
        return fold(mxu(both, jnp.concatenate([wide, wide], 0), TN))
    return mxu(both, jnp.concatenate([right_high, right_high], 0), TN) + mxu(
        left_high, right_low, TN
    )


def head(value, h):
    return value[:, h * LANES : (h + 1) * LANES]


def pair(value, p):
    return jnp.concatenate([head(value, 2 * p), head(value, 2 * p + 1)], 0)


def pair_column(value, p):
    return jnp.concatenate([value[:, 2 * p : 2 * p + 1], value[:, 2 * p + 1 : 2 * p + 2]], 0)


def masks(rows):
    i = lax.broadcasted_iota(jnp.int32, (rows, rows), 0)
    j = lax.broadcasted_iota(jnp.int32, (rows, rows), 1)
    same = (i >= SPAN) == (j >= SPAN)
    strict = jnp.where(same & (j < i), 1.0, 0.0)
    inclusive = jnp.where(same & (j <= i), 1.0, 0.0)
    upper = jnp.where(same & (j >= i), 1.0, 0.0)
    return strict, inclusive, upper, jnp.where(i == j, 1.0, 0.0)


def inverses_of(strict_parts, identity):
    rows = identity.shape[0]
    results = [identity - part for part in strict_parts]
    powers = [split(part) for part in strict_parts]
    powers = [split(product(power, power)) for power in powers]
    for level in range(SPAN.bit_length() - 3):
        both = [
            product(stack(split(result), power), power) for result, power in zip(results, powers)
        ]
        results = [result + pair_[:rows] for result, pair_ in zip(results, both)]
        powers = [split(pair_[rows:]) for pair_ in both]
    return [result + product(result, power) for result, power in zip(results, powers)]


def sigmoid(value):
    return 1.0 / (1.0 + jnp.exp(-value))


HALO = 16


def project_kernel(
    tokens, halo, gain, position, live, query_w, key_w, value_w, gate_w, beta_w, conv,
    normed_out, pre_out, feature_out, gate_out, beta_pre_out, beta_out, normed, pre,
):
    count = tokens.shape[0]

    @pl.when(pl.program_id(0) == 0)
    def _():
        def norm(rows):
            return (
                rows * lax.rsqrt(jnp.mean(rows * rows, -1, keepdims=True) + EPS) * gain[...]
            ).astype(LOW)

        normed[:HALO, :] = norm(halo[...])
        rounded = norm(tokens[...].astype(jnp.float32))
        normed[HALO:, :] = rounded
        normed_out[...] = rounded.astype(jnp.float32).T
        beta_pre = mxu(rounded, beta_w[...], NN)
        beta_pre_out[...] = beta_pre
        beta_out[...] = sigmoid(beta_pre) * live[...]

    gate_out[...] = mxu(normed[HALO:, :], gate_w[...], NN)
    valid = [
        jnp.broadcast_to(
            jnp.where(position[...] >= conv.shape[1] - 1 - tap, 1.0, 0.0), (count, LANES)
        )
        for tap in range(conv.shape[1] - 1)
    ]
    for which, weight in enumerate((query_w, key_w, value_w)):
        pre[which] = mxu(normed[...], weight[...], NN)
        for span in range(count // SPAN):
            start = HALO + span * SPAN
            pre_out[which, span] = pre[which, start - 8 : start + SPAN, :]
        for part in range(pre.shape[2] // LANES):
            lanes = slice(part * LANES, (part + 1) * LANES)
            total = conv_total(pre, which, HALO, count, lanes, conv, valid)
            value = total * sigmoid(total)
            if which < 2:
                value = value * lax.rsqrt(jnp.sum(value * value, -1, keepdims=True) + KEY_EPS)
            if which == 1:
                value = value * live[...]
            feature_out[which, :, lanes] = value


def conv_total(pre, which, first, count, lanes, conv, valid):
    taps = conv.shape[1]
    total = None
    for tap in range(taps):
        start = first - (taps - 1) + tap
        term = conv[which, tap : tap + 1, lanes] * pre[which, start : start + count, lanes]
        if tap < taps - 1:
            term = term * valid[tap]
        total = term if total is None else total + term
    return total


def project(tokens, halo, gain, position, live, query_w, key_w, value_w, gate_w, beta_w, conv):
    count, width = tokens.shape
    heads = beta_w.shape[1]
    block = 2 * LANES
    whole = lambda shape: pl.BlockSpec(shape, lambda j: (0,) * len(shape))
    weight = pl.BlockSpec((width, block), lambda j: (0, j))
    f32 = lambda shape: jax.ShapeDtypeStruct(shape, jnp.float32)
    return pl.pallas_call(
        project_kernel,
        grid=(width // block,),
        in_specs=[
            whole((count, width)), whole((HALO, width)), whole((1, width)), whole((count, 1)),
            whole((count, 1)), weight, weight, weight, weight, whole((width, heads)),
            pl.BlockSpec((3, conv.shape[1], block), lambda j: (0, 0, j)),
        ],
        out_specs=[
            whole((width, count)),
            pl.BlockSpec((3, count // SPAN, SPAN + 8, block), lambda j: (0, 0, 0, j)),
            pl.BlockSpec((3, count, block), lambda j: (0, 0, j)),
            pl.BlockSpec((count, block), lambda j: (0, j)),
            whole((count, heads)), whole((count, heads)),
        ],
        out_shape=[
            f32((width, count)), f32((3, count // SPAN, SPAN + 8, width)), f32((3, count, width)),
            f32((count, width)), f32((count, heads)), f32((count, heads)),
        ],
        scratch_shapes=[
            pltpu.VMEM((HALO + count, width), LOW),
            pltpu.VMEM((3, HALO + count, block), jnp.float32),
        ],
        compiler_params=params(),
        cost_estimate=cost(8 * count * width * width, 8 * width * width + 40 * count * width),
        name="project",
    )(tokens, halo, gain, position, live, query_w, key_w, value_w, gate_w, beta_w, conv)


def prepare_kernel(keep, features, beta, solved_out, inverse_out, attend_out, state):
    span = pl.program_id(0)
    heads = state.shape[0]
    size = state.shape[1]
    strict, inclusive, upper, identity = masks(2 * SPAN)

    @pl.when(span == 0)
    def _():
        i = lax.broadcasted_iota(jnp.int32, (size, 2 * size), 0)
        j = lax.broadcasted_iota(jnp.int32, (size, 2 * size), 1)
        for h in range(heads):
            state[h] = jnp.where(j == i + size, 1.0, 0.0)

    query, key, value = features[0], features[1], features[2]
    betas = beta[...]
    flag = keep[span]
    pairs = range(heads // 2)
    keys = [split(pair(key, p)) for p in pairs]
    columns = [pair_column(betas, p) for p in pairs]
    scores = [product_t(stack(keys[p], split(pair(query, p))), keys[p]) for p in pairs]
    solved = inverses_of([columns[p] * scores[p][: 2 * SPAN] * strict for p in pairs], identity)
    both = [
        product(
            solved[p],
            jnp.concatenate([columns[p] * pair(key, p), columns[p] * pair(value, p)], 1),
        )
        for p in pairs
    ]
    for p in pairs:
        inverse_out[0, p] = solved[p]
        attend_out[0, p] = scores[p][2 * SPAN :] * inclusive
    starts, news = [], []
    for h in range(heads):
        rows = slice(h % 2 * SPAN, (h % 2 + 1) * SPAN)
        erase, update = both[h // 2][rows, :size], both[h // 2][rows, size:]
        solved_out[0, :, h * size : (h + 1) * size] = erase
        solved_out[1, :, h * size : (h + 1) * size] = update
        start = state[h] * flag
        starts.append(start)
        news.append(
            jnp.concatenate([update, jnp.zeros_like(update)], 1) - product(erase, start)
        )
    for h in range(heads):
        rows = slice(h % 2 * SPAN, (h % 2 + 1) * SPAN)
        state[h] = starts[h] + t_product(tuple(k[rows] for k in keys[h // 2]), news[h])


def prepare(keep, features, beta):
    _, count, width = features.shape
    heads = beta.shape[1]
    size = width // heads
    spans = count // SPAN
    f32 = lambda shape: jax.ShapeDtypeStruct(shape, jnp.float32)
    matrix = pl.BlockSpec((1, heads // 2, 2 * SPAN, 2 * SPAN), lambda c: (c, 0, 0, 0))
    return pl.pallas_call(
        prepare_kernel,
        grid=(spans,),
        in_specs=[
            pl.BlockSpec(memory_space=pltpu.SMEM),
            pl.BlockSpec((3, SPAN, width), lambda c: (0, c, 0)),
            pl.BlockSpec((SPAN, heads), lambda c: (c, 0)),
        ],
        out_specs=[
            pl.BlockSpec((2, SPAN, width), lambda c: (0, c, 0)), matrix, matrix,
            pl.BlockSpec((heads, size, 2 * size), lambda c: (0, 0, 0)),
        ],
        out_shape=[
            f32((2, count, width)), f32((spans, heads // 2, 2 * SPAN, 2 * SPAN)),
            f32((spans, heads // 2, 2 * SPAN, 2 * SPAN)), f32((heads, size, 2 * size)),
        ],
        compiler_params=params(),
        cost_estimate=cost(40 * count * width * size * 4, 60 * count * width),
        name="prepare",
    )(keep, features, beta)


def mix_kernel(
    keep, place, features, solved, attend, gate, gain, state_mine, state_other, starts_out, new_out,
    mixed_out, normed_out, state,
):
    span = pl.program_id(0)
    heads = state.shape[0]

    @pl.when(span == 0)
    def _():
        half = heads // 2
        first = place[0] == 0
        state[:half] = jnp.where(first, state_mine[...], state_other[...])
        state[half:] = jnp.where(first, state_other[...], state_mine[...])

    query, key = features[0], features[1]
    erase, update = solved[0], solved[1]
    flag = keep[span]
    every, pairs = range(heads), range(heads // 2)
    starts = [state[h] * flag for h in every]
    both = [
        product(jnp.concatenate([head(erase, h), head(query, h)], 0), starts[h]) for h in every
    ]
    news = [split(head(update, h) - both[h][:SPAN]) for h in every]
    after = [starts[h] + t_product(head(key, h), news[h]) for h in every]
    inner = [product(attend[0, p], stack(news[2 * p], news[2 * p + 1])) for p in pairs]
    for h in every:
        lanes = slice(h * LANES, (h + 1) * LANES)
        starts_out[0, h] = starts[h]
        state[h] = after[h]
        new_out[:, lanes] = head(update, h) - both[h][:SPAN]
        rows = both[h][SPAN:] + inner[h // 2][h % 2 * SPAN : (h % 2 + 1) * SPAN]
        mixed_out[:, lanes] = rows
        shaped = rows * lax.rsqrt(jnp.mean(rows * rows, -1, keepdims=True) + EPS) * gain[...]
        gates = gate[:, lanes]
        normed_out[:, lanes] = (shaped * (gates * sigmoid(gates))).astype(LOW)


def mix(keep, place, features, solved, attend, gate, gain, state_mine, state_other):
    _, count, width = features.shape
    half, size, _ = state_mine.shape
    heads = 2 * half
    spans = count // SPAN
    f32 = lambda shape: jax.ShapeDtypeStruct(shape, jnp.float32)
    rows = pl.BlockSpec((SPAN, width), lambda c: (c, 0))
    pairs = pl.BlockSpec((2, SPAN, width), lambda c: (0, c, 0))
    return pl.pallas_call(
        mix_kernel,
        grid=(spans,),
        in_specs=[
            pl.BlockSpec(memory_space=pltpu.SMEM), pl.BlockSpec(memory_space=pltpu.SMEM), pairs, pairs,
            pl.BlockSpec((1, heads // 2, 2 * SPAN, 2 * SPAN), lambda c: (c, 0, 0, 0)),
            rows, pl.BlockSpec((1, size), lambda c: (0, 0)),
            pl.BlockSpec((half, size, size), lambda c: (0, 0, 0)),
            pl.BlockSpec((half, size, size), lambda c: (0, 0, 0)),
        ],
        out_specs=[
            pl.BlockSpec((1, heads, size, size), lambda c: (c, 0, 0, 0)), rows, rows, rows,
        ],
        out_shape=[
            f32((spans, heads, size, size)), f32((count, width)), f32((count, width)),
            jax.ShapeDtypeStruct((count, width), LOW),
        ],
        scratch_shapes=[pltpu.VMEM((heads, size, size), jnp.float32)],
        compiler_params=params(),
        cost_estimate=cost(8 * count * width * size * 4, 40 * count * width),
        name="mix",
    )(keep, place, features, solved, attend, gate, gain, state_mine, state_other)


def feed_kernel(
    core, tokens, normed_head, grad_top, second_gain, out_w, gate_w, up_w, down_w,
    block_out, normed_out, inner_out, kept_out, sent_out, grad_hidden_out, branch_out, grad_head_out,
    gain_grad_out, head_turned_out, hidden, normed, total, grad_total,
):
    step = pl.program_id(0)

    @pl.when(step == 0)
    def _():
        state = tokens[...].astype(jnp.float32) + mxu(normed_head[...], out_w[...], NN)
        hidden[...] = state
        rounded = (
            state * lax.rsqrt(jnp.mean(state * state, -1, keepdims=True) + EPS) * second_gain[...]
        ).astype(LOW)
        normed[...] = rounded
        normed_out[...] = rounded.astype(jnp.float32).T
        head_turned_out[...] = normed_head[...].astype(jnp.float32).T

    @pl.when(step == 0)
    def _():
        total[...] = jnp.zeros_like(total)
        grad_total[...] = jnp.zeros_like(grad_total)

    first = core[0] == 0
    size = normed.shape[0] // 1
    parts = [slice(i * size, (i + 1) * size) for i in range(1)]
    gates = [mxu(normed[part, :], gate_w[...], NN) for part in parts]
    ups = [mxu(normed[part, :], up_w[...], NN) for part in parts]
    grad_inners = [mxu(grad_top[part, :], down_w[...], NT) for part in parts]
    for part, gate, up, grad_inner in zip(parts, gates, ups, grad_inners):
        sigma = sigmoid(gate)
        act = gate * sigma
        inner = (act * up).astype(LOW)
        inner_out[:, part] = inner.astype(jnp.float32).T
        wide_gate = grad_inner * up * (sigma + act * (1.0 - sigma))
        wide_up = grad_inner * act
        grad_gate, grad_up = wide_gate.astype(LOW), wide_up.astype(LOW)
        kept_out[part, :] = jnp.where(first, wide_gate, wide_up).astype(LOW)
        sent_out[part, :] = jnp.where(first, wide_up, wide_gate).astype(LOW).astype(jnp.float32)
        total[part, :] += mxu(inner, down_w[...], NN)
        grad_total[part, :] += mxu(grad_gate, gate_w[...], NT) + mxu(grad_up, up_w[...], NT)

    @pl.when(step == pl.num_programs(0) - 1)
    def _():
        state = hidden[...]
        block_out[...] = (state + total[...]).astype(LOW)
        part, gain_part = norm_back(state, second_gain[...], grad_total[...])
        gain_grad_out[...] = gain_part
        grad_hidden = grad_top[...].astype(jnp.float32) + part
        grad_hidden_out[...] = grad_hidden
        branch = grad_hidden.astype(LOW)
        branch_out[...] = branch.astype(jnp.float32)
        grad_head_out[...] = mxu(branch, out_w[...], NT)


def norm_back(value, gain, grad):
    scale = lax.rsqrt(jnp.mean(value * value, -1, keepdims=True) + EPS)
    unit = value * scale
    gain_grad = jnp.sum(grad * unit, 0, keepdims=True)
    inward = grad * gain
    return scale * (inward - unit * jnp.mean(inward * unit, -1, keepdims=True)), gain_grad


def feed(core, tokens, normed_head, grad_top, second_gain, out_w, gate_w, up_w, down_w):
    count, width = tokens.shape
    hidden = gate_w.shape[1]
    block = 2 * LANES
    whole = lambda shape: pl.BlockSpec(shape, lambda j: (0,) * len(shape))
    f32 = lambda shape: jax.ShapeDtypeStruct(shape, jnp.float32)
    low = lambda shape: jax.ShapeDtypeStruct(shape, LOW)
    rows = whole((count, width))
    columns = pl.BlockSpec((count, block), lambda j: (0, j))
    return pl.pallas_call(
        feed_kernel,
        grid=(hidden // block,),
        in_specs=[
            pl.BlockSpec(memory_space=pltpu.SMEM), rows, rows, rows, whole((1, width)),
            whole((width, width)), pl.BlockSpec((width, block), lambda j: (0, j)),
            pl.BlockSpec((width, block), lambda j: (0, j)),
            pl.BlockSpec((block, width), lambda j: (j, 0)),
        ],
        out_specs=[
            rows, whole((width, count)), pl.BlockSpec((block, count), lambda j: (j, 0)), columns,
            columns, rows, rows, rows, whole((1, width)), whole((width, count)),
        ],
        out_shape=[
            low((count, width)), f32((width, count)), f32((hidden, count)), low((count, hidden)),
            f32((count, hidden)), f32((count, width)), f32((count, width)), f32((count, width)),
            f32((1, width)), f32((width, count)),
        ],
        scratch_shapes=[
            pltpu.VMEM((count, width), jnp.float32), pltpu.VMEM((count, width), LOW),
            pltpu.VMEM((count, width), jnp.float32), pltpu.VMEM((count, width), jnp.float32),
        ],
        compiler_params=params(),
        cost_estimate=cost(
            12 * count * width * hidden + 4 * count * width * width,
            6 * width * hidden + 10 * count * hidden + 30 * count * width,
        ),
        name="feed",
    )(core, tokens, normed_head, grad_top, second_gain, out_w, gate_w, up_w, down_w)


def gather_kernel(
    keep, core, grad_head, grad_branch, mixed, gate, gain, features, solved, grad_mixed_out,
    grad_gate_out, kept_out, sent_out, gain_out, state,
):
    step = pl.program_id(0)
    span = pl.num_programs(0) - 1 - step
    heads = state.shape[0]
    strict, inclusive, upper, identity = masks(2 * SPAN)

    @pl.when(step == 0)
    def _():
        state[...] = jnp.zeros_like(state)
        gain_out[...] = jnp.zeros_like(gain_out)

    query, key = features[0], features[1]
    erase = solved[0]
    flag = keep[span]
    gain_total = jnp.zeros_like(gain_out[...])
    every, pairs = range(heads), range(heads // 2)
    passes = [product_t(pair(key, p), pair(query, p)) * upper for p in pairs]
    grads = []
    for h in every:
        lanes = slice(h * LANES, (h + 1) * LANES)
        gates = gate[:, lanes]
        sigma = sigmoid(gates)
        rows = mixed[:, lanes]
        grad = grad_head[:, lanes]
        scale = lax.rsqrt(jnp.mean(rows * rows, -1, keepdims=True) + EPS)
        unit = rows * scale
        grad_gate = grad * unit * gain[...] * sigma * (1.0 + gates * (1.0 - sigma))
        grad_gate = grad_gate.astype(LOW).astype(jnp.float32)
        grad_gate_out[:, lanes] = grad_gate
        kept_out[:, lanes] = jnp.where(core[0] == 0, grad_branch[:, lanes], grad_gate).astype(LOW)
        sent_out[:, lanes] = jnp.where(core[0] == 0, grad_gate, grad_branch[:, lanes])
        shaped = grad * gates * sigma
        gain_total = gain_total + jnp.sum(shaped * unit, 0, keepdims=True)
        inward = shaped * gain[...]
        grad_rows = scale * (inward - unit * jnp.mean(inward * unit, -1, keepdims=True))
        grad_mixed_out[:, lanes] = grad_rows
        grads.append(split(grad_rows))
    passed = [product(passes[p], stack(grads[2 * p], grads[2 * p + 1])) for p in pairs]
    ends = [state[h] for h in every]
    grad_new = [
        passed[h // 2][h % 2 * SPAN : (h % 2 + 1) * SPAN] + product(head(key, h), ends[h])
        for h in every
    ]
    for h in every:
        state[h] = flag * (
            ends[h]
            + t_product(
                jnp.concatenate([head(query, h), -head(erase, h)], 0),
                stack(grads[h], split(grad_new[h])),
            )
        )
    gain_out[...] += gain_total


def gather_states(
    keep, core, grad_head, grad_branch, mixed, gate, gain, features, solved, heads
):
    _, count, width = features.shape
    size = width // heads
    spans = count // SPAN
    f32 = lambda shape: jax.ShapeDtypeStruct(shape, jnp.float32)
    rows = pl.BlockSpec((SPAN, width), lambda c: (spans - 1 - c, 0))
    pairs = pl.BlockSpec((2, SPAN, width), lambda c: (0, spans - 1 - c, 0))
    one = pl.BlockSpec((1, SPAN, width), lambda c: (0, spans - 1 - c, 0))
    return pl.pallas_call(
        gather_kernel,
        grid=(spans,),
        in_specs=[
            pl.BlockSpec(memory_space=pltpu.SMEM), pl.BlockSpec(memory_space=pltpu.SMEM), rows, rows,
            rows, rows, pl.BlockSpec((1, size), lambda c: (0, 0)), pairs, one,
        ],
        out_specs=[
            rows, rows, rows, rows, pl.BlockSpec((1, size), lambda c: (0, 0)),
            pl.BlockSpec((heads, size, size), lambda c: (0, 0, 0)),
        ],
        out_shape=[
            f32((count, width)), f32((count, width)), jax.ShapeDtypeStruct((count, width), LOW),
            f32((count, width)), f32((1, size)), f32((heads, size, size)),
        ],
        compiler_params=params(),
        cost_estimate=cost(8 * count * width * size * 4, 32 * count * width),
        name="gather_states",
    )(keep, core, grad_head, grad_branch, mixed, gate, gain, features, solved)


def back_kernel(
    keep, place, features, beta, beta_pre, solved, inverses, starts, news, grad_mixed, state_mine,
    state_other, pre, conv, position, live, grad_pre_out, borrowed_out, conv_out, grad_beta_out, state, later, sums,
):
    step = pl.program_id(0)
    span = pl.num_programs(0) - 1 - step
    heads = state.shape[0]
    taps = conv.shape[1]
    strict, inclusive, upper, identity = masks(2 * SPAN)

    @pl.when(step == 0)
    def _():
        half = heads // 2
        first = place[0] == 0
        state[:half] = jnp.where(first, state_mine[...], state_other[...])
        state[half:] = jnp.where(first, state_other[...], state_mine[...])
        sums[...] = jnp.zeros_like(sums)
        later[...] = jnp.zeros_like(later)

    query, key, value = features[0], features[1], features[2]
    erase, update = solved[0], solved[1]
    betas = beta[...]
    flag = keep[span]
    base = pl.multiple_of(span * SPAN, SPAN)
    places = position[pl.ds(base, SPAN), :]
    lives = live[pl.ds(base, SPAN), :]
    valid = [
        jnp.broadcast_to(jnp.where(places >= taps - 1 - tap, 1.0, 0.0), (SPAN, LANES))
        for tap in range(taps - 1)
    ]
    every, pairs = range(heads), range(heads // 2)
    part = [slice(h % 2 * SPAN, (h % 2 + 1) * SPAN) for h in every]
    q = [split(pair(query, p)) for p in pairs]
    k = [split(pair(key, p)) for p in pairs]
    b = [pair_column(betas, p) for p in pairs]
    grad_out = [split(pair(grad_mixed, p)) for p in pairs]
    new = [split(pair(news, p)) for p in pairs]
    erases = [split(pair(erase, p)) for p in pairs]
    row = lambda value, h: tuple(v[part[h]] for v in value[h // 2])
    scores = [product_t(k[p], stack(k[p], q[p])) for p in pairs]
    passed = [product(scores[p][:, 2 * SPAN :] * upper, grad_out[p]) for p in pairs]
    ends = [split(state[h]) for h in every]
    begin = [split(starts[0, h]) for h in every]
    grad_new = [passed[h // 2][part[h]] + product(row(k, h), ends[h]) for h in every]
    grad_news = [split(value) for value in grad_new]
    both = [product_t(stack(row(grad_out, h), grad_news[h]), begin[h]) for h in every]
    grad_key = [product_t(row(new, h), ends[h]) for h in every]
    for h in every:
        state[h] = flag * (
            state[h]
            + t_product(
                stack(row(q, h), tuple(-v for v in row(erases, h))),
                stack(row(grad_out, h), grad_news[h]),
            )
        )
    grad_attend = [product_t(grad_out[p], new[p]) * inclusive for p in pairs]
    joined = lambda values, p: jnp.concatenate([values[2 * p], values[2 * p + 1]], 0)
    grad_q = [
        joined([value[:SPAN] for value in both], p) + product(grad_attend[p], k[p]) for p in pairs
    ]
    grad_k = [joined(grad_key, p) + product(grad_attend[p].T, q[p]) for p in pairs]
    turned = [
        product(
            inverses[0, p].T,
            jnp.concatenate(
                [joined(grad_new, p), -joined([value[SPAN:] for value in both], p)], 1
            ),
        )
        for p in pairs
    ]
    grad_bv = [value[:, :LANES] for value in turned]
    grad_bk = [value[:, LANES:] for value in turned]
    grad_lower = [
        -strict * (product_t(grad_bv[p], pair(update, p)) + product_t(grad_bk[p], erases[p]))
        for p in pairs
    ]
    inner = [b[p] * grad_lower[p] for p in pairs]
    grad_k = [
        grad_k[p] + product(inner[p] + inner[p].T, k[p]) + b[p] * grad_bk[p] for p in pairs
    ]
    grad_v = [b[p] * grad_bv[p] for p in pairs]
    beta_columns = []
    for p in pairs:
        grad_b = (
            jnp.sum(grad_lower[p] * scores[p][:, : 2 * SPAN], -1, keepdims=True)
            + jnp.sum(grad_bv[p] * pair(value, p), -1, keepdims=True)
            + jnp.sum(grad_bk[p] * pair(key, p), -1, keepdims=True)
        )
        beta_columns += [grad_b[:SPAN], grad_b[SPAN:]]
    chunks = [(which, h) for which in range(3) for h in every]
    for start in range(0, len(chunks), 4):
        group = chunks[start : start + 4]
        places = [(which, slice(h * LANES, (h + 1) * LANES)) for which, h in group]
        grads = [(grad_q, grad_k, grad_v)[which][h // 2][part[h]] for which, h in group]
        shifted = [
            [
                pre[which, 0, pl.ds(8 - (taps - 1) + tap, SPAN), lanes]
                for tap in range(taps)
            ]
            for which, lanes in places
        ]
        shifted = [
            [value * valid[tap] for tap, value in enumerate(moved[:-1])] + moved[-1:]
            for moved in shifted
        ]
        totals = [
            sum(
                conv[which, tap : tap + 1, lanes] * moved[tap] for tap in range(taps)
            )
            for moved, (which, lanes) in zip(shifted, places)
        ]
        sigmas = [sigmoid(total) for total in totals]
        acts = [total * sigma for total, sigma in zip(totals, sigmas)]
        slopes = [sigma + act * (1.0 - sigma) for sigma, act in zip(sigmas, acts)]
        squares = [
            jnp.sum(act * act, -1, keepdims=True) if which < 2 else None
            for act, (which, _) in zip(acts, group)
        ]
        grads = [
            grad * lives if which == 1 else grad for grad, (which, _) in zip(grads, group)
        ]
        scales = [None if square is None else lax.rsqrt(square + KEY_EPS) for square in squares]
        units = [act if scale is None else act * scale for act, scale in zip(acts, scales)]
        along = [
            None if scale is None else jnp.sum(grad * unit, -1, keepdims=True)
            for grad, unit, scale in zip(grads, units, scales)
        ]
        grads = [
            slope * (grad if scale is None else scale * (grad - unit * dot))
            for slope, grad, scale, unit, dot in zip(slopes, grads, scales, units, along)
        ]
        for grad, moved, (which, lanes) in zip(grads, shifted, places):
            result = conv[which, taps - 1 : taps, lanes] * grad
            for tap in range(taps):
                product_ = grad * moved[tap]
                sums[which, tap, :, lanes] += sum(
                    product_[8 * r : 8 * (r + 1)] for r in range(SPAN // 8)
                )
                if tap < taps - 1:
                    masked = grad * valid[tap]
                    later[which, tap, SPAN:, lanes] = later[which, tap, :8, lanes]
                    later[which, tap, :SPAN, lanes] = masked
                    result = result + conv[which, tap : tap + 1, lanes] * (
                        later[which, tap, pl.ds(taps - 1 - tap, SPAN), lanes]
                    )
            grad_pre_out[which, :, lanes] = result
    columns = lax.broadcasted_iota(jnp.int32, (SPAN, heads), 1)
    grad_beta = jnp.zeros((SPAN, heads), jnp.float32)
    for h in range(heads):
        grad_beta = jnp.where(columns == h, beta_columns[h], grad_beta)
    sigma = sigmoid(beta_pre[...])
    grad_beta_out[...] = (
        (grad_beta * lives * sigma * (1.0 - sigma)).astype(LOW).astype(jnp.float32)
    )

    @pl.when(span == 0)
    def _():
        conv_out[...] = jnp.sum(sums[...], 2)
        for which in range(3):
            result = None
            for tap in range(taps - 1):
                ahead = taps - 1 - tap
                rows = jnp.concatenate([jnp.zeros((8, later.shape[3]), jnp.float32), later[which, tap, :8]], 0)
                term = conv[which, tap : tap + 1, :] * rows[ahead:][:8]
                result = term if result is None else result + term
            borrowed_out[which] = result


def back(
    keep, place, features, beta, beta_pre, solved, inverses, starts, news, grad_mixed, state_mine,
    state_other, pre, conv, position, live,
):
    _, count, width = features.shape
    half, size, _ = state_mine.shape
    heads = 2 * half
    spans = count // SPAN
    taps = conv.shape[1]
    f32 = lambda shape: jax.ShapeDtypeStruct(shape, jnp.float32)
    whole = lambda shape: pl.BlockSpec(shape, lambda c: (0,) * len(shape))
    rows = pl.BlockSpec((SPAN, width), lambda c: (spans - 1 - c, 0))
    triple = pl.BlockSpec((3, SPAN, width), lambda c: (0, spans - 1 - c, 0))
    column = pl.BlockSpec((SPAN, heads), lambda c: (spans - 1 - c, 0))
    return pl.pallas_call(
        back_kernel,
        grid=(spans,),
        in_specs=[
            pl.BlockSpec(memory_space=pltpu.SMEM), pl.BlockSpec(memory_space=pltpu.SMEM), triple, column, column,
            pl.BlockSpec((2, SPAN, width), lambda c: (0, spans - 1 - c, 0)),
            pl.BlockSpec((1, heads // 2, 2 * SPAN, 2 * SPAN), lambda c: (spans - 1 - c, 0, 0, 0)),
            pl.BlockSpec((1, heads, size, size), lambda c: (spans - 1 - c, 0, 0, 0)),
            rows, rows, whole((half, size, size)), whole((half, size, size)),
            pl.BlockSpec((3, 1, SPAN + 8, width), lambda c: (0, spans - 1 - c, 0, 0)),
            whole(conv.shape),
            whole(position.shape), whole(live.shape),
        ],
        out_specs=[triple, whole((3, 8, width)), whole((3, taps, width)), column],
        out_shape=[
            f32((3, count, width)), f32((3, 8, width)), f32((3, taps, width)), f32((count, heads)),
        ],
        scratch_shapes=[
            pltpu.VMEM((heads, size, size), jnp.float32),
            pltpu.VMEM((3, taps - 1, SPAN + 8, width), jnp.float32),
            pltpu.VMEM((3, taps, 8, width), jnp.float32),
        ],
        compiler_params=params(),
        cost_estimate=cost(30 * count * width * size * 4, 60 * count * width),
        name="back",
    )(
        keep, place, features, beta, beta_pre, solved, inverses, starts, news, grad_mixed,
        state_mine, state_other, pre, conv, position, live,
    )


def enter_kernel(
    tokens, gain, grad_hidden, grads, grad_gate, grad_beta, query_w, key_w, value_w, gate_w, beta_w,
    input_grad_out, gain_out, total,
):
    step = pl.program_id(0)
    term = mxu(grad_gate[...].astype(LOW), gate_w[...], NT)
    for which, weight in enumerate((query_w, key_w, value_w)):
        term = term + mxu(grads[which], weight[...], NT)

    @pl.when(step == 0)
    def _():
        total[...] = term + mxu(grad_beta[...].astype(LOW), beta_w[...], NT)

    @pl.when(step > 0)
    def _():
        total[...] += term

    @pl.when(step == pl.num_programs(0) - 1)
    def _():
        part, gain_part = norm_back(tokens[...].astype(jnp.float32), gain[...], total[...])
        gain_out[...] = gain_part
        input_grad_out[...] = (grad_hidden[...] + part).astype(LOW)


def enter(
    tokens, gain, grad_hidden, grads, grad_gate, grad_beta, query_w, key_w, value_w, gate_w, beta_w
):
    count, width = tokens.shape
    heads = beta_w.shape[1]
    block = 2 * LANES
    whole = lambda shape: pl.BlockSpec(shape, lambda j: (0,) * len(shape))
    weight = pl.BlockSpec((width, block), lambda j: (0, j))
    return pl.pallas_call(
        enter_kernel,
        grid=(width // block,),
        in_specs=[
            whole((count, width)), whole((1, width)), whole((count, width)),
            pl.BlockSpec((3, count, block), lambda j: (0, 0, j)),
            pl.BlockSpec((count, block), lambda j: (0, j)), whole((count, heads)),
            weight, weight, weight, weight, whole((width, heads)),
        ],
        out_specs=[whole((count, width)), whole((1, width))],
        out_shape=[
            jax.ShapeDtypeStruct((count, width), LOW), jax.ShapeDtypeStruct((1, width), jnp.float32),
        ],
        scratch_shapes=[pltpu.VMEM((count, width), jnp.float32)],
        compiler_params=params(),
        cost_estimate=cost(8 * count * width * width, 8 * width * width + 20 * count * width),
        name="enter",
    )(
        tokens, gain, grad_hidden, grads, grad_gate, grad_beta, query_w, key_w, value_w, gate_w,
        beta_w,
    )


def passed_along(value, axis, by):
    devices = lax.axis_size(axis)
    pairs = [(i, i + by) for i in range(devices) if 0 <= i + by < devices]
    return lax.ppermute(value, axis, pairs)


def tuned():
    return (lax.axis_size("seq"), lax.axis_size("doc")) == (8, 4)


HOPS = {"core": ("doc", 1), "y": ("doc", 2), "x": ("seq", 1), "near": ("seq", 2), "far": ("seq", 4)}


def hop(value, way):
    axis, bit = HOPS[way]
    return lax.ppermute(value, axis, [(i, i ^ bit) for i in range(lax.axis_size(axis))])


def side(way):
    axis, bit = HOPS[way]
    return lax.axis_index(axis) // bit % 2


def apply_kernel(shift, maps, *refs, turned):
    *states, out = refs
    size = maps.shape[1]
    for h in range(maps.shape[0]):
        state = states[0][h]
        for other in states[1:]:
            state = state + other[h]
        moved = (t_product if turned else product)(maps[h, :, size:], state)
        if state.shape[1] == size:
            out[h] = moved + shift[h, :, :size]
        else:
            out[h] = moved + jnp.concatenate([shift[h, :, :size], jnp.zeros((size, size), jnp.float32)], 1)


def apply_map(shift, maps, *states, turned=False):
    return pl.pallas_call(
        lambda *refs: apply_kernel(*refs, turned=turned),
        out_shape=jax.ShapeDtypeStruct(states[0].shape, jnp.float32),
        compiler_params=params(4),
        cost_estimate=cost(0, 0),
        name="apply_map",
    )(shift, maps, *states)


def ends_kernel(here, shift, maps, state, come, stay_out, send_out, *, turned):
    size = maps.shape[1]
    mine = here[0] == 0
    for h in range(maps.shape[0]):
        near = state[h] + come[h]
        far = (t_product if turned else product)(maps[h, :, size:], near) + shift[h, :, :size]
        if turned:
            near, far = far, near
        stay_out[h] = jnp.where(mine, near, far)
        send_out[h] = jnp.where(mine, far, near)


def pair_ends(here, shift, maps, state, come, turned=False):
    shape = jax.ShapeDtypeStruct(state.shape, jnp.float32)
    vmem = pl.BlockSpec(memory_space=pltpu.VMEM)
    return pl.pallas_call(
        lambda *refs: ends_kernel(*refs, turned=turned),
        in_specs=[pl.BlockSpec(memory_space=pltpu.SMEM)] + [vmem] * 4,
        out_specs=[vmem, vmem],
        out_shape=[shape, shape],
        compiler_params=params(4),
        cost_estimate=cost(0, 0),
        name="pair_ends",
    )(here, shift, maps, state, come)


def carried_forward(maps):
    heads, size, _ = maps.shape
    half = heads // 2
    if not tuned():
        gathered = lax.all_gather(maps, "seq")

        def one(lap, state):
            each = lax.dynamic_index_in_dim(gathered, lap, 0, False)
            return apply_map(each, each, state)

        state = lax.fori_loop(
            0, lax.axis_index("seq"), one, jnp.zeros((heads, size, size), jnp.float32)
        )
        return state[:half], state[half:], jnp.zeros((1,), jnp.int32), (maps,)
    place = side("x").astype(jnp.int32).reshape(1)
    here = place[0] == 0
    kept = jnp.where(here, maps[:half], maps[half:])
    other = hop(jnp.where(here, maps[half:], maps[:half]), "x")
    first, second = jnp.where(here, kept, other), jnp.where(here, other, kept)
    pair_map = apply_map(second, second, first)
    state = jnp.zeros((half, size, size), jnp.float32)
    come = state
    for step in range(3):
        if step == 0:
            sent = pair_map[:, :, :size]
        else:
            sent = apply_map(pair_map, pair_map, state, come)
            state = state + come
        come = lax.ppermute(sent, "seq", [(2 * step + x, 2 * step + 2 + x) for x in range(2)])
    mine, send = pair_ends(place, first, first, state, come)
    return mine, hop(send, "x"), place, (first, second, pair_map)


def together(value, *others):
    return lax.optimization_barrier((value, *others))


def carried_back(shift, context, beside=None):
    heads, size, _ = shift.shape
    half = heads // 2
    if not tuned():
        gathered = lax.all_gather(jnp.concatenate([shift, context[0][:, :, size:]], 2), "seq")
        count = lax.axis_size("seq")

        def one(lap, state):
            each = lax.dynamic_index_in_dim(gathered, count - 1 - lap, 0, False)
            return apply_map(each, each, state, turned=True)

        zeros = jnp.zeros((heads, size, size), jnp.float32)
        state = lax.fori_loop(0, count - 1 - lax.axis_index("seq"), one, zeros)
        return state[:half], state[half:], ()
    first, second, pair_map = context
    place = side("x").astype(jnp.int32).reshape(1)
    here = place[0] == 0
    done = []

    def step_with(number, sent, go):
        moves, work = beside[number]
        sent, *values = together(sent, *[value for value, _ in moves])
        come, *rest = together(
            go(sent), *[hop(value, way) for value, (_, way) in zip(values, moves)], *work
        )
        done.append(rest)
        return come

    kept = jnp.where(here, shift[:half], shift[half:])
    other = step_with(0, jnp.where(here, shift[half:], shift[:half]), lambda value: hop(value, "x"))
    first_shift, second_shift = jnp.where(here, kept, other), jnp.where(here, other, kept)
    pair_shift = apply_map(first_shift, first, second_shift, turned=True)
    state = jnp.zeros((half, size, size), jnp.float32)
    come = state
    for step in range(3, 0, -1):
        if step == 3:
            sent = pair_shift
        else:
            sent = apply_map(pair_shift, pair_map, state, come, turned=True)
            state = state + come
        pairs = [(2 * step + x, 2 * step - 2 + x) for x in range(2)]
        come = step_with(4 - step, sent, lambda value: lax.ppermute(value, "seq", pairs))
    mine, send = pair_ends(place, second_shift, second, state, come, turned=True)
    return mine, step_with(4, send, lambda value: hop(value, "x")), done


def outer_kernel(bit, *refs, blocks, post, pieces):
    count = len(blocks)
    lefts, rights = refs[: 2 * count], refs[2 * count : 4 * count]
    *outs, stacked = refs[4 * count :]
    step = pl.program_id(0)
    tokens = lefts[0].shape[1]
    half = outs[0].shape[0]

    @pl.when(step == 0)
    def _():
        for piece in range(count):
            for which in range(2):
                for start in range(0, half, post):
                    for place, mine in ((start, bit[0]), (half + start, 1 - bit[0])):
                        rows = pl.ds(pl.multiple_of(2 * start + mine * post, 8), post)
                        stacked[
                            piece, place : place + post, which * tokens : (which + 1) * tokens
                        ] = lefts[2 * piece + which][rows, :].astype(LOW)

    for piece in range(count):
        low = sum(blocks[:piece])

        @pl.when((step >= low) & (step < low + blocks[piece]))
        def _(piece=piece):
            right = jnp.concatenate(
                [rights[2 * piece][...].astype(LOW), rights[2 * piece + 1][...].astype(LOW)], 0
            )
            place = 0
            for out, size in zip(outs, (half, *pieces)):
                out[...] = mxu(stacked[piece, place : place + size, :], right, NN)
                place += size


def outer(pieces, way, parts=1):
    rows, tokens = pieces[0][0].shape
    block = 2 * LANES
    post = rows // 16 if way == "y" else rows // 8 * {"far": 4, "near": 2, "x": 1}[way]
    counts = [piece[5] for piece in pieces]
    left = pl.BlockSpec((rows, tokens), lambda j: (0, 0), pipeline_mode=pl.Buffered(1))
    lefts, rights, specs = [], [], []
    for index, piece in enumerate(pieces):
        lefts += piece[:2]
        rights += piece[2:4]

        def place(j, low=sum(counts[:index]), first=piece[4], number=piece[5]):
            return 0, first + jnp.clip(j - low, 0, number - 1)

        specs += [pl.BlockSpec((tokens, block), place)] * 2
    total = sum(counts)
    eighth = rows // 16
    sizes = [eighth * 8 // parts // 16 * 16] * (parts - 1)
    sizes = [*sizes, rows // 2 - sum(sizes)]
    outs = [rows // 2, *sizes]
    keep, *sends = pl.pallas_call(
        lambda *refs: outer_kernel(*refs, blocks=counts, post=post, pieces=sizes),
        grid=(total,),
        in_specs=[pl.BlockSpec(memory_space=pltpu.SMEM)] + [left] * len(lefts) + specs,
        out_specs=[pl.BlockSpec((size, block), lambda j: (0, j)) for size in outs],
        out_shape=[jax.ShapeDtypeStruct((size, total * block), jnp.float32) for size in outs],
        scratch_shapes=[pltpu.VMEM((len(pieces), rows, 2 * tokens), LOW)],
        compiler_params=params(),
        cost_estimate=cost(
            4 * rows * tokens * total * block, 4 * rows * total * block + 8 * tokens * rows
        ),
        name="outer",
    )(side(way).astype(jnp.int32).reshape(1), *lefts, *rights)
    return keep, sends


def take(value, place, axis):
    return lax.dynamic_index_in_dim(value, place, axis, False)


class Part:
    def __init__(self, keep, order):
        self.order, self.stage = order, 1
        self.names = [name for name in ("far", "near", "x", "y") if name != order[0]]
        shape = (2, 2, 2, keep.shape[0] // 8, keep.shape[1])
        self.terms = [(keep.reshape(shape), tuple(self.names))]

    def begun(self, pieces):
        come = pieces[0] if len(pieces) == 1 else jnp.concatenate(pieces, 0)
        self.absorb(come)

    def absorb(self, come):
        shape = (2,) * len(self.names) + self.terms[0][0].shape[-2:]
        self.terms.append((come.reshape(shape), tuple(self.names)))

    def chosen(self, bits):
        total = None
        for value, names in self.terms:
            starts, sizes = [], []
            for name in names:
                fixed = name in bits or name not in self.names
                starts.append(bits.get(name, side(name)) if fixed else 0)
                sizes.append(1 if fixed else 2)
            sizes += value.shape[len(names) :]
            starts = [jnp.asarray(start, jnp.int32) for start in [*starts, 0, 0]]
            piece = lax.dynamic_slice(value, starts, sizes)
            piece = piece.reshape([size for size, name in zip(sizes, names) if size > 1] + sizes[-2:])
            total = piece if total is None else total + piece
        return total

    def move(self):
        stage, self.stage = self.stage, self.stage + 1
        if stage < 4 and (stage < 3 or self.order[3] != "y"):
            way = self.order[stage]
            send = self.chosen({way: 1 - side(way)})
            self.names.remove(way)
            return send, way
        if stage < 5:
            self.stage = 5
            self.keep = self.chosen({})
            self.absorb = self.whole if stage == 4 else self.summed
            return self.keep, "y"
        self.absorb = lambda come: setattr(self, "other", come)
        return self.done, "core"

    def whole(self, come):
        first = side("y") == 0
        self.done = jnp.concatenate(
            [jnp.where(first, self.keep, come), jnp.where(first, come, self.keep)], 0
        )

    def summed(self, come):
        self.done = (self.keep + come).reshape(-1, come.shape[-1])


def swaps(moves, *beside):
    values = together(*[value for value, _ in moves])
    comes = [hop(value, way) for value, (_, way) in zip(values, moves)]
    done = together(*comes, *beside)
    return done[: len(moves)], done[len(moves) :]


def advance(parts, extra=()):
    comes, _ = swaps([part.move() for part in parts] + list(extra))
    for part, come in zip(parts, comes):
        part.absorb(come)
    return comes[len(parts) :]


def flatten_small(small):
    first_gain, beta, conv, head_gain, second_gain = small
    seq = lax.axis_size("seq")
    flat = jnp.concatenate(
        [
            first_gain.reshape(seq, -1), beta.reshape(seq, -1),
            conv.reshape(conv.shape[0] * conv.shape[1], seq, -1).transpose(1, 0, 2).reshape(seq, -1),
            head_gain.reshape(seq, -1), second_gain.reshape(seq, -1),
        ],
        1,
    )
    size = flat.shape[1]
    rows = -(-size // 2048) * 16
    return jnp.pad(flat, ((0, 0), (0, rows * 128 - size))).reshape(seq * rows, 128)


def unflatten_small(flat, small):
    first_gain, beta, conv, head_gain, second_gain = small
    seq = lax.axis_size("seq")
    flat = flat.reshape(-1)
    sizes = [a.size // seq for a in small]
    places = [sum(sizes[:i]) for i in range(len(sizes))]
    pieces = [flat[p : p + s] for p, s in zip(places, sizes)]
    return (
        pieces[0], pieces[1].reshape(-1, beta.shape[1]),
        pieces[2].reshape(conv.shape[0], conv.shape[1], -1), pieces[3], pieces[4],
    )


def outer_sum(left, right):
    return mxu(left.astype(LOW), right.astype(LOW), TN)


def local(
    tokens,
    doc_lengths,
    out_grad,
    first_gain,
    query_weight,
    key_weight,
    value_weight,
    gate_weight,
    beta_weight,
    conv_weight,
    head_gain,
    out_weight,
    second_gain,
    hidden_gate,
    hidden_up,
    hidden_down,
):
    count, width = (tokens.shape[1], tokens.shape[2])
    heads = beta_weight.shape[1]
    reach = conv_weight.shape[1] - 1
    first = lax.axis_index("seq") * count
    position, live = doc_info(doc_lengths[0], first, count)
    keep = 1.0 - (position[::CK] == 0).astype(jnp.float32)
    position, live = position[:, None], live[:, None]
    core = (lax.axis_index("doc") % 2).astype(jnp.int32).reshape(1)
    here = core[0] == 0
    rows, top = tokens[0], out_grad[0]
    halo = passed_along(rows[count - HALO :].astype(jnp.float32), "seq", 1)
    normed_one, pre, features, gate_pre, beta_pre, beta = project(
        rows, halo, first_gain[None], position, live, query_weight, key_weight, value_weight,
        gate_weight, beta_weight, conv_weight,
    )
    solved, inverses, attend, maps = prepare(keep, features, beta)
    state_mine, state_other, place, context = carried_forward(maps)
    starts, news, mixed, normed_head = mix(
        keep, place, features, solved, attend, gate_pre, head_gain[None], state_mine, state_other
    )
    (
        block_out, two_turned, inner_turned, kept, sent, grad_hidden, grad_branch, grad_head,
        grad_second_gain, head_turned,
    ) = feed(
        core, rows, normed_head, top, second_gain[None], out_weight, hidden_gate, hidden_up,
        hidden_down,
    )
    if tuned():
        half = width // 2
        units = half // 256

        def pick(zero, one):
            return jnp.where(here, zero, one)

        def both(value, send=None):
            return value, hop(value if send is None else send, "core")

        wide_top = top.astype(jnp.float32)
        tops = both(
            pick(top[:, :half], top[:, half:]), pick(wide_top[:, half:], wide_top[:, :half])
        )
        one = both(normed_one)
        inners = both(inner_turned)
        heads_turned = both(head_turned)
        two = both(two_turned)
        gate_up = both(kept, sent)
    grad_mixed, grad_gate_pre, out_kept, out_sent, grad_head_gain, shift = gather_states(
        keep, core, grad_head, grad_branch, mixed, gate_pre, head_gain[None], features, solved, heads
    )
    if tuned():
        out_left = pick(heads_turned[0], one[0]), pick(heads_turned[1], one[1])
        out_right = both(out_kept, out_sent)
        blocks = hidden_gate.shape[1] // 256
        some = blocks * 3 // 11
        down_keep, down_sends = outer([(*inners, *tops, 0, units)], "y", 5)
        shift, down_keep, *down_sends = together(shift, down_keep, *down_sends)
        rest_keep, rest_sends = outer([(*two, *gate_up, some, blocks - some)], "y", 2)
        out_keep, out_sends = outer([(*out_left, *out_right, 0, width // 256)], "near")
        some_keep, some_sends = outer([(*two, *gate_up, 0, some)], "x")
        work = [
            (rest_keep, *rest_sends), (out_keep, *out_sends), (some_keep, *some_sends), (), (),
        ]
        moves = [[(send, "y")] for send in down_sends]
        grad_mine, grad_other, done = carried_back(
            shift, context, list(zip(moves, work))
        )
        down_come = [value[0] for value in done]
        rest_keep, *rest_sends = done[0][1:]
        out_keep, *out_sends = done[1][1:]
        some_keep, *some_sends = done[2][1:]
        down = Part(down_keep, ("y", "x", "near", "far"))
        rest = Part(rest_keep, ("y", "x", "near", "far"))
        some_part = Part(some_keep, ("x", "near", "far", "y"))
        out = Part(out_keep, ("near", "far", "y", "x"))
        down.begun(down_come)
        moves = [down.move(), (rest_sends[0], "y"), (out_sends[0], "near")]
        grad_mine, *values = together(grad_mine, *[value for value, _ in moves])
        comes = [hop(value, way) for value, (_, way) in zip(values, moves)]
    else:
        grad_mine, grad_other, _ = carried_back(shift, context)
    grads, borrowed, grad_conv, grad_beta_pre = back(
        keep, place, features, beta, beta_pre, solved, inverses, starts, news, grad_mixed, grad_mine,
        grad_other, pre, conv_weight, position, live,
    )
    if tuned():
        borrowed, *comes = together(borrowed, *comes)
        down.absorb(comes[0])
        rest_come = [comes[1]]
        out.begun([comes[2]])
    returned = passed_along(borrowed, "seq", -1)
    tail = grads[:, count - 8 :] + returned
    grads = lax.dynamic_update_slice(grads, tail, (0, count - 8, 0))
    grads = grads.astype(LOW)
    if tuned():
        moves = [(some_sends[0], "x"), (rest_sends[1], "y"), down.move(), out.move()]
        grads, *values = together(grads, *[value for value, _ in moves])
        comes = [hop(value, way) for value, (_, way) in zip(values, moves)]
        wide = grads.astype(jnp.float32)
        query_key = both(pick(grads[0], grads[1]), pick(wide[1], wide[0]))
        value = both(
            pick(grads[2, :, :half], grads[2, :, half:]), pick(wide[2, :, half:], wide[2, :, :half])
        )
        orders = (("y", "x", "near", "far"), ("near", "y", "x", "far"))
        late = (
            outer([(*one, *query_key, 0, units), (*one, *value, 0, units)], "y"),
            outer([(*one, *query_key, units, units)], "near"),
        )
        grads, *late_sends = together(grads, *[send for _, (send,) in late])
        input_grad, grad_first_gain = enter(
            rows, first_gain[None], grad_hidden, grads, grad_gate_pre, grad_beta_pre, query_weight,
            key_weight, value_weight, gate_weight, beta_weight,
        )
        small = (
            grad_first_gain[0], outer_sum(normed_one.T, grad_beta_pre), grad_conv, grad_head_gain[0],
            grad_second_gain[0],
        )
        flat = flatten_small(small)
        late_sends[0], *comes = together(late_sends[0], *comes)
        some_part.begun([comes[0]])
        rest.begun([*rest_come, comes[1]])
        down.absorb(comes[2])
        out.absorb(comes[3])
        late = [Part(keep_, order) for (keep_, _), order in zip(late, orders)]
        comes, (flat, input_grad) = swaps(
            [part.move() for part in (rest, some_part, down)]
            + [(send, order[0]) for send, order in zip(late_sends, orders)],
            flat, input_grad,
        )
        for part, come in zip((rest, some_part, down), comes):
            part.absorb(come)
        for part, come in zip(late, comes[3:]):
            part.begun([come])
        (flat_come,) = advance([out, some_part, rest, *late, down], [(flat, "core")])
        flat = (flat + flat_come).reshape(4, 2, -1, 128)
        bit = side("x")
        tiny = Part(take(flat, bit, 1).reshape(-1, 128), ("x", "y", "near", "far"))
        tiny_send = take(flat, 1 - bit, 1).reshape(-1, 128)
        tiny_come = advance([out, some_part, rest, *late, down], [(tiny_send, "x")])
        tiny.begun(tiny_come)
        advance([rest, out, *late, tiny, some_part])
        advance([*late, tiny, rest, out])
        advance([*late, tiny])
        advance([tiny])
        advance([tiny])
        zero = lambda part: pick(part.done, part.other)
        one_ = lambda part: pick(part.other, part.done)
        columns = half
        query_g = jnp.concatenate([zero(late[0])[:, :columns], zero(late[1])], 1)
        key_g = jnp.concatenate([one_(late[0])[:, :columns], one_(late[1])], 1)
        value_g = jnp.concatenate([zero(late[0])[:, columns:], one_(late[0])[:, columns:]], 1)
        out_g, gate_g = zero(out), one_(out)
        hidden_gate_g = jnp.concatenate([zero(some_part), zero(rest)], 1)
        hidden_up_g = jnp.concatenate([one_(some_part), one_(rest)], 1)
        hidden_down_g = jnp.concatenate([zero(down), one_(down)], 1)
        first_g, beta_g, conv_g, head_g, second_g = unflatten_small(tiny.done, small)
    else:
        input_grad, grad_first_gain = enter(
            rows, first_gain[None], grad_hidden, grads, grad_gate_pre, grad_beta_pre, query_weight,
            key_weight, value_weight, gate_weight, beta_weight,
        )
        small = (
            grad_first_gain[0], outer_sum(normed_one.T, grad_beta_pre), grad_conv, grad_head_gain[0],
            grad_second_gain[0],
        )

        def whole(term, dimension):
            part = lax.psum_scatter(term, "seq", scatter_dimension=dimension, tiled=True)
            return lax.psum(part, "doc")

        gate_grad, up_grad = jnp.where(here, kept, sent), jnp.where(here, sent, kept)
        terms = (
            outer_sum(normed_one.T, grads[0]), outer_sum(normed_one.T, grads[1]),
            outer_sum(normed_one.T, grads[2]), outer_sum(normed_one.T, grad_gate_pre),
            outer_sum(head_turned.T, grad_branch), outer_sum(two_turned.T, gate_grad),
            outer_sum(two_turned.T, up_grad), outer_sum(inner_turned.T, top),
        )
        query_g, key_g, value_g, gate_g, out_g, hidden_gate_g, hidden_up_g, hidden_down_g = (
            whole(term, 0) for term in terms
        )
        first_g, beta_g, conv_g, head_g, second_g = (
            whole(term, d) for term, d in zip(small, (0, 0, 2, 0, 0))
        )
    return (
        block_out[None], input_grad[None], first_g, query_g, key_g, value_g, gate_g, beta_g, conv_g,
        head_g, out_g, second_g, hidden_gate_g, hidden_up_g, hidden_down_g,
    )


def solution(mesh):
    in_specs = (
        P("doc", "seq", None),
        P("doc", None),
        P("doc", "seq", None),
        P(),
        P(),
        P(),
        P(),
        P(),
        P(),
        P(),
        P(),
        P(),
        P(),
        P(),
        P(),
        P(),
    )
    out_specs = (
        P("doc", "seq", None),
        P("doc", "seq", None),
        P("seq"),
        P("seq", None),
        P("seq", None),
        P("seq", None),
        P("seq", None),
        P("seq", None),
        P(None, None, "seq"),
        P("seq"),
        P("seq", None),
        P("seq"),
        P("seq", None),
        P("seq", None),
        P("seq", None),
    )
    return jax.shard_map(local, mesh=mesh, in_specs=in_specs, out_specs=out_specs, check_vma=False)
```

```python
import jax
import jax.numpy as jnp
from jax import lax
from jax.experimental import pallas as pl
from jax.experimental.pallas import tpu as pltpu
from jax.sharding import PartitionSpec as P

CK = 64


EPS = 1e-05
KEY_EPS = 1e-06
HIGH = lax.Precision.HIGHEST


def doc_info(lengths, first, count):
    padded = (lengths + CK - 1) // CK * CK
    ends = jnp.cumsum(padded)
    starts = ends - padded
    place = first + jnp.arange(count, dtype=jnp.int32)
    inside = ((place[:, None] >= starts[None, :]) & (place[:, None] < ends[None, :])).astype(
        jnp.int32
    )
    position = place - jnp.sum(inside * starts[None, :], 1)
    length = jnp.sum(inside * lengths[None, :], 1)
    live = (position < length).astype(jnp.float32)
    return (position, live)


SPAN = CK
LANES = 128
LOW = jnp.bfloat16
NN = (((1,), (0,)), ((), ()))
NT = (((1,), (1,)), ((), ()))
TN = (((0,), (0,)), ((), ()))


def params(mib=52):
    return pltpu.CompilerParams(vmem_limit_bytes=mib * 2**20)


def cost(flops, moved):
    return pl.CostEstimate(flops=1, bytes_accessed=1, transcendentals=0)


def mxu(left, right, dims):
    return lax.dot_general(left, right, dims, preferred_element_type=jnp.float32)


def halves(value):
    high = value.astype(LOW)
    return high, (value - high.astype(jnp.float32)).astype(LOW)


def split(value):
    return value if isinstance(value, tuple) else halves(value)


def stack(first, second):
    return tuple(jnp.concatenate(both, 0) for both in zip(first, second))


def fold(value):
    half = value.shape[1] // 2
    return value[:, :half] + value[:, half:]


def product(left, right):
    left_high, left_low = split(left)
    right_high, right_low = split(right)
    both = jnp.concatenate([left_high, left_low], 1)
    if right_high.shape[1] <= LANES:
        wide = jnp.concatenate([right_high, right_low], 1)
        return fold(mxu(both, jnp.concatenate([wide, wide], 0), NN))
    return mxu(both, jnp.concatenate([right_high, right_high], 0), NN) + mxu(
        left_high, right_low, NN
    )


def product_t(left, right):
    left_high, left_low = split(left)
    right_high, right_low = split(right)
    both = jnp.concatenate([left_high, left_low], 1)
    if right_high.shape[0] <= LANES:
        rows = jnp.concatenate(
            [
                jnp.concatenate([right_high, right_high], 1),
                jnp.concatenate([right_low, right_low], 1),
            ],
            0,
        )
        return fold(mxu(both, rows, NT))
    return mxu(both, jnp.concatenate([right_high, right_high], 1), NT) + mxu(
        left_high, right_low, NT
    )


def t_product(left, right):
    left_high, left_low = split(left)
    right_high, right_low = split(right)
    both = jnp.concatenate([left_high, left_low], 0)
    if right_high.shape[1] <= LANES:
        wide = jnp.concatenate([right_high, right_low], 1)
        return fold(mxu(both, jnp.concatenate([wide, wide], 0), TN))
    return mxu(both, jnp.concatenate([right_high, right_high], 0), TN) + mxu(
        left_high, right_low, TN
    )


def head(value, h):
    return value[:, h * LANES : (h + 1) * LANES]


def pair(value, p):
    return jnp.concatenate([head(value, 2 * p), head(value, 2 * p + 1)], 0)


def pair_column(value, p):
    return jnp.concatenate([value[:, 2 * p : 2 * p + 1], value[:, 2 * p + 1 : 2 * p + 2]], 0)


def masks(rows):
    i = lax.broadcasted_iota(jnp.int32, (rows, rows), 0)
    j = lax.broadcasted_iota(jnp.int32, (rows, rows), 1)
    same = (i >= SPAN) == (j >= SPAN)
    strict = jnp.where(same & (j < i), 1.0, 0.0)
    inclusive = jnp.where(same & (j <= i), 1.0, 0.0)
    upper = jnp.where(same & (j >= i), 1.0, 0.0)
    return strict, inclusive, upper, jnp.where(i == j, 1.0, 0.0)


def inverses_of(strict_parts, identity):
    rows = identity.shape[0]
    results = [identity - part for part in strict_parts]
    powers = [split(part) for part in strict_parts]
    powers = [split(product(power, power)) for power in powers]
    for level in range(SPAN.bit_length() - 3):
        both = [
            product(stack(split(result), power), power) for result, power in zip(results, powers)
        ]
        results = [result + pair_[:rows] for result, pair_ in zip(results, both)]
        powers = [split(pair_[rows:]) for pair_ in both]
    return [result + product(result, power) for result, power in zip(results, powers)]


def sigmoid(value):
    return 1.0 / (1.0 + jnp.exp(-value))


HALO = 16


def project_kernel(
    tokens, halo, gain, position, live, query_w, key_w, value_w, gate_w, beta_w, conv,
    normed_out, pre_out, feature_out, gate_out, beta_pre_out, beta_out, normed, pre,
):
    count = tokens.shape[0]

    @pl.when(pl.program_id(0) == 0)
    def _():
        def norm(rows):
            return (
                rows * lax.rsqrt(jnp.mean(rows * rows, -1, keepdims=True) + EPS) * gain[...]
            ).astype(LOW)

        normed[:HALO, :] = norm(halo[...])
        rounded = norm(tokens[...].astype(jnp.float32))
        normed[HALO:, :] = rounded
        normed_out[...] = rounded.astype(jnp.float32).T
        beta_pre = mxu(rounded, beta_w[...], NT)
        beta_pre_out[...] = beta_pre
        beta_out[...] = sigmoid(beta_pre) * live[...]

    gate_out[...] = mxu(normed[HALO:, :], gate_w[...], NN)
    valid = [
        jnp.broadcast_to(
            jnp.where(position[...] >= conv.shape[1] - 1 - tap, 1.0, 0.0), (count, LANES)
        )
        for tap in range(conv.shape[1] - 1)
    ]
    for which, weight in enumerate((query_w, key_w, value_w)):
        pre[which] = mxu(normed[...], weight[...], NN)
        for span in range(count // SPAN):
            start = HALO + span * SPAN
            pre_out[which, span] = pre[which, start - 8 : start + SPAN, :]
        for part in range(pre.shape[2] // LANES):
            lanes = slice(part * LANES, (part + 1) * LANES)
            total = conv_total(pre, which, HALO, count, lanes, conv, valid)
            value = total * sigmoid(total)
            if which < 2:
                value = value * lax.rsqrt(jnp.sum(value * value, -1, keepdims=True) + KEY_EPS)
            if which == 1:
                value = value * live[...]
            feature_out[which, :, lanes] = value


def conv_total(pre, which, first, count, lanes, conv, valid):
    taps = conv.shape[1]
    total = None
    for tap in range(taps):
        start = first - (taps - 1) + tap
        term = conv[which, tap : tap + 1, lanes] * pre[which, start : start + count, lanes]
        if tap < taps - 1:
            term = term * valid[tap]
        total = term if total is None else total + term
    return total


def project(tokens, halo, gain, position, live, query_w, key_w, value_w, gate_w, beta_w, conv):
    count, width = tokens.shape
    heads = beta_w.shape[0]
    block = 2 * LANES
    whole = lambda shape: pl.BlockSpec(shape, lambda j: (0,) * len(shape))
    weight = pl.BlockSpec((width, block), lambda j: (0, j))
    f32 = lambda shape: jax.ShapeDtypeStruct(shape, jnp.float32)
    return pl.pallas_call(
        project_kernel,
        grid=(width // block,),
        in_specs=[
            whole((count, width)), whole((HALO, width)), whole((1, width)), whole((count, 1)),
            whole((count, 1)), weight, weight, weight, weight, whole((heads, width)),
            pl.BlockSpec((3, conv.shape[1], block), lambda j: (0, 0, j)),
        ],
        out_specs=[
            whole((width, count)),
            pl.BlockSpec((3, count // SPAN, SPAN + 8, block), lambda j: (0, 0, 0, j)),
            pl.BlockSpec((3, count, block), lambda j: (0, 0, j)),
            pl.BlockSpec((count, block), lambda j: (0, j)),
            whole((count, heads)), whole((count, heads)),
        ],
        out_shape=[
            f32((width, count)), f32((3, count // SPAN, SPAN + 8, width)), f32((3, count, width)),
            f32((count, width)), f32((count, heads)), f32((count, heads)),
        ],
        scratch_shapes=[
            pltpu.VMEM((HALO + count, width), LOW),
            pltpu.VMEM((3, HALO + count, block), jnp.float32),
        ],
        compiler_params=params(),
        cost_estimate=cost(8 * count * width * width, 8 * width * width + 40 * count * width),
        name="project",
    )(tokens, halo, gain, position, live, query_w, key_w, value_w, gate_w, beta_w, conv)


def prepare_kernel(keep, features, beta, solved_out, inverse_out, attend_out, state):
    span = pl.program_id(0)
    heads = state.shape[0]
    size = state.shape[1]
    strict, inclusive, upper, identity = masks(2 * SPAN)

    @pl.when(span == 0)
    def _():
        i = lax.broadcasted_iota(jnp.int32, (size, 2 * size), 0)
        j = lax.broadcasted_iota(jnp.int32, (size, 2 * size), 1)
        for h in range(heads):
            state[h] = jnp.where(j == i + size, 1.0, 0.0)

    query, key, value = features[0], features[1], features[2]
    betas = beta[...]
    flag = keep[span]
    pairs = range(heads // 2)
    keys = [split(pair(key, p)) for p in pairs]
    columns = [pair_column(betas, p) for p in pairs]
    scores = [product_t(stack(keys[p], split(pair(query, p))), keys[p]) for p in pairs]
    solved = inverses_of([columns[p] * scores[p][: 2 * SPAN] * strict for p in pairs], identity)
    both = [
        product(
            solved[p],
            jnp.concatenate([columns[p] * pair(key, p), columns[p] * pair(value, p)], 1),
        )
        for p in pairs
    ]
    for p in pairs:
        inverse_out[0, p] = solved[p]
        attend_out[0, p] = scores[p][2 * SPAN :] * inclusive
    starts, news = [], []
    for h in range(heads):
        rows = slice(h % 2 * SPAN, (h % 2 + 1) * SPAN)
        erase, update = both[h // 2][rows, :size], both[h // 2][rows, size:]
        solved_out[0, :, h * size : (h + 1) * size] = erase
        solved_out[1, :, h * size : (h + 1) * size] = update
        start = state[h] * flag
        starts.append(start)
        news.append(
            jnp.concatenate([update, jnp.zeros_like(update)], 1) - product(erase, start)
        )
    for h in range(heads):
        rows = slice(h % 2 * SPAN, (h % 2 + 1) * SPAN)
        state[h] = starts[h] + t_product(tuple(k[rows] for k in keys[h // 2]), news[h])


def prepare(keep, features, beta):
    _, count, width = features.shape
    heads = beta.shape[1]
    size = width // heads
    spans = count // SPAN
    f32 = lambda shape: jax.ShapeDtypeStruct(shape, jnp.float32)
    matrix = pl.BlockSpec((1, heads // 2, 2 * SPAN, 2 * SPAN), lambda c: (c, 0, 0, 0))
    return pl.pallas_call(
        prepare_kernel,
        grid=(spans,),
        in_specs=[
            pl.BlockSpec(memory_space=pltpu.SMEM),
            pl.BlockSpec((3, SPAN, width), lambda c: (0, c, 0)),
            pl.BlockSpec((SPAN, heads), lambda c: (c, 0)),
        ],
        out_specs=[
            pl.BlockSpec((2, SPAN, width), lambda c: (0, c, 0)), matrix, matrix,
            pl.BlockSpec((heads, size, 2 * size), lambda c: (0, 0, 0)),
        ],
        out_shape=[
            f32((2, count, width)), f32((spans, heads // 2, 2 * SPAN, 2 * SPAN)),
            f32((spans, heads // 2, 2 * SPAN, 2 * SPAN)), f32((heads, size, 2 * size)),
        ],
        compiler_params=params(),
        cost_estimate=cost(40 * count * width * size * 4, 60 * count * width),
        name="prepare",
    )(keep, features, beta)


def mix_kernel(
    keep, place, features, solved, attend, gate, gain, state_mine, state_other, starts_out, new_out,
    mixed_out, normed_out, state,
):
    span = pl.program_id(0)
    heads = state.shape[0]

    @pl.when(span == 0)
    def _():
        half = heads // 2
        first = place[0] == 0
        state[:half] = jnp.where(first, state_mine[...], state_other[...])
        state[half:] = jnp.where(first, state_other[...], state_mine[...])

    query, key = features[0], features[1]
    erase, update = solved[0], solved[1]
    flag = keep[span]
    every, pairs = range(heads), range(heads // 2)
    starts = [state[h] * flag for h in every]
    both = [
        product(jnp.concatenate([head(erase, h), head(query, h)], 0), starts[h]) for h in every
    ]
    news = [split(head(update, h) - both[h][:SPAN]) for h in every]
    after = [starts[h] + t_product(head(key, h), news[h]) for h in every]
    inner = [product(attend[0, p], stack(news[2 * p], news[2 * p + 1])) for p in pairs]
    for h in every:
        lanes = slice(h * LANES, (h + 1) * LANES)
        starts_out[0, h] = starts[h]
        state[h] = after[h]
        new_out[:, lanes] = head(update, h) - both[h][:SPAN]
        rows = both[h][SPAN:] + inner[h // 2][h % 2 * SPAN : (h % 2 + 1) * SPAN]
        mixed_out[:, lanes] = rows
        shaped = rows * lax.rsqrt(jnp.mean(rows * rows, -1, keepdims=True) + EPS) * gain[...]
        gates = gate[:, lanes]
        normed_out[:, lanes] = (shaped * (gates * sigmoid(gates))).astype(LOW)


def mix(keep, place, features, solved, attend, gate, gain, state_mine, state_other):
    _, count, width = features.shape
    half, size, _ = state_mine.shape
    heads = 2 * half
    spans = count // SPAN
    f32 = lambda shape: jax.ShapeDtypeStruct(shape, jnp.float32)
    rows = pl.BlockSpec((SPAN, width), lambda c: (c, 0))
    pairs = pl.BlockSpec((2, SPAN, width), lambda c: (0, c, 0))
    return pl.pallas_call(
        mix_kernel,
        grid=(spans,),
        in_specs=[
            pl.BlockSpec(memory_space=pltpu.SMEM), pl.BlockSpec(memory_space=pltpu.SMEM), pairs, pairs,
            pl.BlockSpec((1, heads // 2, 2 * SPAN, 2 * SPAN), lambda c: (c, 0, 0, 0)),
            rows, pl.BlockSpec((1, size), lambda c: (0, 0)),
            pl.BlockSpec((half, size, size), lambda c: (0, 0, 0)),
            pl.BlockSpec((half, size, size), lambda c: (0, 0, 0)),
        ],
        out_specs=[
            pl.BlockSpec((1, heads, size, size), lambda c: (c, 0, 0, 0)), rows, rows, rows,
        ],
        out_shape=[
            f32((spans, heads, size, size)), f32((count, width)), f32((count, width)),
            jax.ShapeDtypeStruct((count, width), LOW),
        ],
        scratch_shapes=[pltpu.VMEM((heads, size, size), jnp.float32)],
        compiler_params=params(),
        cost_estimate=cost(8 * count * width * size * 4, 40 * count * width),
        name="mix",
    )(keep, place, features, solved, attend, gate, gain, state_mine, state_other)


def feed_kernel(
    core, tokens, normed_head, grad_top, second_gain, out_w, gate_w, up_w, down_w,
    block_out, normed_out, inner_out, kept_out, sent_out, grad_hidden_out, branch_out, grad_head_out,
    gain_grad_out, head_turned_out, hidden, normed, total, grad_total,
):
    step = pl.program_id(0)

    @pl.when(step == 0)
    def _():
        state = tokens[...].astype(jnp.float32) + mxu(normed_head[...], out_w[...], NN)
        hidden[...] = state
        rounded = (
            state * lax.rsqrt(jnp.mean(state * state, -1, keepdims=True) + EPS) * second_gain[...]
        ).astype(LOW)
        normed[...] = rounded
        normed_out[...] = rounded.astype(jnp.float32).T
        head_turned_out[...] = normed_head[...].astype(jnp.float32).T

    @pl.when(step == 0)
    def _():
        total[...] = jnp.zeros_like(total)
        grad_total[...] = jnp.zeros_like(grad_total)

    first = core[0] == 0
    size = normed.shape[0] // 1
    parts = [slice(i * size, (i + 1) * size) for i in range(1)]
    gates = [mxu(normed[part, :], gate_w[...], NN) for part in parts]
    ups = [mxu(normed[part, :], up_w[...], NN) for part in parts]
    grad_inners = [mxu(grad_top[part, :], down_w[...], NT) for part in parts]
    for part, gate, up, grad_inner in zip(parts, gates, ups, grad_inners):
        sigma = sigmoid(gate)
        act = gate * sigma
        inner = (act * up).astype(LOW)
        inner_out[:, part] = inner.astype(jnp.float32).T
        wide_gate = grad_inner * up * (sigma + act * (1.0 - sigma))
        wide_up = grad_inner * act
        grad_gate, grad_up = wide_gate.astype(LOW), wide_up.astype(LOW)
        kept_out[part, :] = jnp.where(first, wide_gate, wide_up).astype(LOW)
        sent_out[part, :] = jnp.where(first, wide_up, wide_gate).astype(LOW).astype(jnp.float32)
        total[part, :] += mxu(inner, down_w[...], NN)
        grad_total[part, :] += mxu(grad_gate, gate_w[...], NT) + mxu(grad_up, up_w[...], NT)

    @pl.when(step == pl.num_programs(0) - 1)
    def _():
        state = hidden[...]
        block_out[...] = (state + total[...]).astype(LOW)
        part, gain_part = norm_back(state, second_gain[...], grad_total[...])
        gain_grad_out[...] = gain_part
        grad_hidden = grad_top[...].astype(jnp.float32) + part
        grad_hidden_out[...] = grad_hidden
        branch = grad_hidden.astype(LOW)
        branch_out[...] = branch.astype(jnp.float32)
        grad_head_out[...] = mxu(branch, out_w[...], NT)


def norm_back(value, gain, grad):
    scale = lax.rsqrt(jnp.mean(value * value, -1, keepdims=True) + EPS)
    unit = value * scale
    gain_grad = jnp.sum(grad * unit, 0, keepdims=True)
    inward = grad * gain
    return scale * (inward - unit * jnp.mean(inward * unit, -1, keepdims=True)), gain_grad


def feed(core, tokens, normed_head, grad_top, second_gain, out_w, gate_w, up_w, down_w):
    count, width = tokens.shape
    hidden = gate_w.shape[1]
    block = 2 * LANES
    whole = lambda shape: pl.BlockSpec(shape, lambda j: (0,) * len(shape))
    f32 = lambda shape: jax.ShapeDtypeStruct(shape, jnp.float32)
    low = lambda shape: jax.ShapeDtypeStruct(shape, LOW)
    rows = whole((count, width))
    columns = pl.BlockSpec((count, block), lambda j: (0, j))
    return pl.pallas_call(
        feed_kernel,
        grid=(hidden // block,),
        in_specs=[
            pl.BlockSpec(memory_space=pltpu.SMEM), rows, rows, rows, whole((1, width)),
            whole((width, width)), pl.BlockSpec((width, block), lambda j: (0, j)),
            pl.BlockSpec((width, block), lambda j: (0, j)),
            pl.BlockSpec((block, width), lambda j: (j, 0)),
        ],
        out_specs=[
            rows, whole((width, count)), pl.BlockSpec((block, count), lambda j: (j, 0)), columns,
            columns, rows, rows, rows, whole((1, width)), whole((width, count)),
        ],
        out_shape=[
            low((count, width)), f32((width, count)), f32((hidden, count)), low((count, hidden)),
            f32((count, hidden)), f32((count, width)), f32((count, width)), f32((count, width)),
            f32((1, width)), f32((width, count)),
        ],
        scratch_shapes=[
            pltpu.VMEM((count, width), jnp.float32), pltpu.VMEM((count, width), LOW),
            pltpu.VMEM((count, width), jnp.float32), pltpu.VMEM((count, width), jnp.float32),
        ],
        compiler_params=params(),
        cost_estimate=cost(
            12 * count * width * hidden + 4 * count * width * width,
            6 * width * hidden + 10 * count * hidden + 30 * count * width,
        ),
        name="feed",
    )(core, tokens, normed_head, grad_top, second_gain, out_w, gate_w, up_w, down_w)


def gather_kernel(
    keep, core, grad_head, grad_branch, mixed, gate, gain, features, solved, grad_mixed_out,
    grad_gate_out, kept_out, sent_out, gain_out, state,
):
    step = pl.program_id(0)
    span = pl.num_programs(0) - 1 - step
    heads = state.shape[0]
    strict, inclusive, upper, identity = masks(2 * SPAN)

    @pl.when(step == 0)
    def _():
        state[...] = jnp.zeros_like(state)
        gain_out[...] = jnp.zeros_like(gain_out)

    query, key = features[0], features[1]
    erase = solved[0]
    flag = keep[span]
    gain_total = jnp.zeros_like(gain_out[...])
    every, pairs = range(heads), range(heads // 2)
    passes = [product_t(pair(key, p), pair(query, p)) * upper for p in pairs]
    grads = []
    for h in every:
        lanes = slice(h * LANES, (h + 1) * LANES)
        gates = gate[:, lanes]
        sigma = sigmoid(gates)
        rows = mixed[:, lanes]
        grad = grad_head[:, lanes]
        scale = lax.rsqrt(jnp.mean(rows * rows, -1, keepdims=True) + EPS)
        unit = rows * scale
        grad_gate = grad * unit * gain[...] * sigma * (1.0 + gates * (1.0 - sigma))
        grad_gate = grad_gate.astype(LOW).astype(jnp.float32)
        grad_gate_out[:, lanes] = grad_gate
        shaped = grad * gates * sigma
        gain_total = gain_total + jnp.sum(shaped * unit, 0, keepdims=True)
        inward = shaped * gain[...]
        grad_rows = scale * (inward - unit * jnp.mean(inward * unit, -1, keepdims=True))
        grad_mixed_out[:, lanes] = grad_rows
        grads.append(split(grad_rows))
    passed = [product(passes[p], stack(grads[2 * p], grads[2 * p + 1])) for p in pairs]
    ends = [state[h] for h in every]
    grad_new = [
        passed[h // 2][h % 2 * SPAN : (h % 2 + 1) * SPAN] + product(head(key, h), ends[h])
        for h in every
    ]
    for h in every:
        state[h] = flag * (
            ends[h]
            + t_product(
                jnp.concatenate([head(query, h), -head(erase, h)], 0),
                stack(grads[h], split(grad_new[h])),
            )
        )
    gain_out[...] += gain_total
    half = grad_branch.shape[1] // 2
    first = core[0] == 0
    for place, source in ((0, grad_branch), (half, grad_gate_out)):
        low, high = source[:, :half], source[:, half:]
        kept_out[:, place : place + half] = jnp.where(first, low, high).astype(LOW)
        sent_out[:, place : place + half] = jnp.where(first, high, low)


def gather_states(
    keep, core, grad_head, grad_branch, mixed, gate, gain, features, solved, heads
):
    _, count, width = features.shape
    size = width // heads
    spans = count // SPAN
    f32 = lambda shape: jax.ShapeDtypeStruct(shape, jnp.float32)
    rows = pl.BlockSpec((SPAN, width), lambda c: (spans - 1 - c, 0))
    pairs = pl.BlockSpec((2, SPAN, width), lambda c: (0, spans - 1 - c, 0))
    one = pl.BlockSpec((1, SPAN, width), lambda c: (0, spans - 1 - c, 0))
    return pl.pallas_call(
        gather_kernel,
        grid=(spans,),
        in_specs=[
            pl.BlockSpec(memory_space=pltpu.SMEM), pl.BlockSpec(memory_space=pltpu.SMEM), rows, rows,
            rows, rows, pl.BlockSpec((1, size), lambda c: (0, 0)), pairs, one,
        ],
        out_specs=[
            rows, rows, rows, rows, pl.BlockSpec((1, size), lambda c: (0, 0)),
            pl.BlockSpec((heads, size, size), lambda c: (0, 0, 0)),
        ],
        out_shape=[
            f32((count, width)), f32((count, width)), jax.ShapeDtypeStruct((count, width), LOW),
            f32((count, width)), f32((1, size)), f32((heads, size, size)),
        ],
        compiler_params=params(),
        cost_estimate=cost(8 * count * width * size * 4, 32 * count * width),
        name="gather_states",
    )(keep, core, grad_head, grad_branch, mixed, gate, gain, features, solved)


def back_kernel(
    keep, place, features, beta, beta_pre, solved, inverses, starts, news, grad_mixed, state_mine,
    state_other, pre, conv, position, live, grad_pre_out, borrowed_out, conv_out, grad_beta_out, state, later, sums,
):
    step = pl.program_id(0)
    span = pl.num_programs(0) - 1 - step
    heads = state.shape[0]
    taps = conv.shape[1]
    strict, inclusive, upper, identity = masks(2 * SPAN)

    @pl.when(step == 0)
    def _():
        half = heads // 2
        first = place[0] == 0
        state[:half] = jnp.where(first, state_mine[...], state_other[...])
        state[half:] = jnp.where(first, state_other[...], state_mine[...])
        sums[...] = jnp.zeros_like(sums)
        later[...] = jnp.zeros_like(later)

    query, key, value = features[0], features[1], features[2]
    erase, update = solved[0], solved[1]
    betas = beta[...]
    flag = keep[span]
    base = pl.multiple_of(span * SPAN, SPAN)
    places = position[pl.ds(base, SPAN), :]
    lives = live[pl.ds(base, SPAN), :]
    valid = [
        jnp.broadcast_to(jnp.where(places >= taps - 1 - tap, 1.0, 0.0), (SPAN, LANES))
        for tap in range(taps - 1)
    ]
    every, pairs = range(heads), range(heads // 2)
    part = [slice(h % 2 * SPAN, (h % 2 + 1) * SPAN) for h in every]
    q = [split(pair(query, p)) for p in pairs]
    k = [split(pair(key, p)) for p in pairs]
    b = [pair_column(betas, p) for p in pairs]
    grad_out = [split(pair(grad_mixed, p)) for p in pairs]
    new = [split(pair(news, p)) for p in pairs]
    erases = [split(pair(erase, p)) for p in pairs]
    row = lambda value, h: tuple(v[part[h]] for v in value[h // 2])
    scores = [product_t(k[p], stack(k[p], q[p])) for p in pairs]
    passed = [product(scores[p][:, 2 * SPAN :] * upper, grad_out[p]) for p in pairs]
    ends = [split(state[h]) for h in every]
    begin = [split(starts[0, h]) for h in every]
    grad_new = [passed[h // 2][part[h]] + product(row(k, h), ends[h]) for h in every]
    grad_news = [split(value) for value in grad_new]
    both = [product_t(stack(row(grad_out, h), grad_news[h]), begin[h]) for h in every]
    grad_key = [product_t(row(new, h), ends[h]) for h in every]
    for h in every:
        state[h] = flag * (
            state[h]
            + t_product(
                stack(row(q, h), tuple(-v for v in row(erases, h))),
                stack(row(grad_out, h), grad_news[h]),
            )
        )
    grad_attend = [product_t(grad_out[p], new[p]) * inclusive for p in pairs]
    joined = lambda values, p: jnp.concatenate([values[2 * p], values[2 * p + 1]], 0)
    grad_q = [
        joined([value[:SPAN] for value in both], p) + product(grad_attend[p], k[p]) for p in pairs
    ]
    grad_k = [joined(grad_key, p) + product(grad_attend[p].T, q[p]) for p in pairs]
    turned = [
        product(
            inverses[0, p].T,
            jnp.concatenate(
                [joined(grad_new, p), -joined([value[SPAN:] for value in both], p)], 1
            ),
        )
        for p in pairs
    ]
    grad_bv = [value[:, :LANES] for value in turned]
    grad_bk = [value[:, LANES:] for value in turned]
    grad_lower = [
        -strict * (product_t(grad_bv[p], pair(update, p)) + product_t(grad_bk[p], erases[p]))
        for p in pairs
    ]
    inner = [b[p] * grad_lower[p] for p in pairs]
    grad_k = [
        grad_k[p] + product(inner[p] + inner[p].T, k[p]) + b[p] * grad_bk[p] for p in pairs
    ]
    grad_v = [b[p] * grad_bv[p] for p in pairs]
    beta_columns = []
    for p in pairs:
        grad_b = (
            jnp.sum(grad_lower[p] * scores[p][:, : 2 * SPAN], -1, keepdims=True)
            + jnp.sum(grad_bv[p] * pair(value, p), -1, keepdims=True)
            + jnp.sum(grad_bk[p] * pair(key, p), -1, keepdims=True)
        )
        beta_columns += [grad_b[:SPAN], grad_b[SPAN:]]
    chunks = [(which, h) for which in range(3) for h in every]
    for start in range(0, len(chunks), 4):
        group = chunks[start : start + 4]
        places = [(which, slice(h * LANES, (h + 1) * LANES)) for which, h in group]
        grads = [(grad_q, grad_k, grad_v)[which][h // 2][part[h]] for which, h in group]
        shifted = [
            [
                pre[which, 0, pl.ds(8 - (taps - 1) + tap, SPAN), lanes]
                for tap in range(taps)
            ]
            for which, lanes in places
        ]
        shifted = [
            [value * valid[tap] for tap, value in enumerate(moved[:-1])] + moved[-1:]
            for moved in shifted
        ]
        totals = [
            sum(
                conv[which, tap : tap + 1, lanes] * moved[tap] for tap in range(taps)
            )
            for moved, (which, lanes) in zip(shifted, places)
        ]
        sigmas = [sigmoid(total) for total in totals]
        acts = [total * sigma for total, sigma in zip(totals, sigmas)]
        slopes = [sigma + act * (1.0 - sigma) for sigma, act in zip(sigmas, acts)]
        squares = [
            jnp.sum(act * act, -1, keepdims=True) if which < 2 else None
            for act, (which, _) in zip(acts, group)
        ]
        grads = [
            grad * lives if which == 1 else grad for grad, (which, _) in zip(grads, group)
        ]
        scales = [None if square is None else lax.rsqrt(square + KEY_EPS) for square in squares]
        units = [act if scale is None else act * scale for act, scale in zip(acts, scales)]
        along = [
            None if scale is None else jnp.sum(grad * unit, -1, keepdims=True)
            for grad, unit, scale in zip(grads, units, scales)
        ]
        grads = [
            slope * (grad if scale is None else scale * (grad - unit * dot))
            for slope, grad, scale, unit, dot in zip(slopes, grads, scales, units, along)
        ]
        for grad, moved, (which, lanes) in zip(grads, shifted, places):
            result = conv[which, taps - 1 : taps, lanes] * grad
            for tap in range(taps):
                product_ = grad * moved[tap]
                sums[which, tap, :, lanes] += sum(
                    product_[8 * r : 8 * (r + 1)] for r in range(SPAN // 8)
                )
                if tap < taps - 1:
                    masked = grad * valid[tap]
                    later[which, tap, SPAN:, lanes] = later[which, tap, :8, lanes]
                    later[which, tap, :SPAN, lanes] = masked
                    result = result + conv[which, tap : tap + 1, lanes] * (
                        later[which, tap, pl.ds(taps - 1 - tap, SPAN), lanes]
                    )
            grad_pre_out[which, :, lanes] = result
    columns = lax.broadcasted_iota(jnp.int32, (SPAN, heads), 1)
    grad_beta = jnp.zeros((SPAN, heads), jnp.float32)
    for h in range(heads):
        grad_beta = jnp.where(columns == h, beta_columns[h], grad_beta)
    sigma = sigmoid(beta_pre[...])
    grad_beta_out[...] = (
        (grad_beta * lives * sigma * (1.0 - sigma)).astype(LOW).astype(jnp.float32)
    )

    @pl.when(span == 0)
    def _():
        conv_out[...] = jnp.sum(sums[...], 2)
        for which in range(3):
            result = None
            for tap in range(taps - 1):
                ahead = taps - 1 - tap
                rows = jnp.concatenate([jnp.zeros((8, later.shape[3]), jnp.float32), later[which, tap, :8]], 0)
                term = conv[which, tap : tap + 1, :] * rows[ahead:][:8]
                result = term if result is None else result + term
            borrowed_out[which] = result


def back(
    keep, place, features, beta, beta_pre, solved, inverses, starts, news, grad_mixed, state_mine,
    state_other, pre, conv, position, live,
):
    _, count, width = features.shape
    half, size, _ = state_mine.shape
    heads = 2 * half
    spans = count // SPAN
    taps = conv.shape[1]
    f32 = lambda shape: jax.ShapeDtypeStruct(shape, jnp.float32)
    whole = lambda shape: pl.BlockSpec(shape, lambda c: (0,) * len(shape))
    rows = pl.BlockSpec((SPAN, width), lambda c: (spans - 1 - c, 0))
    triple = pl.BlockSpec((3, SPAN, width), lambda c: (0, spans - 1 - c, 0))
    column = pl.BlockSpec((SPAN, heads), lambda c: (spans - 1 - c, 0))
    return pl.pallas_call(
        back_kernel,
        grid=(spans,),
        in_specs=[
            pl.BlockSpec(memory_space=pltpu.SMEM), pl.BlockSpec(memory_space=pltpu.SMEM), triple, column, column,
            pl.BlockSpec((2, SPAN, width), lambda c: (0, spans - 1 - c, 0)),
            pl.BlockSpec((1, heads // 2, 2 * SPAN, 2 * SPAN), lambda c: (spans - 1 - c, 0, 0, 0)),
            pl.BlockSpec((1, heads, size, size), lambda c: (spans - 1 - c, 0, 0, 0)),
            rows, rows, whole((half, size, size)), whole((half, size, size)),
            pl.BlockSpec((3, 1, SPAN + 8, width), lambda c: (0, spans - 1 - c, 0, 0)),
            whole(conv.shape),
            whole(position.shape), whole(live.shape),
        ],
        out_specs=[triple, whole((3, 8, width)), whole((3, taps, width)), column],
        out_shape=[
            f32((3, count, width)), f32((3, 8, width)), f32((3, taps, width)), f32((count, heads)),
        ],
        scratch_shapes=[
            pltpu.VMEM((heads, size, size), jnp.float32),
            pltpu.VMEM((3, taps - 1, SPAN + 8, width), jnp.float32),
            pltpu.VMEM((3, taps, 8, width), jnp.float32),
        ],
        compiler_params=params(),
        cost_estimate=cost(30 * count * width * size * 4, 60 * count * width),
        name="back",
    )(
        keep, place, features, beta, beta_pre, solved, inverses, starts, news, grad_mixed,
        state_mine, state_other, pre, conv, position, live,
    )


def enter_kernel(
    tokens, gain, grad_hidden, grads, grad_gate, grad_beta, query_w, key_w, value_w, gate_w, beta_w,
    input_grad_out, gain_out, total,
):
    step = pl.program_id(0)
    term = mxu(grad_gate[...].astype(LOW), gate_w[...], NT)
    for which, weight in enumerate((query_w, key_w, value_w)):
        term = term + mxu(grads[which], weight[...], NT)

    @pl.when(step == 0)
    def _():
        total[...] = term + mxu(grad_beta[...].astype(LOW), beta_w[...], NN)

    @pl.when(step > 0)
    def _():
        total[...] += term

    @pl.when(step == pl.num_programs(0) - 1)
    def _():
        part, gain_part = norm_back(tokens[...].astype(jnp.float32), gain[...], total[...])
        gain_out[...] = gain_part
        input_grad_out[...] = (grad_hidden[...] + part).astype(LOW)


def enter(
    tokens, gain, grad_hidden, grads, grad_gate, grad_beta, query_w, key_w, value_w, gate_w, beta_w
):
    count, width = tokens.shape
    heads = beta_w.shape[0]
    block = 2 * LANES
    whole = lambda shape: pl.BlockSpec(shape, lambda j: (0,) * len(shape))
    weight = pl.BlockSpec((width, block), lambda j: (0, j))
    return pl.pallas_call(
        enter_kernel,
        grid=(width // block,),
        in_specs=[
            whole((count, width)), whole((1, width)), whole((count, width)),
            pl.BlockSpec((3, count, block), lambda j: (0, 0, j)),
            pl.BlockSpec((count, block), lambda j: (0, j)), whole((count, heads)),
            weight, weight, weight, weight, whole((heads, width)),
        ],
        out_specs=[whole((count, width)), whole((1, width))],
        out_shape=[
            jax.ShapeDtypeStruct((count, width), LOW), jax.ShapeDtypeStruct((1, width), jnp.float32),
        ],
        scratch_shapes=[pltpu.VMEM((count, width), jnp.float32)],
        compiler_params=params(),
        cost_estimate=cost(8 * count * width * width, 8 * width * width + 20 * count * width),
        name="enter",
    )(
        tokens, gain, grad_hidden, grads, grad_gate, grad_beta, query_w, key_w, value_w, gate_w,
        beta_w,
    )


def passed_along(value, axis, by):
    devices = lax.axis_size(axis)
    pairs = [(i, i + by) for i in range(devices) if 0 <= i + by < devices]
    return lax.ppermute(value, axis, pairs)


def tuned():
    return (lax.axis_size("seq"), lax.axis_size("doc")) == (8, 4)


HOPS = {"core": ("doc", 1), "y": ("doc", 2), "x": ("seq", 1), "near": ("seq", 2), "far": ("seq", 4)}


def hop(value, way, other_way=None):
    if other_way in (None, way):
        axis, bit = HOPS[way]
        return lax.ppermute(value, axis, [(i, i ^ bit) for i in range(lax.axis_size(axis))])
    size = lax.axis_size("doc")
    masks = [bit * size if axis == "seq" else bit for axis, bit in (HOPS[way], HOPS[other_way])]
    pairs = [(i, i ^ masks[i % 2]) for i in range(lax.axis_size("seq") * size)]
    return lax.ppermute(value, ("seq", "doc"), pairs)


def side(way):
    axis, bit = HOPS[way]
    return lax.axis_index(axis) // bit % 2


def apply_kernel(shift, maps, *refs, turned):
    *states, out = refs
    size = maps.shape[1]
    for h in range(maps.shape[0]):
        state = states[0][h]
        for other in states[1:]:
            state = state + other[h]
        moved = (t_product if turned else product)(maps[h, :, size:], state)
        if state.shape[1] == size:
            out[h] = moved + shift[h, :, :size]
        else:
            out[h] = moved + jnp.concatenate([shift[h, :, :size], jnp.zeros((size, size), jnp.float32)], 1)


def apply_map(shift, maps, *states, turned=False):
    return pl.pallas_call(
        lambda *refs: apply_kernel(*refs, turned=turned),
        out_shape=jax.ShapeDtypeStruct(states[0].shape, jnp.float32),
        compiler_params=params(4),
        cost_estimate=cost(0, 0),
        name="apply_map",
    )(shift, maps, *states)


def ends_kernel(here, shift, maps, state, come, stay_out, send_out, *, turned):
    size = maps.shape[1]
    mine = here[0] == 0
    for h in range(maps.shape[0]):
        near = state[h] + come[h]
        far = (t_product if turned else product)(maps[h, :, size:], near) + shift[h, :, :size]
        if turned:
            near, far = far, near
        stay_out[h] = jnp.where(mine, near, far)
        send_out[h] = jnp.where(mine, far, near)


def pair_ends(here, shift, maps, state, come, turned=False):
    shape = jax.ShapeDtypeStruct(state.shape, jnp.float32)
    vmem = pl.BlockSpec(memory_space=pltpu.VMEM)
    return pl.pallas_call(
        lambda *refs: ends_kernel(*refs, turned=turned),
        in_specs=[pl.BlockSpec(memory_space=pltpu.SMEM)] + [vmem] * 4,
        out_specs=[vmem, vmem],
        out_shape=[shape, shape],
        compiler_params=params(4),
        cost_estimate=cost(0, 0),
        name="pair_ends",
    )(here, shift, maps, state, come)


def together(value, *others):
    return lax.optimization_barrier((value, *others))


def carried_forward(maps, beside):
    heads, size, _ = maps.shape
    half = heads // 2
    if not tuned():
        gathered = lax.all_gather(maps, "seq")

        def one(lap, state):
            each = lax.dynamic_index_in_dim(gathered, lap, 0, False)
            return apply_map(each, each, state)

        state = lax.fori_loop(
            0, lax.axis_index("seq"), one, jnp.zeros((heads, size, size), jnp.float32)
        )
        return state[:half], state[half:], jnp.zeros((1,), jnp.int32), (maps,)
    place = side("x").astype(jnp.int32).reshape(1)
    here = place[0] == 0
    kept = jnp.where(here, maps[:half], maps[half:])
    other = hop(jnp.where(here, maps[half:], maps[:half]), "x")
    other, *beside = together(other, *beside)
    first, second = jnp.where(here, kept, other), jnp.where(here, other, kept)
    pair_map = apply_map(second, second, first)
    state = jnp.zeros((half, size, size), jnp.float32)
    come = state
    for step in range(3):
        if step == 0:
            sent = pair_map[:, :, :size]
        else:
            sent = apply_map(pair_map, pair_map, state, come)
            state = state + come
        come = lax.ppermute(sent, "seq", [(2 * step + x, 2 * step + 2 + x) for x in range(2)])
    mine, send = pair_ends(place, first, first, state, come)
    return mine, hop(send, "x"), place, (first, second, pair_map), *beside


def carried_back(shift, context, beside=None):
    heads, size, _ = shift.shape
    half = heads // 2
    if not tuned():
        gathered = lax.all_gather(jnp.concatenate([shift, context[0][:, :, size:]], 2), "seq")
        count = lax.axis_size("seq")

        def one(lap, state):
            each = lax.dynamic_index_in_dim(gathered, count - 1 - lap, 0, False)
            return apply_map(each, each, state, turned=True)

        zeros = jnp.zeros((heads, size, size), jnp.float32)
        state = lax.fori_loop(0, count - 1 - lax.axis_index("seq"), one, zeros)
        return state[:half], state[half:], ()
    first, second, pair_map = context
    place = side("x").astype(jnp.int32).reshape(1)
    here = place[0] == 0
    done = []

    def step_with(number, sent, go):
        moves, work = beside[number]
        sent, *values = together(sent, *[move[0] for move in moves])
        come, *rest = together(
            go(sent), *[hop(value, *move[1:]) for value, move in zip(values, moves)], *work
        )
        done.append(rest)
        return come

    kept = jnp.where(here, shift[:half], shift[half:])
    other = step_with(0, jnp.where(here, shift[half:], shift[:half]), lambda value: hop(value, "x"))
    first_shift, second_shift = jnp.where(here, kept, other), jnp.where(here, other, kept)
    pair_shift = apply_map(first_shift, first, second_shift, turned=True)
    state = jnp.zeros((half, size, size), jnp.float32)
    come = state
    for step in range(3, 0, -1):
        if step == 3:
            sent = pair_shift
        else:
            sent = apply_map(pair_shift, pair_map, state, come, turned=True)
            state = state + come
        pairs = [(2 * step + x, 2 * step - 2 + x) for x in range(2)]
        come = step_with(4 - step, sent, lambda value: lax.ppermute(value, "seq", pairs))
    mine, send = pair_ends(place, second_shift, second, state, come, turned=True)
    return mine, step_with(4, send, lambda value: hop(value, "x")), done


def outer_kernel(table, *refs, blocks, pieces):
    count = len(blocks)
    lefts, rights = refs[: 2 * count], refs[2 * count : 4 * count]
    *outs, stacked = refs[4 * count :]
    step = pl.program_id(0)
    tokens = lefts[0].shape[1]
    size = outs[0].shape[0] // 8

    @pl.when(step == 0)
    def _():
        for piece in range(count):
            for which in range(2):
                for place in range(16):
                    rows = pl.ds(pl.multiple_of(table[place] * size, 16), size)
                    stacked[
                        piece, place * size : (place + 1) * size, which * tokens : (which + 1) * tokens
                    ] = lefts[2 * piece + which][rows, :].astype(LOW)

    for piece in range(count):
        low = sum(blocks[:piece])

        @pl.when((step >= low) & (step < low + blocks[piece]))
        def _(piece=piece):
            right = jnp.concatenate(
                [rights[2 * piece][...].astype(LOW), rights[2 * piece + 1][...].astype(LOW)], 0
            )
            place = 0
            for out, number in zip(outs, (8 * size, *pieces)):
                out[...] = mxu(stacked[piece, place : place + number, :], right, NN)
                place += number


WEIGHTS = {"far": 8, "near": 4, "x": 2, "y": 1}


def by_core(values):
    return jnp.where(side("core") == 0, values[0], values[1])


def outer(pieces, orders, parts=(1,)):
    rows, tokens = pieces[0][0].shape
    block = 2 * LANES
    table = []
    for place in range(16):
        entries = []
        for order in orders:
            bits = [place >> 3 & 1, place >> 2 & 1, place >> 1 & 1, place & 1]
            first = side(order[0]) ^ bits[0]
            rest = sum(bit * WEIGHTS[way] for bit, way in zip(bits[1:], order[1:]))
            entries.append(first * WEIGHTS[order[0]] + rest)
        table.append(by_core(entries))
    table = jnp.stack(table).astype(jnp.int32)
    counts = [piece[5] for piece in pieces]
    left = pl.BlockSpec((rows, tokens), lambda j: (0, 0), pipeline_mode=pl.Buffered(1))
    lefts, rights, specs = [], [], []
    for index, piece in enumerate(pieces):
        lefts += piece[:2]
        rights += piece[2:4]

        def place(j, low=sum(counts[:index]), first=piece[4], number=piece[5]):
            return 0, first + jnp.clip(j - low, 0, number - 1)

        specs += [pl.BlockSpec((tokens, block), place)] * 2
    total = sum(counts)
    sizes = [rows // 2 * part // sum(parts) for part in parts]
    outs = [rows // 2, *sizes]
    keep, *sends = pl.pallas_call(
        lambda *refs: outer_kernel(*refs, blocks=counts, pieces=sizes),
        grid=(total,),
        in_specs=[pl.BlockSpec(memory_space=pltpu.SMEM)] + [left] * len(lefts) + specs,
        out_specs=[pl.BlockSpec((size, block), lambda j: (0, j)) for size in outs],
        out_shape=[jax.ShapeDtypeStruct((size, total * block), jnp.float32) for size in outs],
        scratch_shapes=[pltpu.VMEM((len(pieces), rows, 2 * tokens), LOW)],
        compiler_params=params(),
        cost_estimate=cost(0, 0),
        name="outer",
    )(table, *lefts, *rights)
    return keep, sends


def take(value, place, axis):
    return lax.dynamic_index_in_dim(value, place, axis, False)


class Part:
    def __init__(self, keeps, comes, orders, split_y=True):
        self.orders, self.split_y, self.stage = orders, split_y, 1
        self.groups = [[self.shaped(value) for value in group] for group in zip(keeps, comes)]
        self.terms = []

    def shaped(self, value):
        left = tuple(range(self.stage, len(self.orders[0])))
        columns = value.shape[-1]
        rows = value.size // columns // 2 ** len(left)
        return value.reshape((2,) * len(left) + (rows, columns)), left

    def add(self, come):
        self.terms.append(self.shaped(come))

    def place(self, stage):
        return by_core([side(order[stage]) for order in self.orders])

    def chosen(self, here):
        sums = [self.added(group, here) for group in self.groups]
        total = sums[0] if len(sums) == 1 else jnp.concatenate(sums, -1)
        return total + self.added(self.terms, here) if self.terms else total

    def added(self, terms, here):
        total = None
        for value, left in terms:
            starts, sizes = [], []
            for stage in left:
                fixed = stage <= self.stage
                place = self.place(stage) if fixed else 0
                starts.append(1 - place if stage == self.stage and not here else place)
                sizes.append(1 if fixed else 2)
            sizes += value.shape[len(left) :]
            starts = [jnp.asarray(start, jnp.int32) for start in [*starts, 0, 0]]
            piece = lax.dynamic_slice(value, starts, sizes)
            piece = piece.reshape([size for size in sizes[:-2] if size > 1] + sizes[-2:])
            total = piece if total is None else total + piece
        return total

    def move(self):
        if self.stage < len(self.orders[0]):
            send = self.chosen(False)
            ways = [order[self.stage] for order in self.orders]
            self.stage += 1
            self.absorb = self.add
            return send, *ways
        if self.stage == len(self.orders[0]):
            mine = self.chosen(True)
            self.stage += 1

            def absorb(come):
                self.done = in_order(mine, come) if self.split_y else mine + come

            self.absorb = absorb
            return mine, "y"
        self.absorb = lambda come: setattr(self, "other", come)
        return self.done, "core"


def in_order(mine, come):
    first = side("y") == 0
    return jnp.concatenate([jnp.where(first, mine, come), jnp.where(first, come, mine)], 0)


def advance(parts, extra=(), beside=()):
    moves = [part.move() for part in parts] + list(extra)
    values = together(*[move[0] for move in moves])
    comes = [hop(value, *move[1:]) for value, move in zip(values, moves)]
    done = together(*comes, *beside)
    for part, come in zip(parts, done):
        part.absorb(come)
    done = done[len(parts) :]
    return done[: len(extra)], done[len(extra) :]


def flatten_small(small):
    first_gain, beta, conv, head_gain, second_gain = small
    seq = lax.axis_size("seq")
    flat = jnp.concatenate(
        [
            first_gain.reshape(seq, -1), beta.reshape(seq, -1),
            conv.reshape(conv.shape[0] * conv.shape[1], seq, -1).transpose(1, 0, 2).reshape(seq, -1),
            head_gain.reshape(seq, -1), second_gain.reshape(seq, -1),
        ],
        1,
    )
    size = flat.shape[1]
    rows = -(-size // 2048) * 16
    return jnp.pad(flat, ((0, 0), (0, rows * 128 - size))).reshape(seq * rows, 128)


def unflatten_small(flat, small):
    first_gain, beta, conv, head_gain, second_gain = small
    seq = lax.axis_size("seq")
    flat = flat.reshape(-1)
    sizes = [a.size // seq for a in small]
    places = [sum(sizes[:i]) for i in range(len(sizes))]
    pieces = [flat[p : p + s] for p, s in zip(places, sizes)]
    return (
        pieces[0], pieces[1].reshape(-1, beta.shape[1]),
        pieces[2].reshape(conv.shape[0], conv.shape[1], -1), pieces[3], pieces[4],
    )


def outer_sum(left, right):
    return mxu(left.astype(LOW), right.astype(LOW), TN)


def local(
    tokens,
    doc_lengths,
    out_grad,
    first_gain,
    query_weight,
    key_weight,
    value_weight,
    gate_weight,
    beta_weight,
    conv_weight,
    head_gain,
    out_weight,
    second_gain,
    hidden_gate,
    hidden_up,
    hidden_down,
):
    count, width = (tokens.shape[1], tokens.shape[2])
    heads = beta_weight.shape[1]
    reach = conv_weight.shape[1] - 1
    first = lax.axis_index("seq") * count
    position, live = doc_info(doc_lengths[0], first, count)
    keep = 1.0 - (position[::CK] == 0).astype(jnp.float32)
    position, live = position[:, None], live[:, None]
    core = (lax.axis_index("doc") % 2).astype(jnp.int32).reshape(1)
    here = core[0] == 0
    rows, top = tokens[0], out_grad[0]
    halo = passed_along(rows[count - HALO :].astype(jnp.float32), "seq", 1)
    normed_one, pre, features, gate_pre, beta_pre, beta = project(
        rows, halo, first_gain[None], position, live, query_weight, key_weight, value_weight,
        gate_weight, beta_weight.T, conv_weight,
    )
    solved, inverses, attend, maps = prepare(keep, features, beta)
    if tuned():
        half = width // 2
        units = half // 256

        def pick(zero, one):
            return jnp.where(here, zero, one)

        def both(value, send=None):
            return value, hop(value if send is None else send, "core")

        wide_top = top.astype(jnp.float32)
        tops = both(
            pick(top[:, :half], top[:, half:]), pick(wide_top[:, half:], wide_top[:, :half])
        )
        one = both(normed_one)
    state_mine, state_other, place, context, *beside = carried_forward(
        maps, (*tops, *one) if tuned() else ()
    )
    if tuned():
        tops, one = beside[:2], beside[2:]
    starts, news, mixed, normed_head = mix(
        keep, place, features, solved, attend, gate_pre, head_gain[None], state_mine, state_other
    )
    (
        block_out, two_turned, inner_turned, kept, sent, grad_hidden, grad_branch, grad_head,
        grad_second_gain, head_turned,
    ) = feed(
        core, rows, normed_head, top, second_gain[None], out_weight, hidden_gate, hidden_up,
        hidden_down,
    )
    if tuned():
        heads_turned = both(head_turned)
        two = both(two_turned)
        gate_up = both(kept, sent)
    grad_mixed, grad_gate_pre, out_kept, out_sent, grad_head_gain, shift = gather_states(
        keep, core, grad_head, grad_branch, mixed, gate_pre, head_gain[None], features, solved, heads
    )
    if tuned():
        out_right = both(out_kept, out_sent)
        blocks = hidden_gate.shape[1] // 256
        some = blocks * 3 // 11
        blocks = hidden_gate.shape[1] // 256
        low = blocks * 9 // 11
        orders = ("x", "y", "near", "far"), ("y", "x", "far", "near")
        down_orders = ("near", "x", "y", "far"), ("near", "y", "x", "far")
        firsts = [order[0] for order in orders]
        shift, two_other, gate_up_other, inner_turned = together(
            shift, two[1], gate_up[1], inner_turned
        )
        inners = both(inner_turned)
        two, gate_up = (two[0], two_other), (gate_up[0], gate_up_other)
        out_right = both(out_kept, out_sent)
        wide_keep, wide_sends = outer([(*two, *gate_up, 0, low)], orders, (1, 2, 2, 2, 1))
        shift, wide_keep, *wide_sends = together(shift, wide_keep, *wide_sends)
        down_keep, down_sends = outer([(*inners, *tops, 0, units)], down_orders, (1, 1))
        rest_keep, rest_sends = outer(
            [
                (*two, *gate_up, low, blocks - low), (*heads_turned, *out_right, 0, units),
                (*one, *out_right, units, units),
            ],
            orders,
        )
        work = [(down_keep, *down_sends), (rest_keep, *rest_sends), (), (), ()]
        moves = [[(send, *firsts)] for send in wide_sends]
        grad_mine, grad_other, done = carried_back(shift, context, list(zip(moves, work)))
        down_keep, *down_sends = done[0][1:]
        rest_keep, *rest_sends = done[1][1:]
        wide_come = jnp.concatenate([value[0] for value in done], 0)
        moves = [(rest_sends[0], *firsts), (down_sends[0], "near")]
        grad_other, *values = together(grad_other, *[move[0] for move in moves])
        comes = [hop(value, *move[1:]) for value, move in zip(values, moves)]
    else:
        grad_mine, grad_other, _ = carried_back(shift, context)
    grads, borrowed, grad_conv, grad_beta_pre = back(
        keep, place, features, beta, beta_pre, solved, inverses, starts, news, grad_mixed, grad_mine,
        grad_other, pre, conv_weight, position, live,
    )
    if tuned():
        borrowed, *comes = together(borrowed, *comes)
        wide_part = Part((wide_keep, rest_keep), (wide_come, comes[0]), orders)
        down_come = comes[1]
    returned = passed_along(borrowed, "seq", -1)
    tail = grads[:, count - 8 :] + returned
    grads = lax.dynamic_update_slice(grads, tail, (0, count - 8, 0))
    grads = grads.astype(LOW)
    if tuned():
        moves = [wide_part.move(), (down_sends[1], "near")]
        grads, *values = together(grads, *[move[0] for move in moves])
        comes = [hop(value, *move[1:]) for value, move in zip(values, moves)]
        wide = grads.astype(jnp.float32)
        query_key = both(pick(grads[0], grads[1]), pick(wide[1], wide[0]))
        value = both(
            pick(grads[2, :, :half], grads[2, :, half:]), pick(wide[2, :, half:], wide[2, :, :half])
        )
        late_keep, (late_send,) = outer(
            [(*one, *query_key, 0, 2 * units), (*one, *value, 0, units)], orders
        )
        grads, late_send, *comes = together(grads, late_send, *comes)
        wide_part.absorb(comes[0])
        down = Part((down_keep,), (jnp.concatenate([down_come, comes[1]], 0),), down_orders)
        input_grad, grad_first_gain = enter(
            rows, first_gain[None], grad_hidden, grads, grad_gate_pre, grad_beta_pre, query_weight,
            key_weight, value_weight, gate_weight, beta_weight.T,
        )
        small = (
            grad_first_gain[0], outer_sum(normed_one.T, grad_beta_pre), grad_conv, grad_head_gain[0],
            grad_second_gain[0],
        )
        flat = flatten_small(small)
        (come,), (flat, input_grad) = advance(
            [wide_part, down], [(late_send, *firsts)], (flat, input_grad)
        )
        late = Part((late_keep,), (come,), orders)
        (come,), _ = advance([late, wide_part, down], [(flat, "core")])
        flat = (flat + come).reshape(2, 2, 2, -1, 128).transpose(2, 1, 0, 3, 4)
        bit = side("x")
        tiny_keep, tiny_send = (take(flat, place, 0).reshape(-1, 128) for place in (bit, 1 - bit))
        (come,), _ = advance([late, down, wide_part], [(tiny_send, "x")])
        tiny = Part((tiny_keep,), (come,), (("x", "near", "far"),) * 2, False)
        advance([late, down, wide_part, tiny])
        advance([late, down, tiny])
        advance([late, tiny])
        zero = lambda part: pick(part.done, part.other)
        one_ = lambda part: pick(part.other, part.done)
        split = blocks * 256
        hidden_gate_g, hidden_up_g = (
            of(wide_part)[:, : blocks * 256] for of in (zero, one_)
        )
        out_g, gate_g = (
            jnp.concatenate([zero(wide_part)[:, places], one_(wide_part)[:, places]], 1)
            for places in (slice(split, split + half), slice(split + half, split + width))
        )
        query_g, key_g = zero(late)[:, :width], one_(late)[:, :width]
        value_g = jnp.concatenate([zero(late)[:, width:], one_(late)[:, width:]], 1)
        hidden_down_g = jnp.concatenate([zero(down), one_(down)], 1)
        first_g, beta_g, conv_g, head_g, second_g = unflatten_small(tiny.done, small)
    else:
        input_grad, grad_first_gain = enter(
            rows, first_gain[None], grad_hidden, grads, grad_gate_pre, grad_beta_pre, query_weight,
            key_weight, value_weight, gate_weight, beta_weight.T,
        )
        small = (
            grad_first_gain[0], outer_sum(normed_one.T, grad_beta_pre), grad_conv, grad_head_gain[0],
            grad_second_gain[0],
        )

        def whole(term, dimension):
            part = lax.psum_scatter(term, "seq", scatter_dimension=dimension, tiled=True)
            return lax.psum(part, "doc")

        gate_grad, up_grad = jnp.where(here, kept, sent), jnp.where(here, sent, kept)
        terms = (
            outer_sum(normed_one.T, grads[0]), outer_sum(normed_one.T, grads[1]),
            outer_sum(normed_one.T, grads[2]), outer_sum(normed_one.T, grad_gate_pre),
            outer_sum(head_turned.T, grad_branch), outer_sum(two_turned.T, gate_grad),
            outer_sum(two_turned.T, up_grad), outer_sum(inner_turned.T, top),
        )
        query_g, key_g, value_g, gate_g, out_g, hidden_gate_g, hidden_up_g, hidden_down_g = (
            whole(term, 0) for term in terms
        )
        first_g, beta_g, conv_g, head_g, second_g = (
            whole(term, d) for term, d in zip(small, (0, 0, 2, 0, 0))
        )
    return (
        block_out[None], input_grad[None], first_g, query_g, key_g, value_g, gate_g, beta_g, conv_g,
        head_g, out_g, second_g, hidden_gate_g, hidden_up_g, hidden_down_g,
    )


def solution(mesh):
    in_specs = (
        P("doc", "seq", None),
        P("doc", None),
        P("doc", "seq", None),
        P(),
        P(),
        P(),
        P(),
        P(),
        P(),
        P(),
        P(),
        P(),
        P(),
        P(),
        P(),
        P(),
    )
    out_specs = (
        P("doc", "seq", None),
        P("doc", "seq", None),
        P("seq"),
        P("seq", None),
        P("seq", None),
        P("seq", None),
        P("seq", None),
        P("seq", None),
        P(None, None, "seq"),
        P("seq"),
        P("seq", None),
        P("seq"),
        P("seq", None),
        P("seq", None),
        P("seq", None),
    )
    return jax.shard_map(local, mesh=mesh, in_specs=in_specs, out_specs=out_specs, check_vma=False)
```

```python
import jax
import jax.numpy as jnp
from jax import lax
from jax.experimental import pallas as pl
from jax.experimental.pallas import tpu as pltpu
from jax.sharding import PartitionSpec as P

CK = 64


EPS = 1e-05
KEY_EPS = 1e-06
HIGH = lax.Precision.HIGHEST


def doc_info(lengths, first, count):
    padded = (lengths + CK - 1) // CK * CK
    ends = jnp.cumsum(padded)
    starts = ends - padded
    place = first + jnp.arange(count, dtype=jnp.int32)
    inside = ((place[:, None] >= starts[None, :]) & (place[:, None] < ends[None, :])).astype(
        jnp.int32
    )
    position = place - jnp.sum(inside * starts[None, :], 1)
    length = jnp.sum(inside * lengths[None, :], 1)
    live = (position < length).astype(jnp.float32)
    return (position, live)


SPAN = CK
LANES = 128
LOW = jnp.bfloat16
NN = (((1,), (0,)), ((), ()))
NT = (((1,), (1,)), ((), ()))
TN = (((0,), (0,)), ((), ()))


def params(mib=54):
    return pltpu.CompilerParams(vmem_limit_bytes=mib * 2**20)


def cost(flops, moved):
    return pl.CostEstimate(flops=1, bytes_accessed=1, transcendentals=0)


def mxu(left, right, dims):
    return lax.dot_general(left, right, dims, preferred_element_type=jnp.float32)


def halves(value):
    high = value.astype(LOW)
    return high, (value - high.astype(jnp.float32)).astype(LOW)


def split(value):
    return value if isinstance(value, tuple) else halves(value)


def stack(first, second):
    return tuple(jnp.concatenate(both, 0) for both in zip(first, second))


def fold(value):
    half = value.shape[1] // 2
    return value[:, :half] + value[:, half:]


def product(left, right):
    left_high, left_low = split(left)
    right_high, right_low = split(right)
    both = jnp.concatenate([left_high, left_low], 1)
    if right_high.shape[1] <= LANES:
        wide = jnp.concatenate([right_high, right_low], 1)
        return fold(mxu(both, jnp.concatenate([wide, wide], 0), NN))
    return mxu(both, jnp.concatenate([right_high, right_high], 0), NN) + mxu(
        left_high, right_low, NN
    )


def product_t(left, right):
    left_high, left_low = split(left)
    right_high, right_low = split(right)
    both = jnp.concatenate([left_high, left_low], 1)
    if right_high.shape[0] <= LANES:
        rows = jnp.concatenate(
            [
                jnp.concatenate([right_high, right_high], 1),
                jnp.concatenate([right_low, right_low], 1),
            ],
            0,
        )
        return fold(mxu(both, rows, NT))
    return mxu(both, jnp.concatenate([right_high, right_high], 1), NT) + mxu(
        left_high, right_low, NT
    )


def t_product(left, right):
    left_high, left_low = split(left)
    right_high, right_low = split(right)
    both = jnp.concatenate([left_high, left_low], 0)
    if right_high.shape[1] <= LANES:
        wide = jnp.concatenate([right_high, right_low], 1)
        return fold(mxu(both, jnp.concatenate([wide, wide], 0), TN))
    return mxu(both, jnp.concatenate([right_high, right_high], 0), TN) + mxu(
        left_high, right_low, TN
    )


def head(value, h):
    return value[:, h * LANES : (h + 1) * LANES]


def pair(value, p):
    return jnp.concatenate([head(value, 2 * p), head(value, 2 * p + 1)], 0)


def pair_column(value, p):
    return jnp.concatenate([value[:, 2 * p : 2 * p + 1], value[:, 2 * p + 1 : 2 * p + 2]], 0)


def masks(rows):
    i = lax.broadcasted_iota(jnp.int32, (rows, rows), 0)
    j = lax.broadcasted_iota(jnp.int32, (rows, rows), 1)
    same = (i >= SPAN) == (j >= SPAN)
    strict = jnp.where(same & (j < i), 1.0, 0.0)
    inclusive = jnp.where(same & (j <= i), 1.0, 0.0)
    upper = jnp.where(same & (j >= i), 1.0, 0.0)
    return strict, inclusive, upper, jnp.where(i == j, 1.0, 0.0)


def inverses_of(strict_parts, identity):
    rows = identity.shape[0]
    results = [identity - part for part in strict_parts]
    powers = [split(part) for part in strict_parts]
    powers = [split(product(power, power)) for power in powers]
    for level in range(SPAN.bit_length() - 3):
        both = [
            product(stack(split(result), power), power) for result, power in zip(results, powers)
        ]
        results = [result + pair_[:rows] for result, pair_ in zip(results, both)]
        powers = [split(pair_[rows:]) for pair_ in both]
    return [result + product(result, power) for result, power in zip(results, powers)]


def sigmoid(value):
    return 1.0 / (1.0 + jnp.exp(-value))


HALO = 16


def project_kernel(
    tokens, halo, gain, position, live, query_w, key_w, value_w, gate_w, beta_w, conv,
    normed_out, pre_out, feature_out, gate_out, beta_pre_out, beta_out, normed, pre,
):
    count = tokens.shape[0]

    @pl.when(pl.program_id(0) == 0)
    def _():
        def norm(rows):
            return (
                rows * lax.rsqrt(jnp.mean(rows * rows, -1, keepdims=True) + EPS) * gain[...]
            ).astype(LOW)

        normed[:HALO, :] = norm(halo[...])
        rounded = norm(tokens[...].astype(jnp.float32))
        normed[HALO:, :] = rounded
        normed_out[...] = rounded.astype(jnp.float32).T
        beta_pre = mxu(rounded, beta_w[...], NT)
        beta_pre_out[...] = beta_pre
        beta_out[...] = sigmoid(beta_pre) * live[...]

    gate_out[...] = mxu(normed[HALO:, :], gate_w[...], NN)
    valid = [
        jnp.broadcast_to(
            jnp.where(position[...] >= conv.shape[1] - 1 - tap, 1.0, 0.0), (count, LANES)
        )
        for tap in range(conv.shape[1] - 1)
    ]
    for which, weight in enumerate((query_w, key_w, value_w)):
        pre[which] = mxu(normed[...], weight[...], NN)
        for span in range(count // SPAN):
            start = HALO + span * SPAN
            pre_out[which, span] = pre[which, start - 8 : start + SPAN, :]
        for part in range(pre.shape[2] // LANES):
            lanes = slice(part * LANES, (part + 1) * LANES)
            total = conv_total(pre, which, HALO, count, lanes, conv, valid)
            value = total * sigmoid(total)
            if which < 2:
                value = value * lax.rsqrt(jnp.sum(value * value, -1, keepdims=True) + KEY_EPS)
            if which == 1:
                value = value * live[...]
            feature_out[which, :, lanes] = value


def conv_total(pre, which, first, count, lanes, conv, valid):
    taps = conv.shape[1]
    total = None
    for tap in range(taps):
        start = first - (taps - 1) + tap
        term = conv[which, tap : tap + 1, lanes] * pre[which, start : start + count, lanes]
        if tap < taps - 1:
            term = term * valid[tap]
        total = term if total is None else total + term
    return total


def project(tokens, halo, gain, position, live, query_w, key_w, value_w, gate_w, beta_w, conv):
    count, width = tokens.shape
    heads = beta_w.shape[0]
    block = 2 * LANES
    whole = lambda shape: pl.BlockSpec(shape, lambda j: (0,) * len(shape))
    weight = pl.BlockSpec((width, block), lambda j: (0, j))
    f32 = lambda shape: jax.ShapeDtypeStruct(shape, jnp.float32)
    return pl.pallas_call(
        project_kernel,
        grid=(width // block,),
        in_specs=[
            whole((count, width)), whole((HALO, width)), whole((1, width)), whole((count, 1)),
            whole((count, 1)), weight, weight, weight, weight, whole((heads, width)),
            pl.BlockSpec((3, conv.shape[1], block), lambda j: (0, 0, j)),
        ],
        out_specs=[
            whole((width, count)),
            pl.BlockSpec((3, count // SPAN, SPAN + 8, block), lambda j: (0, 0, 0, j)),
            pl.BlockSpec((3, count, block), lambda j: (0, 0, j)),
            pl.BlockSpec((count, block), lambda j: (0, j)),
            whole((count, heads)), whole((count, heads)),
        ],
        out_shape=[
            f32((width, count)), f32((3, count // SPAN, SPAN + 8, width)), f32((3, count, width)),
            f32((count, width)), f32((count, heads)), f32((count, heads)),
        ],
        scratch_shapes=[
            pltpu.VMEM((HALO + count, width), LOW),
            pltpu.VMEM((3, HALO + count, block), jnp.float32),
        ],
        compiler_params=params(),
        cost_estimate=cost(8 * count * width * width, 8 * width * width + 40 * count * width),
        name="project",
    )(tokens, halo, gain, position, live, query_w, key_w, value_w, gate_w, beta_w, conv)


def prepare_kernel(keep, features, beta, solved_out, inverse_out, attend_out, state):
    span = pl.program_id(0)
    heads = state.shape[0]
    size = state.shape[1]
    strict, inclusive, upper, identity = masks(2 * SPAN)

    @pl.when(span == 0)
    def _():
        i = lax.broadcasted_iota(jnp.int32, (size, 2 * size), 0)
        j = lax.broadcasted_iota(jnp.int32, (size, 2 * size), 1)
        for h in range(heads):
            state[h] = jnp.where(j == i + size, 1.0, 0.0)

    query, key, value = features[0], features[1], features[2]
    betas = beta[...]
    flag = keep[span]
    pairs = range(heads // 2)
    keys = [split(pair(key, p)) for p in pairs]
    columns = [pair_column(betas, p) for p in pairs]
    scores = [product_t(stack(keys[p], split(pair(query, p))), keys[p]) for p in pairs]
    solved = inverses_of([columns[p] * scores[p][: 2 * SPAN] * strict for p in pairs], identity)
    both = [
        product(
            solved[p],
            jnp.concatenate([columns[p] * pair(key, p), columns[p] * pair(value, p)], 1),
        )
        for p in pairs
    ]
    for p in pairs:
        inverse_out[0, p] = solved[p]
        attend_out[0, p] = scores[p][2 * SPAN :] * inclusive
    starts, news = [], []
    for h in range(heads):
        rows = slice(h % 2 * SPAN, (h % 2 + 1) * SPAN)
        erase, update = both[h // 2][rows, :size], both[h // 2][rows, size:]
        solved_out[0, :, h * size : (h + 1) * size] = erase
        solved_out[1, :, h * size : (h + 1) * size] = update
        start = state[h] * flag
        starts.append(start)
        news.append(
            jnp.concatenate([update, jnp.zeros_like(update)], 1) - product(erase, start)
        )
    for h in range(heads):
        rows = slice(h % 2 * SPAN, (h % 2 + 1) * SPAN)
        state[h] = starts[h] + t_product(tuple(k[rows] for k in keys[h // 2]), news[h])


def prepare(keep, features, beta):
    _, count, width = features.shape
    heads = beta.shape[1]
    size = width // heads
    spans = count // SPAN
    f32 = lambda shape: jax.ShapeDtypeStruct(shape, jnp.float32)
    matrix = pl.BlockSpec((1, heads // 2, 2 * SPAN, 2 * SPAN), lambda c: (c, 0, 0, 0))
    return pl.pallas_call(
        prepare_kernel,
        grid=(spans,),
        in_specs=[
            pl.BlockSpec(memory_space=pltpu.SMEM),
            pl.BlockSpec((3, SPAN, width), lambda c: (0, c, 0)),
            pl.BlockSpec((SPAN, heads), lambda c: (c, 0)),
        ],
        out_specs=[
            pl.BlockSpec((2, SPAN, width), lambda c: (0, c, 0)), matrix, matrix,
            pl.BlockSpec((heads, size, 2 * size), lambda c: (0, 0, 0)),
        ],
        out_shape=[
            f32((2, count, width)), f32((spans, heads // 2, 2 * SPAN, 2 * SPAN)),
            f32((spans, heads // 2, 2 * SPAN, 2 * SPAN)), f32((heads, size, 2 * size)),
        ],
        compiler_params=params(),
        cost_estimate=cost(40 * count * width * size * 4, 60 * count * width),
        name="prepare",
    )(keep, features, beta)


def mix_kernel(
    keep, place, features, solved, attend, gate, gain, state_mine, state_other, starts_out, new_out,
    mixed_out, normed_out, state,
):
    span = pl.program_id(0)
    heads = state.shape[0]

    @pl.when(span == 0)
    def _():
        half = heads // 2
        first = place[0] == 0
        state[:half] = jnp.where(first, state_mine[...], state_other[...])
        state[half:] = jnp.where(first, state_other[...], state_mine[...])

    query, key = features[0], features[1]
    erase, update = solved[0], solved[1]
    flag = keep[span]
    every, pairs = range(heads), range(heads // 2)
    starts = [state[h] * flag for h in every]
    both = [
        product(jnp.concatenate([head(erase, h), head(query, h)], 0), starts[h]) for h in every
    ]
    news = [split(head(update, h) - both[h][:SPAN]) for h in every]
    after = [starts[h] + t_product(head(key, h), news[h]) for h in every]
    inner = [product(attend[0, p], stack(news[2 * p], news[2 * p + 1])) for p in pairs]
    for h in every:
        lanes = slice(h * LANES, (h + 1) * LANES)
        starts_out[0, h] = starts[h]
        state[h] = after[h]
        new_out[:, lanes] = head(update, h) - both[h][:SPAN]
        rows = both[h][SPAN:] + inner[h // 2][h % 2 * SPAN : (h % 2 + 1) * SPAN]
        mixed_out[:, lanes] = rows
        shaped = rows * lax.rsqrt(jnp.mean(rows * rows, -1, keepdims=True) + EPS) * gain[...]
        gates = gate[:, lanes]
        normed_out[:, lanes] = (shaped * (gates * sigmoid(gates))).astype(LOW)


def mix(keep, place, features, solved, attend, gate, gain, state_mine, state_other):
    _, count, width = features.shape
    half, size, _ = state_mine.shape
    heads = 2 * half
    spans = count // SPAN
    f32 = lambda shape: jax.ShapeDtypeStruct(shape, jnp.float32)
    rows = pl.BlockSpec((SPAN, width), lambda c: (c, 0))
    pairs = pl.BlockSpec((2, SPAN, width), lambda c: (0, c, 0))
    return pl.pallas_call(
        mix_kernel,
        grid=(spans,),
        in_specs=[
            pl.BlockSpec(memory_space=pltpu.SMEM), pl.BlockSpec(memory_space=pltpu.SMEM), pairs, pairs,
            pl.BlockSpec((1, heads // 2, 2 * SPAN, 2 * SPAN), lambda c: (c, 0, 0, 0)),
            rows, pl.BlockSpec((1, size), lambda c: (0, 0)),
            pl.BlockSpec((half, size, size), lambda c: (0, 0, 0)),
            pl.BlockSpec((half, size, size), lambda c: (0, 0, 0)),
        ],
        out_specs=[
            pl.BlockSpec((1, heads, size, size), lambda c: (c, 0, 0, 0)), rows, rows, rows,
        ],
        out_shape=[
            f32((spans, heads, size, size)), f32((count, width)), f32((count, width)),
            jax.ShapeDtypeStruct((count, width), LOW),
        ],
        scratch_shapes=[pltpu.VMEM((heads, size, size), jnp.float32)],
        compiler_params=params(),
        cost_estimate=cost(8 * count * width * size * 4, 40 * count * width),
        name="mix",
    )(keep, place, features, solved, attend, gate, gain, state_mine, state_other)


def feed_kernel(
    core, tokens, normed_head, grad_top, second_gain, out_w, gate_w, up_w, down_w,
    block_out, normed_out, inner_out, kept_out, sent_out, grad_hidden_out, branch_out, grad_head_out,
    gain_grad_out, head_turned_out, hidden, normed, total, grad_total,
):
    step = pl.program_id(0)

    @pl.when(step == 0)
    def _():
        state = tokens[...].astype(jnp.float32) + mxu(normed_head[...], out_w[...], NN)
        hidden[...] = state
        rounded = (
            state * lax.rsqrt(jnp.mean(state * state, -1, keepdims=True) + EPS) * second_gain[...]
        ).astype(LOW)
        normed[...] = rounded
        normed_out[...] = rounded.astype(jnp.float32).T
        head_turned_out[...] = normed_head[...].astype(jnp.float32).T

    @pl.when(step == 0)
    def _():
        total[...] = jnp.zeros_like(total)
        grad_total[...] = jnp.zeros_like(grad_total)

    first = core[0] == 0
    size = normed.shape[0] // 1
    parts = [slice(i * size, (i + 1) * size) for i in range(1)]
    gates = [mxu(normed[part, :], gate_w[...], NN) for part in parts]
    ups = [mxu(normed[part, :], up_w[...], NN) for part in parts]
    grad_inners = [mxu(grad_top[part, :], down_w[...], NT) for part in parts]
    for part, gate, up, grad_inner in zip(parts, gates, ups, grad_inners):
        sigma = sigmoid(gate)
        act = gate * sigma
        inner = (act * up).astype(LOW)
        inner_out[:, part] = inner.astype(jnp.float32).T
        wide_gate = grad_inner * up * (sigma + act * (1.0 - sigma))
        wide_up = grad_inner * act
        grad_gate, grad_up = wide_gate.astype(LOW), wide_up.astype(LOW)
        kept_out[part, :] = jnp.where(first, wide_gate, wide_up).astype(LOW)
        sent_out[part, :] = jnp.where(first, wide_up, wide_gate).astype(LOW).astype(jnp.float32)
        total[part, :] += mxu(inner, down_w[...], NN)
        grad_total[part, :] += mxu(grad_gate, gate_w[...], NT) + mxu(grad_up, up_w[...], NT)

    @pl.when(step == pl.num_programs(0) - 1)
    def _():
        state = hidden[...]
        block_out[...] = (state + total[...]).astype(LOW)
        part, gain_part = norm_back(state, second_gain[...], grad_total[...])
        gain_grad_out[...] = gain_part
        grad_hidden = grad_top[...].astype(jnp.float32) + part
        grad_hidden_out[...] = grad_hidden
        branch = grad_hidden.astype(LOW)
        branch_out[...] = branch.astype(jnp.float32)
        grad_head_out[...] = mxu(branch, out_w[...], NT)


def norm_back(value, gain, grad):
    scale = lax.rsqrt(jnp.mean(value * value, -1, keepdims=True) + EPS)
    unit = value * scale
    gain_grad = jnp.sum(grad * unit, 0, keepdims=True)
    inward = grad * gain
    return scale * (inward - unit * jnp.mean(inward * unit, -1, keepdims=True)), gain_grad


def feed(core, tokens, normed_head, grad_top, second_gain, out_w, gate_w, up_w, down_w):
    count, width = tokens.shape
    hidden = gate_w.shape[1]
    block = 2 * LANES
    whole = lambda shape: pl.BlockSpec(shape, lambda j: (0,) * len(shape))
    f32 = lambda shape: jax.ShapeDtypeStruct(shape, jnp.float32)
    low = lambda shape: jax.ShapeDtypeStruct(shape, LOW)
    rows = whole((count, width))
    columns = pl.BlockSpec((count, block), lambda j: (0, j))
    return pl.pallas_call(
        feed_kernel,
        grid=(hidden // block,),
        in_specs=[
            pl.BlockSpec(memory_space=pltpu.SMEM), rows, rows, rows, whole((1, width)),
            whole((width, width)), pl.BlockSpec((width, block), lambda j: (0, j)),
            pl.BlockSpec((width, block), lambda j: (0, j)),
            pl.BlockSpec((block, width), lambda j: (j, 0)),
        ],
        out_specs=[
            rows, whole((width, count)), pl.BlockSpec((block, count), lambda j: (j, 0)), columns,
            columns, rows, rows, rows, whole((1, width)), whole((width, count)),
        ],
        out_shape=[
            low((count, width)), f32((width, count)), f32((hidden, count)), low((count, hidden)),
            f32((count, hidden)), f32((count, width)), f32((count, width)), f32((count, width)),
            f32((1, width)), f32((width, count)),
        ],
        scratch_shapes=[
            pltpu.VMEM((count, width), jnp.float32), pltpu.VMEM((count, width), LOW),
            pltpu.VMEM((count, width), jnp.float32), pltpu.VMEM((count, width), jnp.float32),
        ],
        compiler_params=params(),
        cost_estimate=cost(
            12 * count * width * hidden + 4 * count * width * width,
            6 * width * hidden + 10 * count * hidden + 30 * count * width,
        ),
        name="feed",
    )(core, tokens, normed_head, grad_top, second_gain, out_w, gate_w, up_w, down_w)


def gather_kernel(
    keep, core, grad_head, grad_branch, mixed, gate, gain, features, solved, grad_mixed_out,
    grad_gate_out, kept_out, sent_out, gain_out, state,
):
    step = pl.program_id(0)
    span = pl.num_programs(0) - 1 - step
    heads = state.shape[0]
    strict, inclusive, upper, identity = masks(2 * SPAN)

    @pl.when(step == 0)
    def _():
        state[...] = jnp.zeros_like(state)
        gain_out[...] = jnp.zeros_like(gain_out)

    query, key = features[0], features[1]
    erase = solved[0]
    flag = keep[span]
    gain_total = jnp.zeros_like(gain_out[...])
    every, pairs = range(heads), range(heads // 2)
    passes = [product_t(pair(key, p), pair(query, p)) * upper for p in pairs]
    grads = []
    for h in every:
        lanes = slice(h * LANES, (h + 1) * LANES)
        gates = gate[:, lanes]
        sigma = sigmoid(gates)
        rows = mixed[:, lanes]
        grad = grad_head[:, lanes]
        scale = lax.rsqrt(jnp.mean(rows * rows, -1, keepdims=True) + EPS)
        unit = rows * scale
        grad_gate = grad * unit * gain[...] * sigma * (1.0 + gates * (1.0 - sigma))
        grad_gate = grad_gate.astype(LOW).astype(jnp.float32)
        grad_gate_out[:, lanes] = grad_gate
        shaped = grad * gates * sigma
        gain_total = gain_total + jnp.sum(shaped * unit, 0, keepdims=True)
        inward = shaped * gain[...]
        grad_rows = scale * (inward - unit * jnp.mean(inward * unit, -1, keepdims=True))
        grad_mixed_out[:, lanes] = grad_rows
        grads.append(split(grad_rows))
    passed = [product(passes[p], stack(grads[2 * p], grads[2 * p + 1])) for p in pairs]
    ends = [state[h] for h in every]
    grad_new = [
        passed[h // 2][h % 2 * SPAN : (h % 2 + 1) * SPAN] + product(head(key, h), ends[h])
        for h in every
    ]
    for h in every:
        state[h] = flag * (
            ends[h]
            + t_product(
                jnp.concatenate([head(query, h), -head(erase, h)], 0),
                stack(grads[h], split(grad_new[h])),
            )
        )
    gain_out[...] += gain_total
    half = grad_branch.shape[1] // 2
    first = core[0] == 0
    for place, source in ((0, grad_branch), (half, grad_gate_out)):
        low, high = source[:, :half], source[:, half:]
        kept_out[:, place : place + half] = jnp.where(first, low, high).astype(LOW)
        sent_out[:, place : place + half] = jnp.where(first, high, low)


def gather_states(
    keep, core, grad_head, grad_branch, mixed, gate, gain, features, solved, heads
):
    _, count, width = features.shape
    size = width // heads
    spans = count // SPAN
    f32 = lambda shape: jax.ShapeDtypeStruct(shape, jnp.float32)
    rows = pl.BlockSpec((SPAN, width), lambda c: (spans - 1 - c, 0))
    pairs = pl.BlockSpec((2, SPAN, width), lambda c: (0, spans - 1 - c, 0))
    one = pl.BlockSpec((1, SPAN, width), lambda c: (0, spans - 1 - c, 0))
    return pl.pallas_call(
        gather_kernel,
        grid=(spans,),
        in_specs=[
            pl.BlockSpec(memory_space=pltpu.SMEM), pl.BlockSpec(memory_space=pltpu.SMEM), rows, rows,
            rows, rows, pl.BlockSpec((1, size), lambda c: (0, 0)), pairs, one,
        ],
        out_specs=[
            rows, rows, rows, rows, pl.BlockSpec((1, size), lambda c: (0, 0)),
            pl.BlockSpec((heads, size, size), lambda c: (0, 0, 0)),
        ],
        out_shape=[
            f32((count, width)), f32((count, width)), jax.ShapeDtypeStruct((count, width), LOW),
            f32((count, width)), f32((1, size)), f32((heads, size, size)),
        ],
        compiler_params=params(),
        cost_estimate=cost(8 * count * width * size * 4, 32 * count * width),
        name="gather_states",
    )(keep, core, grad_head, grad_branch, mixed, gate, gain, features, solved)


def back_kernel(
    keep, place, features, beta, beta_pre, solved, inverses, starts, news, grad_mixed, state_mine,
    state_other, pre, conv, position, live, grad_pre_out, borrowed_out, conv_out, grad_beta_out, state, later, sums,
):
    step = pl.program_id(0)
    span = pl.num_programs(0) - 1 - step
    heads = state.shape[0]
    taps = conv.shape[1]
    strict, inclusive, upper, identity = masks(2 * SPAN)

    @pl.when(step == 0)
    def _():
        half = heads // 2
        first = place[0] == 0
        state[:half] = jnp.where(first, state_mine[...], state_other[...])
        state[half:] = jnp.where(first, state_other[...], state_mine[...])
        sums[...] = jnp.zeros_like(sums)
        later[...] = jnp.zeros_like(later)

    query, key, value = features[0], features[1], features[2]
    erase, update = solved[0], solved[1]
    betas = beta[...]
    flag = keep[span]
    base = pl.multiple_of(span * SPAN, SPAN)
    places = position[pl.ds(base, SPAN), :]
    lives = live[pl.ds(base, SPAN), :]
    valid = [
        jnp.broadcast_to(jnp.where(places >= taps - 1 - tap, 1.0, 0.0), (SPAN, LANES))
        for tap in range(taps - 1)
    ]
    every, pairs = range(heads), range(heads // 2)
    part = [slice(h % 2 * SPAN, (h % 2 + 1) * SPAN) for h in every]
    q = [split(pair(query, p)) for p in pairs]
    k = [split(pair(key, p)) for p in pairs]
    b = [pair_column(betas, p) for p in pairs]
    grad_out = [split(pair(grad_mixed, p)) for p in pairs]
    new = [split(pair(news, p)) for p in pairs]
    erases = [split(pair(erase, p)) for p in pairs]
    row = lambda value, h: tuple(v[part[h]] for v in value[h // 2])
    scores = [product_t(k[p], stack(k[p], q[p])) for p in pairs]
    passed = [product(scores[p][:, 2 * SPAN :] * upper, grad_out[p]) for p in pairs]
    ends = [split(state[h]) for h in every]
    begin = [split(starts[0, h]) for h in every]
    grad_new = [passed[h // 2][part[h]] + product(row(k, h), ends[h]) for h in every]
    grad_news = [split(value) for value in grad_new]
    both = [product_t(stack(row(grad_out, h), grad_news[h]), begin[h]) for h in every]
    grad_key = [product_t(row(new, h), ends[h]) for h in every]
    for h in every:
        state[h] = flag * (
            state[h]
            + t_product(
                stack(row(q, h), tuple(-v for v in row(erases, h))),
                stack(row(grad_out, h), grad_news[h]),
            )
        )
    grad_attend = [product_t(grad_out[p], new[p]) * inclusive for p in pairs]
    joined = lambda values, p: jnp.concatenate([values[2 * p], values[2 * p + 1]], 0)
    grad_q = [
        joined([value[:SPAN] for value in both], p) + product(grad_attend[p], k[p]) for p in pairs
    ]
    grad_k = [joined(grad_key, p) + product(grad_attend[p].T, q[p]) for p in pairs]
    turned = [
        product(
            inverses[0, p].T,
            jnp.concatenate(
                [joined(grad_new, p), -joined([value[SPAN:] for value in both], p)], 1
            ),
        )
        for p in pairs
    ]
    grad_bv = [value[:, :LANES] for value in turned]
    grad_bk = [value[:, LANES:] for value in turned]
    grad_lower = [
        -strict * (product_t(grad_bv[p], pair(update, p)) + product_t(grad_bk[p], erases[p]))
        for p in pairs
    ]
    inner = [b[p] * grad_lower[p] for p in pairs]
    grad_k = [
        grad_k[p] + product(inner[p] + inner[p].T, k[p]) + b[p] * grad_bk[p] for p in pairs
    ]
    grad_v = [b[p] * grad_bv[p] for p in pairs]
    beta_columns = []
    for p in pairs:
        grad_b = (
            jnp.sum(grad_lower[p] * scores[p][:, : 2 * SPAN], -1, keepdims=True)
            + jnp.sum(grad_bv[p] * pair(value, p), -1, keepdims=True)
            + jnp.sum(grad_bk[p] * pair(key, p), -1, keepdims=True)
        )
        beta_columns += [grad_b[:SPAN], grad_b[SPAN:]]
    chunks = [(which, h) for which in range(3) for h in every]
    for start in range(0, len(chunks), 4):
        group = chunks[start : start + 4]
        places = [(which, slice(h * LANES, (h + 1) * LANES)) for which, h in group]
        grads = [(grad_q, grad_k, grad_v)[which][h // 2][part[h]] for which, h in group]
        shifted = [
            [
                pre[which, 0, pl.ds(8 - (taps - 1) + tap, SPAN), lanes]
                for tap in range(taps)
            ]
            for which, lanes in places
        ]
        shifted = [
            [value * valid[tap] for tap, value in enumerate(moved[:-1])] + moved[-1:]
            for moved in shifted
        ]
        totals = [
            sum(
                conv[which, tap : tap + 1, lanes] * moved[tap] for tap in range(taps)
            )
            for moved, (which, lanes) in zip(shifted, places)
        ]
        sigmas = [sigmoid(total) for total in totals]
        acts = [total * sigma for total, sigma in zip(totals, sigmas)]
        slopes = [sigma + act * (1.0 - sigma) for sigma, act in zip(sigmas, acts)]
        squares = [
            jnp.sum(act * act, -1, keepdims=True) if which < 2 else None
            for act, (which, _) in zip(acts, group)
        ]
        grads = [
            grad * lives if which == 1 else grad for grad, (which, _) in zip(grads, group)
        ]
        scales = [None if square is None else lax.rsqrt(square + KEY_EPS) for square in squares]
        units = [act if scale is None else act * scale for act, scale in zip(acts, scales)]
        along = [
            None if scale is None else jnp.sum(grad * unit, -1, keepdims=True)
            for grad, unit, scale in zip(grads, units, scales)
        ]
        grads = [
            slope * (grad if scale is None else scale * (grad - unit * dot))
            for slope, grad, scale, unit, dot in zip(slopes, grads, scales, units, along)
        ]
        for grad, moved, (which, lanes) in zip(grads, shifted, places):
            result = conv[which, taps - 1 : taps, lanes] * grad
            for tap in range(taps):
                product_ = grad * moved[tap]
                sums[which, tap, :, lanes] += sum(
                    product_[8 * r : 8 * (r + 1)] for r in range(SPAN // 8)
                )
                if tap < taps - 1:
                    masked = grad * valid[tap]
                    later[which, tap, SPAN:, lanes] = later[which, tap, :8, lanes]
                    later[which, tap, :SPAN, lanes] = masked
                    result = result + conv[which, tap : tap + 1, lanes] * (
                        later[which, tap, pl.ds(taps - 1 - tap, SPAN), lanes]
                    )
            grad_pre_out[which, :, lanes] = result
    columns = lax.broadcasted_iota(jnp.int32, (SPAN, heads), 1)
    grad_beta = jnp.zeros((SPAN, heads), jnp.float32)
    for h in range(heads):
        grad_beta = jnp.where(columns == h, beta_columns[h], grad_beta)
    sigma = sigmoid(beta_pre[...])
    grad_beta_out[...] = (
        (grad_beta * lives * sigma * (1.0 - sigma)).astype(LOW).astype(jnp.float32)
    )

    @pl.when(span == 0)
    def _():
        conv_out[...] = jnp.sum(sums[...], 2)
        for which in range(3):
            result = None
            for tap in range(taps - 1):
                ahead = taps - 1 - tap
                rows = jnp.concatenate([jnp.zeros((8, later.shape[3]), jnp.float32), later[which, tap, :8]], 0)
                term = conv[which, tap : tap + 1, :] * rows[ahead:][:8]
                result = term if result is None else result + term
            borrowed_out[which] = result


def back(
    keep, place, features, beta, beta_pre, solved, inverses, starts, news, grad_mixed, state_mine,
    state_other, pre, conv, position, live,
):
    _, count, width = features.shape
    half, size, _ = state_mine.shape
    heads = 2 * half
    spans = count // SPAN
    taps = conv.shape[1]
    f32 = lambda shape: jax.ShapeDtypeStruct(shape, jnp.float32)
    whole = lambda shape: pl.BlockSpec(shape, lambda c: (0,) * len(shape))
    rows = pl.BlockSpec((SPAN, width), lambda c: (spans - 1 - c, 0))
    triple = pl.BlockSpec((3, SPAN, width), lambda c: (0, spans - 1 - c, 0))
    column = pl.BlockSpec((SPAN, heads), lambda c: (spans - 1 - c, 0))
    return pl.pallas_call(
        back_kernel,
        grid=(spans,),
        in_specs=[
            pl.BlockSpec(memory_space=pltpu.SMEM), pl.BlockSpec(memory_space=pltpu.SMEM), triple, column, column,
            pl.BlockSpec((2, SPAN, width), lambda c: (0, spans - 1 - c, 0)),
            pl.BlockSpec((1, heads // 2, 2 * SPAN, 2 * SPAN), lambda c: (spans - 1 - c, 0, 0, 0)),
            pl.BlockSpec((1, heads, size, size), lambda c: (spans - 1 - c, 0, 0, 0)),
            rows, rows, whole((half, size, size)), whole((half, size, size)),
            pl.BlockSpec((3, 1, SPAN + 8, width), lambda c: (0, spans - 1 - c, 0, 0)),
            whole(conv.shape),
            whole(position.shape), whole(live.shape),
        ],
        out_specs=[triple, whole((3, 8, width)), whole((3, taps, width)), column],
        out_shape=[
            f32((3, count, width)), f32((3, 8, width)), f32((3, taps, width)), f32((count, heads)),
        ],
        scratch_shapes=[
            pltpu.VMEM((heads, size, size), jnp.float32),
            pltpu.VMEM((3, taps - 1, SPAN + 8, width), jnp.float32),
            pltpu.VMEM((3, taps, 8, width), jnp.float32),
        ],
        compiler_params=params(),
        cost_estimate=cost(30 * count * width * size * 4, 60 * count * width),
        name="back",
    )(
        keep, place, features, beta, beta_pre, solved, inverses, starts, news, grad_mixed,
        state_mine, state_other, pre, conv, position, live,
    )


def enter_kernel(
    tokens, gain, grad_hidden, grads, grad_gate, grad_beta, query_w, key_w, value_w, gate_w, beta_w,
    input_grad_out, gain_out, total,
):
    step = pl.program_id(0)
    term = mxu(grad_gate[...].astype(LOW), gate_w[...], NT)
    for which, weight in enumerate((query_w, key_w, value_w)):
        term = term + mxu(grads[which], weight[...], NT)

    @pl.when(step == 0)
    def _():
        total[...] = term + mxu(grad_beta[...].astype(LOW), beta_w[...], NN)

    @pl.when(step > 0)
    def _():
        total[...] += term

    @pl.when(step == pl.num_programs(0) - 1)
    def _():
        part, gain_part = norm_back(tokens[...].astype(jnp.float32), gain[...], total[...])
        gain_out[...] = gain_part
        input_grad_out[...] = (grad_hidden[...] + part).astype(LOW)


def enter(
    tokens, gain, grad_hidden, grads, grad_gate, grad_beta, query_w, key_w, value_w, gate_w, beta_w
):
    count, width = tokens.shape
    heads = beta_w.shape[0]
    block = 2 * LANES
    whole = lambda shape: pl.BlockSpec(shape, lambda j: (0,) * len(shape))
    weight = pl.BlockSpec((width, block), lambda j: (0, j))
    return pl.pallas_call(
        enter_kernel,
        grid=(width // block,),
        in_specs=[
            whole((count, width)), whole((1, width)), whole((count, width)),
            pl.BlockSpec((3, count, block), lambda j: (0, 0, j)),
            pl.BlockSpec((count, block), lambda j: (0, j)), whole((count, heads)),
            weight, weight, weight, weight, whole((heads, width)),
        ],
        out_specs=[whole((count, width)), whole((1, width))],
        out_shape=[
            jax.ShapeDtypeStruct((count, width), LOW), jax.ShapeDtypeStruct((1, width), jnp.float32),
        ],
        scratch_shapes=[pltpu.VMEM((count, width), jnp.float32)],
        compiler_params=params(),
        cost_estimate=cost(8 * count * width * width, 8 * width * width + 20 * count * width),
        name="enter",
    )(
        tokens, gain, grad_hidden, grads, grad_gate, grad_beta, query_w, key_w, value_w, gate_w,
        beta_w,
    )


def passed_along(value, axis, by):
    devices = lax.axis_size(axis)
    pairs = [(i, i + by) for i in range(devices) if 0 <= i + by < devices]
    return lax.ppermute(value, axis, pairs)


def tuned():
    return (lax.axis_size("seq"), lax.axis_size("doc")) == (8, 4)


HOPS = {"core": ("doc", 1), "y": ("doc", 2), "x": ("seq", 1), "near": ("seq", 2), "far": ("seq", 4)}


def hop(value, way, other_way=None):
    if other_way in (None, way):
        axis, bit = HOPS[way]
        return lax.ppermute(value, axis, [(i, i ^ bit) for i in range(lax.axis_size(axis))])
    size = lax.axis_size("doc")
    masks = [bit * size if axis == "seq" else bit for axis, bit in (HOPS[way], HOPS[other_way])]
    pairs = [(i, i ^ masks[i % 2]) for i in range(lax.axis_size("seq") * size)]
    return lax.ppermute(value, ("seq", "doc"), pairs)


def side(way):
    axis, bit = HOPS[way]
    return lax.axis_index(axis) // bit % 2


def apply_kernel(shift, maps, *refs, turned):
    *states, out = refs
    size = maps.shape[1]
    for h in range(maps.shape[0]):
        state = states[0][h]
        for other in states[1:]:
            state = state + other[h]
        moved = (t_product if turned else product)(maps[h, :, size:], state)
        if state.shape[1] == size:
            out[h] = moved + shift[h, :, :size]
        else:
            out[h] = moved + jnp.concatenate([shift[h, :, :size], jnp.zeros((size, size), jnp.float32)], 1)


def apply_map(shift, maps, *states, turned=False):
    return pl.pallas_call(
        lambda *refs: apply_kernel(*refs, turned=turned),
        out_shape=jax.ShapeDtypeStruct(states[0].shape, jnp.float32),
        compiler_params=params(4),
        cost_estimate=cost(0, 0),
        name="apply_map",
    )(shift, maps, *states)


def ends_kernel(here, shift, maps, state, come, stay_out, send_out, *, turned):
    size = maps.shape[1]
    mine = here[0] == 0
    for h in range(maps.shape[0]):
        near = state[h] + come[h]
        far = (t_product if turned else product)(maps[h, :, size:], near) + shift[h, :, :size]
        if turned:
            near, far = far, near
        stay_out[h] = jnp.where(mine, near, far)
        send_out[h] = jnp.where(mine, far, near)


def pair_ends(here, shift, maps, state, come, turned=False):
    shape = jax.ShapeDtypeStruct(state.shape, jnp.float32)
    vmem = pl.BlockSpec(memory_space=pltpu.VMEM)
    return pl.pallas_call(
        lambda *refs: ends_kernel(*refs, turned=turned),
        in_specs=[pl.BlockSpec(memory_space=pltpu.SMEM)] + [vmem] * 4,
        out_specs=[vmem, vmem],
        out_shape=[shape, shape],
        compiler_params=params(4),
        cost_estimate=cost(0, 0),
        name="pair_ends",
    )(here, shift, maps, state, come)


def together(value, *others):
    return lax.optimization_barrier((value, *others))


def carried_forward(maps, beside):
    heads, size, _ = maps.shape
    half = heads // 2
    if not tuned():
        gathered = lax.all_gather(maps, "seq")

        def one(lap, state):
            each = lax.dynamic_index_in_dim(gathered, lap, 0, False)
            return apply_map(each, each, state)

        state = lax.fori_loop(
            0, lax.axis_index("seq"), one, jnp.zeros((heads, size, size), jnp.float32)
        )
        return state[:half], state[half:], jnp.zeros((1,), jnp.int32), (maps,)
    place = side("x").astype(jnp.int32).reshape(1)
    here = place[0] == 0
    kept = jnp.where(here, maps[:half], maps[half:])
    other = hop(jnp.where(here, maps[half:], maps[:half]), "x")
    other, *beside = together(other, *beside)
    first, second = jnp.where(here, kept, other), jnp.where(here, other, kept)
    pair_map = apply_map(second, second, first)
    state = jnp.zeros((half, size, size), jnp.float32)
    come = state
    for step in range(3):
        if step == 0:
            sent = pair_map[:, :, :size]
        else:
            sent = apply_map(pair_map, pair_map, state, come)
            state = state + come
        come = lax.ppermute(sent, "seq", [(2 * step + x, 2 * step + 2 + x) for x in range(2)])
    mine, send = pair_ends(place, first, first, state, come)
    return mine, hop(send, "x"), place, (first, second, pair_map), *beside


def carried_back(shift, context, beside=None):
    heads, size, _ = shift.shape
    half = heads // 2
    if not tuned():
        gathered = lax.all_gather(jnp.concatenate([shift, context[0][:, :, size:]], 2), "seq")
        count = lax.axis_size("seq")

        def one(lap, state):
            each = lax.dynamic_index_in_dim(gathered, count - 1 - lap, 0, False)
            return apply_map(each, each, state, turned=True)

        zeros = jnp.zeros((heads, size, size), jnp.float32)
        state = lax.fori_loop(0, count - 1 - lax.axis_index("seq"), one, zeros)
        return state[:half], state[half:], ()
    first, second, pair_map = context
    place = side("x").astype(jnp.int32).reshape(1)
    here = place[0] == 0
    done = []

    def step_with(number, sent, go):
        moves, work = beside[number]
        sent, *values = together(sent, *[move[0] for move in moves])
        come, *rest = together(
            go(sent), *[hop(value, *move[1:]) for value, move in zip(values, moves)], *work
        )
        done.append(rest)
        return come

    kept = jnp.where(here, shift[:half], shift[half:])
    other = step_with(0, jnp.where(here, shift[half:], shift[:half]), lambda value: hop(value, "x"))
    first_shift, second_shift = jnp.where(here, kept, other), jnp.where(here, other, kept)
    pair_shift = apply_map(first_shift, first, second_shift, turned=True)
    state = jnp.zeros((half, size, size), jnp.float32)
    come = state
    for step in range(3, 0, -1):
        if step == 3:
            sent = pair_shift
        else:
            sent = apply_map(pair_shift, pair_map, state, come, turned=True)
            state = state + come
        pairs = [(2 * step + x, 2 * step - 2 + x) for x in range(2)]
        come = step_with(4 - step, sent, lambda value: lax.ppermute(value, "seq", pairs))
    mine, send = pair_ends(place, second_shift, second, state, come, turned=True)
    return mine, step_with(4, send, lambda value: hop(value, "x")), done


def outer_kernel(table, *refs, blocks, pieces):
    count = len(blocks)
    lefts, rights = refs[: 2 * count], refs[2 * count : 4 * count]
    *outs, stacked = refs[4 * count :]
    step = pl.program_id(0)
    tokens = lefts[0].shape[1]
    size = outs[0].shape[0] // 8

    @pl.when(step == 0)
    def _():
        for piece in range(count):
            for which in range(2):
                for place in range(16):
                    rows = pl.ds(pl.multiple_of(table[place] * size, 16), size)
                    stacked[
                        piece, place * size : (place + 1) * size, which * tokens : (which + 1) * tokens
                    ] = lefts[2 * piece + which][rows, :].astype(LOW)

    for piece in range(count):
        low = sum(blocks[:piece])

        @pl.when((step >= low) & (step < low + blocks[piece]))
        def _(piece=piece):
            right = jnp.concatenate(
                [rights[2 * piece][...].astype(LOW), rights[2 * piece + 1][...].astype(LOW)], 0
            )
            place = 0
            for out, number in zip(outs, (8 * size, *pieces)):
                out[...] = mxu(stacked[piece, place : place + number, :], right, NN)
                place += number


WEIGHTS = {"far": 8, "near": 4, "x": 2, "y": 1}


def by_core(values):
    return jnp.where(side("core") == 0, values[0], values[1])


def outer(pieces, orders, parts=(1,)):
    rows, tokens = pieces[0][0].shape
    block = 2 * LANES
    table = []
    for place in range(16):
        entries = []
        for order in orders:
            bits = [place >> 3 & 1, place >> 2 & 1, place >> 1 & 1, place & 1]
            first = side(order[0]) ^ bits[0]
            rest = sum(bit * WEIGHTS[way] for bit, way in zip(bits[1:], order[1:]))
            entries.append(first * WEIGHTS[order[0]] + rest)
        table.append(by_core(entries))
    table = jnp.stack(table).astype(jnp.int32)
    counts = [piece[5] for piece in pieces]
    left = pl.BlockSpec((rows, tokens), lambda j: (0, 0), pipeline_mode=pl.Buffered(1))
    lefts, rights, specs = [], [], []
    for index, piece in enumerate(pieces):
        lefts += piece[:2]
        rights += piece[2:4]

        def place(j, low=sum(counts[:index]), first=piece[4], number=piece[5]):
            return 0, first + jnp.clip(j - low, 0, number - 1)

        specs += [pl.BlockSpec((tokens, block), place)] * 2
    total = sum(counts)
    sizes = [rows // 2 * part // sum(parts) // 16 * 16 for part in parts[:-1]]
    sizes = [*sizes, rows // 2 - sum(sizes)]
    outs = [rows // 2, *sizes]
    keep, *sends = pl.pallas_call(
        lambda *refs: outer_kernel(*refs, blocks=counts, pieces=sizes),
        grid=(total,),
        in_specs=[pl.BlockSpec(memory_space=pltpu.SMEM)] + [left] * len(lefts) + specs,
        out_specs=[pl.BlockSpec((size, block), lambda j: (0, j)) for size in outs],
        out_shape=[jax.ShapeDtypeStruct((size, total * block), jnp.float32) for size in outs],
        scratch_shapes=[pltpu.VMEM((len(pieces), rows, 2 * tokens), LOW)],
        compiler_params=params(),
        cost_estimate=cost(0, 0),
        name="outer",
    )(table, *lefts, *rights)
    return keep, sends


def take(value, place, axis):
    return lax.dynamic_index_in_dim(value, place, axis, False)


class Part:
    def __init__(self, keeps, comes, orders, split_y=True):
        self.orders, self.split_y, self.stage = orders, split_y, 1
        self.groups = [[self.shaped(value) for value in group] for group in zip(keeps, comes)]
        self.terms = []

    def shaped(self, value):
        left = tuple(range(self.stage, len(self.orders[0])))
        columns = value.shape[-1]
        rows = value.size // columns // 2 ** len(left)
        return value.reshape((2,) * len(left) + (rows, columns)), left

    def add(self, come):
        self.terms.append(self.shaped(come))

    def place(self, stage):
        return by_core([side(order[stage]) for order in self.orders])

    def chosen(self, here):
        sums = [self.added(group, here) for group in self.groups]
        total = sums[0] if len(sums) == 1 else jnp.concatenate(sums, -1)
        return total + self.added(self.terms, here) if self.terms else total

    def added(self, terms, here):
        total = None
        for value, left in terms:
            starts, sizes = [], []
            for stage in left:
                fixed = stage <= self.stage
                place = self.place(stage) if fixed else 0
                starts.append(1 - place if stage == self.stage and not here else place)
                sizes.append(1 if fixed else 2)
            sizes += value.shape[len(left) :]
            starts = [jnp.asarray(start, jnp.int32) for start in [*starts, 0, 0]]
            piece = lax.dynamic_slice(value, starts, sizes)
            piece = piece.reshape([size for size in sizes[:-2] if size > 1] + sizes[-2:])
            total = piece if total is None else total + piece
        return total

    def move(self):
        if self.stage < len(self.orders[0]):
            send = self.chosen(False)
            ways = [order[self.stage] for order in self.orders]
            self.stage += 1
            self.absorb = self.add
            return send, *ways
        if self.stage == len(self.orders[0]):
            mine = self.chosen(True)
            self.stage += 1

            def absorb(come):
                self.done = in_order(mine, come) if self.split_y else mine + come

            self.absorb = absorb
            return mine, "y"
        self.absorb = lambda come: setattr(self, "other", come)
        return self.done, "core"


def in_order(mine, come):
    first = side("y") == 0
    return jnp.concatenate([jnp.where(first, mine, come), jnp.where(first, come, mine)], 0)


def advance(parts, extra=(), beside=()):
    moves = [part.move() for part in parts] + list(extra)
    values = together(*[move[0] for move in moves])
    comes = [hop(value, *move[1:]) for value, move in zip(values, moves)]
    done = together(*comes, *beside)
    for part, come in zip(parts, done):
        part.absorb(come)
    done = done[len(parts) :]
    return done[: len(extra)], done[len(extra) :]


def flatten_small(small):
    first_gain, beta, conv, head_gain, second_gain = small
    seq = lax.axis_size("seq")
    flat = jnp.concatenate(
        [
            first_gain.reshape(seq, -1), beta.reshape(seq, -1),
            conv.reshape(conv.shape[0] * conv.shape[1], seq, -1).transpose(1, 0, 2).reshape(seq, -1),
            head_gain.reshape(seq, -1), second_gain.reshape(seq, -1),
        ],
        1,
    )
    size = flat.shape[1]
    rows = -(-size // 2048) * 16
    return jnp.pad(flat, ((0, 0), (0, rows * 128 - size))).reshape(seq * rows, 128)


def unflatten_small(flat, small):
    first_gain, beta, conv, head_gain, second_gain = small
    seq = lax.axis_size("seq")
    flat = flat.reshape(-1)
    sizes = [a.size // seq for a in small]
    places = [sum(sizes[:i]) for i in range(len(sizes))]
    pieces = [flat[p : p + s] for p, s in zip(places, sizes)]
    return (
        pieces[0], pieces[1].reshape(-1, beta.shape[1]),
        pieces[2].reshape(conv.shape[0], conv.shape[1], -1), pieces[3], pieces[4],
    )


def outer_sum(left, right):
    return mxu(left.astype(LOW), right.astype(LOW), TN)


def local(
    tokens,
    doc_lengths,
    out_grad,
    first_gain,
    query_weight,
    key_weight,
    value_weight,
    gate_weight,
    beta_weight,
    conv_weight,
    head_gain,
    out_weight,
    second_gain,
    hidden_gate,
    hidden_up,
    hidden_down,
):
    count, width = (tokens.shape[1], tokens.shape[2])
    heads = beta_weight.shape[1]
    reach = conv_weight.shape[1] - 1
    first = lax.axis_index("seq") * count
    position, live = doc_info(doc_lengths[0], first, count)
    keep = 1.0 - (position[::CK] == 0).astype(jnp.float32)
    position, live = position[:, None], live[:, None]
    core = (lax.axis_index("doc") % 2).astype(jnp.int32).reshape(1)
    here = core[0] == 0
    rows, top = tokens[0], out_grad[0]
    halo = passed_along(rows[count - HALO :].astype(jnp.float32), "seq", 1)
    normed_one, pre, features, gate_pre, beta_pre, beta = project(
        rows, halo, first_gain[None], position, live, query_weight, key_weight, value_weight,
        gate_weight, beta_weight.T, conv_weight,
    )
    solved, inverses, attend, maps = prepare(keep, features, beta)
    if tuned():
        half = width // 2
        units = half // 256

        def pick(zero, one):
            return jnp.where(here, zero, one)

        def both(value, send=None):
            return value, hop(value if send is None else send, "core")

        wide_top = top.astype(jnp.float32)
        tops = both(
            pick(top[:, :half], top[:, half:]), pick(wide_top[:, half:], wide_top[:, :half])
        )
        one = both(normed_one)
    state_mine, state_other, place, context, *beside = carried_forward(
        maps, (*tops, *one) if tuned() else ()
    )
    if tuned():
        tops, one = beside[:2], beside[2:]
    starts, news, mixed, normed_head = mix(
        keep, place, features, solved, attend, gate_pre, head_gain[None], state_mine, state_other
    )
    (
        block_out, two_turned, inner_turned, kept, sent, grad_hidden, grad_branch, grad_head,
        grad_second_gain, head_turned,
    ) = feed(
        core, rows, normed_head, top, second_gain[None], out_weight, hidden_gate, hidden_up,
        hidden_down,
    )
    if tuned():
        heads_turned = both(head_turned)
        two = both(two_turned)
        gate_up = both(kept, sent)
    grad_mixed, grad_gate_pre, out_kept, out_sent, grad_head_gain, shift = gather_states(
        keep, core, grad_head, grad_branch, mixed, gate_pre, head_gain[None], features, solved, heads
    )
    if tuned():
        out_right = both(out_kept, out_sent)
        blocks = hidden_gate.shape[1] // 256
        some = blocks * 3 // 11
        blocks = hidden_gate.shape[1] // 256
        low = blocks * 8 // 11
        orders = ("x", "y", "near", "far"), ("y", "x", "far", "near")
        down_orders = ("near", "x", "y", "far"), ("near", "y", "x", "far")
        firsts = [order[0] for order in orders]
        shift, two_other, gate_up_other, inner_turned = together(
            shift, two[1], gate_up[1], inner_turned
        )
        inners = both(inner_turned)
        two, gate_up = (two[0], two_other), (gate_up[0], gate_up_other)
        out_right = both(out_kept, out_sent)
        wide_keep, wide_sends = outer([(*two, *gate_up, 0, low)], orders, (9, 9, 9, 5))
        down_keep, down_sends = outer([(*inners, *tops, 0, units)], down_orders, (3, 4))
        rest_keep, rest_sends = outer(
            [
                (*two, *gate_up, low, blocks - low), (*heads_turned, *out_right, 0, units),
                (*one, *out_right, units, units),
            ],
            orders,
        )
        work = [
            (wide_keep, *wide_sends), (down_keep, *down_sends), (rest_keep, *rest_sends), (), (),
        ]
        moves = [(), *([(send, *firsts)] for send in wide_sends)]
        grad_mine, grad_other, done = carried_back(shift, context, list(zip(moves, work)))
        down_keep, *down_sends = done[1][1:]
        rest_keep, *rest_sends = done[2][1:]
        wide_come = jnp.concatenate([value[0] for value in done[1:]], 0)
        moves = [(rest_sends[0], *firsts), (down_sends[0], "near")]
        grad_other, *values = together(grad_other, *[move[0] for move in moves])
        comes = [hop(value, *move[1:]) for value, move in zip(values, moves)]
    else:
        grad_mine, grad_other, _ = carried_back(shift, context)
    grads, borrowed, grad_conv, grad_beta_pre = back(
        keep, place, features, beta, beta_pre, solved, inverses, starts, news, grad_mixed, grad_mine,
        grad_other, pre, conv_weight, position, live,
    )
    if tuned():
        borrowed, *comes = together(borrowed, *comes)
        wide_part = Part((wide_keep, rest_keep), (wide_come, comes[0]), orders)
        down_come = comes[1]
    returned = passed_along(borrowed, "seq", -1)
    tail = grads[:, count - 8 :] + returned
    grads = lax.dynamic_update_slice(grads, tail, (0, count - 8, 0))
    grads = grads.astype(LOW)
    if tuned():
        moves = [wide_part.move(), (down_sends[1], "near")]
        grads, *values = together(grads, *[move[0] for move in moves])
        comes = [hop(value, *move[1:]) for value, move in zip(values, moves)]
        wide = grads.astype(jnp.float32)
        query_key = both(pick(grads[0], grads[1]), pick(wide[1], wide[0]))
        value = both(
            pick(grads[2, :, :half], grads[2, :, half:]), pick(wide[2, :, half:], wide[2, :, :half])
        )
        late_keep, (late_send,) = outer(
            [(*one, *query_key, 0, 2 * units), (*one, *value, 0, units)], orders
        )
        grads, late_send, *comes = together(grads, late_send, *comes)
        wide_part.absorb(comes[0])
        down = Part((down_keep,), (jnp.concatenate([down_come, comes[1]], 0),), down_orders)
        input_grad, grad_first_gain = enter(
            rows, first_gain[None], grad_hidden, grads, grad_gate_pre, grad_beta_pre, query_weight,
            key_weight, value_weight, gate_weight, beta_weight.T,
        )
        small = (
            grad_first_gain[0], outer_sum(normed_one.T, grad_beta_pre), grad_conv, grad_head_gain[0],
            grad_second_gain[0],
        )
        flat = flatten_small(small)
        (come,), (flat, input_grad) = advance(
            [wide_part, down], [(late_send, *firsts)], (flat, input_grad)
        )
        late = Part((late_keep,), (come,), orders)
        (come,), _ = advance([late, wide_part, down], [(flat, "core")])
        flat = (flat + come).reshape(2, 2, 2, -1, 128).transpose(2, 1, 0, 3, 4)
        bit = side("x")
        tiny_keep, tiny_send = (take(flat, place, 0).reshape(-1, 128) for place in (bit, 1 - bit))
        (come,), _ = advance([late, down, wide_part], [(tiny_send, "x")])
        tiny = Part((tiny_keep,), (come,), (("x", "near", "far"),) * 2, False)
        advance([late, down, wide_part, tiny])
        advance([late, down, tiny])
        advance([late, tiny])
        zero = lambda part: pick(part.done, part.other)
        one_ = lambda part: pick(part.other, part.done)
        split = blocks * 256
        hidden_gate_g, hidden_up_g = (
            of(wide_part)[:, : blocks * 256] for of in (zero, one_)
        )
        out_g, gate_g = (
            jnp.concatenate([zero(wide_part)[:, places], one_(wide_part)[:, places]], 1)
            for places in (slice(split, split + half), slice(split + half, split + width))
        )
        query_g, key_g = zero(late)[:, :width], one_(late)[:, :width]
        value_g = jnp.concatenate([zero(late)[:, width:], one_(late)[:, width:]], 1)
        hidden_down_g = jnp.concatenate([zero(down), one_(down)], 1)
        first_g, beta_g, conv_g, head_g, second_g = unflatten_small(tiny.done, small)
    else:
        input_grad, grad_first_gain = enter(
            rows, first_gain[None], grad_hidden, grads, grad_gate_pre, grad_beta_pre, query_weight,
            key_weight, value_weight, gate_weight, beta_weight.T,
        )
        small = (
            grad_first_gain[0], outer_sum(normed_one.T, grad_beta_pre), grad_conv, grad_head_gain[0],
            grad_second_gain[0],
        )

        def whole(term, dimension):
            part = lax.psum_scatter(term, "seq", scatter_dimension=dimension, tiled=True)
            return lax.psum(part, "doc")

        gate_grad, up_grad = jnp.where(here, kept, sent), jnp.where(here, sent, kept)
        terms = (
            outer_sum(normed_one.T, grads[0]), outer_sum(normed_one.T, grads[1]),
            outer_sum(normed_one.T, grads[2]), outer_sum(normed_one.T, grad_gate_pre),
            outer_sum(head_turned.T, grad_branch), outer_sum(two_turned.T, gate_grad),
            outer_sum(two_turned.T, up_grad), outer_sum(inner_turned.T, top),
        )
        query_g, key_g, value_g, gate_g, out_g, hidden_gate_g, hidden_up_g, hidden_down_g = (
            whole(term, 0) for term in terms
        )
        first_g, beta_g, conv_g, head_g, second_g = (
            whole(term, d) for term, d in zip(small, (0, 0, 2, 0, 0))
        )
    return (
        block_out[None], input_grad[None], first_g, query_g, key_g, value_g, gate_g, beta_g, conv_g,
        head_g, out_g, second_g, hidden_gate_g, hidden_up_g, hidden_down_g,
    )


def solution(mesh):
    in_specs = (
        P("doc", "seq", None),
        P("doc", None),
        P("doc", "seq", None),
        P(),
        P(),
        P(),
        P(),
        P(),
        P(),
        P(),
        P(),
        P(),
        P(),
        P(),
        P(),
        P(),
    )
    out_specs = (
        P("doc", "seq", None),
        P("doc", "seq", None),
        P("seq"),
        P("seq", None),
        P("seq", None),
        P("seq", None),
        P("seq", None),
        P("seq", None),
        P(None, None, "seq"),
        P("seq"),
        P("seq", None),
        P("seq"),
        P("seq", None),
        P("seq", None),
        P("seq", None),
    )
    return jax.shard_map(local, mesh=mesh, in_specs=in_specs, out_specs=out_specs, check_vma=False)
```

```python
import jax
import jax.numpy as jnp
from jax import lax
from jax.experimental import pallas as pl
from jax.experimental.pallas import tpu as pltpu
from jax.sharding import PartitionSpec as P

CK = 64


EPS = 1e-05
KEY_EPS = 1e-06
HIGH = lax.Precision.HIGHEST


SPAN = CK
LANES = 128
LOW = jnp.bfloat16
NN = (((1,), (0,)), ((), ()))
NT = (((1,), (1,)), ((), ()))
TN = (((0,), (0,)), ((), ()))


def params(mib=54):
    return pltpu.CompilerParams(vmem_limit_bytes=mib * 2**20)


def cost(flops, moved):
    return pl.CostEstimate(flops=1, bytes_accessed=1, transcendentals=0)


def mxu(left, right, dims):
    return lax.dot_general(left, right, dims, preferred_element_type=jnp.float32)


def halves(value):
    high = value.astype(LOW)
    return high, (value - high.astype(jnp.float32)).astype(LOW)


def split(value):
    return value if isinstance(value, tuple) else halves(value)


def stack(first, second):
    return tuple(jnp.concatenate(both, 0) for both in zip(first, second))


def fold(value):
    half = value.shape[1] // 2
    return value[:, :half] + value[:, half:]


def product(left, right):
    left_high, left_low = split(left)
    right_high, right_low = split(right)
    both = jnp.concatenate([left_high, left_low], 1)
    if right_high.shape[1] <= LANES:
        wide = jnp.concatenate([right_high, right_low], 1)
        return fold(mxu(both, jnp.concatenate([wide, wide], 0), NN))
    return mxu(both, jnp.concatenate([right_high, right_high], 0), NN) + mxu(
        left_high, right_low, NN
    )


def product_t(left, right):
    left_high, left_low = split(left)
    right_high, right_low = split(right)
    both = jnp.concatenate([left_high, left_low], 1)
    if right_high.shape[0] <= LANES:
        rows = jnp.concatenate(
            [
                jnp.concatenate([right_high, right_high], 1),
                jnp.concatenate([right_low, right_low], 1),
            ],
            0,
        )
        return fold(mxu(both, rows, NT))
    return mxu(both, jnp.concatenate([right_high, right_high], 1), NT) + mxu(
        left_high, right_low, NT
    )


def t_product(left, right):
    left_high, left_low = split(left)
    right_high, right_low = split(right)
    both = jnp.concatenate([left_high, left_low], 0)
    if right_high.shape[1] <= LANES:
        wide = jnp.concatenate([right_high, right_low], 1)
        return fold(mxu(both, jnp.concatenate([wide, wide], 0), TN))
    return mxu(both, jnp.concatenate([right_high, right_high], 0), TN) + mxu(
        left_high, right_low, TN
    )


def head(value, h):
    return value[:, h * LANES : (h + 1) * LANES]


def pair(value, p):
    return jnp.concatenate([head(value, 2 * p), head(value, 2 * p + 1)], 0)


def pair_column(value, p):
    return jnp.concatenate([value[:, 2 * p : 2 * p + 1], value[:, 2 * p + 1 : 2 * p + 2]], 0)


def masks(rows):
    i = lax.broadcasted_iota(jnp.int32, (rows, rows), 0)
    j = lax.broadcasted_iota(jnp.int32, (rows, rows), 1)
    same = (i >= SPAN) == (j >= SPAN)
    strict = jnp.where(same & (j < i), 1.0, 0.0)
    inclusive = jnp.where(same & (j <= i), 1.0, 0.0)
    upper = jnp.where(same & (j >= i), 1.0, 0.0)
    return strict, inclusive, upper, jnp.where(i == j, 1.0, 0.0)


def inverses_of(strict_parts, identity):
    rows = identity.shape[0]
    results = [identity - part for part in strict_parts]
    powers = [split(part) for part in strict_parts]
    powers = [split(product(power, power)) for power in powers]
    for level in range(SPAN.bit_length() - 3):
        both = [
            product(stack(split(result), power), power) for result, power in zip(results, powers)
        ]
        results = [result + pair_[:rows] for result, pair_ in zip(results, both)]
        powers = [split(pair_[rows:]) for pair_ in both]
    return [result + product(result, power) for result, power in zip(results, powers)]


def sigmoid(value):
    return 1.0 / (1.0 + jnp.exp(-value))


def doc_starts(docs):
    begin = jnp.int32(0)
    for index in range(1, docs.shape[0]):
        yield begin, docs[index]
        begin = begin + jnp.bitwise_and(docs[index] + (SPAN - 1), -SPAN)


def span_flag(docs, span):
    place, flag = docs[0] + span * SPAN, jnp.float32(1.0)
    for begin, _ in doc_starts(docs):
        flag = jnp.where(begin == place, 0.0, flag)
    return flag


def token_places(docs, count):
    place = docs[0] + lax.broadcasted_iota(jnp.int32, (count, 1), 0)
    position, live = place, jnp.zeros((count, 1), jnp.float32)
    for begin, length in doc_starts(docs):
        here = place >= begin
        position = jnp.where(here, place - begin, position)
        live = jnp.where(here, jnp.where(place - begin < length, 1.0, 0.0), live)
    return position, live


HALO = 16


def project_kernel(
    docs, tokens, halo, gain, query_w, key_w, value_w, gate_w, beta_w, conv,
    normed_out, pre_out, feature_out, gate_out, beta_pre_out, beta_out, position, live, normed, pre,
):
    count = tokens.shape[0]

    @pl.when(pl.program_id(0) == 0)
    def _():
        def norm(rows):
            return (
                rows * lax.rsqrt(jnp.mean(rows * rows, -1, keepdims=True) + EPS) * gain[...]
            ).astype(LOW)

        normed[:HALO, :] = norm(halo[...])
        rounded = norm(tokens[...].astype(jnp.float32))
        normed[HALO:, :] = rounded
        normed_out[...] = rounded.astype(jnp.float32).T
        beta_pre = mxu(rounded, beta_w[...], NT)
        beta_pre_out[...] = beta_pre
        position[...], live[...] = token_places(docs, count)
        beta_out[...] = sigmoid(beta_pre) * live[...]

    gate_out[...] = mxu(normed[HALO:, :], gate_w[...], NN)
    valid = [
        jnp.broadcast_to(
            jnp.where(position[...] >= conv.shape[1] - 1 - tap, 1.0, 0.0), (count, LANES)
        )
        for tap in range(conv.shape[1] - 1)
    ]
    for which, weight in enumerate((query_w, key_w, value_w)):
        pre[which] = mxu(normed[...], weight[...], NN)
        for span in range(count // SPAN):
            start = HALO + span * SPAN
            pre_out[which, span] = pre[which, start - 8 : start + SPAN, :]
        for part in range(pre.shape[2] // LANES):
            lanes = slice(part * LANES, (part + 1) * LANES)
            total = conv_total(pre, which, HALO, count, lanes, conv, valid)
            value = total * sigmoid(total)
            if which < 2:
                value = value * lax.rsqrt(jnp.sum(value * value, -1, keepdims=True) + KEY_EPS)
            if which == 1:
                value = value * live[...]
            feature_out[which, :, lanes] = value


def conv_total(pre, which, first, count, lanes, conv, valid):
    taps = conv.shape[1]
    total = None
    for tap in range(taps):
        start = first - (taps - 1) + tap
        term = conv[which, tap : tap + 1, lanes] * pre[which, start : start + count, lanes]
        if tap < taps - 1:
            term = term * valid[tap]
        total = term if total is None else total + term
    return total


def project(docs, tokens, halo, gain, query_w, key_w, value_w, gate_w, beta_w, conv):
    count, width = tokens.shape
    heads = beta_w.shape[0]
    block = 2 * LANES
    whole = lambda shape: pl.BlockSpec(shape, lambda j: (0,) * len(shape))
    weight = pl.BlockSpec((width, block), lambda j: (0, j))
    f32 = lambda shape: jax.ShapeDtypeStruct(shape, jnp.float32)
    return pl.pallas_call(
        project_kernel,
        grid=(width // block,),
        in_specs=[
            pl.BlockSpec(memory_space=pltpu.SMEM), whole((count, width)), whole((HALO, width)),
            whole((1, width)), weight, weight, weight, weight, whole((heads, width)),
            pl.BlockSpec((3, conv.shape[1], block), lambda j: (0, 0, j)),
        ],
        out_specs=[
            whole((width, count)),
            pl.BlockSpec((3, count // SPAN, SPAN + 8, block), lambda j: (0, 0, 0, j)),
            pl.BlockSpec((3, count, block), lambda j: (0, 0, j)),
            pl.BlockSpec((count, block), lambda j: (0, j)),
            whole((count, heads)), whole((count, heads)), whole((count, 1)), whole((count, 1)),
        ],
        out_shape=[
            f32((width, count)), f32((3, count // SPAN, SPAN + 8, width)), f32((3, count, width)),
            f32((count, width)), f32((count, heads)), f32((count, heads)),
            jax.ShapeDtypeStruct((count, 1), jnp.int32), f32((count, 1)),
        ],
        scratch_shapes=[
            pltpu.VMEM((HALO + count, width), LOW),
            pltpu.VMEM((3, HALO + count, block), jnp.float32),
        ],
        compiler_params=params(),
        cost_estimate=cost(8 * count * width * width, 8 * width * width + 40 * count * width),
        name="project",
    )(docs, tokens, halo, gain, query_w, key_w, value_w, gate_w, beta_w, conv)


def prepare_kernel(docs, features, beta, solved_out, inverse_out, attend_out, state):
    span = pl.program_id(0)
    heads = state.shape[0]
    size = state.shape[1]
    strict, inclusive, upper, identity = masks(2 * SPAN)

    @pl.when(span == 0)
    def _():
        i = lax.broadcasted_iota(jnp.int32, (size, 2 * size), 0)
        j = lax.broadcasted_iota(jnp.int32, (size, 2 * size), 1)
        for h in range(heads):
            state[h] = jnp.where(j == i + size, 1.0, 0.0)

    query, key, value = features[0], features[1], features[2]
    betas = beta[...]
    flag = span_flag(docs, span)
    pairs = range(heads // 2)
    keys = [split(pair(key, p)) for p in pairs]
    columns = [pair_column(betas, p) for p in pairs]
    scores = [product_t(stack(keys[p], split(pair(query, p))), keys[p]) for p in pairs]
    solved = inverses_of([columns[p] * scores[p][: 2 * SPAN] * strict for p in pairs], identity)
    both = [
        product(
            solved[p],
            jnp.concatenate([columns[p] * pair(key, p), columns[p] * pair(value, p)], 1),
        )
        for p in pairs
    ]
    for p in pairs:
        inverse_out[0, p] = solved[p]
        attend_out[0, p] = scores[p][2 * SPAN :] * inclusive
    starts, news = [], []
    for h in range(heads):
        rows = slice(h % 2 * SPAN, (h % 2 + 1) * SPAN)
        erase, update = both[h // 2][rows, :size], both[h // 2][rows, size:]
        solved_out[0, :, h * size : (h + 1) * size] = erase
        solved_out[1, :, h * size : (h + 1) * size] = update
        start = state[h] * flag
        starts.append(start)
        news.append(
            jnp.concatenate([update, jnp.zeros_like(update)], 1) - product(erase, start)
        )
    for h in range(heads):
        rows = slice(h % 2 * SPAN, (h % 2 + 1) * SPAN)
        state[h] = starts[h] + t_product(tuple(k[rows] for k in keys[h // 2]), news[h])


def prepare(docs, features, beta):
    _, count, width = features.shape
    heads = beta.shape[1]
    size = width // heads
    spans = count // SPAN
    f32 = lambda shape: jax.ShapeDtypeStruct(shape, jnp.float32)
    matrix = pl.BlockSpec((1, heads // 2, 2 * SPAN, 2 * SPAN), lambda c: (c, 0, 0, 0))
    return pl.pallas_call(
        prepare_kernel,
        grid=(spans,),
        in_specs=[
            pl.BlockSpec(memory_space=pltpu.SMEM),
            pl.BlockSpec((3, SPAN, width), lambda c: (0, c, 0)),
            pl.BlockSpec((SPAN, heads), lambda c: (c, 0)),
        ],
        out_specs=[
            pl.BlockSpec((2, SPAN, width), lambda c: (0, c, 0)), matrix, matrix,
            pl.BlockSpec((heads, size, 2 * size), lambda c: (0, 0, 0)),
        ],
        out_shape=[
            f32((2, count, width)), f32((spans, heads // 2, 2 * SPAN, 2 * SPAN)),
            f32((spans, heads // 2, 2 * SPAN, 2 * SPAN)), f32((heads, size, 2 * size)),
        ],
        compiler_params=params(),
        cost_estimate=cost(40 * count * width * size * 4, 60 * count * width),
        name="prepare",
    )(docs, features, beta)


def mix_kernel(
    docs, place, features, solved, attend, gate, gain, state_mine, state_other, starts_out, new_out,
    mixed_out, normed_out, state,
):
    span = pl.program_id(0)
    heads = state.shape[0]

    @pl.when(span == 0)
    def _():
        half = heads // 2
        first = place[0] == 0
        state[:half] = jnp.where(first, state_mine[...], state_other[...])
        state[half:] = jnp.where(first, state_other[...], state_mine[...])

    query, key = features[0], features[1]
    erase, update = solved[0], solved[1]
    flag = span_flag(docs, span)
    every, pairs = range(heads), range(heads // 2)
    starts = [state[h] * flag for h in every]
    both = [
        product(jnp.concatenate([head(erase, h), head(query, h)], 0), starts[h]) for h in every
    ]
    news = [split(head(update, h) - both[h][:SPAN]) for h in every]
    after = [starts[h] + t_product(head(key, h), news[h]) for h in every]
    inner = [product(attend[0, p], stack(news[2 * p], news[2 * p + 1])) for p in pairs]
    for h in every:
        lanes = slice(h * LANES, (h + 1) * LANES)
        starts_out[0, h] = starts[h]
        state[h] = after[h]
        new_out[:, lanes] = head(update, h) - both[h][:SPAN]
        rows = both[h][SPAN:] + inner[h // 2][h % 2 * SPAN : (h % 2 + 1) * SPAN]
        mixed_out[:, lanes] = rows
        shaped = rows * lax.rsqrt(jnp.mean(rows * rows, -1, keepdims=True) + EPS) * gain[...]
        gates = gate[:, lanes]
        normed_out[:, lanes] = (shaped * (gates * sigmoid(gates))).astype(LOW)


def mix(docs, place, features, solved, attend, gate, gain, state_mine, state_other):
    _, count, width = features.shape
    half, size, _ = state_mine.shape
    heads = 2 * half
    spans = count // SPAN
    f32 = lambda shape: jax.ShapeDtypeStruct(shape, jnp.float32)
    rows = pl.BlockSpec((SPAN, width), lambda c: (c, 0))
    pairs = pl.BlockSpec((2, SPAN, width), lambda c: (0, c, 0))
    return pl.pallas_call(
        mix_kernel,
        grid=(spans,),
        in_specs=[
            pl.BlockSpec(memory_space=pltpu.SMEM), pl.BlockSpec(memory_space=pltpu.SMEM), pairs, pairs,
            pl.BlockSpec((1, heads // 2, 2 * SPAN, 2 * SPAN), lambda c: (c, 0, 0, 0)),
            rows, pl.BlockSpec((1, size), lambda c: (0, 0)),
            pl.BlockSpec((half, size, size), lambda c: (0, 0, 0)),
            pl.BlockSpec((half, size, size), lambda c: (0, 0, 0)),
        ],
        out_specs=[
            pl.BlockSpec((1, heads, size, size), lambda c: (c, 0, 0, 0)), rows, rows, rows,
        ],
        out_shape=[
            f32((spans, heads, size, size)), f32((count, width)), f32((count, width)),
            jax.ShapeDtypeStruct((count, width), LOW),
        ],
        scratch_shapes=[pltpu.VMEM((heads, size, size), jnp.float32)],
        compiler_params=params(),
        cost_estimate=cost(8 * count * width * size * 4, 40 * count * width),
        name="mix",
    )(docs, place, features, solved, attend, gate, gain, state_mine, state_other)


def feed_kernel(
    core, tokens, normed_head, grad_top, second_gain, out_w, gate_w, up_w, down_w,
    block_out, normed_out, inner_out, kept_out, sent_out, grad_hidden_out, branch_out, grad_head_out,
    gain_grad_out, head_turned_out, hidden, normed, total, grad_total,
):
    step = pl.program_id(0)

    @pl.when(step == 0)
    def _():
        state = tokens[...].astype(jnp.float32) + mxu(normed_head[...], out_w[...], NN)
        hidden[...] = state
        rounded = (
            state * lax.rsqrt(jnp.mean(state * state, -1, keepdims=True) + EPS) * second_gain[...]
        ).astype(LOW)
        normed[...] = rounded
        normed_out[...] = rounded.astype(jnp.float32).T
        head_turned_out[...] = normed_head[...].astype(jnp.float32).T

    @pl.when(step == 0)
    def _():
        total[...] = jnp.zeros_like(total)
        grad_total[...] = jnp.zeros_like(grad_total)

    first = core[0] == 0
    size = normed.shape[0] // 1
    parts = [slice(i * size, (i + 1) * size) for i in range(1)]
    gates = [mxu(normed[part, :], gate_w[...], NN) for part in parts]
    ups = [mxu(normed[part, :], up_w[...], NN) for part in parts]
    grad_inners = [mxu(grad_top[part, :], down_w[...], NT) for part in parts]
    for part, gate, up, grad_inner in zip(parts, gates, ups, grad_inners):
        sigma = sigmoid(gate)
        act = gate * sigma
        inner = (act * up).astype(LOW)
        inner_out[:, part] = inner.astype(jnp.float32).T
        wide_gate = grad_inner * up * (sigma + act * (1.0 - sigma))
        wide_up = grad_inner * act
        grad_gate, grad_up = wide_gate.astype(LOW), wide_up.astype(LOW)
        kept_out[part, :] = jnp.where(first, wide_gate, wide_up).astype(LOW)
        sent_out[part, :] = jnp.where(first, wide_up, wide_gate).astype(LOW).astype(jnp.float32)
        total[part, :] += mxu(inner, down_w[...], NN)
        grad_total[part, :] += mxu(grad_gate, gate_w[...], NT) + mxu(grad_up, up_w[...], NT)

    @pl.when(step == pl.num_programs(0) - 1)
    def _():
        state = hidden[...]
        block_out[...] = (state + total[...]).astype(LOW)
        part, gain_part = norm_back(state, second_gain[...], grad_total[...])
        gain_grad_out[...] = gain_part
        grad_hidden = grad_top[...].astype(jnp.float32) + part
        grad_hidden_out[...] = grad_hidden
        branch = grad_hidden.astype(LOW)
        branch_out[...] = branch.astype(jnp.float32)
        grad_head_out[...] = mxu(branch, out_w[...], NT)


def norm_back(value, gain, grad):
    scale = lax.rsqrt(jnp.mean(value * value, -1, keepdims=True) + EPS)
    unit = value * scale
    gain_grad = jnp.sum(grad * unit, 0, keepdims=True)
    inward = grad * gain
    return scale * (inward - unit * jnp.mean(inward * unit, -1, keepdims=True)), gain_grad


def feed(core, tokens, normed_head, grad_top, second_gain, out_w, gate_w, up_w, down_w):
    count, width = tokens.shape
    hidden = gate_w.shape[1]
    block = 2 * LANES
    whole = lambda shape: pl.BlockSpec(shape, lambda j: (0,) * len(shape))
    f32 = lambda shape: jax.ShapeDtypeStruct(shape, jnp.float32)
    low = lambda shape: jax.ShapeDtypeStruct(shape, LOW)
    rows = whole((count, width))
    columns = pl.BlockSpec((count, block), lambda j: (0, j))
    return pl.pallas_call(
        feed_kernel,
        grid=(hidden // block,),
        in_specs=[
            pl.BlockSpec(memory_space=pltpu.SMEM), rows, rows, rows, whole((1, width)),
            whole((width, width)), pl.BlockSpec((width, block), lambda j: (0, j)),
            pl.BlockSpec((width, block), lambda j: (0, j)),
            pl.BlockSpec((block, width), lambda j: (j, 0)),
        ],
        out_specs=[
            rows, whole((width, count)), pl.BlockSpec((block, count), lambda j: (j, 0)), columns,
            columns, rows, rows, rows, whole((1, width)), whole((width, count)),
        ],
        out_shape=[
            low((count, width)), f32((width, count)), f32((hidden, count)), low((count, hidden)),
            f32((count, hidden)), f32((count, width)), f32((count, width)), f32((count, width)),
            f32((1, width)), f32((width, count)),
        ],
        scratch_shapes=[
            pltpu.VMEM((count, width), jnp.float32), pltpu.VMEM((count, width), LOW),
            pltpu.VMEM((count, width), jnp.float32), pltpu.VMEM((count, width), jnp.float32),
        ],
        compiler_params=params(),
        cost_estimate=cost(
            12 * count * width * hidden + 4 * count * width * width,
            6 * width * hidden + 10 * count * hidden + 30 * count * width,
        ),
        name="feed",
    )(core, tokens, normed_head, grad_top, second_gain, out_w, gate_w, up_w, down_w)


def gather_kernel(
    docs, core, grad_head, grad_branch, mixed, gate, gain, features, solved, grad_mixed_out,
    grad_gate_out, kept_out, sent_out, gain_out, state,
):
    step = pl.program_id(0)
    span = pl.num_programs(0) - 1 - step
    heads = state.shape[0]
    strict, inclusive, upper, identity = masks(2 * SPAN)

    @pl.when(step == 0)
    def _():
        state[...] = jnp.zeros_like(state)
        gain_out[...] = jnp.zeros_like(gain_out)

    query, key = features[0], features[1]
    erase = solved[0]
    flag = span_flag(docs, span)
    gain_total = jnp.zeros_like(gain_out[...])
    every, pairs = range(heads), range(heads // 2)
    passes = [product_t(pair(key, p), pair(query, p)) * upper for p in pairs]
    grads = []
    for h in every:
        lanes = slice(h * LANES, (h + 1) * LANES)
        gates = gate[:, lanes]
        sigma = sigmoid(gates)
        rows = mixed[:, lanes]
        grad = grad_head[:, lanes]
        scale = lax.rsqrt(jnp.mean(rows * rows, -1, keepdims=True) + EPS)
        unit = rows * scale
        grad_gate = grad * unit * gain[...] * sigma * (1.0 + gates * (1.0 - sigma))
        grad_gate = grad_gate.astype(LOW).astype(jnp.float32)
        grad_gate_out[:, lanes] = grad_gate
        shaped = grad * gates * sigma
        gain_total = gain_total + jnp.sum(shaped * unit, 0, keepdims=True)
        inward = shaped * gain[...]
        grad_rows = scale * (inward - unit * jnp.mean(inward * unit, -1, keepdims=True))
        grad_mixed_out[:, lanes] = grad_rows
        grads.append(split(grad_rows))
    passed = [product(passes[p], stack(grads[2 * p], grads[2 * p + 1])) for p in pairs]
    ends = [state[h] for h in every]
    grad_new = [
        passed[h // 2][h % 2 * SPAN : (h % 2 + 1) * SPAN] + product(head(key, h), ends[h])
        for h in every
    ]
    for h in every:
        state[h] = flag * (
            ends[h]
            + t_product(
                jnp.concatenate([head(query, h), -head(erase, h)], 0),
                stack(grads[h], split(grad_new[h])),
            )
        )
    gain_out[...] += gain_total
    half = grad_branch.shape[1] // 2
    first = core[0] == 0
    for place, source in ((0, grad_branch), (half, grad_gate_out)):
        low, high = source[:, :half], source[:, half:]
        kept_out[:, place : place + half] = jnp.where(first, low, high).astype(LOW)
        sent_out[:, place : place + half] = jnp.where(first, high, low)


def gather_states(
    docs, core, grad_head, grad_branch, mixed, gate, gain, features, solved, heads
):
    _, count, width = features.shape
    size = width // heads
    spans = count // SPAN
    f32 = lambda shape: jax.ShapeDtypeStruct(shape, jnp.float32)
    rows = pl.BlockSpec((SPAN, width), lambda c: (spans - 1 - c, 0))
    pairs = pl.BlockSpec((2, SPAN, width), lambda c: (0, spans - 1 - c, 0))
    one = pl.BlockSpec((1, SPAN, width), lambda c: (0, spans - 1 - c, 0))
    return pl.pallas_call(
        gather_kernel,
        grid=(spans,),
        in_specs=[
            pl.BlockSpec(memory_space=pltpu.SMEM), pl.BlockSpec(memory_space=pltpu.SMEM), rows, rows,
            rows, rows, pl.BlockSpec((1, size), lambda c: (0, 0)), pairs, one,
        ],
        out_specs=[
            rows, rows, rows, rows, pl.BlockSpec((1, size), lambda c: (0, 0)),
            pl.BlockSpec((heads, size, size), lambda c: (0, 0, 0)),
        ],
        out_shape=[
            f32((count, width)), f32((count, width)), jax.ShapeDtypeStruct((count, width), LOW),
            f32((count, width)), f32((1, size)), f32((heads, size, size)),
        ],
        compiler_params=params(),
        cost_estimate=cost(8 * count * width * size * 4, 32 * count * width),
        name="gather_states",
    )(docs, core, grad_head, grad_branch, mixed, gate, gain, features, solved)


def back_kernel(
    docs, place, features, beta, beta_pre, solved, inverses, starts, news, grad_mixed, state_mine,
    state_other, pre, conv, position, live, grad_pre_out, borrowed_out, conv_out, grad_beta_out, state, later, sums,
):
    step = pl.program_id(0)
    span = pl.num_programs(0) - 1 - step
    heads = state.shape[0]
    taps = conv.shape[1]
    strict, inclusive, upper, identity = masks(2 * SPAN)

    @pl.when(step == 0)
    def _():
        half = heads // 2
        first = place[0] == 0
        state[:half] = jnp.where(first, state_mine[...], state_other[...])
        state[half:] = jnp.where(first, state_other[...], state_mine[...])
        sums[...] = jnp.zeros_like(sums)
        later[...] = jnp.zeros_like(later)

    query, key, value = features[0], features[1], features[2]
    erase, update = solved[0], solved[1]
    betas = beta[...]
    flag = span_flag(docs, span)
    base = pl.multiple_of(span * SPAN, SPAN)
    places = position[pl.ds(base, SPAN), :]
    lives = live[pl.ds(base, SPAN), :]
    valid = [
        jnp.broadcast_to(jnp.where(places >= taps - 1 - tap, 1.0, 0.0), (SPAN, LANES))
        for tap in range(taps - 1)
    ]
    every, pairs = range(heads), range(heads // 2)
    part = [slice(h % 2 * SPAN, (h % 2 + 1) * SPAN) for h in every]
    q = [split(pair(query, p)) for p in pairs]
    k = [split(pair(key, p)) for p in pairs]
    b = [pair_column(betas, p) for p in pairs]
    grad_out = [split(pair(grad_mixed, p)) for p in pairs]
    new = [split(pair(news, p)) for p in pairs]
    erases = [split(pair(erase, p)) for p in pairs]
    row = lambda value, h: tuple(v[part[h]] for v in value[h // 2])
    scores = [product_t(k[p], stack(k[p], q[p])) for p in pairs]
    passed = [product(scores[p][:, 2 * SPAN :] * upper, grad_out[p]) for p in pairs]
    ends = [split(state[h]) for h in every]
    begin = [split(starts[0, h]) for h in every]
    grad_new = [passed[h // 2][part[h]] + product(row(k, h), ends[h]) for h in every]
    grad_news = [split(value) for value in grad_new]
    both = [product_t(stack(row(grad_out, h), grad_news[h]), begin[h]) for h in every]
    grad_key = [product_t(row(new, h), ends[h]) for h in every]
    for h in every:
        state[h] = flag * (
            state[h]
            + t_product(
                stack(row(q, h), tuple(-v for v in row(erases, h))),
                stack(row(grad_out, h), grad_news[h]),
            )
        )
    grad_attend = [product_t(grad_out[p], new[p]) * inclusive for p in pairs]
    joined = lambda values, p: jnp.concatenate([values[2 * p], values[2 * p + 1]], 0)
    grad_q = [
        joined([value[:SPAN] for value in both], p) + product(grad_attend[p], k[p]) for p in pairs
    ]
    grad_k = [joined(grad_key, p) + product(grad_attend[p].T, q[p]) for p in pairs]
    turned = [
        product(
            inverses[0, p].T,
            jnp.concatenate(
                [joined(grad_new, p), -joined([value[SPAN:] for value in both], p)], 1
            ),
        )
        for p in pairs
    ]
    grad_bv = [value[:, :LANES] for value in turned]
    grad_bk = [value[:, LANES:] for value in turned]
    grad_lower = [
        -strict * (product_t(grad_bv[p], pair(update, p)) + product_t(grad_bk[p], erases[p]))
        for p in pairs
    ]
    inner = [b[p] * grad_lower[p] for p in pairs]
    grad_k = [
        grad_k[p] + product(inner[p] + inner[p].T, k[p]) + b[p] * grad_bk[p] for p in pairs
    ]
    grad_v = [b[p] * grad_bv[p] for p in pairs]
    beta_columns = []
    for p in pairs:
        grad_b = (
            jnp.sum(grad_lower[p] * scores[p][:, : 2 * SPAN], -1, keepdims=True)
            + jnp.sum(grad_bv[p] * pair(value, p), -1, keepdims=True)
            + jnp.sum(grad_bk[p] * pair(key, p), -1, keepdims=True)
        )
        beta_columns += [grad_b[:SPAN], grad_b[SPAN:]]
    chunks = [(which, h) for which in range(3) for h in every]
    for start in range(0, len(chunks), 4):
        group = chunks[start : start + 4]
        places = [(which, slice(h * LANES, (h + 1) * LANES)) for which, h in group]
        grads = [(grad_q, grad_k, grad_v)[which][h // 2][part[h]] for which, h in group]
        shifted = [
            [
                pre[which, 0, pl.ds(8 - (taps - 1) + tap, SPAN), lanes]
                for tap in range(taps)
            ]
            for which, lanes in places
        ]
        shifted = [
            [value * valid[tap] for tap, value in enumerate(moved[:-1])] + moved[-1:]
            for moved in shifted
        ]
        totals = [
            sum(
                conv[which, tap : tap + 1, lanes] * moved[tap] for tap in range(taps)
            )
            for moved, (which, lanes) in zip(shifted, places)
        ]
        sigmas = [sigmoid(total) for total in totals]
        acts = [total * sigma for total, sigma in zip(totals, sigmas)]
        slopes = [sigma + act * (1.0 - sigma) for sigma, act in zip(sigmas, acts)]
        squares = [
            jnp.sum(act * act, -1, keepdims=True) if which < 2 else None
            for act, (which, _) in zip(acts, group)
        ]
        grads = [
            grad * lives if which == 1 else grad for grad, (which, _) in zip(grads, group)
        ]
        scales = [None if square is None else lax.rsqrt(square + KEY_EPS) for square in squares]
        units = [act if scale is None else act * scale for act, scale in zip(acts, scales)]
        along = [
            None if scale is None else jnp.sum(grad * unit, -1, keepdims=True)
            for grad, unit, scale in zip(grads, units, scales)
        ]
        grads = [
            slope * (grad if scale is None else scale * (grad - unit * dot))
            for slope, grad, scale, unit, dot in zip(slopes, grads, scales, units, along)
        ]
        for grad, moved, (which, lanes) in zip(grads, shifted, places):
            result = conv[which, taps - 1 : taps, lanes] * grad
            for tap in range(taps):
                product_ = grad * moved[tap]
                sums[which, tap, :, lanes] += sum(
                    product_[8 * r : 8 * (r + 1)] for r in range(SPAN // 8)
                )
                if tap < taps - 1:
                    masked = grad * valid[tap]
                    later[which, tap, SPAN:, lanes] = later[which, tap, :8, lanes]
                    later[which, tap, :SPAN, lanes] = masked
                    result = result + conv[which, tap : tap + 1, lanes] * (
                        later[which, tap, pl.ds(taps - 1 - tap, SPAN), lanes]
                    )
            grad_pre_out[which, :, lanes] = result
    columns = lax.broadcasted_iota(jnp.int32, (SPAN, heads), 1)
    grad_beta = jnp.zeros((SPAN, heads), jnp.float32)
    for h in range(heads):
        grad_beta = jnp.where(columns == h, beta_columns[h], grad_beta)
    sigma = sigmoid(beta_pre[...])
    grad_beta_out[...] = (
        (grad_beta * lives * sigma * (1.0 - sigma)).astype(LOW).astype(jnp.float32)
    )

    @pl.when(span == 0)
    def _():
        conv_out[...] = jnp.sum(sums[...], 2)
        for which in range(3):
            result = None
            for tap in range(taps - 1):
                ahead = taps - 1 - tap
                rows = jnp.concatenate([jnp.zeros((8, later.shape[3]), jnp.float32), later[which, tap, :8]], 0)
                term = conv[which, tap : tap + 1, :] * rows[ahead:][:8]
                result = term if result is None else result + term
            borrowed_out[which] = result


def back(
    docs, place, features, beta, beta_pre, solved, inverses, starts, news, grad_mixed, state_mine,
    state_other, pre, conv, position, live,
):
    _, count, width = features.shape
    half, size, _ = state_mine.shape
    heads = 2 * half
    spans = count // SPAN
    taps = conv.shape[1]
    f32 = lambda shape: jax.ShapeDtypeStruct(shape, jnp.float32)
    whole = lambda shape: pl.BlockSpec(shape, lambda c: (0,) * len(shape))
    rows = pl.BlockSpec((SPAN, width), lambda c: (spans - 1 - c, 0))
    triple = pl.BlockSpec((3, SPAN, width), lambda c: (0, spans - 1 - c, 0))
    column = pl.BlockSpec((SPAN, heads), lambda c: (spans - 1 - c, 0))
    return pl.pallas_call(
        back_kernel,
        grid=(spans,),
        in_specs=[
            pl.BlockSpec(memory_space=pltpu.SMEM), pl.BlockSpec(memory_space=pltpu.SMEM), triple, column, column,
            pl.BlockSpec((2, SPAN, width), lambda c: (0, spans - 1 - c, 0)),
            pl.BlockSpec((1, heads // 2, 2 * SPAN, 2 * SPAN), lambda c: (spans - 1 - c, 0, 0, 0)),
            pl.BlockSpec((1, heads, size, size), lambda c: (spans - 1 - c, 0, 0, 0)),
            rows, rows, whole((half, size, size)), whole((half, size, size)),
            pl.BlockSpec((3, 1, SPAN + 8, width), lambda c: (0, spans - 1 - c, 0, 0)),
            whole(conv.shape),
            whole(position.shape), whole(live.shape),
        ],
        out_specs=[triple, whole((3, 8, width)), whole((3, taps, width)), column],
        out_shape=[
            f32((3, count, width)), f32((3, 8, width)), f32((3, taps, width)), f32((count, heads)),
        ],
        scratch_shapes=[
            pltpu.VMEM((heads, size, size), jnp.float32),
            pltpu.VMEM((3, taps - 1, SPAN + 8, width), jnp.float32),
            pltpu.VMEM((3, taps, 8, width), jnp.float32),
        ],
        compiler_params=params(),
        cost_estimate=cost(30 * count * width * size * 4, 60 * count * width),
        name="back",
    )(
        docs, place, features, beta, beta_pre, solved, inverses, starts, news, grad_mixed,
        state_mine, state_other, pre, conv, position, live,
    )


def enter_kernel(
    tokens, gain, grad_hidden, grads, grad_gate, grad_beta, query_w, key_w, value_w, gate_w, beta_w,
    input_grad_out, gain_out, total,
):
    step = pl.program_id(0)
    term = mxu(grad_gate[...].astype(LOW), gate_w[...], NT)
    for which, weight in enumerate((query_w, key_w, value_w)):
        term = term + mxu(grads[which], weight[...], NT)

    @pl.when(step == 0)
    def _():
        total[...] = term + mxu(grad_beta[...].astype(LOW), beta_w[...], NN)

    @pl.when(step > 0)
    def _():
        total[...] += term

    @pl.when(step == pl.num_programs(0) - 1)
    def _():
        part, gain_part = norm_back(tokens[...].astype(jnp.float32), gain[...], total[...])
        gain_out[...] = gain_part
        input_grad_out[...] = (grad_hidden[...] + part).astype(LOW)


def enter(
    tokens, gain, grad_hidden, grads, grad_gate, grad_beta, query_w, key_w, value_w, gate_w, beta_w
):
    count, width = tokens.shape
    heads = beta_w.shape[0]
    block = 2 * LANES
    whole = lambda shape: pl.BlockSpec(shape, lambda j: (0,) * len(shape))
    weight = pl.BlockSpec((width, block), lambda j: (0, j))
    return pl.pallas_call(
        enter_kernel,
        grid=(width // block,),
        in_specs=[
            whole((count, width)), whole((1, width)), whole((count, width)),
            pl.BlockSpec((3, count, block), lambda j: (0, 0, j)),
            pl.BlockSpec((count, block), lambda j: (0, j)), whole((count, heads)),
            weight, weight, weight, weight, whole((heads, width)),
        ],
        out_specs=[whole((count, width)), whole((1, width))],
        out_shape=[
            jax.ShapeDtypeStruct((count, width), LOW), jax.ShapeDtypeStruct((1, width), jnp.float32),
        ],
        scratch_shapes=[pltpu.VMEM((count, width), jnp.float32)],
        compiler_params=params(),
        cost_estimate=cost(8 * count * width * width, 8 * width * width + 20 * count * width),
        name="enter",
    )(
        tokens, gain, grad_hidden, grads, grad_gate, grad_beta, query_w, key_w, value_w, gate_w,
        beta_w,
    )


def passed_along(value, axis, by):
    devices = lax.axis_size(axis)
    pairs = [(i, i + by) for i in range(devices) if 0 <= i + by < devices]
    return lax.ppermute(value, axis, pairs)


def tuned():
    return (lax.axis_size("seq"), lax.axis_size("doc")) == (8, 4)


HOPS = {"core": ("doc", 1), "y": ("doc", 2), "x": ("seq", 1), "near": ("seq", 2), "far": ("seq", 4)}


def hop(value, way, other_way=None):
    if other_way in (None, way):
        axis, bit = HOPS[way]
        return lax.ppermute(value, axis, [(i, i ^ bit) for i in range(lax.axis_size(axis))])
    size = lax.axis_size("doc")
    masks = [bit * size if axis == "seq" else bit for axis, bit in (HOPS[way], HOPS[other_way])]
    pairs = [(i, i ^ masks[i % 2]) for i in range(lax.axis_size("seq") * size)]
    return lax.ppermute(value, ("seq", "doc"), pairs)


def side(way):
    axis, bit = HOPS[way]
    return lax.axis_index(axis) // bit % 2


def apply_kernel(shift, maps, *refs, turned):
    *states, out = refs
    size = maps.shape[1]
    for h in range(maps.shape[0]):
        state = states[0][h]
        for other in states[1:]:
            state = state + other[h]
        moved = (t_product if turned else product)(maps[h, :, size:], state)
        if state.shape[1] == size:
            out[h] = moved + shift[h, :, :size]
        else:
            out[h] = moved + jnp.concatenate([shift[h, :, :size], jnp.zeros((size, size), jnp.float32)], 1)


def apply_map(shift, maps, *states, turned=False):
    return pl.pallas_call(
        lambda *refs: apply_kernel(*refs, turned=turned),
        out_shape=jax.ShapeDtypeStruct(states[0].shape, jnp.float32),
        compiler_params=params(4),
        cost_estimate=cost(0, 0),
        name="apply_map",
    )(shift, maps, *states)


def ends_kernel(here, shift, maps, state, come, stay_out, send_out, *, turned):
    size = maps.shape[1]
    mine = here[0] == 0
    for h in range(maps.shape[0]):
        near = state[h] + come[h]
        far = (t_product if turned else product)(maps[h, :, size:], near) + shift[h, :, :size]
        if turned:
            near, far = far, near
        stay_out[h] = jnp.where(mine, near, far)
        send_out[h] = jnp.where(mine, far, near)


def pair_ends(here, shift, maps, state, come, turned=False):
    shape = jax.ShapeDtypeStruct(state.shape, jnp.float32)
    vmem = pl.BlockSpec(memory_space=pltpu.VMEM)
    return pl.pallas_call(
        lambda *refs: ends_kernel(*refs, turned=turned),
        in_specs=[pl.BlockSpec(memory_space=pltpu.SMEM)] + [vmem] * 4,
        out_specs=[vmem, vmem],
        out_shape=[shape, shape],
        compiler_params=params(4),
        cost_estimate=cost(0, 0),
        name="pair_ends",
    )(here, shift, maps, state, come)


def together(value, *others):
    return lax.optimization_barrier((value, *others))


def carried_forward(maps, beside):
    heads, size, _ = maps.shape
    half = heads // 2
    if not tuned():
        gathered = lax.all_gather(maps, "seq")

        def one(lap, state):
            each = lax.dynamic_index_in_dim(gathered, lap, 0, False)
            return apply_map(each, each, state)

        state = lax.fori_loop(
            0, lax.axis_index("seq"), one, jnp.zeros((heads, size, size), jnp.float32)
        )
        return state[:half], state[half:], jnp.zeros((1,), jnp.int32), (maps,)
    place = side("x").astype(jnp.int32).reshape(1)
    here = place[0] == 0
    kept = jnp.where(here, maps[:half], maps[half:])
    other = hop(jnp.where(here, maps[half:], maps[:half]), "x")
    other, *beside = together(other, *beside)
    first, second = jnp.where(here, kept, other), jnp.where(here, other, kept)
    pair_map = apply_map(second, second, first)
    state = jnp.zeros((half, size, size), jnp.float32)
    come = state
    for step in range(3):
        if step == 0:
            sent = pair_map[:, :, :size]
        else:
            sent = apply_map(pair_map, pair_map, state, come)
            state = state + come
        come = lax.ppermute(sent, "seq", [(2 * step + x, 2 * step + 2 + x) for x in range(2)])
    mine, send = pair_ends(place, first, first, state, come)
    return mine, hop(send, "x"), place, (first, second, pair_map), *beside


def carried_back(shift, context, beside=None):
    heads, size, _ = shift.shape
    half = heads // 2
    if not tuned():
        gathered = lax.all_gather(jnp.concatenate([shift, context[0][:, :, size:]], 2), "seq")
        count = lax.axis_size("seq")

        def one(lap, state):
            each = lax.dynamic_index_in_dim(gathered, count - 1 - lap, 0, False)
            return apply_map(each, each, state, turned=True)

        zeros = jnp.zeros((heads, size, size), jnp.float32)
        state = lax.fori_loop(0, count - 1 - lax.axis_index("seq"), one, zeros)
        return state[:half], state[half:], ()
    first, second, pair_map = context
    place = side("x").astype(jnp.int32).reshape(1)
    here = place[0] == 0
    done = []

    def step_with(number, sent, go):
        moves, work = beside[number]
        sent, *values = together(sent, *[move[0] for move in moves])
        come, *rest = together(
            go(sent), *[hop(value, *move[1:]) for value, move in zip(values, moves)], *work
        )
        done.append(rest)
        return come

    kept = jnp.where(here, shift[:half], shift[half:])
    other = step_with(0, jnp.where(here, shift[half:], shift[:half]), lambda value: hop(value, "x"))
    first_shift, second_shift = jnp.where(here, kept, other), jnp.where(here, other, kept)
    pair_shift = apply_map(first_shift, first, second_shift, turned=True)
    state = jnp.zeros((half, size, size), jnp.float32)
    come = state
    for step in range(3, 0, -1):
        if step == 3:
            sent = pair_shift
        else:
            sent = apply_map(pair_shift, pair_map, state, come, turned=True)
            state = state + come
        pairs = [(2 * step + x, 2 * step - 2 + x) for x in range(2)]
        come = step_with(4 - step, sent, lambda value: lax.ppermute(value, "seq", pairs))
    mine, send = pair_ends(place, second_shift, second, state, come, turned=True)
    return mine, step_with(4, send, lambda value: hop(value, "x")), done


def outer_kernel(table, *refs, blocks, pieces):
    count = len(blocks)
    lefts, rights = refs[: 2 * count], refs[2 * count : 4 * count]
    *outs, stacked = refs[4 * count :]
    step = pl.program_id(0)
    tokens = lefts[0].shape[1]
    size = outs[0].shape[0] // 8

    @pl.when(step == 0)
    def _():
        for piece in range(count):
            for which in range(2):
                for place in range(16):
                    rows = pl.ds(pl.multiple_of(table[place] * size, 16), size)
                    stacked[
                        piece, place * size : (place + 1) * size, which * tokens : (which + 1) * tokens
                    ] = lefts[2 * piece + which][rows, :].astype(LOW)

    for piece in range(count):
        low = sum(blocks[:piece])

        @pl.when((step >= low) & (step < low + blocks[piece]))
        def _(piece=piece):
            right = jnp.concatenate(
                [rights[2 * piece][...].astype(LOW), rights[2 * piece + 1][...].astype(LOW)], 0
            )
            place = 0
            for out, number in zip(outs, (8 * size, *pieces)):
                out[...] = mxu(stacked[piece, place : place + number, :], right, NN)
                place += number


WEIGHTS = {"far": 8, "near": 4, "x": 2, "y": 1}


def by_core(values):
    return jnp.where(side("core") == 0, values[0], values[1])


def outer(pieces, orders, parts=(1,)):
    rows, tokens = pieces[0][0].shape
    double = all(piece[4] % 2 == 0 and piece[5] % 2 == 0 for piece in pieces)
    block = (4 if double else 2) * LANES
    table = []
    for place in range(16):
        entries = []
        for order in orders:
            bits = [place >> 3 & 1, place >> 2 & 1, place >> 1 & 1, place & 1]
            first = side(order[0]) ^ bits[0]
            rest = sum(bit * WEIGHTS[way] for bit, way in zip(bits[1:], order[1:]))
            entries.append(first * WEIGHTS[order[0]] + rest)
        table.append(by_core(entries))
    table = jnp.stack(table).astype(jnp.int32)
    if double:
        pieces = [(*piece[:4], piece[4] // 2, piece[5] // 2) for piece in pieces]
    counts = [piece[5] for piece in pieces]
    left = pl.BlockSpec((rows, tokens), lambda j: (0, 0), pipeline_mode=pl.Buffered(1))
    lefts, rights, specs = [], [], []
    for index, piece in enumerate(pieces):
        lefts += piece[:2]
        rights += piece[2:4]

        def place(j, low=sum(counts[:index]), first=piece[4], number=piece[5]):
            return 0, first + jnp.clip(j - low, 0, number - 1)

        specs += [pl.BlockSpec((tokens, block), place)] * 2
    total = sum(counts)
    sizes = [rows // 2 * part // sum(parts) // 16 * 16 for part in parts[:-1]]
    sizes = [*sizes, rows // 2 - sum(sizes)]
    outs = [rows // 2, *sizes]
    keep, *sends = pl.pallas_call(
        lambda *refs: outer_kernel(*refs, blocks=counts, pieces=sizes),
        grid=(total,),
        in_specs=[pl.BlockSpec(memory_space=pltpu.SMEM)] + [left] * len(lefts) + specs,
        out_specs=[pl.BlockSpec((size, block), lambda j: (0, j)) for size in outs],
        out_shape=[jax.ShapeDtypeStruct((size, total * block), jnp.float32) for size in outs],
        scratch_shapes=[pltpu.VMEM((len(pieces), rows, 2 * tokens), LOW)],
        compiler_params=params(),
        cost_estimate=cost(0, 0),
        name="outer",
    )(table, *lefts, *rights)
    return keep, sends


def take(value, place, axis):
    return lax.dynamic_index_in_dim(value, place, axis, False)


class Part:
    def __init__(self, keeps, comes, orders, split_y=True):
        self.orders, self.split_y, self.stage = orders, split_y, 1
        self.groups = [[self.shaped(value) for value in group] for group in zip(keeps, comes)]
        self.terms = []

    def shaped(self, value):
        left = tuple(range(self.stage, len(self.orders[0])))
        columns = value.shape[-1]
        rows = value.size // columns // 2 ** len(left)
        return value.reshape((2,) * len(left) + (rows, columns)), left

    def add(self, come):
        self.terms.append(self.shaped(come))

    def place(self, stage):
        return by_core([side(order[stage]) for order in self.orders])

    def chosen(self, here):
        sums = [self.added(group, here) for group in self.groups]
        total = sums[0] if len(sums) == 1 else jnp.concatenate(sums, -1)
        return total + self.added(self.terms, here) if self.terms else total

    def added(self, terms, here):
        total = None
        for value, left in terms:
            starts, sizes = [], []
            for stage in left:
                fixed = stage <= self.stage
                place = self.place(stage) if fixed else 0
                starts.append(1 - place if stage == self.stage and not here else place)
                sizes.append(1 if fixed else 2)
            sizes += value.shape[len(left) :]
            starts = [jnp.asarray(start, jnp.int32) for start in [*starts, 0, 0]]
            piece = lax.dynamic_slice(value, starts, sizes)
            piece = piece.reshape([size for size in sizes[:-2] if size > 1] + sizes[-2:])
            total = piece if total is None else total + piece
        return total

    def move(self):
        if self.stage < len(self.orders[0]):
            send = self.chosen(False)
            ways = [order[self.stage] for order in self.orders]
            self.stage += 1
            self.absorb = self.add
            return send, *ways
        if self.stage == len(self.orders[0]):
            mine = self.chosen(True)
            self.stage += 1

            def absorb(come):
                self.done = in_order(mine, come) if self.split_y else mine + come

            self.absorb = absorb
            return mine, "y"
        self.absorb = lambda come: setattr(self, "other", come)
        return self.done, "core"


def in_order(mine, come):
    first = side("y") == 0
    return jnp.concatenate([jnp.where(first, mine, come), jnp.where(first, come, mine)], 0)


def advance(parts, extra=(), beside=()):
    moves = [part.move() for part in parts] + list(extra)
    values = together(*[move[0] for move in moves])
    comes = [hop(value, *move[1:]) for value, move in zip(values, moves)]
    done = together(*comes, *beside)
    for part, come in zip(parts, done):
        part.absorb(come)
    done = done[len(parts) :]
    return done[: len(extra)], done[len(extra) :]


def flatten_small(small):
    first_gain, beta, conv, head_gain, second_gain = small
    seq = lax.axis_size("seq")
    flat = jnp.concatenate(
        [
            first_gain.reshape(seq, -1), beta.reshape(seq, -1),
            conv.reshape(conv.shape[0] * conv.shape[1], seq, -1).transpose(1, 0, 2).reshape(seq, -1),
            head_gain.reshape(seq, -1), second_gain.reshape(seq, -1),
        ],
        1,
    )
    size = flat.shape[1]
    rows = -(-size // 2048) * 16
    return jnp.pad(flat, ((0, 0), (0, rows * 128 - size))).reshape(seq * rows, 128)


def unflatten_small(flat, small):
    first_gain, beta, conv, head_gain, second_gain = small
    seq = lax.axis_size("seq")
    flat = flat.reshape(-1)
    sizes = [a.size // seq for a in small]
    places = [sum(sizes[:i]) for i in range(len(sizes))]
    pieces = [flat[p : p + s] for p, s in zip(places, sizes)]
    return (
        pieces[0], pieces[1].reshape(-1, beta.shape[1]),
        pieces[2].reshape(conv.shape[0], conv.shape[1], -1), pieces[3], pieces[4],
    )


def outer_sum(left, right):
    return mxu(left.astype(LOW), right.astype(LOW), TN)


def local(
    tokens,
    doc_lengths,
    out_grad,
    first_gain,
    query_weight,
    key_weight,
    value_weight,
    gate_weight,
    beta_weight,
    conv_weight,
    head_gain,
    out_weight,
    second_gain,
    hidden_gate,
    hidden_up,
    hidden_down,
):
    count, width = (tokens.shape[1], tokens.shape[2])
    heads = beta_weight.shape[1]
    reach = conv_weight.shape[1] - 1
    first = lax.axis_index("seq") * count
    docs = jnp.concatenate([first.astype(jnp.int32)[None], doc_lengths[0]])
    core = (lax.axis_index("doc") % 2).astype(jnp.int32).reshape(1)
    here = core[0] == 0
    rows, top = tokens[0], out_grad[0]
    halo = passed_along(rows[count - HALO :].astype(jnp.float32), "seq", 1)
    normed_one, pre, features, gate_pre, beta_pre, beta, position, live = project(
        docs, rows, halo, first_gain[None], query_weight, key_weight, value_weight,
        gate_weight, beta_weight.T, conv_weight,
    )
    solved, inverses, attend, maps = prepare(docs, features, beta)
    if tuned():
        half = width // 2
        units = half // 256

        def pick(zero, one):
            return jnp.where(here, zero, one)

        def both(value, send=None):
            return value, hop(value if send is None else send, "core")

        wide_top = top.astype(jnp.float32)
        tops = both(
            pick(top[:, :half], top[:, half:]), pick(wide_top[:, half:], wide_top[:, :half])
        )
        one = both(normed_one)
    state_mine, state_other, place, context, *beside = carried_forward(
        maps, (*tops, *one) if tuned() else ()
    )
    if tuned():
        tops, one = beside[:2], beside[2:]
    starts, news, mixed, normed_head = mix(
        docs, place, features, solved, attend, gate_pre, head_gain[None], state_mine, state_other
    )
    (
        block_out, two_turned, inner_turned, kept, sent, grad_hidden, grad_branch, grad_head,
        grad_second_gain, head_turned,
    ) = feed(
        core, rows, normed_head, top, second_gain[None], out_weight, hidden_gate, hidden_up,
        hidden_down,
    )
    if tuned():
        heads_turned = both(head_turned)
        two = both(two_turned)
        gate_up = both(kept, sent)
    grad_mixed, grad_gate_pre, out_kept, out_sent, grad_head_gain, shift = gather_states(
        docs, core, grad_head, grad_branch, mixed, gate_pre, head_gain[None], features, solved, heads
    )
    if tuned():
        out_right = both(out_kept, out_sent)
        blocks = hidden_gate.shape[1] // 256
        some = blocks * 3 // 11
        blocks = hidden_gate.shape[1] // 256
        low = blocks * 8 // 11
        orders = ("x", "y", "near", "far"), ("y", "x", "far", "near")
        down_orders = ("near", "x", "y", "far"), ("near", "y", "x", "far")
        firsts = [order[0] for order in orders]
        shift, two_other, gate_up_other, inner_turned = together(
            shift, two[1], gate_up[1], inner_turned
        )
        inners = both(inner_turned)
        two, gate_up = (two[0], two_other), (gate_up[0], gate_up_other)
        out_right = both(out_kept, out_sent)
        wide_keep, wide_sends = outer([(*two, *gate_up, 0, low)], orders, (9, 9, 9, 5))
        down_keep, down_sends = outer([(*inners, *tops, 0, units)], down_orders, (3, 4))
        rest_keep, rest_sends = outer(
            [
                (*two, *gate_up, low, blocks - low), (*heads_turned, *out_right, 0, units),
                (*one, *out_right, units, units),
            ],
            orders,
        )
        work = [
            (wide_keep, *wide_sends), (down_keep, *down_sends), (rest_keep, *rest_sends), (), (),
        ]
        moves = [(), *([(send, *firsts)] for send in wide_sends)]
        grad_mine, grad_other, done = carried_back(shift, context, list(zip(moves, work)))
        down_keep, *down_sends = done[1][1:]
        rest_keep, *rest_sends = done[2][1:]
        wide_come = jnp.concatenate([value[0] for value in done[1:]], 0)
        moves = [(rest_sends[0], *firsts), (down_sends[0], "near")]
        grad_other, *values = together(grad_other, *[move[0] for move in moves])
        comes = [hop(value, *move[1:]) for value, move in zip(values, moves)]
    else:
        grad_mine, grad_other, _ = carried_back(shift, context)
    grads, borrowed, grad_conv, grad_beta_pre = back(
        docs, place, features, beta, beta_pre, solved, inverses, starts, news, grad_mixed, grad_mine,
        grad_other, pre, conv_weight, position, live,
    )
    if tuned():
        borrowed, *comes = together(borrowed, *comes)
        wide_part = Part((wide_keep, rest_keep), (wide_come, comes[0]), orders)
        down_come = comes[1]
    returned = passed_along(borrowed, "seq", -1)
    tail = grads[:, count - 8 :] + returned
    grads = lax.dynamic_update_slice(grads, tail, (0, count - 8, 0))
    grads = grads.astype(LOW)
    if tuned():
        moves = [wide_part.move(), (down_sends[1], "near")]
        grads, *values = together(grads, *[move[0] for move in moves])
        comes = [hop(value, *move[1:]) for value, move in zip(values, moves)]
        wide = grads.astype(jnp.float32)
        query_key = both(pick(grads[0], grads[1]), pick(wide[1], wide[0]))
        value = both(
            pick(grads[2, :, :half], grads[2, :, half:]), pick(wide[2, :, half:], wide[2, :, :half])
        )
        late_keep, (late_send,) = outer(
            [(*one, *query_key, 0, 2 * units), (*one, *value, 0, units)], orders
        )
        grads, late_send, *comes = together(grads, late_send, *comes)
        wide_part.absorb(comes[0])
        down = Part((down_keep,), (jnp.concatenate([down_come, comes[1]], 0),), down_orders)
        input_grad, grad_first_gain = enter(
            rows, first_gain[None], grad_hidden, grads, grad_gate_pre, grad_beta_pre, query_weight,
            key_weight, value_weight, gate_weight, beta_weight.T,
        )
        small = (
            grad_first_gain[0], outer_sum(normed_one.T, grad_beta_pre), grad_conv, grad_head_gain[0],
            grad_second_gain[0],
        )
        flat = flatten_small(small)
        (come,), (flat, input_grad) = advance(
            [wide_part, down], [(late_send, *firsts)], (flat, input_grad)
        )
        late = Part((late_keep,), (come,), orders)
        (come,), _ = advance([late, wide_part, down], [(flat, "core")])
        flat = (flat + come).reshape(2, 2, 2, -1, 128).transpose(2, 1, 0, 3, 4)
        bit = side("x")
        tiny_keep, tiny_send = (take(flat, place, 0).reshape(-1, 128) for place in (bit, 1 - bit))
        (come,), _ = advance([late, down, wide_part], [(tiny_send, "x")])
        tiny = Part((tiny_keep,), (come,), (("x", "near", "far"),) * 2, False)
        advance([late, down, wide_part, tiny])
        advance([late, down, tiny])
        advance([late, tiny])
        zero = lambda part: pick(part.done, part.other)
        one_ = lambda part: pick(part.other, part.done)
        split = blocks * 256
        hidden_gate_g, hidden_up_g = (
            of(wide_part)[:, : blocks * 256] for of in (zero, one_)
        )
        out_g, gate_g = (
            jnp.concatenate([zero(wide_part)[:, places], one_(wide_part)[:, places]], 1)
            for places in (slice(split, split + half), slice(split + half, split + width))
        )
        query_g, key_g = zero(late)[:, :width], one_(late)[:, :width]
        value_g = jnp.concatenate([zero(late)[:, width:], one_(late)[:, width:]], 1)
        hidden_down_g = jnp.concatenate([zero(down), one_(down)], 1)
        first_g, beta_g, conv_g, head_g, second_g = unflatten_small(tiny.done, small)
    else:
        input_grad, grad_first_gain = enter(
            rows, first_gain[None], grad_hidden, grads, grad_gate_pre, grad_beta_pre, query_weight,
            key_weight, value_weight, gate_weight, beta_weight.T,
        )
        small = (
            grad_first_gain[0], outer_sum(normed_one.T, grad_beta_pre), grad_conv, grad_head_gain[0],
            grad_second_gain[0],
        )

        def whole(term, dimension):
            part = lax.psum_scatter(term, "seq", scatter_dimension=dimension, tiled=True)
            return lax.psum(part, "doc")

        gate_grad, up_grad = jnp.where(here, kept, sent), jnp.where(here, sent, kept)
        terms = (
            outer_sum(normed_one.T, grads[0]), outer_sum(normed_one.T, grads[1]),
            outer_sum(normed_one.T, grads[2]), outer_sum(normed_one.T, grad_gate_pre),
            outer_sum(head_turned.T, grad_branch), outer_sum(two_turned.T, gate_grad),
            outer_sum(two_turned.T, up_grad), outer_sum(inner_turned.T, top),
        )
        query_g, key_g, value_g, gate_g, out_g, hidden_gate_g, hidden_up_g, hidden_down_g = (
            whole(term, 0) for term in terms
        )
        first_g, beta_g, conv_g, head_g, second_g = (
            whole(term, d) for term, d in zip(small, (0, 0, 2, 0, 0))
        )
    return (
        block_out[None], input_grad[None], first_g, query_g, key_g, value_g, gate_g, beta_g, conv_g,
        head_g, out_g, second_g, hidden_gate_g, hidden_up_g, hidden_down_g,
    )


def solution(mesh):
    in_specs = (
        P("doc", "seq", None),
        P("doc", None),
        P("doc", "seq", None),
        P(),
        P(),
        P(),
        P(),
        P(),
        P(),
        P(),
        P(),
        P(),
        P(),
        P(),
        P(),
        P(),
    )
    out_specs = (
        P("doc", "seq", None),
        P("doc", "seq", None),
        P("seq"),
        P("seq", None),
        P("seq", None),
        P("seq", None),
        P("seq", None),
        P("seq", None),
        P(None, None, "seq"),
        P("seq"),
        P("seq", None),
        P("seq"),
        P("seq", None),
        P("seq", None),
        P("seq", None),
    )
    return jax.shard_map(local, mesh=mesh, in_specs=in_specs, out_specs=out_specs, check_vma=False)
```

```python
import jax
import jax.numpy as jnp
from jax import lax
from jax.experimental import pallas as pl
from jax.experimental.pallas import tpu as pltpu
from jax.sharding import PartitionSpec as P

CK = 64


EPS = 1e-05
KEY_EPS = 1e-06
HIGH = lax.Precision.HIGHEST


SPAN = CK
LANES = 128
LOW = jnp.bfloat16
NN = (((1,), (0,)), ((), ()))
NT = (((1,), (1,)), ((), ()))
TN = (((0,), (0,)), ((), ()))


def params(mib=54):
    return pltpu.CompilerParams(vmem_limit_bytes=mib * 2**20)


def cost(flops, moved):
    return pl.CostEstimate(flops=1, bytes_accessed=1, transcendentals=0)


def mxu(left, right, dims):
    return lax.dot_general(left, right, dims, preferred_element_type=jnp.float32)


def halves(value):
    high = value.astype(LOW)
    return high, (value - high.astype(jnp.float32)).astype(LOW)


def split(value):
    return value if isinstance(value, tuple) else halves(value)


def stack(first, second):
    return tuple(jnp.concatenate(both, 0) for both in zip(first, second))


def fold(value):
    half = value.shape[1] // 2
    return value[:, :half] + value[:, half:]


def product(left, right):
    left_high, left_low = split(left)
    right_high, right_low = split(right)
    both = jnp.concatenate([left_high, left_low], 1)
    if right_high.shape[1] <= LANES:
        wide = jnp.concatenate([right_high, right_low], 1)
        return fold(mxu(both, jnp.concatenate([wide, wide], 0), NN))
    return mxu(both, jnp.concatenate([right_high, right_high], 0), NN) + mxu(
        left_high, right_low, NN
    )


def product_t(left, right):
    left_high, left_low = split(left)
    right_high, right_low = split(right)
    both = jnp.concatenate([left_high, left_low], 1)
    if right_high.shape[0] <= LANES:
        rows = jnp.concatenate(
            [
                jnp.concatenate([right_high, right_high], 1),
                jnp.concatenate([right_low, right_low], 1),
            ],
            0,
        )
        return fold(mxu(both, rows, NT))
    return mxu(both, jnp.concatenate([right_high, right_high], 1), NT) + mxu(
        left_high, right_low, NT
    )


def t_product(left, right):
    left_high, left_low = split(left)
    right_high, right_low = split(right)
    both = jnp.concatenate([left_high, left_low], 0)
    if right_high.shape[1] <= LANES:
        wide = jnp.concatenate([right_high, right_low], 1)
        return fold(mxu(both, jnp.concatenate([wide, wide], 0), TN))
    return mxu(both, jnp.concatenate([right_high, right_high], 0), TN) + mxu(
        left_high, right_low, TN
    )


def head(value, h):
    return value[:, h * LANES : (h + 1) * LANES]


def pair(value, p):
    return jnp.concatenate([head(value, 2 * p), head(value, 2 * p + 1)], 0)


def pair_column(value, p):
    return jnp.concatenate([value[:, 2 * p : 2 * p + 1], value[:, 2 * p + 1 : 2 * p + 2]], 0)


def masks(rows):
    i = lax.broadcasted_iota(jnp.int32, (rows, rows), 0)
    j = lax.broadcasted_iota(jnp.int32, (rows, rows), 1)
    same = (i >= SPAN) == (j >= SPAN)
    strict = jnp.where(same & (j < i), 1.0, 0.0)
    inclusive = jnp.where(same & (j <= i), 1.0, 0.0)
    upper = jnp.where(same & (j >= i), 1.0, 0.0)
    return strict, inclusive, upper, jnp.where(i == j, 1.0, 0.0)


def inverses_of(strict_parts, identity):
    rows = identity.shape[0]
    results = [identity - part for part in strict_parts]
    powers = [split(part) for part in strict_parts]
    powers = [split(product(power, power)) for power in powers]
    for level in range(SPAN.bit_length() - 3):
        both = [
            product(stack(split(result), power), power) for result, power in zip(results, powers)
        ]
        results = [result + pair_[:rows] for result, pair_ in zip(results, both)]
        powers = [split(pair_[rows:]) for pair_ in both]
    return [result + product(result, power) for result, power in zip(results, powers)]


def sigmoid(value):
    return 1.0 / (1.0 + jnp.exp(-value))


def doc_starts(docs):
    begin = jnp.int32(0)
    for index in range(1, docs.shape[0]):
        yield begin, docs[index]
        begin = begin + jnp.bitwise_and(docs[index] + (SPAN - 1), -SPAN)


def span_flag(docs, span):
    place, flag = docs[0] + span * SPAN, jnp.float32(1.0)
    for begin, _ in doc_starts(docs):
        flag = jnp.where(begin == place, 0.0, flag)
    return flag


def token_places(docs, count):
    place = docs[0] + lax.broadcasted_iota(jnp.int32, (count, 1), 0)
    position, live = place, jnp.zeros((count, 1), jnp.float32)
    for begin, length in doc_starts(docs):
        here = place >= begin
        position = jnp.where(here, place - begin, position)
        live = jnp.where(here, jnp.where(place - begin < length, 1.0, 0.0), live)
    return position, live


HALO = 16


def project_kernel(
    docs, tokens, halo, gain, query_w, key_w, value_w, gate_w, beta_w, conv,
    normed_out, pre_out, feature_out, gate_out, beta_pre_out, beta_out, position, live, normed, pre,
):
    count = tokens.shape[0]

    @pl.when(pl.program_id(0) == 0)
    def _():
        def norm(rows):
            return (
                rows * lax.rsqrt(jnp.mean(rows * rows, -1, keepdims=True) + EPS) * gain[...]
            ).astype(LOW)

        normed[:HALO, :] = norm(halo[...])
        rounded = norm(tokens[...].astype(jnp.float32))
        normed[HALO:, :] = rounded
        beta_pre = mxu(rounded, beta_w[...], NT)
        beta_pre_out[...] = beta_pre
        position[...], live[...] = token_places(docs, count)
        beta_out[...] = sigmoid(beta_pre) * live[...]

    lanes = pl.ds(pl.multiple_of(pl.program_id(0) * normed_out.shape[0], LANES), normed_out.shape[0])
    normed_out[...] = normed[HALO:, lanes].astype(jnp.float32).T
    gate_out[...] = mxu(normed[HALO:, :], gate_w[...], NN)
    valid = [
        jnp.broadcast_to(
            jnp.where(position[...] >= conv.shape[1] - 1 - tap, 1.0, 0.0), (count, LANES)
        )
        for tap in range(conv.shape[1] - 1)
    ]
    for which, weight in enumerate((query_w, key_w, value_w)):
        pre[which] = mxu(normed[...], weight[...], NN)
        for span in range(count // SPAN):
            start = HALO + span * SPAN
            pre_out[which, span] = pre[which, start - 8 : start + SPAN, :]
        for part in range(pre.shape[2] // LANES):
            lanes = slice(part * LANES, (part + 1) * LANES)
            total = conv_total(pre, which, HALO, count, lanes, conv, valid)
            value = total * sigmoid(total)
            if which < 2:
                value = value * lax.rsqrt(jnp.sum(value * value, -1, keepdims=True) + KEY_EPS)
            if which == 1:
                value = value * live[...]
            feature_out[which, :, lanes] = value


def conv_total(pre, which, first, count, lanes, conv, valid):
    taps = conv.shape[1]
    total = None
    for tap in range(taps):
        start = first - (taps - 1) + tap
        term = conv[which, tap : tap + 1, lanes] * pre[which, start : start + count, lanes]
        if tap < taps - 1:
            term = term * valid[tap]
        total = term if total is None else total + term
    return total


def project(docs, tokens, halo, gain, query_w, key_w, value_w, gate_w, beta_w, conv):
    count, width = tokens.shape
    heads = beta_w.shape[0]
    block = 2 * LANES
    whole = lambda shape: pl.BlockSpec(shape, lambda j: (0,) * len(shape))
    weight = pl.BlockSpec((width, block), lambda j: (0, j))
    f32 = lambda shape: jax.ShapeDtypeStruct(shape, jnp.float32)
    return pl.pallas_call(
        project_kernel,
        grid=(width // block,),
        in_specs=[
            pl.BlockSpec(memory_space=pltpu.SMEM), whole((count, width)), whole((HALO, width)),
            whole((1, width)), weight, weight, weight, weight, whole((heads, width)),
            pl.BlockSpec((3, conv.shape[1], block), lambda j: (0, 0, j)),
        ],
        out_specs=[
            pl.BlockSpec((block, count), lambda j: (j, 0)),
            pl.BlockSpec((3, count // SPAN, SPAN + 8, block), lambda j: (0, 0, 0, j)),
            pl.BlockSpec((3, count, block), lambda j: (0, 0, j)),
            pl.BlockSpec((count, block), lambda j: (0, j)),
            whole((count, heads)), whole((count, heads)), whole((count, 1)), whole((count, 1)),
        ],
        out_shape=[
            f32((width, count)), f32((3, count // SPAN, SPAN + 8, width)), f32((3, count, width)),
            f32((count, width)), f32((count, heads)), f32((count, heads)),
            jax.ShapeDtypeStruct((count, 1), jnp.int32), f32((count, 1)),
        ],
        scratch_shapes=[
            pltpu.VMEM((HALO + count, width), LOW),
            pltpu.VMEM((3, HALO + count, block), jnp.float32),
        ],
        compiler_params=params(),
        cost_estimate=cost(8 * count * width * width, 8 * width * width + 40 * count * width),
        name="project",
    )(docs, tokens, halo, gain, query_w, key_w, value_w, gate_w, beta_w, conv)


def prepare_kernel(docs, features, beta, solved_out, inverse_out, attend_out, state):
    span = pl.program_id(0)
    heads = state.shape[0]
    size = state.shape[1]
    strict, inclusive, upper, identity = masks(2 * SPAN)

    @pl.when(span == 0)
    def _():
        i = lax.broadcasted_iota(jnp.int32, (size, 2 * size), 0)
        j = lax.broadcasted_iota(jnp.int32, (size, 2 * size), 1)
        for h in range(heads):
            state[h] = jnp.where(j == i + size, 1.0, 0.0)

    query, key, value = features[0], features[1], features[2]
    betas = beta[...]
    flag = span_flag(docs, span)
    pairs = range(heads // 2)
    keys = [split(pair(key, p)) for p in pairs]
    columns = [pair_column(betas, p) for p in pairs]
    scores = [product_t(stack(keys[p], split(pair(query, p))), keys[p]) for p in pairs]
    solved = inverses_of([columns[p] * scores[p][: 2 * SPAN] * strict for p in pairs], identity)
    both = [
        product(
            solved[p],
            jnp.concatenate([columns[p] * pair(key, p), columns[p] * pair(value, p)], 1),
        )
        for p in pairs
    ]
    for p in pairs:
        inverse_out[0, p] = solved[p]
        attend_out[0, p] = scores[p][2 * SPAN :] * inclusive
    starts, news = [], []
    for h in range(heads):
        rows = slice(h % 2 * SPAN, (h % 2 + 1) * SPAN)
        erase, update = both[h // 2][rows, :size], both[h // 2][rows, size:]
        solved_out[0, :, h * size : (h + 1) * size] = erase
        solved_out[1, :, h * size : (h + 1) * size] = update
        start = state[h] * flag
        starts.append(start)
        news.append(
            jnp.concatenate([update, jnp.zeros_like(update)], 1) - product(erase, start)
        )
    for h in range(heads):
        rows = slice(h % 2 * SPAN, (h % 2 + 1) * SPAN)
        state[h] = starts[h] + t_product(tuple(k[rows] for k in keys[h // 2]), news[h])


def prepare(docs, features, beta):
    _, count, width = features.shape
    heads = beta.shape[1]
    size = width // heads
    spans = count // SPAN
    f32 = lambda shape: jax.ShapeDtypeStruct(shape, jnp.float32)
    matrix = pl.BlockSpec((1, heads // 2, 2 * SPAN, 2 * SPAN), lambda c: (c, 0, 0, 0))
    return pl.pallas_call(
        prepare_kernel,
        grid=(spans,),
        in_specs=[
            pl.BlockSpec(memory_space=pltpu.SMEM),
            pl.BlockSpec((3, SPAN, width), lambda c: (0, c, 0)),
            pl.BlockSpec((SPAN, heads), lambda c: (c, 0)),
        ],
        out_specs=[
            pl.BlockSpec((2, SPAN, width), lambda c: (0, c, 0)), matrix, matrix,
            pl.BlockSpec((heads, size, 2 * size), lambda c: (0, 0, 0)),
        ],
        out_shape=[
            f32((2, count, width)), f32((spans, heads // 2, 2 * SPAN, 2 * SPAN)),
            f32((spans, heads // 2, 2 * SPAN, 2 * SPAN)), f32((heads, size, 2 * size)),
        ],
        compiler_params=params(),
        cost_estimate=cost(40 * count * width * size * 4, 60 * count * width),
        name="prepare",
    )(docs, features, beta)


def mix_kernel(
    docs, place, features, solved, attend, gate, gain, state_mine, state_other, starts_out, new_out,
    mixed_out, normed_out, state,
):
    span = pl.program_id(0)
    heads = state.shape[0]

    @pl.when(span == 0)
    def _():
        half = heads // 2
        first = place[0] == 0
        state[:half] = jnp.where(first, state_mine[...], state_other[...])
        state[half:] = jnp.where(first, state_other[...], state_mine[...])

    query, key = features[0], features[1]
    erase, update = solved[0], solved[1]
    flag = span_flag(docs, span)
    every, pairs = range(heads), range(heads // 2)
    starts = [state[h] * flag for h in every]
    both = [
        product(jnp.concatenate([head(erase, h), head(query, h)], 0), starts[h]) for h in every
    ]
    news = [split(head(update, h) - both[h][:SPAN]) for h in every]
    after = [starts[h] + t_product(head(key, h), news[h]) for h in every]
    inner = [product(attend[0, p], stack(news[2 * p], news[2 * p + 1])) for p in pairs]
    for h in every:
        lanes = slice(h * LANES, (h + 1) * LANES)
        starts_out[0, h] = starts[h]
        state[h] = after[h]
        new_out[:, lanes] = head(update, h) - both[h][:SPAN]
        rows = both[h][SPAN:] + inner[h // 2][h % 2 * SPAN : (h % 2 + 1) * SPAN]
        mixed_out[:, lanes] = rows
        shaped = rows * lax.rsqrt(jnp.mean(rows * rows, -1, keepdims=True) + EPS) * gain[...]
        gates = gate[:, lanes]
        normed_out[:, lanes] = (shaped * (gates * sigmoid(gates))).astype(LOW)


def mix(docs, place, features, solved, attend, gate, gain, state_mine, state_other):
    _, count, width = features.shape
    half, size, _ = state_mine.shape
    heads = 2 * half
    spans = count // SPAN
    f32 = lambda shape: jax.ShapeDtypeStruct(shape, jnp.float32)
    rows = pl.BlockSpec((SPAN, width), lambda c: (c, 0))
    pairs = pl.BlockSpec((2, SPAN, width), lambda c: (0, c, 0))
    return pl.pallas_call(
        mix_kernel,
        grid=(spans,),
        in_specs=[
            pl.BlockSpec(memory_space=pltpu.SMEM), pl.BlockSpec(memory_space=pltpu.SMEM), pairs, pairs,
            pl.BlockSpec((1, heads // 2, 2 * SPAN, 2 * SPAN), lambda c: (c, 0, 0, 0)),
            rows, pl.BlockSpec((1, size), lambda c: (0, 0)),
            pl.BlockSpec((half, size, size), lambda c: (0, 0, 0)),
            pl.BlockSpec((half, size, size), lambda c: (0, 0, 0)),
        ],
        out_specs=[
            pl.BlockSpec((1, heads, size, size), lambda c: (c, 0, 0, 0)), rows, rows, rows,
        ],
        out_shape=[
            f32((spans, heads, size, size)), f32((count, width)), f32((count, width)),
            jax.ShapeDtypeStruct((count, width), LOW),
        ],
        scratch_shapes=[pltpu.VMEM((heads, size, size), jnp.float32)],
        compiler_params=params(),
        cost_estimate=cost(8 * count * width * size * 4, 40 * count * width),
        name="mix",
    )(docs, place, features, solved, attend, gate, gain, state_mine, state_other)


def feed_kernel(
    core, tokens, normed_head, grad_top, second_gain, out_w, gate_w, up_w, down_w,
    block_out, normed_out, inner_out, kept_out, sent_out, grad_hidden_out, branch_out, grad_head_out,
    gain_grad_out, head_turned_out, hidden, normed, total, grad_total,
):
    step = pl.program_id(0)

    @pl.when(step == 0)
    def _():
        state = tokens[...].astype(jnp.float32) + mxu(normed_head[...], out_w[...], NN)
        hidden[...] = state
        rounded = (
            state * lax.rsqrt(jnp.mean(state * state, -1, keepdims=True) + EPS) * second_gain[...]
        ).astype(LOW)
        normed[...] = rounded

    @pl.when(step == 0)
    def _():
        total[...] = jnp.zeros_like(total)
        grad_total[...] = jnp.zeros_like(grad_total)

    first = core[0] == 0
    size = normed.shape[0] // 1
    parts = [slice(i * size, (i + 1) * size) for i in range(1)]
    @pl.when(step < normed.shape[1] // LANES)
    def _():
        lanes = pl.ds(pl.multiple_of(step * LANES, LANES), LANES)
        normed_out[...] = normed[:, lanes].astype(jnp.float32).T
        head_turned_out[...] = normed_head[:, lanes].astype(jnp.float32).T

    gates = [mxu(normed[part, :], gate_w[...], NN) for part in parts]
    ups = [mxu(normed[part, :], up_w[...], NN) for part in parts]
    grad_inners = [mxu(grad_top[part, :], down_w[...], NT) for part in parts]
    for part, gate, up, grad_inner in zip(parts, gates, ups, grad_inners):
        sigma = sigmoid(gate)
        act = gate * sigma
        inner = (act * up).astype(LOW)
        inner_out[:, part] = inner.astype(jnp.float32).T
        wide_gate = grad_inner * up * (sigma + act * (1.0 - sigma))
        wide_up = grad_inner * act
        grad_gate, grad_up = wide_gate.astype(LOW), wide_up.astype(LOW)
        kept_out[part, :] = jnp.where(first, wide_gate, wide_up).astype(LOW)
        sent_out[part, :] = jnp.where(first, wide_up, wide_gate).astype(LOW).astype(jnp.float32)
        total[part, :] += mxu(inner, down_w[...], NN)
        grad_total[part, :] += mxu(grad_gate, gate_w[...], NT) + mxu(grad_up, up_w[...], NT)

    @pl.when(step == pl.num_programs(0) - 1)
    def _():
        state = hidden[...]
        block_out[...] = (state + total[...]).astype(LOW)
        part, gain_part = norm_back(state, second_gain[...], grad_total[...])
        gain_grad_out[...] = gain_part
        grad_hidden = grad_top[...].astype(jnp.float32) + part
        grad_hidden_out[...] = grad_hidden
        branch = grad_hidden.astype(LOW)
        branch_out[...] = branch
        grad_head_out[...] = mxu(branch, out_w[...], NT)


def norm_back(value, gain, grad):
    scale = lax.rsqrt(jnp.mean(value * value, -1, keepdims=True) + EPS)
    unit = value * scale
    gain_grad = jnp.sum(grad * unit, 0, keepdims=True)
    inward = grad * gain
    return scale * (inward - unit * jnp.mean(inward * unit, -1, keepdims=True)), gain_grad


def feed(core, tokens, normed_head, grad_top, second_gain, out_w, gate_w, up_w, down_w):
    count, width = tokens.shape
    hidden = gate_w.shape[1]
    block = 2 * LANES
    whole = lambda shape: pl.BlockSpec(shape, lambda j: (0,) * len(shape))
    f32 = lambda shape: jax.ShapeDtypeStruct(shape, jnp.float32)
    low = lambda shape: jax.ShapeDtypeStruct(shape, LOW)
    rows = whole((count, width))
    columns = pl.BlockSpec((count, block), lambda j: (0, j))
    turned = pl.BlockSpec((LANES, count), lambda j: (jnp.minimum(j, width // LANES - 1), 0))
    return pl.pallas_call(
        feed_kernel,
        grid=(hidden // block,),
        in_specs=[
            pl.BlockSpec(memory_space=pltpu.SMEM), rows, rows, rows, whole((1, width)),
            whole((width, width)), pl.BlockSpec((width, block), lambda j: (0, j)),
            pl.BlockSpec((width, block), lambda j: (0, j)),
            pl.BlockSpec((block, width), lambda j: (j, 0)),
        ],
        out_specs=[
            rows, turned, pl.BlockSpec((block, count), lambda j: (j, 0)), columns,
            columns, rows, rows, rows, whole((1, width)), turned,
        ],
        out_shape=[
            low((count, width)), f32((width, count)), f32((hidden, count)), low((count, hidden)),
            f32((count, hidden)), f32((count, width)), low((count, width)), f32((count, width)),
            f32((1, width)), f32((width, count)),
        ],
        scratch_shapes=[
            pltpu.VMEM((count, width), jnp.float32), pltpu.VMEM((count, width), LOW),
            pltpu.VMEM((count, width), jnp.float32), pltpu.VMEM((count, width), jnp.float32),
        ],
        compiler_params=params(),
        cost_estimate=cost(
            12 * count * width * hidden + 4 * count * width * width,
            6 * width * hidden + 10 * count * hidden + 30 * count * width,
        ),
        name="feed",
    )(core, tokens, normed_head, grad_top, second_gain, out_w, gate_w, up_w, down_w)


def gather_kernel(
    docs, core, grad_head, grad_branch, mixed, gate, gain, features, solved, grad_mixed_out,
    grad_gate_out, kept_out, sent_out, gain_out, state,
):
    step = pl.program_id(0)
    span = pl.num_programs(0) - 1 - step
    heads = state.shape[0]
    strict, inclusive, upper, identity = masks(2 * SPAN)

    @pl.when(step == 0)
    def _():
        state[...] = jnp.zeros_like(state)
        gain_out[...] = jnp.zeros_like(gain_out)

    query, key = features[0], features[1]
    erase = solved[0]
    flag = span_flag(docs, span)
    gain_total = jnp.zeros_like(gain_out[...])
    every, pairs = range(heads), range(heads // 2)
    passes = [product_t(pair(key, p), pair(query, p)) * upper for p in pairs]
    grads = []
    for h in every:
        lanes = slice(h * LANES, (h + 1) * LANES)
        gates = gate[:, lanes]
        sigma = sigmoid(gates)
        rows = mixed[:, lanes]
        grad = grad_head[:, lanes]
        scale = lax.rsqrt(jnp.mean(rows * rows, -1, keepdims=True) + EPS)
        unit = rows * scale
        grad_gate = grad * unit * gain[...] * sigma * (1.0 + gates * (1.0 - sigma))
        grad_gate = grad_gate.astype(LOW).astype(jnp.float32)
        grad_gate_out[:, lanes] = grad_gate
        shaped = grad * gates * sigma
        gain_total = gain_total + jnp.sum(shaped * unit, 0, keepdims=True)
        inward = shaped * gain[...]
        grad_rows = scale * (inward - unit * jnp.mean(inward * unit, -1, keepdims=True))
        grad_mixed_out[:, lanes] = grad_rows
        grads.append(split(grad_rows))
    passed = [product(passes[p], stack(grads[2 * p], grads[2 * p + 1])) for p in pairs]
    ends = [state[h] for h in every]
    grad_new = [
        passed[h // 2][h % 2 * SPAN : (h % 2 + 1) * SPAN] + product(head(key, h), ends[h])
        for h in every
    ]
    for h in every:
        state[h] = flag * (
            ends[h]
            + t_product(
                jnp.concatenate([head(query, h), -head(erase, h)], 0),
                stack(grads[h], split(grad_new[h])),
            )
        )
    gain_out[...] += gain_total
    half = grad_branch.shape[1] // 2
    first = core[0] == 0
    for place, source in ((0, grad_branch), (half, grad_gate_out)):
        low, high = source[:, :half], source[:, half:]
        low, high = low.astype(jnp.float32), high.astype(jnp.float32)
        kept_out[:, place : place + half] = jnp.where(first, low, high).astype(LOW)
        sent_out[:, place : place + half] = jnp.where(first, high, low)


def gather_states(
    docs, core, grad_head, grad_branch, mixed, gate, gain, features, solved, heads
):
    _, count, width = features.shape
    size = width // heads
    spans = count // SPAN
    f32 = lambda shape: jax.ShapeDtypeStruct(shape, jnp.float32)
    rows = pl.BlockSpec((SPAN, width), lambda c: (spans - 1 - c, 0))
    pairs = pl.BlockSpec((2, SPAN, width), lambda c: (0, spans - 1 - c, 0))
    one = pl.BlockSpec((1, SPAN, width), lambda c: (0, spans - 1 - c, 0))
    return pl.pallas_call(
        gather_kernel,
        grid=(spans,),
        in_specs=[
            pl.BlockSpec(memory_space=pltpu.SMEM), pl.BlockSpec(memory_space=pltpu.SMEM), rows, rows,
            rows, rows, pl.BlockSpec((1, size), lambda c: (0, 0)), pairs, one,
        ],
        out_specs=[
            rows, rows, rows, rows, pl.BlockSpec((1, size), lambda c: (0, 0)),
            pl.BlockSpec((heads, size, size), lambda c: (0, 0, 0)),
        ],
        out_shape=[
            f32((count, width)), f32((count, width)), jax.ShapeDtypeStruct((count, width), LOW),
            f32((count, width)), f32((1, size)), f32((heads, size, size)),
        ],
        compiler_params=params(),
        cost_estimate=cost(8 * count * width * size * 4, 32 * count * width),
        name="gather_states",
    )(docs, core, grad_head, grad_branch, mixed, gate, gain, features, solved)


def back_kernel(
    docs, place, features, beta, beta_pre, solved, inverses, starts, news, grad_mixed, state_mine,
    state_other, pre, conv, position, live, grad_pre_out, borrowed_out, conv_out, grad_beta_out, state, later, sums,
):
    step = pl.program_id(0)
    span = pl.num_programs(0) - 1 - step
    heads = state.shape[0]
    taps = conv.shape[1]
    strict, inclusive, upper, identity = masks(2 * SPAN)

    @pl.when(step == 0)
    def _():
        half = heads // 2
        first = place[0] == 0
        state[:half] = jnp.where(first, state_mine[...], state_other[...])
        state[half:] = jnp.where(first, state_other[...], state_mine[...])
        sums[...] = jnp.zeros_like(sums)
        later[...] = jnp.zeros_like(later)

    query, key, value = features[0], features[1], features[2]
    erase, update = solved[0], solved[1]
    betas = beta[...]
    flag = span_flag(docs, span)
    base = pl.multiple_of(span * SPAN, SPAN)
    places = position[pl.ds(base, SPAN), :]
    lives = live[pl.ds(base, SPAN), :]
    valid = [
        jnp.broadcast_to(jnp.where(places >= taps - 1 - tap, 1.0, 0.0), (SPAN, LANES))
        for tap in range(taps - 1)
    ]
    every, pairs = range(heads), range(heads // 2)
    part = [slice(h % 2 * SPAN, (h % 2 + 1) * SPAN) for h in every]
    q = [split(pair(query, p)) for p in pairs]
    k = [split(pair(key, p)) for p in pairs]
    b = [pair_column(betas, p) for p in pairs]
    grad_out = [split(pair(grad_mixed, p)) for p in pairs]
    new = [split(pair(news, p)) for p in pairs]
    erases = [split(pair(erase, p)) for p in pairs]
    row = lambda value, h: tuple(v[part[h]] for v in value[h // 2])
    scores = [product_t(k[p], stack(k[p], q[p])) for p in pairs]
    passed = [product(scores[p][:, 2 * SPAN :] * upper, grad_out[p]) for p in pairs]
    ends = [split(state[h]) for h in every]
    begin = [split(starts[0, h]) for h in every]
    grad_new = [passed[h // 2][part[h]] + product(row(k, h), ends[h]) for h in every]
    grad_news = [split(value) for value in grad_new]
    both = [product_t(stack(row(grad_out, h), grad_news[h]), begin[h]) for h in every]
    grad_key = [product_t(row(new, h), ends[h]) for h in every]
    for h in every:
        state[h] = flag * (
            state[h]
            + t_product(
                stack(row(q, h), tuple(-v for v in row(erases, h))),
                stack(row(grad_out, h), grad_news[h]),
            )
        )
    grad_attend = [product_t(grad_out[p], new[p]) * inclusive for p in pairs]
    joined = lambda values, p: jnp.concatenate([values[2 * p], values[2 * p + 1]], 0)
    grad_q = [
        joined([value[:SPAN] for value in both], p) + product(grad_attend[p], k[p]) for p in pairs
    ]
    grad_k = [joined(grad_key, p) + product(grad_attend[p].T, q[p]) for p in pairs]
    turned = [
        product(
            inverses[0, p].T,
            jnp.concatenate(
                [joined(grad_new, p), -joined([value[SPAN:] for value in both], p)], 1
            ),
        )
        for p in pairs
    ]
    grad_bv = [value[:, :LANES] for value in turned]
    grad_bk = [value[:, LANES:] for value in turned]
    grad_lower = [
        -strict * (product_t(grad_bv[p], pair(update, p)) + product_t(grad_bk[p], erases[p]))
        for p in pairs
    ]
    inner = [b[p] * grad_lower[p] for p in pairs]
    grad_k = [
        grad_k[p] + product(inner[p] + inner[p].T, k[p]) + b[p] * grad_bk[p] for p in pairs
    ]
    grad_v = [b[p] * grad_bv[p] for p in pairs]
    beta_columns = []
    for p in pairs:
        grad_b = (
            jnp.sum(grad_lower[p] * scores[p][:, : 2 * SPAN], -1, keepdims=True)
            + jnp.sum(grad_bv[p] * pair(value, p), -1, keepdims=True)
            + jnp.sum(grad_bk[p] * pair(key, p), -1, keepdims=True)
        )
        beta_columns += [grad_b[:SPAN], grad_b[SPAN:]]
    chunks = [(which, h) for which in range(3) for h in every]
    for start in range(0, len(chunks), 4):
        group = chunks[start : start + 4]
        places = [(which, slice(h * LANES, (h + 1) * LANES)) for which, h in group]
        grads = [(grad_q, grad_k, grad_v)[which][h // 2][part[h]] for which, h in group]
        shifted = [
            [
                pre[which, 0, pl.ds(8 - (taps - 1) + tap, SPAN), lanes]
                for tap in range(taps)
            ]
            for which, lanes in places
        ]
        shifted = [
            [value * valid[tap] for tap, value in enumerate(moved[:-1])] + moved[-1:]
            for moved in shifted
        ]
        totals = [
            sum(
                conv[which, tap : tap + 1, lanes] * moved[tap] for tap in range(taps)
            )
            for moved, (which, lanes) in zip(shifted, places)
        ]
        sigmas = [sigmoid(total) for total in totals]
        acts = [total * sigma for total, sigma in zip(totals, sigmas)]
        slopes = [sigma + act * (1.0 - sigma) for sigma, act in zip(sigmas, acts)]
        squares = [
            jnp.sum(act * act, -1, keepdims=True) if which < 2 else None
            for act, (which, _) in zip(acts, group)
        ]
        grads = [
            grad * lives if which == 1 else grad for grad, (which, _) in zip(grads, group)
        ]
        scales = [None if square is None else lax.rsqrt(square + KEY_EPS) for square in squares]
        units = [act if scale is None else act * scale for act, scale in zip(acts, scales)]
        along = [
            None if scale is None else jnp.sum(grad * unit, -1, keepdims=True)
            for grad, unit, scale in zip(grads, units, scales)
        ]
        grads = [
            slope * (grad if scale is None else scale * (grad - unit * dot))
            for slope, grad, scale, unit, dot in zip(slopes, grads, scales, units, along)
        ]
        for grad, moved, (which, lanes) in zip(grads, shifted, places):
            result = conv[which, taps - 1 : taps, lanes] * grad
            for tap in range(taps):
                product_ = grad * moved[tap]
                sums[which, tap, :, lanes] += sum(
                    product_[8 * r : 8 * (r + 1)] for r in range(SPAN // 8)
                )
                if tap < taps - 1:
                    masked = grad * valid[tap]
                    later[which, tap, SPAN:, lanes] = later[which, tap, :8, lanes]
                    later[which, tap, :SPAN, lanes] = masked
                    result = result + conv[which, tap : tap + 1, lanes] * (
                        later[which, tap, pl.ds(taps - 1 - tap, SPAN), lanes]
                    )
            grad_pre_out[which, :, lanes] = result
    columns = lax.broadcasted_iota(jnp.int32, (SPAN, heads), 1)
    grad_beta = jnp.zeros((SPAN, heads), jnp.float32)
    for h in range(heads):
        grad_beta = jnp.where(columns == h, beta_columns[h], grad_beta)
    sigma = sigmoid(beta_pre[...])
    grad_beta_out[...] = (
        (grad_beta * lives * sigma * (1.0 - sigma)).astype(LOW).astype(jnp.float32)
    )

    @pl.when(span == 0)
    def _():
        conv_out[...] = jnp.sum(sums[...], 2)
        for which in range(3):
            result = None
            for tap in range(taps - 1):
                ahead = taps - 1 - tap
                rows = jnp.concatenate([jnp.zeros((8, later.shape[3]), jnp.float32), later[which, tap, :8]], 0)
                term = conv[which, tap : tap + 1, :] * rows[ahead:][:8]
                result = term if result is None else result + term
            borrowed_out[which] = result


def back(
    docs, place, features, beta, beta_pre, solved, inverses, starts, news, grad_mixed, state_mine,
    state_other, pre, conv, position, live,
):
    _, count, width = features.shape
    half, size, _ = state_mine.shape
    heads = 2 * half
    spans = count // SPAN
    taps = conv.shape[1]
    f32 = lambda shape: jax.ShapeDtypeStruct(shape, jnp.float32)
    whole = lambda shape: pl.BlockSpec(shape, lambda c: (0,) * len(shape))
    rows = pl.BlockSpec((SPAN, width), lambda c: (spans - 1 - c, 0))
    triple = pl.BlockSpec((3, SPAN, width), lambda c: (0, spans - 1 - c, 0))
    column = pl.BlockSpec((SPAN, heads), lambda c: (spans - 1 - c, 0))
    return pl.pallas_call(
        back_kernel,
        grid=(spans,),
        in_specs=[
            pl.BlockSpec(memory_space=pltpu.SMEM), pl.BlockSpec(memory_space=pltpu.SMEM), triple, column, column,
            pl.BlockSpec((2, SPAN, width), lambda c: (0, spans - 1 - c, 0)),
            pl.BlockSpec((1, heads // 2, 2 * SPAN, 2 * SPAN), lambda c: (spans - 1 - c, 0, 0, 0)),
            pl.BlockSpec((1, heads, size, size), lambda c: (spans - 1 - c, 0, 0, 0)),
            rows, rows, whole((half, size, size)), whole((half, size, size)),
            pl.BlockSpec((3, 1, SPAN + 8, width), lambda c: (0, spans - 1 - c, 0, 0)),
            whole(conv.shape),
            whole(position.shape), whole(live.shape),
        ],
        out_specs=[triple, whole((3, 8, width)), whole((3, taps, width)), column],
        out_shape=[
            f32((3, count, width)), f32((3, 8, width)), f32((3, taps, width)), f32((count, heads)),
        ],
        scratch_shapes=[
            pltpu.VMEM((heads, size, size), jnp.float32),
            pltpu.VMEM((3, taps - 1, SPAN + 8, width), jnp.float32),
            pltpu.VMEM((3, taps, 8, width), jnp.float32),
        ],
        compiler_params=params(),
        cost_estimate=cost(30 * count * width * size * 4, 60 * count * width),
        name="back",
    )(
        docs, place, features, beta, beta_pre, solved, inverses, starts, news, grad_mixed,
        state_mine, state_other, pre, conv, position, live,
    )


def enter_kernel(
    tokens, gain, grad_hidden, grads, grad_gate, grad_beta, query_w, key_w, value_w, gate_w, beta_w,
    input_grad_out, gain_out, total,
):
    step = pl.program_id(0)
    term = mxu(grad_gate[...].astype(LOW), gate_w[...], NT)
    for which, weight in enumerate((query_w, key_w, value_w)):
        term = term + mxu(grads[which], weight[...], NT)

    @pl.when(step == 0)
    def _():
        total[...] = term + mxu(grad_beta[...].astype(LOW), beta_w[...], NN)

    @pl.when(step > 0)
    def _():
        total[...] += term

    @pl.when(step == pl.num_programs(0) - 1)
    def _():
        part, gain_part = norm_back(tokens[...].astype(jnp.float32), gain[...], total[...])
        gain_out[...] = gain_part
        input_grad_out[...] = (grad_hidden[...] + part).astype(LOW)


def enter(
    tokens, gain, grad_hidden, grads, grad_gate, grad_beta, query_w, key_w, value_w, gate_w, beta_w
):
    count, width = tokens.shape
    heads = beta_w.shape[0]
    block = 2 * LANES
    whole = lambda shape: pl.BlockSpec(shape, lambda j: (0,) * len(shape))
    weight = pl.BlockSpec((width, block), lambda j: (0, j))
    return pl.pallas_call(
        enter_kernel,
        grid=(width // block,),
        in_specs=[
            whole((count, width)), whole((1, width)), whole((count, width)),
            pl.BlockSpec((3, count, block), lambda j: (0, 0, j)),
            pl.BlockSpec((count, block), lambda j: (0, j)), whole((count, heads)),
            weight, weight, weight, weight, whole((heads, width)),
        ],
        out_specs=[whole((count, width)), whole((1, width))],
        out_shape=[
            jax.ShapeDtypeStruct((count, width), LOW), jax.ShapeDtypeStruct((1, width), jnp.float32),
        ],
        scratch_shapes=[pltpu.VMEM((count, width), jnp.float32)],
        compiler_params=params(),
        cost_estimate=cost(8 * count * width * width, 8 * width * width + 20 * count * width),
        name="enter",
    )(
        tokens, gain, grad_hidden, grads, grad_gate, grad_beta, query_w, key_w, value_w, gate_w,
        beta_w,
    )


def passed_along(value, axis, by):
    devices = lax.axis_size(axis)
    pairs = [(i, i + by) for i in range(devices) if 0 <= i + by < devices]
    return lax.ppermute(value, axis, pairs)


def tuned():
    return (lax.axis_size("seq"), lax.axis_size("doc")) == (8, 4)


HOPS = {"core": ("doc", 1), "y": ("doc", 2), "x": ("seq", 1), "near": ("seq", 2), "far": ("seq", 4)}


def hop(value, way, other_way=None):
    if other_way in (None, way):
        axis, bit = HOPS[way]
        return lax.ppermute(value, axis, [(i, i ^ bit) for i in range(lax.axis_size(axis))])
    size = lax.axis_size("doc")
    masks = [bit * size if axis == "seq" else bit for axis, bit in (HOPS[way], HOPS[other_way])]
    pairs = [(i, i ^ masks[i % 2]) for i in range(lax.axis_size("seq") * size)]
    return lax.ppermute(value, ("seq", "doc"), pairs)


def side(way):
    axis, bit = HOPS[way]
    return lax.axis_index(axis) // bit % 2


def apply_kernel(shift, maps, *refs, turned):
    *states, out = refs
    size = maps.shape[1]
    for h in range(maps.shape[0]):
        state = states[0][h]
        for other in states[1:]:
            state = state + other[h]
        moved = (t_product if turned else product)(maps[h, :, size:], state)
        if state.shape[1] == size:
            out[h] = moved + shift[h, :, :size]
        else:
            out[h] = moved + jnp.concatenate([shift[h, :, :size], jnp.zeros((size, size), jnp.float32)], 1)


def apply_map(shift, maps, *states, turned=False):
    return pl.pallas_call(
        lambda *refs: apply_kernel(*refs, turned=turned),
        out_shape=jax.ShapeDtypeStruct(states[0].shape, jnp.float32),
        compiler_params=params(4),
        cost_estimate=cost(0, 0),
        name="apply_map",
    )(shift, maps, *states)


def ends_kernel(here, shift, maps, state, come, stay_out, send_out, *, turned):
    size = maps.shape[1]
    mine = here[0] == 0
    for h in range(maps.shape[0]):
        near = state[h] + come[h]
        far = (t_product if turned else product)(maps[h, :, size:], near) + shift[h, :, :size]
        if turned:
            near, far = far, near
        stay_out[h] = jnp.where(mine, near, far)
        send_out[h] = jnp.where(mine, far, near)


def pair_ends(here, shift, maps, state, come, turned=False):
    shape = jax.ShapeDtypeStruct(state.shape, jnp.float32)
    vmem = pl.BlockSpec(memory_space=pltpu.VMEM)
    return pl.pallas_call(
        lambda *refs: ends_kernel(*refs, turned=turned),
        in_specs=[pl.BlockSpec(memory_space=pltpu.SMEM)] + [vmem] * 4,
        out_specs=[vmem, vmem],
        out_shape=[shape, shape],
        compiler_params=params(4),
        cost_estimate=cost(0, 0),
        name="pair_ends",
    )(here, shift, maps, state, come)


def together(value, *others):
    return lax.optimization_barrier((value, *others))


def carried_forward(maps, beside):
    heads, size, _ = maps.shape
    half = heads // 2
    if not tuned():
        gathered = lax.all_gather(maps, "seq")

        def one(lap, state):
            each = lax.dynamic_index_in_dim(gathered, lap, 0, False)
            return apply_map(each, each, state)

        state = lax.fori_loop(
            0, lax.axis_index("seq"), one, jnp.zeros((heads, size, size), jnp.float32)
        )
        return state[:half], state[half:], jnp.zeros((1,), jnp.int32), (maps,)
    place = side("x").astype(jnp.int32).reshape(1)
    here = place[0] == 0
    kept = jnp.where(here, maps[:half], maps[half:])
    other = hop(jnp.where(here, maps[half:], maps[:half]), "x")
    other, *beside = together(other, *beside)
    first, second = jnp.where(here, kept, other), jnp.where(here, other, kept)
    pair_map = apply_map(second, second, first)
    state = jnp.zeros((half, size, size), jnp.float32)
    come = state
    for step in range(3):
        if step == 0:
            sent = pair_map[:, :, :size]
        else:
            sent = apply_map(pair_map, pair_map, state, come)
            state = state + come
        come = lax.ppermute(sent, "seq", [(2 * step + x, 2 * step + 2 + x) for x in range(2)])
    mine, send = pair_ends(place, first, first, state, come)
    return mine, hop(send, "x"), place, (first, second, pair_map), *beside


def carried_back(shift, context, beside=None):
    heads, size, _ = shift.shape
    half = heads // 2
    if not tuned():
        gathered = lax.all_gather(jnp.concatenate([shift, context[0][:, :, size:]], 2), "seq")
        count = lax.axis_size("seq")

        def one(lap, state):
            each = lax.dynamic_index_in_dim(gathered, count - 1 - lap, 0, False)
            return apply_map(each, each, state, turned=True)

        zeros = jnp.zeros((heads, size, size), jnp.float32)
        state = lax.fori_loop(0, count - 1 - lax.axis_index("seq"), one, zeros)
        return state[:half], state[half:], ()
    first, second, pair_map = context
    place = side("x").astype(jnp.int32).reshape(1)
    here = place[0] == 0
    done = []

    def step_with(number, sent, go):
        moves, work = beside[number]
        sent, *values = together(sent, *[move[0] for move in moves])
        come, *rest = together(
            go(sent), *[hop(value, *move[1:]) for value, move in zip(values, moves)], *work
        )
        done.append(rest)
        return come

    kept = jnp.where(here, shift[:half], shift[half:])
    other = step_with(0, jnp.where(here, shift[half:], shift[:half]), lambda value: hop(value, "x"))
    first_shift, second_shift = jnp.where(here, kept, other), jnp.where(here, other, kept)
    pair_shift = apply_map(first_shift, first, second_shift, turned=True)
    state = jnp.zeros((half, size, size), jnp.float32)
    come = state
    for step in range(3, 0, -1):
        if step == 3:
            sent = pair_shift
        else:
            sent = apply_map(pair_shift, pair_map, state, come, turned=True)
            state = state + come
        pairs = [(2 * step + x, 2 * step - 2 + x) for x in range(2)]
        come = step_with(4 - step, sent, lambda value: lax.ppermute(value, "seq", pairs))
    mine, send = pair_ends(place, second_shift, second, state, come, turned=True)
    return mine, step_with(4, send, lambda value: hop(value, "x")), done


def outer_kernel(table, *refs, blocks, pieces):
    count = len(blocks)
    lefts, rights = refs[: 2 * count], refs[2 * count : 4 * count]
    *outs, stacked = refs[4 * count :]
    step = pl.program_id(0)
    tokens = lefts[0].shape[1]
    size = outs[0].shape[0] // 8

    @pl.when(step == 0)
    def _():
        for piece in range(count):
            for which in range(2):
                for place in range(16):
                    rows = pl.ds(pl.multiple_of(table[place] * size, 16), size)
                    stacked[
                        piece, place * size : (place + 1) * size, which * tokens : (which + 1) * tokens
                    ] = lefts[2 * piece + which][rows, :].astype(LOW)

    for piece in range(count):
        low = sum(blocks[:piece])

        @pl.when((step >= low) & (step < low + blocks[piece]))
        def _(piece=piece):
            right = jnp.concatenate(
                [rights[2 * piece][...].astype(LOW), rights[2 * piece + 1][...].astype(LOW)], 0
            )
            place = 0
            for out, number in zip(outs, (8 * size, *pieces)):
                out[...] = mxu(stacked[piece, place : place + number, :], right, NN)
                place += number


WEIGHTS = {"far": 8, "near": 4, "x": 2, "y": 1}


def by_core(values):
    return jnp.where(side("core") == 0, values[0], values[1])


def outer(pieces, orders, parts=(1,)):
    rows, tokens = pieces[0][0].shape
    double = all(piece[4] % 2 == 0 and piece[5] % 2 == 0 for piece in pieces)
    block = (4 if double else 2) * LANES
    table = []
    for place in range(16):
        entries = []
        for order in orders:
            bits = [place >> 3 & 1, place >> 2 & 1, place >> 1 & 1, place & 1]
            first = side(order[0]) ^ bits[0]
            rest = sum(bit * WEIGHTS[way] for bit, way in zip(bits[1:], order[1:]))
            entries.append(first * WEIGHTS[order[0]] + rest)
        table.append(by_core(entries))
    table = jnp.stack(table).astype(jnp.int32)
    if double:
        pieces = [(*piece[:4], piece[4] // 2, piece[5] // 2) for piece in pieces]
    counts = [piece[5] for piece in pieces]
    left = pl.BlockSpec((rows, tokens), lambda j: (0, 0), pipeline_mode=pl.Buffered(1))
    lefts, rights, specs = [], [], []
    for index, piece in enumerate(pieces):
        lefts += piece[:2]
        rights += piece[2:4]

        def place(j, low=sum(counts[:index]), first=piece[4], number=piece[5]):
            return 0, first + jnp.clip(j - low, 0, number - 1)

        specs += [pl.BlockSpec((tokens, block), place)] * 2
    total = sum(counts)
    sizes = [rows // 2 * part // sum(parts) // 16 * 16 for part in parts[:-1]]
    sizes = [*sizes, rows // 2 - sum(sizes)]
    outs = [rows // 2, *sizes]
    keep, *sends = pl.pallas_call(
        lambda *refs: outer_kernel(*refs, blocks=counts, pieces=sizes),
        grid=(total,),
        in_specs=[pl.BlockSpec(memory_space=pltpu.SMEM)] + [left] * len(lefts) + specs,
        out_specs=[pl.BlockSpec((size, block), lambda j: (0, j)) for size in outs],
        out_shape=[jax.ShapeDtypeStruct((size, total * block), jnp.float32) for size in outs],
        scratch_shapes=[pltpu.VMEM((len(pieces), rows, 2 * tokens), LOW)],
        compiler_params=params(),
        cost_estimate=cost(0, 0),
        name="outer",
    )(table, *lefts, *rights)
    return keep, sends


def take(value, place, axis):
    return lax.dynamic_index_in_dim(value, place, axis, False)


class Part:
    def __init__(self, keeps, comes, orders, split_y=True):
        self.orders, self.split_y, self.stage = orders, split_y, 1
        self.groups = [[self.shaped(value) for value in group] for group in zip(keeps, comes)]
        self.terms = []

    def shaped(self, value):
        left = tuple(range(self.stage, len(self.orders[0])))
        columns = value.shape[-1]
        rows = value.size // columns // 2 ** len(left)
        return value.reshape((2,) * len(left) + (rows, columns)), left

    def add(self, come):
        self.terms.append(self.shaped(come))

    def place(self, stage):
        return by_core([side(order[stage]) for order in self.orders])

    def chosen(self, here):
        sums = [self.added(group, here) for group in self.groups]
        total = sums[0] if len(sums) == 1 else jnp.concatenate(sums, -1)
        return total + self.added(self.terms, here) if self.terms else total

    def added(self, terms, here):
        total = None
        for value, left in terms:
            starts, sizes = [], []
            for stage in left:
                fixed = stage <= self.stage
                place = self.place(stage) if fixed else 0
                starts.append(1 - place if stage == self.stage and not here else place)
                sizes.append(1 if fixed else 2)
            sizes += value.shape[len(left) :]
            starts = [jnp.asarray(start, jnp.int32) for start in [*starts, 0, 0]]
            piece = lax.dynamic_slice(value, starts, sizes)
            piece = piece.reshape([size for size in sizes[:-2] if size > 1] + sizes[-2:])
            total = piece if total is None else total + piece
        return total

    def move(self):
        if self.stage < len(self.orders[0]):
            send = self.chosen(False)
            ways = [order[self.stage] for order in self.orders]
            self.stage += 1
            self.absorb = self.add
            return send, *ways
        if self.stage == len(self.orders[0]):
            mine = self.chosen(True)
            self.stage += 1

            def absorb(come):
                self.done = in_order(mine, come) if self.split_y else mine + come

            self.absorb = absorb
            return mine, "y"
        self.absorb = lambda come: setattr(self, "other", come)
        return self.done, "core"


def in_order(mine, come):
    first = side("y") == 0
    return jnp.concatenate([jnp.where(first, mine, come), jnp.where(first, come, mine)], 0)


def advance(parts, extra=(), beside=()):
    moves = [part.move() for part in parts] + list(extra)
    values = together(*[move[0] for move in moves])
    comes = [hop(value, *move[1:]) for value, move in zip(values, moves)]
    done = together(*comes, *beside)
    for part, come in zip(parts, done):
        part.absorb(come)
    done = done[len(parts) :]
    return done[: len(extra)], done[len(extra) :]


def flatten_small(small):
    first_gain, beta, conv, head_gain, second_gain = small
    seq = lax.axis_size("seq")
    flat = jnp.concatenate(
        [
            first_gain.reshape(seq, -1), beta.reshape(seq, -1),
            conv.reshape(conv.shape[0] * conv.shape[1], seq, -1).transpose(1, 0, 2).reshape(seq, -1),
            head_gain.reshape(seq, -1), second_gain.reshape(seq, -1),
        ],
        1,
    )
    size = flat.shape[1]
    rows = -(-size // 2048) * 16
    return jnp.pad(flat, ((0, 0), (0, rows * 128 - size))).reshape(seq * rows, 128)


def unflatten_small(flat, small):
    first_gain, beta, conv, head_gain, second_gain = small
    seq = lax.axis_size("seq")
    flat = flat.reshape(-1)
    sizes = [a.size // seq for a in small]
    places = [sum(sizes[:i]) for i in range(len(sizes))]
    pieces = [flat[p : p + s] for p, s in zip(places, sizes)]
    return (
        pieces[0], pieces[1].reshape(-1, beta.shape[1]),
        pieces[2].reshape(conv.shape[0], conv.shape[1], -1), pieces[3], pieces[4],
    )


def outer_sum(left, right):
    return mxu(left.astype(LOW), right.astype(LOW), TN)


def local(
    tokens,
    doc_lengths,
    out_grad,
    first_gain,
    query_weight,
    key_weight,
    value_weight,
    gate_weight,
    beta_weight,
    conv_weight,
    head_gain,
    out_weight,
    second_gain,
    hidden_gate,
    hidden_up,
    hidden_down,
):
    count, width = (tokens.shape[1], tokens.shape[2])
    heads = beta_weight.shape[1]
    reach = conv_weight.shape[1] - 1
    first = lax.axis_index("seq") * count
    docs = jnp.concatenate([first.astype(jnp.int32)[None], doc_lengths[0]])
    core = (lax.axis_index("doc") % 2).astype(jnp.int32).reshape(1)
    here = core[0] == 0
    rows, top = tokens[0], out_grad[0]
    halo = passed_along(rows[count - HALO :].astype(jnp.float32), "seq", 1)
    normed_one, pre, features, gate_pre, beta_pre, beta, position, live = project(
        docs, rows, halo, first_gain[None], query_weight, key_weight, value_weight,
        gate_weight, beta_weight.T, conv_weight,
    )
    solved, inverses, attend, maps = prepare(docs, features, beta)
    if tuned():
        half = width // 2
        units = half // 256

        def pick(zero, one):
            return jnp.where(here, zero, one)

        def both(value, send=None):
            return value, hop(value if send is None else send, "core")

        wide_top = top.astype(jnp.float32)
        tops = both(
            pick(top[:, :half], top[:, half:]), pick(wide_top[:, half:], wide_top[:, :half])
        )
        one = both(normed_one)
    state_mine, state_other, place, context, *beside = carried_forward(
        maps, (*tops, *one) if tuned() else ()
    )
    if tuned():
        tops, one = beside[:2], beside[2:]
    starts, news, mixed, normed_head = mix(
        docs, place, features, solved, attend, gate_pre, head_gain[None], state_mine, state_other
    )
    (
        block_out, two_turned, inner_turned, kept, sent, grad_hidden, grad_branch, grad_head,
        grad_second_gain, head_turned,
    ) = feed(
        core, rows, normed_head, top, second_gain[None], out_weight, hidden_gate, hidden_up,
        hidden_down,
    )
    if tuned():
        heads_turned = both(head_turned)
        two = both(two_turned)
        gate_up = both(kept, sent)
    grad_mixed, grad_gate_pre, out_kept, out_sent, grad_head_gain, shift = gather_states(
        docs, core, grad_head, grad_branch, mixed, gate_pre, head_gain[None], features, solved, heads
    )
    if tuned():
        out_right = both(out_kept, out_sent)
        blocks = hidden_gate.shape[1] // 256
        some = blocks * 3 // 11
        blocks = hidden_gate.shape[1] // 256
        low = blocks * 8 // 11
        orders = ("x", "y", "near", "far"), ("y", "x", "far", "near")
        down_orders = ("near", "x", "y", "far"), ("near", "y", "x", "far")
        firsts = [order[0] for order in orders]
        shift, two_other, gate_up_other, inner_turned = together(
            shift, two[1], gate_up[1], inner_turned
        )
        inners = both(inner_turned)
        two, gate_up = (two[0], two_other), (gate_up[0], gate_up_other)
        out_right = both(out_kept, out_sent)
        wide_keep, wide_sends = outer([(*two, *gate_up, 0, low)], orders, (9, 9, 9, 5))
        down_keep, down_sends = outer([(*inners, *tops, 0, units)], down_orders, (3, 4))
        rest_keep, rest_sends = outer(
            [
                (*two, *gate_up, low, blocks - low), (*heads_turned, *out_right, 0, units),
                (*one, *out_right, units, units),
            ],
            orders,
        )
        work = [
            (wide_keep, *wide_sends), (down_keep, *down_sends), (rest_keep, *rest_sends), (), (),
        ]
        moves = [(), *([(send, *firsts)] for send in wide_sends)]
        grad_mine, grad_other, done = carried_back(shift, context, list(zip(moves, work)))
        down_keep, *down_sends = done[1][1:]
        rest_keep, *rest_sends = done[2][1:]
        wide_come = jnp.concatenate([value[0] for value in done[1:]], 0)
        moves = [(rest_sends[0], *firsts), (down_sends[0], "near")]
        grad_other, *values = together(grad_other, *[move[0] for move in moves])
        comes = [hop(value, *move[1:]) for value, move in zip(values, moves)]
    else:
        grad_mine, grad_other, _ = carried_back(shift, context)
    grads, borrowed, grad_conv, grad_beta_pre = back(
        docs, place, features, beta, beta_pre, solved, inverses, starts, news, grad_mixed, grad_mine,
        grad_other, pre, conv_weight, position, live,
    )
    if tuned():
        borrowed, *comes = together(borrowed, *comes)
        wide_part = Part((wide_keep, rest_keep), (wide_come, comes[0]), orders)
        down_come = comes[1]
    returned = passed_along(borrowed, "seq", -1)
    tail = grads[:, count - 8 :] + returned
    grads = lax.dynamic_update_slice(grads, tail, (0, count - 8, 0))
    grads = grads.astype(LOW)
    if tuned():
        moves = [wide_part.move(), (down_sends[1], "near")]
        grads, *values = together(grads, *[move[0] for move in moves])
        comes = [hop(value, *move[1:]) for value, move in zip(values, moves)]
        wide = grads.astype(jnp.float32)
        query_key = both(pick(grads[0], grads[1]), pick(wide[1], wide[0]))
        value = both(
            pick(grads[2, :, :half], grads[2, :, half:]), pick(wide[2, :, half:], wide[2, :, :half])
        )
        late_keep, (late_send,) = outer(
            [(*one, *query_key, 0, 2 * units), (*one, *value, 0, units)], orders
        )
        grads, late_send, *comes = together(grads, late_send, *comes)
        wide_part.absorb(comes[0])
        down = Part((down_keep,), (jnp.concatenate([down_come, comes[1]], 0),), down_orders)
        input_grad, grad_first_gain = enter(
            rows, first_gain[None], grad_hidden, grads, grad_gate_pre, grad_beta_pre, query_weight,
            key_weight, value_weight, gate_weight, beta_weight.T,
        )
        small = (
            grad_first_gain[0], outer_sum(normed_one.T, grad_beta_pre), grad_conv, grad_head_gain[0],
            grad_second_gain[0],
        )
        flat = flatten_small(small)
        (come,), (flat, input_grad) = advance(
            [wide_part, down], [(late_send, *firsts)], (flat, input_grad)
        )
        late = Part((late_keep,), (come,), orders)
        (come,), _ = advance([late, wide_part, down], [(flat, "core")])
        flat = (flat + come).reshape(2, 2, 2, -1, 128).transpose(2, 1, 0, 3, 4)
        bit = side("x")
        tiny_keep, tiny_send = (take(flat, place, 0).reshape(-1, 128) for place in (bit, 1 - bit))
        (come,), _ = advance([late, down, wide_part], [(tiny_send, "x")])
        tiny = Part((tiny_keep,), (come,), (("x", "near", "far"),) * 2, False)
        advance([late, down, wide_part, tiny])
        advance([late, down, tiny])
        advance([late, tiny])
        zero = lambda part: pick(part.done, part.other)
        one_ = lambda part: pick(part.other, part.done)
        split = blocks * 256
        hidden_gate_g, hidden_up_g = (
            of(wide_part)[:, : blocks * 256] for of in (zero, one_)
        )
        out_g, gate_g = (
            jnp.concatenate([zero(wide_part)[:, places], one_(wide_part)[:, places]], 1)
            for places in (slice(split, split + half), slice(split + half, split + width))
        )
        query_g, key_g = zero(late)[:, :width], one_(late)[:, :width]
        value_g = jnp.concatenate([zero(late)[:, width:], one_(late)[:, width:]], 1)
        hidden_down_g = jnp.concatenate([zero(down), one_(down)], 1)
        first_g, beta_g, conv_g, head_g, second_g = unflatten_small(tiny.done, small)
    else:
        input_grad, grad_first_gain = enter(
            rows, first_gain[None], grad_hidden, grads, grad_gate_pre, grad_beta_pre, query_weight,
            key_weight, value_weight, gate_weight, beta_weight.T,
        )
        small = (
            grad_first_gain[0], outer_sum(normed_one.T, grad_beta_pre), grad_conv, grad_head_gain[0],
            grad_second_gain[0],
        )

        def whole(term, dimension):
            part = lax.psum_scatter(term, "seq", scatter_dimension=dimension, tiled=True)
            return lax.psum(part, "doc")

        gate_grad, up_grad = jnp.where(here, kept, sent), jnp.where(here, sent, kept)
        terms = (
            outer_sum(normed_one.T, grads[0]), outer_sum(normed_one.T, grads[1]),
            outer_sum(normed_one.T, grads[2]), outer_sum(normed_one.T, grad_gate_pre),
            outer_sum(head_turned.T, grad_branch), outer_sum(two_turned.T, gate_grad),
            outer_sum(two_turned.T, up_grad), outer_sum(inner_turned.T, top),
        )
        query_g, key_g, value_g, gate_g, out_g, hidden_gate_g, hidden_up_g, hidden_down_g = (
            whole(term, 0) for term in terms
        )
        first_g, beta_g, conv_g, head_g, second_g = (
            whole(term, d) for term, d in zip(small, (0, 0, 2, 0, 0))
        )
    return (
        block_out[None], input_grad[None], first_g, query_g, key_g, value_g, gate_g, beta_g, conv_g,
        head_g, out_g, second_g, hidden_gate_g, hidden_up_g, hidden_down_g,
    )


def solution(mesh):
    in_specs = (
        P("doc", "seq", None),
        P("doc", None),
        P("doc", "seq", None),
        P(),
        P(),
        P(),
        P(),
        P(),
        P(),
        P(),
        P(),
        P(),
        P(),
        P(),
        P(),
        P(),
    )
    out_specs = (
        P("doc", "seq", None),
        P("doc", "seq", None),
        P("seq"),
        P("seq", None),
        P("seq", None),
        P("seq", None),
        P("seq", None),
        P("seq", None),
        P(None, None, "seq"),
        P("seq"),
        P("seq", None),
        P("seq"),
        P("seq", None),
        P("seq", None),
        P("seq", None),
    )
    return jax.shard_map(local, mesh=mesh, in_specs=in_specs, out_specs=out_specs, check_vma=False)
```
